32 devices in a mesh: parts: 2 (over y), gx: 16 (over z, x, core).
Axes of the slice: x: 2, y: 2, z: 4, core: 2. Of those that a mesh axis runs over, the one named last changes fastest.
Arguments:
- embeddings: bfloat16 [8192, 1024], P(('parts', 'gx')), parts along dimension 0, may hold values from -6 to 6
- cluster_ids: int32 [8192], P(('parts', 'gx')), parts along dimension 0, may hold values from 0 to 15, as said below
Outputs:
- density: float32 [8192], P(('parts', 'gx')), parts along dimension 0
The draws below stay inside these ranges and needn't reach their ends.
There are 2 independent parts, one for each index of `parts`. The reference program is written for one: setup_inputs(seed, part) draws one part's arguments, and reference() takes and returns one part's arrays. A program takes and returns all parts, laid end to end along the dimension named above; each array names one. Nothing has to cross between parts.
Inputs may be any that keep to these rules, and one draw needn't show every extreme that they name: `cluster_ids`: the owner of cluster c is c. Among the 256 rows of one device, at most 48 belong to clusters of one owner, and in every device's rows some owner has exactly 48.
All inputs are finite; a program needn't handle non-finite values.
Results may differ from the reference program's by a relative error of at most 0.0003.
Values may be sent and summed in bfloat16 or wider, within the bound.
No kernel may reach another device: no remote copies, remote signals or barrier semaphores. Data moves between devices by JAX's collectives and lax.ppermute only.
A program may use at most 64 MiB of HBM per device.

```python
import jax
import jax.numpy as jnp
from jax import lax

D = 1024
ROWS_DEV = 256
CLU_DEV = 1
ROWS = 4096
CAP = 48
N_GX = 16


def draw_cluster_ids(key, part):
    key = jax.random.fold_in(key, 7)
    slots_all = N_GX * CAP
    bias_key, block_key = jax.random.split(key)
    owner_bias = jax.random.randint(bias_key, (N_GX,), 0, slots_all)
    slot_owner = jnp.arange(slots_all, dtype=jnp.int32) // CAP
    slot_within = jnp.arange(slots_all, dtype=jnp.int32) % CAP

    def one_block(sub):
        rank_key, hot_key, shuffle_key, local_key = jax.random.split(sub, 4)
        rank_order = jax.random.permutation(rank_key, slots_all).astype(jnp.int32)
        hot_owner = jax.random.randint(hot_key, (), 0, N_GX)
        priority = (rank_order + owner_bias[slot_owner]) * slots_all + rank_order
        priority = jnp.where(slot_owner == hot_owner, slot_within - CAP, priority)
        chosen = jnp.argsort(priority, stable=True)[:ROWS_DEV]
        owner_rows = slot_owner[chosen]
        owner_rows = owner_rows[jax.random.permutation(shuffle_key, ROWS_DEV)]
        local_cluster = jax.random.randint(local_key, (ROWS_DEV,), 0, CLU_DEV)
        return owner_rows * CLU_DEV + local_cluster
    blocks = jax.vmap(one_block)(jax.random.split(block_key, N_GX))
    return blocks.reshape(-1).astype(jnp.int32)


def levels(stream_key, dims, cuts, least, largest):
    level = 1.0
    for position, shards_of in cuts:
        draws = jax.random.uniform(jax.random.fold_in(jax.random.fold_in(stream_key, 6), position), (shards_of,), jnp.float32, least / len(cuts), largest / len(cuts))
        level = level * jnp.repeat(jnp.exp(draws), dims[position] // shards_of).reshape((-1,) + (1,) * (len(dims) - 1 - position))
    return level


def gaussian(key, dims, scale, limit, shards=(), kind=jnp.bfloat16):
    entries = scale * jax.random.normal(key, dims, jnp.float32)
    if shards:
        entries = entries * levels(key, dims, shards, -0.22, 0.18)
    return jnp.clip(entries, -limit, limit).astype(kind)


def setup_inputs(seed: int = 0, part: int = 0) -> dict:
    streams_of = jax.random.split(jax.random.key(seed), 3)
    part_splits = jax.random.split(jax.random.fold_in(streams_of[2], part), 3)
    embeddings = gaussian(part_splits[0], (ROWS, D), 1.0, 6.0, ((0, 16),))
    cluster_ids = draw_cluster_ids(jax.random.fold_in(jax.random.fold_in(streams_of[2], part), 71), part)
    return dict(embeddings=embeddings, cluster_ids=cluster_ids)


inverse_temp = 20.0

def reference(embeddings, cluster_ids):
    features_f = embeddings.astype(jnp.float32)
    squares = lax.optimization_barrier(jnp.sum(features_f * features_f, axis=1))
    unit_rows = (features_f * lax.rsqrt(squares + 1e-06)[:, None]).astype(jnp.bfloat16)
    owner_of = (cluster_ids // CLU_DEV).astype(jnp.int32)
    sorted_order = jnp.argsort(owner_of, stable=True).astype(jnp.int32)
    sorted_rows = unit_rows[sorted_order]
    sorted_ids = cluster_ids[sorted_order]
    owner_range = jnp.arange(N_GX, dtype=jnp.int32)
    counts = lax.optimization_barrier(jnp.sum((owner_of[:, None] == owner_range[None, :]).astype(jnp.int32), axis=0)).astype(jnp.int32)
    starts = (jnp.cumsum(counts) - counts).astype(jnp.int32)
    window = N_GX * CAP
    padded_rows = jnp.concatenate([sorted_rows, jnp.zeros((window, D), sorted_rows.dtype)], axis=0)
    padded_ids = jnp.concatenate([sorted_ids, jnp.full((window,), -1, jnp.int32)], axis=0)
    positions = jnp.arange(window, dtype=jnp.int32)

    def one_owner(owner):
        start = starts[owner]
        block_rows = lax.dynamic_slice_in_dim(padded_rows, start, window, 0).astype(jnp.float32)
        block_ids = lax.dynamic_slice_in_dim(padded_ids, start, window, 0)
        block_ids = jnp.where(positions < counts[owner], block_ids, -1)
        similar = jnp.dot(block_rows, block_rows.T, precision=lax.Precision.HIGHEST)
        mate_mask = (block_ids[:, None] == block_ids[None, :]) & (block_ids[:, None] >= 0)
        mate_mask = mate_mask & (positions[:, None] != positions[None, :])
        mass_sum = lax.optimization_barrier(jnp.sum(jnp.where(mate_mask, jnp.exp(similar * inverse_temp), 0.0), axis=1))
        return jnp.log1p(mass_sum)
    per_owner = lax.map(one_owner, owner_range)
    targets = starts[:, None] + positions[None, :]
    valid = positions[None, :] < counts[:, None]
    targets = jnp.where(valid, targets, ROWS).astype(jnp.int32)
    sorted_scores = jnp.zeros((ROWS,), jnp.float32).at[targets.reshape(-1)].add(jnp.where(valid, per_owner, 0.0).reshape(-1), mode='drop')
    return jnp.zeros((ROWS,), jnp.float32).at[sorted_order].set(sorted_scores)
```

```python
import functools

import jax
import jax.numpy as jnp
from jax import lax
from jax.experimental import pallas as pl
from jax.experimental.pallas import tpu as pltpu
from jax.sharding import PartitionSpec as P

CLU_DEV = 1
PAD_MARK = 64.0
inverse_temp = 20.0


def tile_mass(query_rows, key_rows, query_ids, key_ids, query_start):
    similar = lax.dot_general(
        query_rows, key_rows, (((1,), (1,)), ((), ())), preferred_element_type=jnp.float32
    )
    query_pos = jnp.arange(query_rows.shape[0], dtype=jnp.int32) + query_start
    key_pos = jnp.arange(key_rows.shape[0], dtype=jnp.int32)
    mate_mask = (query_ids[:, None] == key_ids[None, :]) & (query_ids[:, None] >= 0)
    mate_mask = mate_mask & (query_pos[:, None] != key_pos[None, :])
    return jnp.where(mate_mask, jnp.exp(similar * inverse_temp), 0.0)


def density_scores(key_rows, key_ids):
    total_rows = key_rows.shape[0]
    block_rows = total_rows // 3
    pieces = [key_rows[i * block_rows : (i + 1) * block_rows] for i in range(3)]
    piece_ids = [key_ids[i * block_rows : (i + 1) * block_rows] for i in range(3)]
    sums = []
    for first in range(3):
        masses = tile_mass(pieces[first], key_rows, piece_ids[first], key_ids, first * block_rows)
        sums.append(jnp.sum(masses, axis=1))
    mass_sum = jnp.concatenate(sums, axis=0)
    return jnp.log1p(mass_sum)


def plain_plan(embeddings, cluster_ids):
    peer_count = lax.axis_size("gx")
    row_count = embeddings.shape[0]
    features = embeddings.shape[1]
    capacity = 3 * row_count // peer_count
    slot_total = peer_count * capacity
    squares = jnp.sum(jnp.square(embeddings.astype(jnp.float32)), axis=1)
    unit_rows = (embeddings.astype(jnp.float32) * lax.rsqrt(squares + 1e-06)[:, None]).astype(
        jnp.bfloat16
    )
    owner_of = cluster_ids // CLU_DEV
    onehot = (owner_of[:, None] == jnp.arange(peer_count, dtype=jnp.int32)[None, :]).astype(
        jnp.bfloat16
    )
    row_range = jnp.arange(row_count, dtype=jnp.int32)
    lower_tri = (row_range[:, None] >= row_range[None, :]).astype(jnp.bfloat16)
    running = jnp.dot(lower_tri, onehot, preferred_element_type=jnp.float32)
    slot_index = (jnp.sum(running * onehot.astype(jnp.float32), axis=1) - 1.0).astype(jnp.int32)
    target_slot = owner_of * capacity + slot_index
    slot_range = jnp.arange(slot_total, dtype=jnp.int32)
    select_mask = slot_range[:, None] == target_slot[None, :]
    outgoing = jnp.dot(
        select_mask.astype(jnp.bfloat16), unit_rows, preferred_element_type=jnp.float32
    )
    outgoing = outgoing.astype(jnp.bfloat16).reshape(peer_count, capacity, features)
    outgoing_ids = jnp.sum(jnp.where(select_mask, cluster_ids[None, :] + 1, 0), axis=1) - 1
    outgoing_ids = outgoing_ids.reshape(peer_count, capacity)
    arrived, arrived_ids = (
        lax.all_to_all(outgoing, "gx", split_axis=0, concat_axis=0, tiled=True),
        lax.all_to_all(outgoing_ids, "gx", split_axis=0, concat_axis=0, tiled=True),
    )
    key_rows = arrived.reshape(slot_total, features)
    key_ids = arrived_ids.reshape(slot_total)
    scores = density_scores(key_rows, key_ids)
    returned = lax.all_to_all(
        scores.reshape(peer_count, capacity), "gx", split_axis=0, concat_axis=0, tiled=True
    )
    flat_scores = returned.reshape(slot_total)
    pick_mask = target_slot[:, None] == slot_range[None, :]
    return jnp.sum(jnp.where(pick_mask, flat_scores[None, :], 0.0), axis=1)


LANES = 128
PLANE = 4
ID_ROWS = 16


def unit_kernel(rows_ref, ids_ref, block_ref):
    row_count, width = rows_ref.shape
    features = rows_ref[...].astype(jnp.float32)
    squares = jnp.sum(features * features, axis=1, keepdims=True)
    block_ref[:row_count, :] = (features * lax.rsqrt(squares + 1e-06)).astype(jnp.bfloat16)
    block_ref[row_count:, :] = jnp.zeros((ID_ROWS, width), jnp.bfloat16)
    block_ref[row_count:, :row_count] = jnp.broadcast_to(
        ids_ref[...].astype(jnp.float32), (ID_ROWS, row_count)
    ).astype(jnp.bfloat16)


def ids_along_lanes(block_ref):
    row_count = block_ref.shape[0] - ID_ROWS
    return block_ref[row_count:, :row_count].astype(jnp.float32)[:1]


def ids_along_rows(block_ref):
    ids = ids_along_lanes(block_ref)
    return jnp.broadcast_to(ids, (LANES, ids.shape[1])).T


def mate_mass(query_rows, query_ids, key_rows, key_ids, same_block):
    similar = lax.dot_general(
        query_rows, key_rows, (((1,), (1,)), ((), ())), preferred_element_type=jnp.float32
    )
    repeats = similar.shape[1] // LANES
    mates = jnp.concatenate([query_ids] * repeats, axis=1) == key_ids
    if same_block:
        query_pos = lax.broadcasted_iota(jnp.int32, similar.shape, 0)
        key_pos = lax.broadcasted_iota(jnp.int32, similar.shape, 1)
        mates = mates & (query_pos != key_pos)
    return jnp.where(mates, jnp.exp(similar * inverse_temp), 0.0)


def score_kernel(planes, *refs):
    plane_refs, line_refs = refs[:PLANE], refs[PLANE : PLANE + 2]
    row_refs, column_refs = refs[PLANE + 2 : 2 * PLANE + 2], refs[2 * PLANE + 2 : -2]
    row_ids, lane_sums = refs[-2:]
    rows = row_refs[0].shape[1]
    plane = lax.axis_index("gx") // PLANE
    own_ref = plane_refs[0]
    own_ids = ids_along_lanes(own_ref)
    own_mass = jnp.zeros((1, rows), jnp.float32)
    for m in range(PLANE):
        part = pl.ds(m * rows, rows)
        query_ids = ids_along_rows(plane_refs[m])
        row_ids[part, :] = query_ids
        masses = mate_mass(
            plane_refs[m][:rows, :], query_ids, own_ref[:rows, :], own_ids, m == 0
        )
        own_mass = own_mass + jnp.sum(masses, axis=0, keepdims=True)
    lane_sums[...] = jnp.zeros_like(lane_sums)
    for n in range(2):
        line_ref, column_ref = line_refs[n], column_refs[n]
        column_ref[...] = jnp.zeros_like(column_ref)
        arrived = plane != (planes - 1 if n == 0 else 0)

        @pl.when(arrived)
        def _():
            key_ids = ids_along_lanes(line_ref)
            for m in range(PLANE):
                part = pl.ds(m * rows, rows)
                masses = mate_mass(
                    plane_refs[m][:rows, :], row_ids[part, :], line_ref[:rows, :], key_ids, False
                )
                column_ref[...] += jnp.sum(masses, axis=0, keepdims=True)
                folded = masses[:, :LANES]
                for first in range(LANES, rows, LANES):
                    folded = folded + masses[:, first : first + LANES]
                lane_sums[part, :] += folded

    for m in range(PLANE):
        part = pl.ds(m * rows, rows)
        row_sum = jnp.sum(lane_sums[part, :].T, axis=0, keepdims=True)
        row_refs[m][...] = own_mass + row_sum if m == 0 else row_sum


def grid_plan(embeddings, cluster_ids):
    peers = lax.axis_size("gx")
    row_count, features = embeddings.shape
    planes = peers // PLANE

    def in_plane(value, step):
        return lax.ppermute(value, "gx", [(i, i ^ step) for i in range(peers)])

    def on_line(value, moves):
        pairs = [(a * PLANE + n, b * PLANE + n) for a, b in moves for n in range(PLANE)]
        return lax.ppermute(value, "gx", pairs)

    first_moves = [(0, 1), (3, 2), (2, 0)]
    second_moves = [(1, 2), (0, 3), (3, 1)]
    first_back = [(b, a) for a, b in first_moves]
    second_back = [(b, a) for a, b in second_moves]

    block = pl.pallas_call(
        unit_kernel,
        out_shape=jax.ShapeDtypeStruct((row_count + ID_ROWS, features), jnp.bfloat16),
    )(embeddings, cluster_ids.reshape(1, row_count))
    plane_blocks = [block] + [in_plane(block, step) for step in range(1, PLANE)]
    line_blocks = [on_line(block, first_moves), on_line(block, second_moves)]
    vector = jax.ShapeDtypeStruct((1, row_count), jnp.float32)
    sums = pl.pallas_call(
        functools.partial(score_kernel, planes),
        out_shape=[vector] * (PLANE + 2),
        scratch_shapes=[pltpu.VMEM((PLANE * row_count, LANES), jnp.float32)] * 2,
    )(*plane_blocks, *line_blocks)
    mass = sums[0]
    for step in range(1, PLANE):
        mass = mass + in_plane(sums[step], step)
    mass = mass + on_line(sums[PLANE], first_back) + on_line(sums[PLANE + 1], second_back)
    return jnp.log1p(mass).reshape(row_count)


def on_device(embeddings, cluster_ids):
    if lax.axis_size("gx") == 4 * PLANE and embeddings.shape[0] % LANES == 0:
        return grid_plan(embeddings, cluster_ids)
    return plain_plan(embeddings, cluster_ids)


def solution(mesh):
    in_specs = (P(("parts", "gx"), None), P(("parts", "gx")))
    out_specs = P(("parts", "gx"))
    return jax.shard_map(
        on_device, mesh=mesh, in_specs=in_specs, out_specs=out_specs, check_vma=False
    )
```

```python
import functools

import jax
import jax.numpy as jnp
from jax import lax
from jax.experimental import pallas as pl
from jax.experimental.pallas import tpu as pltpu
from jax.sharding import PartitionSpec as P

CLU_DEV = 1
PAD_MARK = 64.0
inverse_temp = 20.0


def tile_mass(query_rows, key_rows, query_ids, key_ids, query_start):
    similar = lax.dot_general(
        query_rows, key_rows, (((1,), (1,)), ((), ())), preferred_element_type=jnp.float32
    )
    query_pos = jnp.arange(query_rows.shape[0], dtype=jnp.int32) + query_start
    key_pos = jnp.arange(key_rows.shape[0], dtype=jnp.int32)
    mate_mask = (query_ids[:, None] == key_ids[None, :]) & (query_ids[:, None] >= 0)
    mate_mask = mate_mask & (query_pos[:, None] != key_pos[None, :])
    return jnp.where(mate_mask, jnp.exp(similar * inverse_temp), 0.0)


def density_scores(key_rows, key_ids):
    total_rows = key_rows.shape[0]
    block_rows = total_rows // 3
    pieces = [key_rows[i * block_rows : (i + 1) * block_rows] for i in range(3)]
    piece_ids = [key_ids[i * block_rows : (i + 1) * block_rows] for i in range(3)]
    sums = []
    for first in range(3):
        masses = tile_mass(pieces[first], key_rows, piece_ids[first], key_ids, first * block_rows)
        sums.append(jnp.sum(masses, axis=1))
    mass_sum = jnp.concatenate(sums, axis=0)
    return jnp.log1p(mass_sum)


def plain_plan(embeddings, cluster_ids):
    peer_count = lax.axis_size("gx")
    row_count = embeddings.shape[0]
    features = embeddings.shape[1]
    capacity = 3 * row_count // peer_count
    slot_total = peer_count * capacity
    squares = jnp.sum(jnp.square(embeddings.astype(jnp.float32)), axis=1)
    unit_rows = (embeddings.astype(jnp.float32) * lax.rsqrt(squares + 1e-06)[:, None]).astype(
        jnp.bfloat16
    )
    owner_of = cluster_ids // CLU_DEV
    onehot = (owner_of[:, None] == jnp.arange(peer_count, dtype=jnp.int32)[None, :]).astype(
        jnp.bfloat16
    )
    row_range = jnp.arange(row_count, dtype=jnp.int32)
    lower_tri = (row_range[:, None] >= row_range[None, :]).astype(jnp.bfloat16)
    running = jnp.dot(lower_tri, onehot, preferred_element_type=jnp.float32)
    slot_index = (jnp.sum(running * onehot.astype(jnp.float32), axis=1) - 1.0).astype(jnp.int32)
    target_slot = owner_of * capacity + slot_index
    slot_range = jnp.arange(slot_total, dtype=jnp.int32)
    select_mask = slot_range[:, None] == target_slot[None, :]
    outgoing = jnp.dot(
        select_mask.astype(jnp.bfloat16), unit_rows, preferred_element_type=jnp.float32
    )
    outgoing = outgoing.astype(jnp.bfloat16).reshape(peer_count, capacity, features)
    outgoing_ids = jnp.sum(jnp.where(select_mask, cluster_ids[None, :] + 1, 0), axis=1) - 1
    outgoing_ids = outgoing_ids.reshape(peer_count, capacity)
    arrived, arrived_ids = (
        lax.all_to_all(outgoing, "gx", split_axis=0, concat_axis=0, tiled=True),
        lax.all_to_all(outgoing_ids, "gx", split_axis=0, concat_axis=0, tiled=True),
    )
    key_rows = arrived.reshape(slot_total, features)
    key_ids = arrived_ids.reshape(slot_total)
    scores = density_scores(key_rows, key_ids)
    returned = lax.all_to_all(
        scores.reshape(peer_count, capacity), "gx", split_axis=0, concat_axis=0, tiled=True
    )
    flat_scores = returned.reshape(slot_total)
    pick_mask = target_slot[:, None] == slot_range[None, :]
    return jnp.sum(jnp.where(pick_mask, flat_scores[None, :], 0.0), axis=1)


LANES = 128
PLANE = 4
VMEM_BYTES = 16 * 1024 * 1024


def along_rows(values):
    return jnp.broadcast_to(values, (LANES, values.shape[1])).T


def unit_rows(raw, scale):
    features = raw.astype(jnp.float32)
    wide = jnp.concatenate([scale] * (features.shape[1] // LANES), axis=1)
    return (features * wide).astype(jnp.bfloat16)


def mate_mass(query_rows, query_ids, key_rows, key_ids, same_block):
    similar = lax.dot_general(
        query_rows, key_rows, (((1,), (1,)), ((), ())), preferred_element_type=jnp.float32
    )
    repeats = similar.shape[1] // LANES
    mates = jnp.concatenate([query_ids] * repeats, axis=1) == key_ids
    if same_block:
        query_pos = lax.broadcasted_iota(jnp.int32, similar.shape, 0)
        key_pos = lax.broadcasted_iota(jnp.int32, similar.shape, 1)
        mates = mates & (query_pos != key_pos)
    return jnp.where(mates, jnp.exp(similar * inverse_temp), 0.0)


def info_kernel(rows_ref, ids_ref, info_ref):
    peers, _, width = info_ref.shape
    rows = width // 2
    features = rows_ref[...].astype(jnp.float32)
    squares = jnp.sum(features * features, axis=1, keepdims=True)
    scale = jnp.broadcast_to(lax.rsqrt(squares + 1e-06), (rows, LANES)).T[:1]
    info = jnp.concatenate([ids_ref[...].astype(jnp.float32), scale], axis=1)
    for peer in range(peers):
        info_ref[peer] = info


def plane_kernel(info_ref, *refs):
    block_refs, (units_ref, ids_ref, mass_ref) = refs[:-3], refs[-3:]
    rows = mass_ref.shape[1]
    here = lax.axis_index("gx")
    own_ids = info_ref[here][:, :rows]
    first = 0
    for ref in block_refs:
        block = first // rows
        info = info_ref[here ^ block]
        size = ref.shape[0]
        inside = first % rows
        scale = along_rows(info[:, rows:])[inside : inside + size]
        units_ref[first : first + size, :] = unit_rows(ref[...], scale)
        first += size
    mass = jnp.zeros((1, rows), jnp.float32)
    for m in range(PLANE):
        part = pl.ds(m * rows, rows)
        query_ids = along_rows(info_ref[here ^ m][:, :rows])
        ids_ref[part, :] = query_ids
        masses = mate_mass(units_ref[part, :], query_ids, units_ref[:rows, :], own_ids, m == 0)
        mass = mass + jnp.sum(masses, axis=0, keepdims=True)
    mass_ref[...] = mass


def line_kernel(moves, info_ref, units_ref, ids_ref, mass_ref, *refs):
    line_refs, sums_ref, lane_sums = refs[:-2], refs[-2], refs[-1]
    rows = mass_ref.shape[1]
    here = lax.axis_index("gx")
    plane, line = here // PLANE, here % PLANE
    sums_ref[...] = jnp.zeros_like(sums_ref)
    lane_sums[...] = jnp.zeros_like(lane_sums)
    for line_ref, pairs in zip(line_refs, moves):
        source = jnp.int32(-1)
        for sender, receiver in pairs:
            source = jnp.where(plane == receiver, sender, source)

        @pl.when(source >= 0)
        def _():
            sender = source * PLANE + line
            info = info_ref[sender]
            key_ids = info[:, :rows]
            key_rows = unit_rows(line_ref[...], along_rows(info[:, rows:]))
            column = jnp.zeros((1, rows), jnp.float32)
            for m in range(PLANE):
                part = pl.ds(m * rows, rows)
                masses = mate_mass(units_ref[part, :], ids_ref[part, :], key_rows, key_ids, False)
                column = column + jnp.sum(masses, axis=0, keepdims=True)
                folded = masses[:, :LANES]
                for first in range(LANES, rows, LANES):
                    folded = folded + masses[:, first : first + LANES]
                lane_sums[part, :] += folded
            sums_ref[sender] = column

    for m in range(PLANE):
        part = pl.ds(m * rows, rows)
        row_sum = jnp.sum(lane_sums[part, :].T, axis=0, keepdims=True)
        sums_ref[here ^ m] = mass_ref[...] + row_sum if m == 0 else row_sum


def grid_plan(embeddings, cluster_ids):
    peers = lax.axis_size("gx")
    row_count, features = embeddings.shape
    params = pltpu.CompilerParams(vmem_limit_bytes=VMEM_BYTES)

    def in_plane(value, step):
        return lax.ppermute(value, "gx", [(i, i ^ step) for i in range(peers)])

    def on_line(value, moves):
        pairs = [(a * PLANE + n, b * PLANE + n) for a, b in moves for n in range(PLANE)]
        return lax.ppermute(value, "gx", pairs)

    def to_all(value):
        return lax.all_to_all(value, "gx", split_axis=0, concat_axis=0, tiled=True)

    moves = [[(0, 1), (3, 2), (2, 0)], [(1, 2), (0, 3), (3, 1)]]
    lines = [on_line(embeddings, pairs) for pairs in moves]
    across = in_plane(embeddings, 2)
    sibling = in_plane(embeddings, 1)
    info = to_all(
        pl.pallas_call(
            info_kernel,
            out_shape=jax.ShapeDtypeStruct((peers, 1, 2 * row_count), jnp.float32),
            compiler_params=params,
        )(embeddings, cluster_ids.reshape(1, row_count))
    )
    across, info = lax.optimization_barrier((across, info))
    cut = row_count // 2
    corner = [in_plane(part, 1) for part in (across[:cut], across[cut:])]
    plane_rows = PLANE * row_count
    units, ids, mass = pl.pallas_call(
        plane_kernel,
        out_shape=(
            jax.ShapeDtypeStruct((plane_rows, features), jnp.bfloat16),
            jax.ShapeDtypeStruct((plane_rows, LANES), jnp.float32),
            jax.ShapeDtypeStruct((1, row_count), jnp.float32),
        ),
        cost_estimate=pl.CostEstimate(flops=1, bytes_accessed=1, transcendentals=0),
        compiler_params=params,
    )(info, embeddings, sibling, across, *corner)
    sums = pl.pallas_call(
        functools.partial(line_kernel, moves),
        out_shape=jax.ShapeDtypeStruct((peers, 1, row_count), jnp.float32),
        scratch_shapes=[pltpu.VMEM((plane_rows, LANES), jnp.float32)],
        compiler_params=params,
    )(info, units, ids, mass, *lines)
    return jnp.log1p(jnp.sum(to_all(sums), axis=0)).reshape(row_count)


def on_device(embeddings, cluster_ids):
    if lax.axis_size("gx") == 4 * PLANE and embeddings.shape[0] % (2 * LANES) == 0:
        return grid_plan(embeddings, cluster_ids)
    return plain_plan(embeddings, cluster_ids)


def solution(mesh):
    in_specs = (P(("parts", "gx"), None), P(("parts", "gx")))
    out_specs = P(("parts", "gx"))
    return jax.shard_map(
        on_device, mesh=mesh, in_specs=in_specs, out_specs=out_specs, check_vma=False
    )
```

```python
import functools

import jax
import jax.numpy as jnp
from jax import lax
from jax.experimental import pallas as pl
from jax.experimental.pallas import tpu as pltpu
from jax.sharding import PartitionSpec as P

CLU_DEV = 1
PAD_MARK = 64.0
inverse_temp = 20.0


def tile_mass(query_rows, key_rows, query_ids, key_ids, query_start):
    similar = lax.dot_general(
        query_rows, key_rows, (((1,), (1,)), ((), ())), preferred_element_type=jnp.float32
    )
    query_pos = jnp.arange(query_rows.shape[0], dtype=jnp.int32) + query_start
    key_pos = jnp.arange(key_rows.shape[0], dtype=jnp.int32)
    mate_mask = (query_ids[:, None] == key_ids[None, :]) & (query_ids[:, None] >= 0)
    mate_mask = mate_mask & (query_pos[:, None] != key_pos[None, :])
    return jnp.where(mate_mask, jnp.exp(similar * inverse_temp), 0.0)


def density_scores(key_rows, key_ids):
    total_rows = key_rows.shape[0]
    block_rows = total_rows // 3
    pieces = [key_rows[i * block_rows : (i + 1) * block_rows] for i in range(3)]
    piece_ids = [key_ids[i * block_rows : (i + 1) * block_rows] for i in range(3)]
    sums = []
    for first in range(3):
        masses = tile_mass(pieces[first], key_rows, piece_ids[first], key_ids, first * block_rows)
        sums.append(jnp.sum(masses, axis=1))
    mass_sum = jnp.concatenate(sums, axis=0)
    return jnp.log1p(mass_sum)


def plain_plan(embeddings, cluster_ids):
    peer_count = lax.axis_size("gx")
    row_count = embeddings.shape[0]
    features = embeddings.shape[1]
    capacity = 3 * row_count // peer_count
    slot_total = peer_count * capacity
    squares = jnp.sum(jnp.square(embeddings.astype(jnp.float32)), axis=1)
    unit_rows = (embeddings.astype(jnp.float32) * lax.rsqrt(squares + 1e-06)[:, None]).astype(
        jnp.bfloat16
    )
    owner_of = cluster_ids // CLU_DEV
    onehot = (owner_of[:, None] == jnp.arange(peer_count, dtype=jnp.int32)[None, :]).astype(
        jnp.bfloat16
    )
    row_range = jnp.arange(row_count, dtype=jnp.int32)
    lower_tri = (row_range[:, None] >= row_range[None, :]).astype(jnp.bfloat16)
    running = jnp.dot(lower_tri, onehot, preferred_element_type=jnp.float32)
    slot_index = (jnp.sum(running * onehot.astype(jnp.float32), axis=1) - 1.0).astype(jnp.int32)
    target_slot = owner_of * capacity + slot_index
    slot_range = jnp.arange(slot_total, dtype=jnp.int32)
    select_mask = slot_range[:, None] == target_slot[None, :]
    outgoing = jnp.dot(
        select_mask.astype(jnp.bfloat16), unit_rows, preferred_element_type=jnp.float32
    )
    outgoing = outgoing.astype(jnp.bfloat16).reshape(peer_count, capacity, features)
    outgoing_ids = jnp.sum(jnp.where(select_mask, cluster_ids[None, :] + 1, 0), axis=1) - 1
    outgoing_ids = outgoing_ids.reshape(peer_count, capacity)
    arrived, arrived_ids = (
        lax.all_to_all(outgoing, "gx", split_axis=0, concat_axis=0, tiled=True),
        lax.all_to_all(outgoing_ids, "gx", split_axis=0, concat_axis=0, tiled=True),
    )
    key_rows = arrived.reshape(slot_total, features)
    key_ids = arrived_ids.reshape(slot_total)
    scores = density_scores(key_rows, key_ids)
    returned = lax.all_to_all(
        scores.reshape(peer_count, capacity), "gx", split_axis=0, concat_axis=0, tiled=True
    )
    flat_scores = returned.reshape(slot_total)
    pick_mask = target_slot[:, None] == slot_range[None, :]
    return jnp.sum(jnp.where(pick_mask, flat_scores[None, :], 0.0), axis=1)


LANES = 128
PLANE = 4
VMEM_BYTES = 16 * 1024 * 1024


def along_rows(values):
    return jnp.broadcast_to(values, (LANES, values.shape[1])).T


def unit_rows(raw, scale):
    features = raw.astype(jnp.float32)
    wide = jnp.concatenate([scale] * (features.shape[1] // LANES), axis=1)
    return (features * wide).astype(jnp.bfloat16)


def mate_mass(query_rows, query_ids, key_rows, key_ids, same_block):
    similar = lax.dot_general(
        query_rows, key_rows, (((1,), (1,)), ((), ())), preferred_element_type=jnp.float32
    )
    repeats = similar.shape[1] // LANES
    mates = jnp.concatenate([query_ids] * repeats, axis=1) == key_ids
    if same_block:
        query_pos = lax.broadcasted_iota(jnp.int32, similar.shape, 0)
        key_pos = lax.broadcasted_iota(jnp.int32, similar.shape, 1)
        mates = mates & (query_pos != key_pos)
    return jnp.where(mates, jnp.exp(similar * inverse_temp), 0.0)


def info_kernel(rows_ref, ids_ref, info_ref):
    peers, _, width = info_ref.shape
    rows = width // 2
    features = rows_ref[...].astype(jnp.float32)
    squares = jnp.sum(features * features, axis=1, keepdims=True)
    scale = jnp.broadcast_to(lax.rsqrt(squares + 1e-06), (rows, LANES)).T[:1]
    info = jnp.concatenate([ids_ref[...].astype(jnp.float32), scale], axis=1)
    for peer in range(peers):
        info_ref[peer] = info


def plane_kernel(info_ref, *refs):
    block_refs, (units_ref, ids_ref, mass_ref) = refs[:-3], refs[-3:]
    rows = mass_ref.shape[1]
    here = lax.axis_index("gx")
    own_ids = info_ref[here][:, :rows]
    first = 0
    for ref in block_refs:
        block = first // rows
        info = info_ref[here ^ block]
        size = ref.shape[0]
        inside = first % rows
        scale = along_rows(info[:, rows:])[inside : inside + size]
        units_ref[first : first + size, :] = unit_rows(ref[...], scale)
        first += size
    mass = jnp.zeros((1, rows), jnp.float32)
    for m in range(PLANE):
        part = pl.ds(m * rows, rows)
        query_ids = along_rows(info_ref[here ^ m][:, :rows])
        ids_ref[part, :] = query_ids
        masses = mate_mass(units_ref[part, :], query_ids, units_ref[:rows, :], own_ids, m == 0)
        mass = mass + jnp.sum(masses, axis=0, keepdims=True)
    mass_ref[...] = mass


def line_kernel(moves, info_ref, units_ref, ids_ref, mass_ref, *refs):
    line_refs, sums_ref, lane_sums = refs[:-2], refs[-2], refs[-1]
    rows = mass_ref.shape[1]
    here = lax.axis_index("gx")
    plane, line = here // PLANE, here % PLANE
    sums_ref[...] = jnp.zeros_like(sums_ref)
    lane_sums[...] = jnp.zeros_like(lane_sums)
    for line_ref, pairs in zip(line_refs, moves):
        source = jnp.int32(-1)
        for sender, receiver in pairs:
            source = jnp.where(plane == receiver, sender, source)

        @pl.when(source >= 0)
        def _():
            sender = source * PLANE + line
            info = info_ref[sender]
            key_ids = info[:, :rows]
            key_rows = unit_rows(line_ref[...], along_rows(info[:, rows:]))
            column = jnp.zeros((1, rows), jnp.float32)
            for m in range(PLANE):
                part = pl.ds(m * rows, rows)
                masses = mate_mass(units_ref[part, :], ids_ref[part, :], key_rows, key_ids, False)
                column = column + jnp.sum(masses, axis=0, keepdims=True)
                folded = masses[:, :LANES]
                for first in range(LANES, rows, LANES):
                    folded = folded + masses[:, first : first + LANES]
                lane_sums[part, :] += folded
            sums_ref[sender] = column

    for m in range(PLANE):
        part = pl.ds(m * rows, rows)
        row_sum = jnp.sum(lane_sums[part, :].T, axis=0, keepdims=True)
        sums_ref[here ^ m] = mass_ref[...] + row_sum if m == 0 else row_sum


def grid_plan(embeddings, cluster_ids):
    peers = lax.axis_size("gx")
    row_count, features = embeddings.shape
    params = pltpu.CompilerParams(vmem_limit_bytes=VMEM_BYTES)

    def in_plane(value, step):
        return lax.ppermute(value, "gx", [(i, i ^ step) for i in range(peers)])

    def on_line(value, moves):
        pairs = [(a * PLANE + n, b * PLANE + n) for a, b in moves for n in range(PLANE)]
        return lax.ppermute(value, "gx", pairs)

    def to_all(value):
        return lax.all_to_all(value, "gx", split_axis=0, concat_axis=0, tiled=True)

    moves = [[(0, 1), (3, 2), (2, 0)], [(1, 2), (0, 3), (3, 1)]]
    lines = [on_line(embeddings, pairs) for pairs in moves]
    across = in_plane(embeddings, 2)
    sibling = in_plane(embeddings, 1)
    across, rows, row_ids = lax.optimization_barrier((across, embeddings, cluster_ids))
    info = to_all(
        pl.pallas_call(
            info_kernel,
            out_shape=jax.ShapeDtypeStruct((peers, 1, 2 * row_count), jnp.float32),
            compiler_params=params,
        )(rows, row_ids.reshape(1, row_count))
    )
    corner = [in_plane(part, 1) for part in jnp.split(across, 2)]
    plane_rows = PLANE * row_count
    units, ids, mass = pl.pallas_call(
        plane_kernel,
        out_shape=(
            jax.ShapeDtypeStruct((plane_rows, features), jnp.bfloat16),
            jax.ShapeDtypeStruct((plane_rows, LANES), jnp.float32),
            jax.ShapeDtypeStruct((1, row_count), jnp.float32),
        ),
        cost_estimate=pl.CostEstimate(flops=1, bytes_accessed=1, transcendentals=0),
        compiler_params=params,
    )(info, embeddings, sibling, across, *corner)
    sums = pl.pallas_call(
        functools.partial(line_kernel, moves),
        out_shape=jax.ShapeDtypeStruct((peers, 1, row_count), jnp.float32),
        scratch_shapes=[pltpu.VMEM((plane_rows, LANES), jnp.float32)],
        compiler_params=params,
    )(info, units, ids, mass, *lines)
    return jnp.log1p(jnp.sum(to_all(sums), axis=0)).reshape(row_count)


def on_device(embeddings, cluster_ids):
    if lax.axis_size("gx") == 4 * PLANE and embeddings.shape[0] % (2 * LANES) == 0:
        return grid_plan(embeddings, cluster_ids)
    return plain_plan(embeddings, cluster_ids)


def solution(mesh):
    in_specs = (P(("parts", "gx"), None), P(("parts", "gx")))
    out_specs = P(("parts", "gx"))
    return jax.shard_map(
        on_device, mesh=mesh, in_specs=in_specs, out_specs=out_specs, check_vma=False
    )
```

```python
import functools

import jax
import jax.numpy as jnp
from jax import lax
from jax.experimental import pallas as pl
from jax.experimental.pallas import tpu as pltpu
from jax.sharding import PartitionSpec as P

CLU_DEV = 1
PAD_MARK = 64.0
inverse_temp = 20.0


def tile_mass(query_rows, key_rows, query_ids, key_ids, query_start):
    similar = lax.dot_general(
        query_rows, key_rows, (((1,), (1,)), ((), ())), preferred_element_type=jnp.float32
    )
    query_pos = jnp.arange(query_rows.shape[0], dtype=jnp.int32) + query_start
    key_pos = jnp.arange(key_rows.shape[0], dtype=jnp.int32)
    mate_mask = (query_ids[:, None] == key_ids[None, :]) & (query_ids[:, None] >= 0)
    mate_mask = mate_mask & (query_pos[:, None] != key_pos[None, :])
    return jnp.where(mate_mask, jnp.exp(similar * inverse_temp), 0.0)


def density_scores(key_rows, key_ids):
    total_rows = key_rows.shape[0]
    block_rows = total_rows // 3
    pieces = [key_rows[i * block_rows : (i + 1) * block_rows] for i in range(3)]
    piece_ids = [key_ids[i * block_rows : (i + 1) * block_rows] for i in range(3)]
    sums = []
    for first in range(3):
        masses = tile_mass(pieces[first], key_rows, piece_ids[first], key_ids, first * block_rows)
        sums.append(jnp.sum(masses, axis=1))
    mass_sum = jnp.concatenate(sums, axis=0)
    return jnp.log1p(mass_sum)


def plain_plan(embeddings, cluster_ids):
    peer_count = lax.axis_size("gx")
    row_count = embeddings.shape[0]
    features = embeddings.shape[1]
    capacity = 3 * row_count // peer_count
    slot_total = peer_count * capacity
    squares = jnp.sum(jnp.square(embeddings.astype(jnp.float32)), axis=1)
    unit_rows = (embeddings.astype(jnp.float32) * lax.rsqrt(squares + 1e-06)[:, None]).astype(
        jnp.bfloat16
    )
    owner_of = cluster_ids // CLU_DEV
    onehot = (owner_of[:, None] == jnp.arange(peer_count, dtype=jnp.int32)[None, :]).astype(
        jnp.bfloat16
    )
    row_range = jnp.arange(row_count, dtype=jnp.int32)
    lower_tri = (row_range[:, None] >= row_range[None, :]).astype(jnp.bfloat16)
    running = jnp.dot(lower_tri, onehot, preferred_element_type=jnp.float32)
    slot_index = (jnp.sum(running * onehot.astype(jnp.float32), axis=1) - 1.0).astype(jnp.int32)
    target_slot = owner_of * capacity + slot_index
    slot_range = jnp.arange(slot_total, dtype=jnp.int32)
    select_mask = slot_range[:, None] == target_slot[None, :]
    outgoing = jnp.dot(
        select_mask.astype(jnp.bfloat16), unit_rows, preferred_element_type=jnp.float32
    )
    outgoing = outgoing.astype(jnp.bfloat16).reshape(peer_count, capacity, features)
    outgoing_ids = jnp.sum(jnp.where(select_mask, cluster_ids[None, :] + 1, 0), axis=1) - 1
    outgoing_ids = outgoing_ids.reshape(peer_count, capacity)
    arrived, arrived_ids = (
        lax.all_to_all(outgoing, "gx", split_axis=0, concat_axis=0, tiled=True),
        lax.all_to_all(outgoing_ids, "gx", split_axis=0, concat_axis=0, tiled=True),
    )
    key_rows = arrived.reshape(slot_total, features)
    key_ids = arrived_ids.reshape(slot_total)
    scores = density_scores(key_rows, key_ids)
    returned = lax.all_to_all(
        scores.reshape(peer_count, capacity), "gx", split_axis=0, concat_axis=0, tiled=True
    )
    flat_scores = returned.reshape(slot_total)
    pick_mask = target_slot[:, None] == slot_range[None, :]
    return jnp.sum(jnp.where(pick_mask, flat_scores[None, :], 0.0), axis=1)


LANES = 128
PLANE = 4
VMEM_BYTES = 16 * 1024 * 1024


def along_rows(values):
    return jnp.broadcast_to(values, (LANES, values.shape[1])).T


def unit_rows(raw, scale):
    features = raw.astype(jnp.float32)
    wide = jnp.concatenate([scale] * (features.shape[1] // LANES), axis=1)
    return (features * wide).astype(jnp.bfloat16)


def mate_mass(query_rows, query_ids, key_rows, key_ids, same_block):
    similar = lax.dot_general(
        query_rows, key_rows, (((1,), (1,)), ((), ())), preferred_element_type=jnp.float32
    )
    repeats = similar.shape[1] // LANES
    mates = jnp.concatenate([query_ids] * repeats, axis=1) == key_ids
    if same_block:
        query_pos = lax.broadcasted_iota(jnp.int32, similar.shape, 0)
        key_pos = lax.broadcasted_iota(jnp.int32, similar.shape, 1)
        mates = mates & (query_pos != key_pos)
    return jnp.where(mates, jnp.exp(similar * inverse_temp), 0.0)


def info_kernel(rows_ref, ids_ref, info_ref):
    rows = rows_ref.shape[0]
    features = rows_ref[...].astype(jnp.float32)
    squares = jnp.sum(features * features, axis=1, keepdims=True)
    scale = jnp.broadcast_to(lax.rsqrt(squares + 1e-06), (rows, LANES)).T[:1]
    info_ref[:, :rows] = ids_ref[...].astype(jnp.float32)
    info_ref[:, rows:] = scale


def plane_kernel(*refs):
    info_refs, block_refs = refs[:PLANE], refs[PLANE:-3]
    units_ref, ids_ref, mass_ref = refs[-3:]
    rows = mass_ref.shape[1]
    first = 0
    for ref in block_refs:
        size, inside = ref.shape[0], first % rows
        scale = along_rows(info_refs[first // rows][:, rows:])[inside : inside + size]
        units_ref[first : first + size, :] = unit_rows(ref[...], scale)
        first += size
    own_ids = info_refs[0][:, :rows]
    mass = jnp.zeros((1, rows), jnp.float32)
    for m in range(PLANE):
        part = pl.ds(m * rows, rows)
        query_ids = along_rows(info_refs[m][:, :rows])
        ids_ref[part, :] = query_ids
        masses = mate_mass(units_ref[part, :], query_ids, units_ref[:rows, :], own_ids, m == 0)
        mass = mass + jnp.sum(masses, axis=0, keepdims=True)
    mass_ref[...] = mass


def line_sums(moves, info_ref, line_ref, units_ref, ids_ref, column_ref, sums_ref):
    rows = column_ref.shape[1]
    plane = lax.axis_index("gx") // PLANE
    arrived = functools.reduce(jnp.logical_or, [plane == receiver for _, receiver in moves])
    column_ref[...] = jnp.zeros_like(column_ref)

    @pl.when(arrived)
    def _():
        key_ids = info_ref[:, :rows]
        key_rows = unit_rows(line_ref[...], along_rows(info_ref[:, rows:]))
        column = jnp.zeros((1, rows), jnp.float32)
        for m in range(PLANE):
            part = pl.ds(m * rows, rows)
            masses = mate_mass(units_ref[part, :], ids_ref[part, :], key_rows, key_ids, False)
            column = column + jnp.sum(masses, axis=0, keepdims=True)
            folded = masses[:, :LANES]
            for first in range(LANES, rows, LANES):
                folded = folded + masses[:, first : first + LANES]
            sums_ref[part, :] += folded
        column_ref[...] = column


def first_line_kernel(moves, info_ref, line_ref, units_ref, ids_ref, column_ref, sums_ref):
    sums_ref[...] = jnp.zeros_like(sums_ref)
    line_sums(moves, info_ref, line_ref, units_ref, ids_ref, column_ref, sums_ref)


def last_line_kernel(moves, info_ref, line_ref, units_ref, ids_ref, earlier_ref, *refs):
    mass_refs, column_ref, row_refs, sums_ref = refs[:2], refs[2], refs[3:-1], refs[-1]
    rows = column_ref.shape[1]
    sums_ref[...] = earlier_ref[...]
    line_sums(moves, info_ref, line_ref, units_ref, ids_ref, column_ref, sums_ref)
    for m in range(PLANE):
        row_sum = jnp.sum(sums_ref[pl.ds(m * rows, rows), :].T, axis=0, keepdims=True)
        if m == 0:
            row_sum = row_sum + mass_refs[0][...] + mass_refs[1][...]
        row_refs[m][...] = row_sum


def grid_plan(embeddings, cluster_ids):
    peers = lax.axis_size("gx")
    row_count, features = embeddings.shape
    plane_rows = PLANE * row_count
    params = pltpu.CompilerParams(vmem_limit_bytes=VMEM_BYTES)
    vector = jax.ShapeDtypeStruct((1, row_count), jnp.float32)
    lanes = jax.ShapeDtypeStruct((plane_rows, LANES), jnp.float32)

    def in_plane(value, step):
        return lax.ppermute(value, "gx", [(i, i ^ step) for i in range(peers)])

    def on_line(value, moves):
        pairs = [(a * PLANE + n, b * PLANE + n) for a, b in moves for n in range(PLANE)]
        return lax.ppermute(value, "gx", pairs)

    first_moves = [(0, 1), (3, 2), (2, 0)]
    last_moves = [(1, 2), (0, 3), (3, 1)]
    first_back = [(b, a) for a, b in first_moves]
    last_back = [(b, a) for a, b in last_moves]

    first_line = on_line(embeddings, first_moves)
    last_line = on_line(embeddings, last_moves)
    across = in_plane(embeddings, 2)
    sibling = in_plane(embeddings, 1)
    across, rows, row_ids = lax.optimization_barrier((across, embeddings, cluster_ids))
    info = pl.pallas_call(
        info_kernel,
        out_shape=jax.ShapeDtypeStruct((1, 2 * row_count), jnp.float32),
        compiler_params=params,
    )(rows, row_ids.reshape(1, row_count))
    plane_info = [info] + [in_plane(info, step) for step in range(1, PLANE)]
    first_info = on_line(info, first_moves)
    last_info = on_line(info, last_moves)
    corner = [in_plane(part, 1) for part in jnp.split(across, 2)]
    units, ids, mass = pl.pallas_call(
        plane_kernel,
        out_shape=(jax.ShapeDtypeStruct((plane_rows, features), jnp.bfloat16), lanes, vector),
        cost_estimate=pl.CostEstimate(flops=1, bytes_accessed=1, transcendentals=0),
        compiler_params=params,
    )(*plane_info, embeddings, sibling, across, *corner)
    first_column, first_sums = pl.pallas_call(
        functools.partial(first_line_kernel, first_moves),
        out_shape=(vector, lanes),
        cost_estimate=pl.CostEstimate(flops=1, bytes_accessed=1, transcendentals=0),
        compiler_params=params,
    )(first_info, first_line, units, ids)
    last_column, *row_sums = pl.pallas_call(
        functools.partial(last_line_kernel, last_moves),
        out_shape=[vector] * (1 + PLANE),
        scratch_shapes=[pltpu.VMEM(lanes.shape, lanes.dtype)],
        compiler_params=params,
    )(last_info, last_line, units, ids, first_sums, mass, on_line(first_column, first_back))
    returned = [in_plane(row_sums[step], step) for step in range(1, PLANE)]
    returned.append(on_line(last_column, last_back))
    return jnp.log1p(sum(returned, row_sums[0])).reshape(row_count)


def on_device(embeddings, cluster_ids):
    if lax.axis_size("gx") == 4 * PLANE and embeddings.shape[0] % (2 * LANES) == 0:
        return grid_plan(embeddings, cluster_ids)
    return plain_plan(embeddings, cluster_ids)


def solution(mesh):
    in_specs = (P(("parts", "gx"), None), P(("parts", "gx")))
    out_specs = P(("parts", "gx"))
    return jax.shard_map(
        on_device, mesh=mesh, in_specs=in_specs, out_specs=out_specs, check_vma=False
    )
```

```python
import functools

import jax
import jax.numpy as jnp
from jax import lax
from jax.experimental import pallas as pl
from jax.experimental.pallas import tpu as pltpu
from jax.sharding import PartitionSpec as P

CLU_DEV = 1
PAD_MARK = 64.0
inverse_temp = 20.0


def tile_mass(query_rows, key_rows, query_ids, key_ids, query_start):
    similar = lax.dot_general(
        query_rows, key_rows, (((1,), (1,)), ((), ())), preferred_element_type=jnp.float32
    )
    query_pos = jnp.arange(query_rows.shape[0], dtype=jnp.int32) + query_start
    key_pos = jnp.arange(key_rows.shape[0], dtype=jnp.int32)
    mate_mask = (query_ids[:, None] == key_ids[None, :]) & (query_ids[:, None] >= 0)
    mate_mask = mate_mask & (query_pos[:, None] != key_pos[None, :])
    return jnp.where(mate_mask, jnp.exp(similar * inverse_temp), 0.0)


def density_scores(key_rows, key_ids):
    total_rows = key_rows.shape[0]
    block_rows = total_rows // 3
    pieces = [key_rows[i * block_rows : (i + 1) * block_rows] for i in range(3)]
    piece_ids = [key_ids[i * block_rows : (i + 1) * block_rows] for i in range(3)]
    sums = []
    for first in range(3):
        masses = tile_mass(pieces[first], key_rows, piece_ids[first], key_ids, first * block_rows)
        sums.append(jnp.sum(masses, axis=1))
    mass_sum = jnp.concatenate(sums, axis=0)
    return jnp.log1p(mass_sum)


def plain_plan(embeddings, cluster_ids):
    peer_count = lax.axis_size("gx")
    row_count = embeddings.shape[0]
    features = embeddings.shape[1]
    capacity = 3 * row_count // peer_count
    slot_total = peer_count * capacity
    squares = jnp.sum(jnp.square(embeddings.astype(jnp.float32)), axis=1)
    unit_rows = (embeddings.astype(jnp.float32) * lax.rsqrt(squares + 1e-06)[:, None]).astype(
        jnp.bfloat16
    )
    owner_of = cluster_ids // CLU_DEV
    onehot = (owner_of[:, None] == jnp.arange(peer_count, dtype=jnp.int32)[None, :]).astype(
        jnp.bfloat16
    )
    row_range = jnp.arange(row_count, dtype=jnp.int32)
    lower_tri = (row_range[:, None] >= row_range[None, :]).astype(jnp.bfloat16)
    running = jnp.dot(lower_tri, onehot, preferred_element_type=jnp.float32)
    slot_index = (jnp.sum(running * onehot.astype(jnp.float32), axis=1) - 1.0).astype(jnp.int32)
    target_slot = owner_of * capacity + slot_index
    slot_range = jnp.arange(slot_total, dtype=jnp.int32)
    select_mask = slot_range[:, None] == target_slot[None, :]
    outgoing = jnp.dot(
        select_mask.astype(jnp.bfloat16), unit_rows, preferred_element_type=jnp.float32
    )
    outgoing = outgoing.astype(jnp.bfloat16).reshape(peer_count, capacity, features)
    outgoing_ids = jnp.sum(jnp.where(select_mask, cluster_ids[None, :] + 1, 0), axis=1) - 1
    outgoing_ids = outgoing_ids.reshape(peer_count, capacity)
    arrived, arrived_ids = (
        lax.all_to_all(outgoing, "gx", split_axis=0, concat_axis=0, tiled=True),
        lax.all_to_all(outgoing_ids, "gx", split_axis=0, concat_axis=0, tiled=True),
    )
    key_rows = arrived.reshape(slot_total, features)
    key_ids = arrived_ids.reshape(slot_total)
    scores = density_scores(key_rows, key_ids)
    returned = lax.all_to_all(
        scores.reshape(peer_count, capacity), "gx", split_axis=0, concat_axis=0, tiled=True
    )
    flat_scores = returned.reshape(slot_total)
    pick_mask = target_slot[:, None] == slot_range[None, :]
    return jnp.sum(jnp.where(pick_mask, flat_scores[None, :], 0.0), axis=1)


LANES = 128
PLANE = 4
VMEM_BYTES = 16 * 1024 * 1024


def along_rows(values):
    return jnp.broadcast_to(values, (LANES, values.shape[1])).T


def unit_rows(raw, scale):
    features = raw.astype(jnp.float32)
    wide = jnp.concatenate([scale] * (features.shape[1] // LANES), axis=1)
    return (features * wide).astype(jnp.bfloat16)


def mate_mass(query_rows, query_ids, key_rows, key_ids, same_block):
    similar = lax.dot_general(
        query_rows, key_rows, (((1,), (1,)), ((), ())), preferred_element_type=jnp.float32
    )
    repeats = similar.shape[1] // LANES
    mates = jnp.concatenate([query_ids] * repeats, axis=1) == key_ids
    if same_block:
        query_pos = lax.broadcasted_iota(jnp.int32, similar.shape, 0)
        key_pos = lax.broadcasted_iota(jnp.int32, similar.shape, 1)
        mates = mates & (query_pos != key_pos)
    return jnp.where(mates, jnp.exp(similar * inverse_temp), 0.0)


def info_kernel(rows_ref, ids_ref, info_ref):
    rows = rows_ref.shape[0]
    features = rows_ref[...].astype(jnp.float32)
    squares = jnp.sum(features * features, axis=1, keepdims=True)
    scale = jnp.broadcast_to(lax.rsqrt(squares + 1e-06), (rows, LANES)).T[:1]
    info_ref[:, :rows] = ids_ref[...].astype(jnp.float32)
    info_ref[:, rows:] = scale


def plane_kernel(*refs):
    infos, block_refs = [ref[...] for ref in refs[:PLANE]], refs[PLANE:-3]
    units_ref, ids_ref, mass_ref = refs[-3:]
    rows = mass_ref.shape[1]
    first = 0
    for ref in block_refs:
        size, inside = ref.shape[0], first % rows
        scale = along_rows(infos[first // rows][:, rows:])[inside : inside + size]
        units_ref[first : first + size, :] = unit_rows(ref[...], scale)
        first += size
    own_ids = infos[0][:, :rows]
    mass = jnp.zeros((1, rows), jnp.float32)
    for m in range(PLANE):
        part = pl.ds(m * rows, rows)
        query_ids = along_rows(infos[m][:, :rows])
        ids_ref[part, :] = query_ids
        masses = mate_mass(units_ref[part, :], query_ids, units_ref[:rows, :], own_ids, m == 0)
        mass = mass + jnp.sum(masses, axis=0, keepdims=True)
    mass_ref[...] = mass


def line_sums(moves, info_ref, line_ref, units_ref, ids_ref, column_ref, sums_ref):
    rows = column_ref.shape[1]
    plane = lax.axis_index("gx") // PLANE
    arrived = functools.reduce(jnp.logical_or, [plane == receiver for _, receiver in moves])
    column_ref[...] = jnp.zeros_like(column_ref)

    @pl.when(arrived)
    def _():
        key_ids = info_ref[:, :rows]
        key_rows = unit_rows(line_ref[...], along_rows(info_ref[:, rows:]))
        column = jnp.zeros((1, rows), jnp.float32)
        for m in range(PLANE):
            part = pl.ds(m * rows, rows)
            masses = mate_mass(units_ref[part, :], ids_ref[part, :], key_rows, key_ids, False)
            column = column + jnp.sum(masses, axis=0, keepdims=True)
            folded = masses[:, :LANES]
            for first in range(LANES, rows, LANES):
                folded = folded + masses[:, first : first + LANES]
            sums_ref[part, :] += folded
        column_ref[...] = column


def first_line_kernel(moves, info_ref, line_ref, units_ref, ids_ref, column_ref, sums_ref):
    sums_ref[...] = jnp.zeros_like(sums_ref)
    line_sums(moves, info_ref, line_ref, units_ref, ids_ref, column_ref, sums_ref)


def last_line_kernel(moves, info_ref, line_ref, units_ref, ids_ref, earlier_ref, *refs):
    mass_refs, column_ref, row_refs, sums_ref = refs[:2], refs[2], refs[3:-1], refs[-1]
    rows = column_ref.shape[1]
    sums_ref[...] = earlier_ref[...]
    line_sums(moves, info_ref, line_ref, units_ref, ids_ref, column_ref, sums_ref)
    for m in range(PLANE):
        row_sum = jnp.sum(sums_ref[pl.ds(m * rows, rows), :].T, axis=0, keepdims=True)
        if m == 0:
            row_sum = row_sum + mass_refs[0][...] + mass_refs[1][...]
        row_refs[m][...] = row_sum


def grid_plan(embeddings, cluster_ids):
    peers = lax.axis_size("gx")
    row_count, features = embeddings.shape
    plane_rows = PLANE * row_count
    params = pltpu.CompilerParams(vmem_limit_bytes=VMEM_BYTES)
    vector = jax.ShapeDtypeStruct((1, row_count), jnp.float32)
    lanes = jax.ShapeDtypeStruct((plane_rows, LANES), jnp.float32)

    def in_plane(value, step):
        return lax.ppermute(value, "gx", [(i, i ^ step) for i in range(peers)])

    def on_line(value, moves):
        pairs = [(a * PLANE + n, b * PLANE + n) for a, b in moves for n in range(PLANE)]
        return lax.ppermute(value, "gx", pairs)

    first_moves = [(0, 1), (1, 2), (2, 3), (3, 0)]
    last_moves = [(0, 2), (3, 1)]
    first_back = [(b, a) for a, b in first_moves]
    last_back = [(b, a) for a, b in last_moves]

    first_line = on_line(embeddings, first_moves)
    last_line = on_line(embeddings, last_moves)
    across = in_plane(embeddings, 2)
    sibling = in_plane(embeddings, 1)
    info = pl.pallas_call(
        info_kernel,
        out_shape=jax.ShapeDtypeStruct((1, 2 * row_count), jnp.float32),
        cost_estimate=pl.CostEstimate(flops=1, bytes_accessed=1, transcendentals=0),
        compiler_params=params,
    )(embeddings, cluster_ids.reshape(1, row_count))
    plane_info = [in_plane(info, step) for step in range(1, PLANE)]
    first_info = on_line(info, first_moves)
    last_info = on_line(info, last_moves)
    across, *plane_info = lax.optimization_barrier((across, *plane_info))
    corner = [in_plane(part, 1) for part in jnp.split(across, 2)]
    units, ids, mass = pl.pallas_call(
        plane_kernel,
        out_shape=(jax.ShapeDtypeStruct((plane_rows, features), jnp.bfloat16), lanes, vector),
        cost_estimate=pl.CostEstimate(flops=1, bytes_accessed=1, transcendentals=0),
        compiler_params=params,
    )(info, *plane_info, embeddings, sibling, across, *corner)
    first_column, first_sums = pl.pallas_call(
        functools.partial(first_line_kernel, first_moves),
        out_shape=(vector, lanes),
        cost_estimate=pl.CostEstimate(flops=1, bytes_accessed=1, transcendentals=0),
        compiler_params=params,
    )(first_info, first_line, units, ids)
    last_column, *row_sums = pl.pallas_call(
        functools.partial(last_line_kernel, last_moves),
        out_shape=[vector] * (1 + PLANE),
        scratch_shapes=[pltpu.VMEM(lanes.shape, lanes.dtype)],
        compiler_params=params,
    )(last_info, last_line, units, ids, first_sums, mass, on_line(first_column, first_back))
    returned = [on_line(last_column, last_back)]
    returned += [in_plane(row_sums[step], step) for step in (2, 3, 1)]
    return jnp.log1p(sum(returned, row_sums[0])).reshape(row_count)


def on_device(embeddings, cluster_ids):
    if lax.axis_size("gx") == 4 * PLANE and embeddings.shape[0] % (2 * LANES) == 0:
        return grid_plan(embeddings, cluster_ids)
    return plain_plan(embeddings, cluster_ids)


def solution(mesh):
    in_specs = (P(("parts", "gx"), None), P(("parts", "gx")))
    out_specs = P(("parts", "gx"))
    return jax.shard_map(
        on_device, mesh=mesh, in_specs=in_specs, out_specs=out_specs, check_vma=False
    )
```

```python
import functools

import jax
import jax.numpy as jnp
from jax import lax
from jax.experimental import pallas as pl
from jax.experimental.pallas import tpu as pltpu
from jax.sharding import PartitionSpec as P

CLU_DEV = 1
PAD_MARK = 64.0
inverse_temp = 20.0


def tile_mass(query_rows, key_rows, query_ids, key_ids, query_start):
    similar = lax.dot_general(
        query_rows, key_rows, (((1,), (1,)), ((), ())), preferred_element_type=jnp.float32
    )
    query_pos = jnp.arange(query_rows.shape[0], dtype=jnp.int32) + query_start
    key_pos = jnp.arange(key_rows.shape[0], dtype=jnp.int32)
    mate_mask = (query_ids[:, None] == key_ids[None, :]) & (query_ids[:, None] >= 0)
    mate_mask = mate_mask & (query_pos[:, None] != key_pos[None, :])
    return jnp.where(mate_mask, jnp.exp(similar * inverse_temp), 0.0)


def density_scores(key_rows, key_ids):
    total_rows = key_rows.shape[0]
    block_rows = total_rows // 3
    pieces = [key_rows[i * block_rows : (i + 1) * block_rows] for i in range(3)]
    piece_ids = [key_ids[i * block_rows : (i + 1) * block_rows] for i in range(3)]
    sums = []
    for first in range(3):
        masses = tile_mass(pieces[first], key_rows, piece_ids[first], key_ids, first * block_rows)
        sums.append(jnp.sum(masses, axis=1))
    mass_sum = jnp.concatenate(sums, axis=0)
    return jnp.log1p(mass_sum)


def plain_plan(embeddings, cluster_ids):
    peer_count = lax.axis_size("gx")
    row_count = embeddings.shape[0]
    features = embeddings.shape[1]
    capacity = 3 * row_count // peer_count
    slot_total = peer_count * capacity
    squares = jnp.sum(jnp.square(embeddings.astype(jnp.float32)), axis=1)
    unit_rows = (embeddings.astype(jnp.float32) * lax.rsqrt(squares + 1e-06)[:, None]).astype(
        jnp.bfloat16
    )
    owner_of = cluster_ids // CLU_DEV
    onehot = (owner_of[:, None] == jnp.arange(peer_count, dtype=jnp.int32)[None, :]).astype(
        jnp.bfloat16
    )
    row_range = jnp.arange(row_count, dtype=jnp.int32)
    lower_tri = (row_range[:, None] >= row_range[None, :]).astype(jnp.bfloat16)
    running = jnp.dot(lower_tri, onehot, preferred_element_type=jnp.float32)
    slot_index = (jnp.sum(running * onehot.astype(jnp.float32), axis=1) - 1.0).astype(jnp.int32)
    target_slot = owner_of * capacity + slot_index
    slot_range = jnp.arange(slot_total, dtype=jnp.int32)
    select_mask = slot_range[:, None] == target_slot[None, :]
    outgoing = jnp.dot(
        select_mask.astype(jnp.bfloat16), unit_rows, preferred_element_type=jnp.float32
    )
    outgoing = outgoing.astype(jnp.bfloat16).reshape(peer_count, capacity, features)
    outgoing_ids = jnp.sum(jnp.where(select_mask, cluster_ids[None, :] + 1, 0), axis=1) - 1
    outgoing_ids = outgoing_ids.reshape(peer_count, capacity)
    arrived, arrived_ids = (
        lax.all_to_all(outgoing, "gx", split_axis=0, concat_axis=0, tiled=True),
        lax.all_to_all(outgoing_ids, "gx", split_axis=0, concat_axis=0, tiled=True),
    )
    key_rows = arrived.reshape(slot_total, features)
    key_ids = arrived_ids.reshape(slot_total)
    scores = density_scores(key_rows, key_ids)
    returned = lax.all_to_all(
        scores.reshape(peer_count, capacity), "gx", split_axis=0, concat_axis=0, tiled=True
    )
    flat_scores = returned.reshape(slot_total)
    pick_mask = target_slot[:, None] == slot_range[None, :]
    return jnp.sum(jnp.where(pick_mask, flat_scores[None, :], 0.0), axis=1)


LANES = 128
PLANE = 4
ID_ROWS = 16
VMEM_BYTES = 16 * 1024 * 1024


def along_rows(values):
    return jnp.broadcast_to(values, (LANES, values.shape[1])).T


def ids_block(ids, width):
    wide = jnp.concatenate([ids, jnp.zeros((1, width - ids.shape[1]), jnp.float32)], axis=1)
    return jnp.broadcast_to(wide, (ID_ROWS, width)).astype(jnp.bfloat16)


def ids_of(ref):
    first = ref.shape[0] - ID_ROWS
    return ref[first:, :].astype(jnp.float32)[:1]


def mate_mass(query_rows, query_ids, key_rows, key_ids, shift=None):
    similar = lax.dot_general(
        query_rows, key_rows, (((1,), (1,)), ((), ())), preferred_element_type=jnp.float32
    )
    repeats = similar.shape[1] // LANES
    mates = jnp.concatenate([query_ids] * repeats, axis=1) == key_ids
    if shift is not None:
        query_pos = lax.broadcasted_iota(jnp.int32, similar.shape, 0) + shift
        key_pos = lax.broadcasted_iota(jnp.int32, similar.shape, 1)
        mates = mates & (query_pos != key_pos)
    return jnp.where(mates, jnp.exp(similar * inverse_temp), 0.0)


def unit_kernel(rows_ref, ids_ref, block_ref, info_ref):
    rows, width = rows_ref.shape
    features = rows_ref[...].astype(jnp.float32)
    scale = lax.rsqrt(jnp.sum(features * features, axis=1, keepdims=True) + 1e-06)
    ids = ids_ref[...].astype(jnp.float32)
    block_ref[:rows, :] = (features * scale).astype(jnp.bfloat16)
    block_ref[rows:, :] = ids_block(ids, width)
    info_ref[:, :rows] = ids
    info_ref[:, rows:] = jnp.broadcast_to(scale, (rows, LANES)).T[:1]


def across_kernel(rows_ref, info_ref, *piece_refs):
    rows, width = rows_ref.shape
    wide = jnp.concatenate([along_rows(info_ref[:, rows:])] * (width // LANES), axis=1)
    units = (rows_ref[...].astype(jnp.float32) * wide).astype(jnp.bfloat16)
    first = 0
    for ref in piece_refs:
        size = min(ref.shape[0], rows - first)
        ref[:size, :] = units[first : first + size]
        first += size
    piece_refs[-1][size:, :] = ids_block(info_ref[:, :rows], width)


def line_sums(moves, query_parts, ids_ref, line_ref, column_ref, sums_ref):
    rows = column_ref.shape[1]
    plane = lax.axis_index("gx") // PLANE
    arrived = functools.reduce(jnp.logical_or, [plane == receiver for _, receiver in moves])
    column_ref[...] = jnp.zeros_like(column_ref)

    @pl.when(arrived)
    def _():
        key_ids = ids_of(line_ref)[:, :rows]
        column = jnp.zeros((1, rows), jnp.float32)
        first = 0
        for query_ref, size in query_parts:
            part = pl.ds(first, size)
            masses = mate_mass(query_ref[:size, :], ids_ref[part, :], line_ref[:rows, :], key_ids)
            column = column + jnp.sum(masses, axis=0, keepdims=True)
            folded = masses[:, :LANES]
            for lane in range(LANES, rows, LANES):
                folded = folded + masses[:, lane : lane + LANES]
            sums_ref[part, :] += folded
            first += size
        column_ref[...] = column


def query_parts_of(refs, rows):
    sizes = [min(ref.shape[0], rows) for ref in refs[:2]]
    sizes += [rows // 2] * (len(refs) - 2)
    return list(zip(refs, sizes))


def first_kernel(moves, line_ref, *refs):
    query_refs, (ids_ref, column_ref, sums_ref, mass_ref) = refs[:-4], refs[-4:]
    rows = mass_ref.shape[1]
    query_parts = query_parts_of(query_refs, rows)
    own_ref = query_refs[0]
    own_ids = ids_of(own_ref)[:, :rows]
    for m, ref in enumerate((query_refs[0], query_refs[1], query_refs[3], query_refs[5])):
        ids_ref[pl.ds(m * rows, rows), :] = along_rows(ids_of(ref)[:, :rows])
    mass = jnp.zeros((1, rows), jnp.float32)
    first = 0
    for ref, size in query_parts:
        shift = first if first < rows else None
        masses = mate_mass(
            ref[:size, :], ids_ref[pl.ds(first, size), :], own_ref[:rows, :], own_ids, shift
        )
        mass = mass + jnp.sum(masses, axis=0, keepdims=True)
        first += size
    mass_ref[...] = mass
    sums_ref[...] = jnp.zeros_like(sums_ref)
    line_sums(moves, query_parts, ids_ref, line_ref, column_ref, sums_ref)


def last_kernel(moves, line_ref, ids_ref, earlier_ref, mass_ref, back_ref, *refs):
    query_refs, refs = refs[: -PLANE - 2], refs[-PLANE - 2 :]
    column_ref, row_refs, sums_ref = refs[0], refs[1:-1], refs[-1]
    rows = column_ref.shape[1]
    sums_ref[...] = earlier_ref[...]
    line_sums(moves, query_parts_of(query_refs, rows), ids_ref, line_ref, column_ref, sums_ref)
    for m in range(PLANE):
        row_sum = jnp.sum(sums_ref[pl.ds(m * rows, rows), :].T, axis=0, keepdims=True)
        if m == 0:
            row_sum = row_sum + mass_ref[...] + back_ref[...]
        row_refs[m][...] = row_sum


def grid_plan(embeddings, cluster_ids):
    peers = lax.axis_size("gx")
    row_count, features = embeddings.shape
    plane_rows = PLANE * row_count
    params = pltpu.CompilerParams(vmem_limit_bytes=VMEM_BYTES)
    small = pl.CostEstimate(flops=1, bytes_accessed=1, transcendentals=0)
    vector = jax.ShapeDtypeStruct((1, row_count), jnp.float32)
    lanes = jax.ShapeDtypeStruct((plane_rows, LANES), jnp.float32)

    def rows_of(count):
        return jax.ShapeDtypeStruct((count, features), jnp.bfloat16)

    def in_plane(value, step):
        return lax.ppermute(value, "gx", [(i, i ^ step) for i in range(peers)])

    def on_line(value, moves):
        pairs = [(a * PLANE + n, b * PLANE + n) for a, b in moves for n in range(PLANE)]
        return lax.ppermute(value, "gx", pairs)

    first_moves = [(0, 1), (1, 2), (2, 3), (3, 0)]
    last_moves = [(0, 2), (3, 1)]
    first_back = [(b, a) for a, b in first_moves]
    last_back = [(b, a) for a, b in last_moves]

    across_raw = in_plane(embeddings, 2)
    block, info = pl.pallas_call(
        unit_kernel,
        out_shape=(
            rows_of(row_count + ID_ROWS),
            jax.ShapeDtypeStruct((1, 2 * row_count), jnp.float32),
        ),
        cost_estimate=small,
        compiler_params=params,
    )(embeddings, cluster_ids.reshape(1, row_count))
    first_line = on_line(block, first_moves)
    last_line = on_line(block, last_moves)
    sibling = in_plane(block, 1)
    across = pl.pallas_call(
        across_kernel,
        out_shape=(rows_of(row_count // 2), rows_of(row_count // 2 + ID_ROWS)),
        cost_estimate=small,
        compiler_params=params,
    )(across_raw, in_plane(info, 2))
    corner = [in_plane(piece, 1) for piece in across]
    queries = (block, sibling, *across, *corner)
    ids, first_column, first_sums, mass = pl.pallas_call(
        functools.partial(first_kernel, first_moves),
        out_shape=(lanes, vector, lanes, vector),
        cost_estimate=small,
        compiler_params=params,
    )(first_line, *queries)
    returned_first = on_line(first_column, first_back)
    last_column, *row_sums = pl.pallas_call(
        functools.partial(last_kernel, last_moves),
        out_shape=[vector] * (1 + PLANE),
        scratch_shapes=[pltpu.VMEM(lanes.shape, lanes.dtype)],
        compiler_params=params,
    )(last_line, ids, first_sums, mass, returned_first, *queries)
    returned = [on_line(last_column, last_back)]
    returned += [in_plane(row_sums[step], step) for step in (2, 3, 1)]
    return jnp.log1p(sum(returned, row_sums[0])).reshape(row_count)


def on_device(embeddings, cluster_ids):
    if lax.axis_size("gx") == 4 * PLANE and embeddings.shape[0] % (2 * LANES) == 0:
        return grid_plan(embeddings, cluster_ids)
    return plain_plan(embeddings, cluster_ids)


def solution(mesh):
    in_specs = (P(("parts", "gx"), None), P(("parts", "gx")))
    out_specs = P(("parts", "gx"))
    return jax.shard_map(
        on_device, mesh=mesh, in_specs=in_specs, out_specs=out_specs, check_vma=False
    )
```

```python
import functools

import jax
import jax.numpy as jnp
from jax import lax
from jax.experimental import pallas as pl
from jax.experimental.pallas import tpu as pltpu
from jax.sharding import PartitionSpec as P

CLU_DEV = 1
PAD_MARK = 64.0
inverse_temp = 20.0


def tile_mass(query_rows, key_rows, query_ids, key_ids, query_start):
    similar = lax.dot_general(
        query_rows, key_rows, (((1,), (1,)), ((), ())), preferred_element_type=jnp.float32
    )
    query_pos = jnp.arange(query_rows.shape[0], dtype=jnp.int32) + query_start
    key_pos = jnp.arange(key_rows.shape[0], dtype=jnp.int32)
    mate_mask = (query_ids[:, None] == key_ids[None, :]) & (query_ids[:, None] >= 0)
    mate_mask = mate_mask & (query_pos[:, None] != key_pos[None, :])
    return jnp.where(mate_mask, jnp.exp(similar * inverse_temp), 0.0)


def density_scores(key_rows, key_ids):
    total_rows = key_rows.shape[0]
    block_rows = total_rows // 3
    pieces = [key_rows[i * block_rows : (i + 1) * block_rows] for i in range(3)]
    piece_ids = [key_ids[i * block_rows : (i + 1) * block_rows] for i in range(3)]
    sums = []
    for first in range(3):
        masses = tile_mass(pieces[first], key_rows, piece_ids[first], key_ids, first * block_rows)
        sums.append(jnp.sum(masses, axis=1))
    mass_sum = jnp.concatenate(sums, axis=0)
    return jnp.log1p(mass_sum)


def plain_plan(embeddings, cluster_ids):
    peer_count = lax.axis_size("gx")
    row_count = embeddings.shape[0]
    features = embeddings.shape[1]
    capacity = 3 * row_count // peer_count
    slot_total = peer_count * capacity
    squares = jnp.sum(jnp.square(embeddings.astype(jnp.float32)), axis=1)
    unit_rows = (embeddings.astype(jnp.float32) * lax.rsqrt(squares + 1e-06)[:, None]).astype(
        jnp.bfloat16
    )
    owner_of = cluster_ids // CLU_DEV
    onehot = (owner_of[:, None] == jnp.arange(peer_count, dtype=jnp.int32)[None, :]).astype(
        jnp.bfloat16
    )
    row_range = jnp.arange(row_count, dtype=jnp.int32)
    lower_tri = (row_range[:, None] >= row_range[None, :]).astype(jnp.bfloat16)
    running = jnp.dot(lower_tri, onehot, preferred_element_type=jnp.float32)
    slot_index = (jnp.sum(running * onehot.astype(jnp.float32), axis=1) - 1.0).astype(jnp.int32)
    target_slot = owner_of * capacity + slot_index
    slot_range = jnp.arange(slot_total, dtype=jnp.int32)
    select_mask = slot_range[:, None] == target_slot[None, :]
    outgoing = jnp.dot(
        select_mask.astype(jnp.bfloat16), unit_rows, preferred_element_type=jnp.float32
    )
    outgoing = outgoing.astype(jnp.bfloat16).reshape(peer_count, capacity, features)
    outgoing_ids = jnp.sum(jnp.where(select_mask, cluster_ids[None, :] + 1, 0), axis=1) - 1
    outgoing_ids = outgoing_ids.reshape(peer_count, capacity)
    arrived, arrived_ids = (
        lax.all_to_all(outgoing, "gx", split_axis=0, concat_axis=0, tiled=True),
        lax.all_to_all(outgoing_ids, "gx", split_axis=0, concat_axis=0, tiled=True),
    )
    key_rows = arrived.reshape(slot_total, features)
    key_ids = arrived_ids.reshape(slot_total)
    scores = density_scores(key_rows, key_ids)
    returned = lax.all_to_all(
        scores.reshape(peer_count, capacity), "gx", split_axis=0, concat_axis=0, tiled=True
    )
    flat_scores = returned.reshape(slot_total)
    pick_mask = target_slot[:, None] == slot_range[None, :]
    return jnp.sum(jnp.where(pick_mask, flat_scores[None, :], 0.0), axis=1)


LANES = 128
PLANE = 4
ID_ROWS = 16
VMEM_BYTES = 16 * 1024 * 1024


def along_rows(values):
    return jnp.broadcast_to(values, (LANES, values.shape[1])).T


def ids_block(ids, width):
    wide = jnp.concatenate([ids, jnp.zeros((1, width - ids.shape[1]), jnp.float32)], axis=1)
    return jnp.broadcast_to(wide, (ID_ROWS, width)).astype(jnp.bfloat16)


def ids_of(ref):
    first = ref.shape[0] - ID_ROWS
    return ref[first:, :].astype(jnp.float32)[:1]


def mate_mass(query_rows, query_ids, key_rows, key_ids, shift=None):
    similar = lax.dot_general(
        query_rows, key_rows, (((1,), (1,)), ((), ())), preferred_element_type=jnp.float32
    )
    repeats = similar.shape[1] // LANES
    mates = jnp.concatenate([query_ids] * repeats, axis=1) == key_ids
    if shift is not None:
        query_pos = lax.broadcasted_iota(jnp.int32, similar.shape, 0) + shift
        key_pos = lax.broadcasted_iota(jnp.int32, similar.shape, 1)
        mates = mates & (query_pos != key_pos)
    return jnp.where(mates, jnp.exp(similar * inverse_temp), 0.0)


def unit_kernel(rows_ref, ids_ref, units_ref, info_ref, *block_refs):
    rows, width = rows_ref.shape
    features = rows_ref[...].astype(jnp.float32)
    scale = lax.rsqrt(jnp.sum(features * features, axis=1, keepdims=True) + 1e-06)
    ids = ids_ref[...].astype(jnp.float32)
    units = (features * scale).astype(jnp.bfloat16)
    units_ref[...] = units
    info_ref[:, :rows] = ids
    info_ref[:, rows:] = jnp.broadcast_to(scale, (rows, LANES)).T[:1]
    first = 0
    for ref in block_refs:
        size = min(ref.shape[0], rows - first)
        ref[:size, :] = units[first : first + size]
        if ref.shape[0] > size:
            ref[size:, :] = ids_block(ids, width)
        first = (first + size) % rows


def scaled_rows(rows_ref, info_ref):
    rows, width = rows_ref.shape
    wide = jnp.concatenate([along_rows(info_ref[:, rows:])] * (width // LANES), axis=1)
    return (rows_ref[...].astype(jnp.float32) * wide).astype(jnp.bfloat16)


def line_sums(moves, query_parts, ids_ref, info_ref, line_ref, is_raw, column_ref, sums_ref):
    rows = column_ref.shape[1]
    plane = lax.axis_index("gx") // PLANE
    arrived = functools.reduce(jnp.logical_or, [plane == receiver for _, receiver in moves])
    column_ref[...] = jnp.zeros_like(column_ref)

    @pl.when(arrived)
    def _():
        key_ids = info_ref[:, :rows]
        key_rows = scaled_rows(line_ref, info_ref) if is_raw else line_ref[...]
        column = jnp.zeros((1, rows), jnp.float32)
        first = 0
        for query_ref, size in query_parts:
            part = pl.ds(first, size)
            masses = mate_mass(query_ref[:size, :], ids_ref[part, :], key_rows, key_ids)
            column = column + jnp.sum(masses, axis=0, keepdims=True)
            folded = masses[:, :LANES]
            for lane in range(LANES, rows, LANES):
                folded = folded + masses[:, lane : lane + LANES]
            sums_ref[part, :] += folded
            first += size
        column_ref[...] = column


def query_parts_of(refs, rows):
    return [(ref, rows) for ref in refs[:3]] + [(ref, rows // 2) for ref in refs[3:]]


def first_kernel(moves, info_ref, line_ref, *refs):
    query_refs, (ids_ref, column_ref, sums_ref, mass_ref) = refs[:-4], refs[-4:]
    rows = mass_ref.shape[1]
    query_parts = query_parts_of(query_refs, rows)
    own_ref = query_refs[0]
    own_ids = ids_of(own_ref)[:, :rows]
    for m, ref in enumerate((*query_refs[:3], query_refs[4])):
        ids_ref[pl.ds(m * rows, rows), :] = along_rows(ids_of(ref)[:, :rows])
    mass = jnp.zeros((1, rows), jnp.float32)
    first = 0
    for ref, size in query_parts:
        shift = first if first < rows else None
        masses = mate_mass(
            ref[:size, :], ids_ref[pl.ds(first, size), :], own_ref[:rows, :], own_ids, shift
        )
        mass = mass + jnp.sum(masses, axis=0, keepdims=True)
        first += size
    mass_ref[...] = mass
    sums_ref[...] = jnp.zeros_like(sums_ref)
    line_sums(moves, query_parts, ids_ref, info_ref, line_ref, True, column_ref, sums_ref)


def last_kernel(moves, info_ref, line_ref, ids_ref, earlier_ref, mass_ref, back_ref, *refs):
    query_refs, refs = refs[: -PLANE - 2], refs[-PLANE - 2 :]
    column_ref, row_refs, sums_ref = refs[0], refs[1:-1], refs[-1]
    rows = column_ref.shape[1]
    sums_ref[...] = earlier_ref[...]
    query_parts = query_parts_of(query_refs, rows)
    line_sums(moves, query_parts, ids_ref, info_ref, line_ref, False, column_ref, sums_ref)
    for m in range(PLANE):
        row_sum = jnp.sum(sums_ref[pl.ds(m * rows, rows), :].T, axis=0, keepdims=True)
        if m == 0:
            row_sum = row_sum + mass_ref[...] + back_ref[...]
        row_refs[m][...] = row_sum


def grid_plan(embeddings, cluster_ids):
    peers = lax.axis_size("gx")
    row_count, features = embeddings.shape
    plane_rows = PLANE * row_count
    params = pltpu.CompilerParams(vmem_limit_bytes=VMEM_BYTES)
    small = pl.CostEstimate(flops=1, bytes_accessed=1, transcendentals=0)
    vector = jax.ShapeDtypeStruct((1, row_count), jnp.float32)
    lanes = jax.ShapeDtypeStruct((plane_rows, LANES), jnp.float32)

    def rows_of(count):
        return jax.ShapeDtypeStruct((count, features), jnp.bfloat16)

    def in_plane(value, step):
        return lax.ppermute(value, "gx", [(i, i ^ step) for i in range(peers)])

    def on_line(value, moves):
        pairs = [(a * PLANE + n, b * PLANE + n) for a, b in moves for n in range(PLANE)]
        return lax.ppermute(value, "gx", pairs)

    first_moves = [(0, 1), (1, 2), (2, 3), (3, 0)]
    last_moves = [(0, 2), (3, 1)]
    first_back = [(b, a) for a, b in first_moves]
    last_back = [(b, a) for a, b in last_moves]

    half = row_count // 2
    first_line = on_line(embeddings, first_moves)
    units, info, block = pl.pallas_call(
        unit_kernel,
        out_shape=(
            rows_of(row_count),
            jax.ShapeDtypeStruct((1, 2 * row_count), jnp.float32),
            rows_of(row_count + ID_ROWS),
        ),
        cost_estimate=small,
        compiler_params=params,
    )(embeddings, cluster_ids.reshape(1, row_count))
    across = in_plane(block, 2)
    sibling = in_plane(block, 1)
    first_info, last_info = on_line(info, first_moves), on_line(info, last_moves)
    first_line, first_info, last_info, units = lax.optimization_barrier(
        (first_line, first_info, last_info, units)
    )
    last_line = on_line(units, last_moves)
    corner = [in_plane(piece, 1) for piece in (across[:half], across[half:])]
    queries = (block, sibling, across, *corner)
    ids, first_column, first_sums, mass = pl.pallas_call(
        functools.partial(first_kernel, first_moves),
        out_shape=(lanes, vector, lanes, vector),
        cost_estimate=small,
        compiler_params=params,
    )(first_info, first_line, *queries)
    returned_first = on_line(first_column, first_back)
    last_column, *row_sums = pl.pallas_call(
        functools.partial(last_kernel, last_moves),
        out_shape=[vector] * (1 + PLANE),
        scratch_shapes=[pltpu.VMEM(lanes.shape, lanes.dtype)],
        compiler_params=params,
    )(last_info, last_line, ids, first_sums, mass, returned_first, *queries)
    returned = [on_line(last_column, last_back)]
    returned += [in_plane(row_sums[step], step) for step in (2, 3, 1)]
    return jnp.log1p(sum(returned, row_sums[0])).reshape(row_count)


def on_device(embeddings, cluster_ids):
    if lax.axis_size("gx") == 4 * PLANE and embeddings.shape[0] % (2 * LANES) == 0:
        return grid_plan(embeddings, cluster_ids)
    return plain_plan(embeddings, cluster_ids)


def solution(mesh):
    in_specs = (P(("parts", "gx"), None), P(("parts", "gx")))
    out_specs = P(("parts", "gx"))
    return jax.shard_map(
        on_device, mesh=mesh, in_specs=in_specs, out_specs=out_specs, check_vma=False
    )
```

```python
import functools

import jax
import jax.numpy as jnp
from jax import lax
from jax.experimental import pallas as pl
from jax.experimental.pallas import tpu as pltpu
from jax.sharding import PartitionSpec as P

CLU_DEV = 1
PAD_MARK = 64.0
inverse_temp = 20.0


def tile_mass(query_rows, key_rows, query_ids, key_ids, query_start):
    similar = lax.dot_general(
        query_rows, key_rows, (((1,), (1,)), ((), ())), preferred_element_type=jnp.float32
    )
    query_pos = jnp.arange(query_rows.shape[0], dtype=jnp.int32) + query_start
    key_pos = jnp.arange(key_rows.shape[0], dtype=jnp.int32)
    mate_mask = (query_ids[:, None] == key_ids[None, :]) & (query_ids[:, None] >= 0)
    mate_mask = mate_mask & (query_pos[:, None] != key_pos[None, :])
    return jnp.where(mate_mask, jnp.exp(similar * inverse_temp), 0.0)


def density_scores(key_rows, key_ids):
    total_rows = key_rows.shape[0]
    block_rows = total_rows // 3
    pieces = [key_rows[i * block_rows : (i + 1) * block_rows] for i in range(3)]
    piece_ids = [key_ids[i * block_rows : (i + 1) * block_rows] for i in range(3)]
    sums = []
    for first in range(3):
        masses = tile_mass(pieces[first], key_rows, piece_ids[first], key_ids, first * block_rows)
        sums.append(jnp.sum(masses, axis=1))
    mass_sum = jnp.concatenate(sums, axis=0)
    return jnp.log1p(mass_sum)


def plain_plan(embeddings, cluster_ids):
    peer_count = lax.axis_size("gx")
    row_count = embeddings.shape[0]
    features = embeddings.shape[1]
    capacity = 3 * row_count // peer_count
    slot_total = peer_count * capacity
    squares = jnp.sum(jnp.square(embeddings.astype(jnp.float32)), axis=1)
    unit_rows = (embeddings.astype(jnp.float32) * lax.rsqrt(squares + 1e-06)[:, None]).astype(
        jnp.bfloat16
    )
    owner_of = cluster_ids // CLU_DEV
    onehot = (owner_of[:, None] == jnp.arange(peer_count, dtype=jnp.int32)[None, :]).astype(
        jnp.bfloat16
    )
    row_range = jnp.arange(row_count, dtype=jnp.int32)
    lower_tri = (row_range[:, None] >= row_range[None, :]).astype(jnp.bfloat16)
    running = jnp.dot(lower_tri, onehot, preferred_element_type=jnp.float32)
    slot_index = (jnp.sum(running * onehot.astype(jnp.float32), axis=1) - 1.0).astype(jnp.int32)
    target_slot = owner_of * capacity + slot_index
    slot_range = jnp.arange(slot_total, dtype=jnp.int32)
    select_mask = slot_range[:, None] == target_slot[None, :]
    outgoing = jnp.dot(
        select_mask.astype(jnp.bfloat16), unit_rows, preferred_element_type=jnp.float32
    )
    outgoing = outgoing.astype(jnp.bfloat16).reshape(peer_count, capacity, features)
    outgoing_ids = jnp.sum(jnp.where(select_mask, cluster_ids[None, :] + 1, 0), axis=1) - 1
    outgoing_ids = outgoing_ids.reshape(peer_count, capacity)
    arrived, arrived_ids = (
        lax.all_to_all(outgoing, "gx", split_axis=0, concat_axis=0, tiled=True),
        lax.all_to_all(outgoing_ids, "gx", split_axis=0, concat_axis=0, tiled=True),
    )
    key_rows = arrived.reshape(slot_total, features)
    key_ids = arrived_ids.reshape(slot_total)
    scores = density_scores(key_rows, key_ids)
    returned = lax.all_to_all(
        scores.reshape(peer_count, capacity), "gx", split_axis=0, concat_axis=0, tiled=True
    )
    flat_scores = returned.reshape(slot_total)
    pick_mask = target_slot[:, None] == slot_range[None, :]
    return jnp.sum(jnp.where(pick_mask, flat_scores[None, :], 0.0), axis=1)


LANES = 128
PLANE = 4
ID_ROWS = 16
VMEM_BYTES = 16 * 1024 * 1024


def along_rows(values):
    return jnp.broadcast_to(values, (LANES, values.shape[1])).T


def ids_block(ids, width):
    wide = jnp.concatenate([ids, jnp.zeros((1, width - ids.shape[1]), jnp.float32)], axis=1)
    return jnp.broadcast_to(wide, (ID_ROWS, width)).astype(jnp.bfloat16)


def ids_of(ref):
    first = ref.shape[0] - ID_ROWS
    return ref[first:, :].astype(jnp.float32)[:1]


def mate_mass(query_rows, query_ids, key_rows, key_ids, shift=None):
    similar = lax.dot_general(
        query_rows, key_rows, (((1,), (1,)), ((), ())), preferred_element_type=jnp.float32
    )
    repeats = similar.shape[1] // LANES
    mates = jnp.concatenate([query_ids] * repeats, axis=1) == key_ids
    if shift is not None:
        query_pos = lax.broadcasted_iota(jnp.int32, similar.shape, 0) + shift
        key_pos = lax.broadcasted_iota(jnp.int32, similar.shape, 1)
        mates = mates & (query_pos != key_pos)
    return jnp.where(mates, jnp.exp(similar * inverse_temp), 0.0)


def unit_kernel(rows_ref, ids_ref, *block_refs):
    rows, width = rows_ref.shape
    features = rows_ref[...].astype(jnp.float32)
    scale = lax.rsqrt(jnp.sum(features * features, axis=1, keepdims=True) + 1e-06)
    units = (features * scale).astype(jnp.bfloat16)
    ids = ids_block(ids_ref[...].astype(jnp.float32), width)
    first = 0
    for ref in block_refs:
        size = min(ref.shape[0], rows - first)
        ref[:size, :] = units[first : first + size]
        if ref.shape[0] > size:
            ref[size:, :] = ids
        first = (first + size) % rows


def line_sums(moves, query_parts, ids_ref, line_ref, column_ref, sums_ref):
    rows = column_ref.shape[1]
    plane = lax.axis_index("gx") // PLANE
    arrived = functools.reduce(jnp.logical_or, [plane == receiver for _, receiver in moves])
    column_ref[...] = jnp.zeros_like(column_ref)

    @pl.when(arrived)
    def _():
        key_ids = ids_of(line_ref)[:, :rows]
        column = jnp.zeros((1, rows), jnp.float32)
        first = 0
        for query_ref, size in query_parts:
            part = pl.ds(first, size)
            masses = mate_mass(query_ref[:size, :], ids_ref[part, :], line_ref[:rows, :], key_ids)
            column = column + jnp.sum(masses, axis=0, keepdims=True)
            folded = masses[:, :LANES]
            for lane in range(LANES, rows, LANES):
                folded = folded + masses[:, lane : lane + LANES]
            sums_ref[part, :] += folded
            first += size
        column_ref[...] = column


def query_parts_of(refs, rows):
    head = refs[2].shape[0]
    sizes = [rows, rows] + [head, rows - head] * (PLANE - 2)
    return list(zip(refs, sizes))


def first_kernel(moves, line_ref, *refs):
    query_refs, (ids_ref, column_ref, sums_ref, mass_ref) = refs[:-4], refs[-4:]
    rows = mass_ref.shape[1]
    query_parts = query_parts_of(query_refs, rows)
    own_ref = query_refs[0]
    own_ids = ids_of(own_ref)[:, :rows]
    for m, ref in enumerate((*query_refs[:2], query_refs[3], query_refs[5])):
        ids_ref[pl.ds(m * rows, rows), :] = along_rows(ids_of(ref)[:, :rows])
    mass = jnp.zeros((1, rows), jnp.float32)
    first = 0
    for ref, size in query_parts:
        shift = first if first < rows else None
        masses = mate_mass(
            ref[:size, :], ids_ref[pl.ds(first, size), :], own_ref[:rows, :], own_ids, shift
        )
        mass = mass + jnp.sum(masses, axis=0, keepdims=True)
        first += size
    mass_ref[...] = mass
    sums_ref[...] = jnp.zeros_like(sums_ref)
    line_sums(moves, query_parts, ids_ref, line_ref, column_ref, sums_ref)


def last_kernel(moves, line_ref, ids_ref, earlier_ref, mass_ref, back_ref, *refs):
    query_refs, refs = refs[: -PLANE - 2], refs[-PLANE - 2 :]
    column_ref, row_refs, sums_ref = refs[0], refs[1:-1], refs[-1]
    rows = column_ref.shape[1]
    sums_ref[...] = earlier_ref[...]
    query_parts = query_parts_of(query_refs, rows)
    line_sums(moves, query_parts, ids_ref, line_ref, column_ref, sums_ref)
    for m in range(PLANE):
        row_sum = jnp.sum(sums_ref[pl.ds(m * rows, rows), :].T, axis=0, keepdims=True)
        if m == 0:
            row_sum = row_sum + mass_ref[...] + back_ref[...]
        row_refs[m][...] = row_sum


def grid_plan(embeddings, cluster_ids):
    peers = lax.axis_size("gx")
    row_count, features = embeddings.shape
    plane_rows = PLANE * row_count
    params = pltpu.CompilerParams(vmem_limit_bytes=VMEM_BYTES)
    small = pl.CostEstimate(flops=1, bytes_accessed=1, transcendentals=0)
    vector = jax.ShapeDtypeStruct((1, row_count), jnp.float32)
    lanes = jax.ShapeDtypeStruct((plane_rows, LANES), jnp.float32)

    def rows_of(count):
        return jax.ShapeDtypeStruct((count, features), jnp.bfloat16)

    def in_plane(value, step):
        return lax.ppermute(value, "gx", [(i, i ^ step) for i in range(peers)])

    def on_line(value, moves):
        pairs = [(a * PLANE + n, b * PLANE + n) for a, b in moves for n in range(PLANE)]
        return lax.ppermute(value, "gx", pairs)

    first_moves = [(0, 1), (1, 2), (2, 3), (3, 0)]
    last_moves = [(1, 3), (2, 0)]
    first_back = [(b, a) for a, b in first_moves]
    last_back = [(b, a) for a, b in last_moves]

    head = 3 * row_count // 8
    block, *pieces = pl.pallas_call(
        unit_kernel,
        out_shape=(
            rows_of(row_count + ID_ROWS),
            rows_of(head),
            rows_of(row_count - head + ID_ROWS),
        ),
        cost_estimate=small,
        compiler_params=params,
    )(embeddings, cluster_ids.reshape(1, row_count))
    first_line = on_line(block, first_moves)
    last_line = on_line(block, last_moves)
    across = [in_plane(piece, 2) for piece in pieces]
    sibling = in_plane(block, 1)
    first_line, across[1] = lax.optimization_barrier((first_line, across[1]))
    corner = [in_plane(piece, 1) for piece in across]
    queries = (block, sibling, *across, *corner)
    ids, first_column, first_sums, mass = pl.pallas_call(
        functools.partial(first_kernel, first_moves),
        out_shape=(lanes, vector, lanes, vector),
        cost_estimate=small,
        compiler_params=params,
    )(first_line, *queries)
    returned_first = on_line(first_column, first_back)
    last_column, *row_sums = pl.pallas_call(
        functools.partial(last_kernel, last_moves),
        out_shape=[vector] * (1 + PLANE),
        scratch_shapes=[pltpu.VMEM(lanes.shape, lanes.dtype)],
        compiler_params=params,
    )(last_line, ids, first_sums, mass, returned_first, *queries)
    returned = [on_line(last_column, last_back)]
    returned += [in_plane(row_sums[step], step) for step in (2, 3, 1)]
    return jnp.log1p(sum(returned, row_sums[0])).reshape(row_count)


def on_device(embeddings, cluster_ids):
    if lax.axis_size("gx") == 4 * PLANE and embeddings.shape[0] % (2 * LANES) == 0:
        return grid_plan(embeddings, cluster_ids)
    return plain_plan(embeddings, cluster_ids)


def solution(mesh):
    in_specs = (P(("parts", "gx"), None), P(("parts", "gx")))
    out_specs = P(("parts", "gx"))
    return jax.shard_map(
        on_device, mesh=mesh, in_specs=in_specs, out_specs=out_specs, check_vma=False
    )
```

```python
import functools

import jax
import jax.numpy as jnp
from jax import lax
from jax.experimental import pallas as pl
from jax.experimental.pallas import tpu as pltpu
from jax.sharding import PartitionSpec as P

CLU_DEV = 1
PAD_MARK = 64.0
inverse_temp = 20.0


def tile_mass(query_rows, key_rows, query_ids, key_ids, query_start):
    similar = lax.dot_general(
        query_rows, key_rows, (((1,), (1,)), ((), ())), preferred_element_type=jnp.float32
    )
    query_pos = jnp.arange(query_rows.shape[0], dtype=jnp.int32) + query_start
    key_pos = jnp.arange(key_rows.shape[0], dtype=jnp.int32)
    mate_mask = (query_ids[:, None] == key_ids[None, :]) & (query_ids[:, None] >= 0)
    mate_mask = mate_mask & (query_pos[:, None] != key_pos[None, :])
    return jnp.where(mate_mask, jnp.exp(similar * inverse_temp), 0.0)


def density_scores(key_rows, key_ids):
    total_rows = key_rows.shape[0]
    block_rows = total_rows // 3
    pieces = [key_rows[i * block_rows : (i + 1) * block_rows] for i in range(3)]
    piece_ids = [key_ids[i * block_rows : (i + 1) * block_rows] for i in range(3)]
    sums = []
    for first in range(3):
        masses = tile_mass(pieces[first], key_rows, piece_ids[first], key_ids, first * block_rows)
        sums.append(jnp.sum(masses, axis=1))
    mass_sum = jnp.concatenate(sums, axis=0)
    return jnp.log1p(mass_sum)


def plain_plan(embeddings, cluster_ids):
    peer_count = lax.axis_size("gx")
    row_count = embeddings.shape[0]
    features = embeddings.shape[1]
    capacity = 3 * row_count // peer_count
    slot_total = peer_count * capacity
    squares = jnp.sum(jnp.square(embeddings.astype(jnp.float32)), axis=1)
    unit_rows = (embeddings.astype(jnp.float32) * lax.rsqrt(squares + 1e-06)[:, None]).astype(
        jnp.bfloat16
    )
    owner_of = cluster_ids // CLU_DEV
    onehot = (owner_of[:, None] == jnp.arange(peer_count, dtype=jnp.int32)[None, :]).astype(
        jnp.bfloat16
    )
    row_range = jnp.arange(row_count, dtype=jnp.int32)
    lower_tri = (row_range[:, None] >= row_range[None, :]).astype(jnp.bfloat16)
    running = jnp.dot(lower_tri, onehot, preferred_element_type=jnp.float32)
    slot_index = (jnp.sum(running * onehot.astype(jnp.float32), axis=1) - 1.0).astype(jnp.int32)
    target_slot = owner_of * capacity + slot_index
    slot_range = jnp.arange(slot_total, dtype=jnp.int32)
    select_mask = slot_range[:, None] == target_slot[None, :]
    outgoing = jnp.dot(
        select_mask.astype(jnp.bfloat16), unit_rows, preferred_element_type=jnp.float32
    )
    outgoing = outgoing.astype(jnp.bfloat16).reshape(peer_count, capacity, features)
    outgoing_ids = jnp.sum(jnp.where(select_mask, cluster_ids[None, :] + 1, 0), axis=1) - 1
    outgoing_ids = outgoing_ids.reshape(peer_count, capacity)
    arrived, arrived_ids = (
        lax.all_to_all(outgoing, "gx", split_axis=0, concat_axis=0, tiled=True),
        lax.all_to_all(outgoing_ids, "gx", split_axis=0, concat_axis=0, tiled=True),
    )
    key_rows = arrived.reshape(slot_total, features)
    key_ids = arrived_ids.reshape(slot_total)
    scores = density_scores(key_rows, key_ids)
    returned = lax.all_to_all(
        scores.reshape(peer_count, capacity), "gx", split_axis=0, concat_axis=0, tiled=True
    )
    flat_scores = returned.reshape(slot_total)
    pick_mask = target_slot[:, None] == slot_range[None, :]
    return jnp.sum(jnp.where(pick_mask, flat_scores[None, :], 0.0), axis=1)


LANES = 128
PLANE = 4
ID_ROWS = 16
VMEM_BYTES = 16 * 1024 * 1024


def along_rows(values):
    return jnp.broadcast_to(values, (LANES, values.shape[1])).T


def ids_block(ids, width):
    wide = jnp.concatenate([ids, jnp.zeros((1, width - ids.shape[1]), jnp.float32)], axis=1)
    return jnp.broadcast_to(wide, (ID_ROWS, width)).astype(jnp.bfloat16)


def ids_of(ref):
    first = ref.shape[0] - ID_ROWS
    return ref[first:, :].astype(jnp.float32)[:1]


def mate_mass(query_rows, query_ids, key_rows, key_ids, shift=None):
    similar = lax.dot_general(
        query_rows, key_rows, (((1,), (1,)), ((), ())), preferred_element_type=jnp.float32
    )
    repeats = similar.shape[1] // LANES
    mates = jnp.concatenate([query_ids] * repeats, axis=1) == key_ids
    if shift is not None:
        query_pos = lax.broadcasted_iota(jnp.int32, similar.shape, 0) + shift
        key_pos = lax.broadcasted_iota(jnp.int32, similar.shape, 1)
        mates = mates & (query_pos != key_pos)
    return jnp.where(mates, jnp.exp(similar * inverse_temp), 0.0)


def unit_kernel(rows_ref, ids_ref, *block_refs):
    rows, width = rows_ref.shape
    features = rows_ref[...].astype(jnp.float32)
    scale = lax.rsqrt(jnp.sum(features * features, axis=1, keepdims=True) + 1e-06)
    units = (features * scale).astype(jnp.bfloat16)
    ids = ids_block(ids_ref[...].astype(jnp.float32), width)
    first = 0
    for ref in block_refs:
        size = min(ref.shape[0], rows - first)
        ref[:size, :] = units[first : first + size]
        if ref.shape[0] > size:
            ref[size:, :] = ids
        first = (first + size) % rows


def line_sums(moves, query_parts, ids_ref, line_ref, column_ref, sums_ref):
    rows = column_ref.shape[1]
    plane = lax.axis_index("gx") // PLANE
    arrived = functools.reduce(jnp.logical_or, [plane == receiver for _, receiver in moves])
    column_ref[...] = jnp.zeros_like(column_ref)

    @pl.when(arrived)
    def _():
        key_ids = ids_of(line_ref)[:, :rows]
        column = jnp.zeros((1, rows), jnp.float32)
        first = 0
        for query_ref, size in query_parts:
            part = pl.ds(first, size)
            masses = mate_mass(query_ref[:size, :], ids_ref[part, :], line_ref[:rows, :], key_ids)
            column = column + jnp.sum(masses, axis=0, keepdims=True)
            folded = masses[:, :LANES]
            for lane in range(LANES, rows, LANES):
                folded = folded + masses[:, lane : lane + LANES]
            sums_ref[part, :] += folded
            first += size
        column_ref[...] = column


def query_parts_of(refs, rows):
    head = refs[2].shape[0]
    sizes = [rows, rows] + [head, rows - head] * (PLANE - 2)
    return list(zip(refs, sizes))


def first_kernel(moves, line_ref, *refs):
    query_refs, (ids_ref, column_ref, sums_ref, mass_ref) = refs[:-4], refs[-4:]
    rows = mass_ref.shape[1]
    query_parts = query_parts_of(query_refs, rows)
    own_ref = query_refs[0]
    own_ids = ids_of(own_ref)[:, :rows]
    for m, ref in enumerate((*query_refs[:2], query_refs[3], query_refs[5])):
        ids_ref[pl.ds(m * rows, rows), :] = along_rows(ids_of(ref)[:, :rows])
    mass = jnp.zeros((1, rows), jnp.float32)
    first = 0
    for ref, size in query_parts:
        shift = first if first < rows else None
        masses = mate_mass(
            ref[:size, :], ids_ref[pl.ds(first, size), :], own_ref[:rows, :], own_ids, shift
        )
        mass = mass + jnp.sum(masses, axis=0, keepdims=True)
        first += size
    mass_ref[...] = mass
    sums_ref[...] = jnp.zeros_like(sums_ref)
    line_sums(moves, query_parts, ids_ref, line_ref, column_ref, sums_ref)


def last_kernel(moves, line_ref, ids_ref, earlier_ref, mass_ref, back_ref, *refs):
    query_refs, refs = refs[: -PLANE - 2], refs[-PLANE - 2 :]
    column_ref, row_refs, sums_ref = refs[0], refs[1:-1], refs[-1]
    rows = column_ref.shape[1]
    sums_ref[...] = earlier_ref[...]
    query_parts = query_parts_of(query_refs, rows)
    line_sums(moves, query_parts, ids_ref, line_ref, column_ref, sums_ref)
    for m in range(PLANE):
        row_sum = jnp.sum(sums_ref[pl.ds(m * rows, rows), :].T, axis=0, keepdims=True)
        if m == 0:
            row_sum = row_sum + mass_ref[...] + back_ref[...]
        row_refs[m][...] = row_sum


def grid_plan(embeddings, cluster_ids):
    peers = lax.axis_size("gx")
    row_count, features = embeddings.shape
    plane_rows = PLANE * row_count
    params = pltpu.CompilerParams(vmem_limit_bytes=VMEM_BYTES)
    small = pl.CostEstimate(flops=1, bytes_accessed=1, transcendentals=0)
    vector = jax.ShapeDtypeStruct((1, row_count), jnp.float32)
    lanes = jax.ShapeDtypeStruct((plane_rows, LANES), jnp.float32)

    def rows_of(count):
        return jax.ShapeDtypeStruct((count, features), jnp.bfloat16)

    def in_plane(value, step):
        return lax.ppermute(value, "gx", [(i, i ^ step) for i in range(peers)])

    def on_line(value, moves):
        pairs = [(a * PLANE + n, b * PLANE + n) for a, b in moves for n in range(PLANE)]
        return lax.ppermute(value, "gx", pairs)

    first_moves = [(0, 1), (1, 2), (2, 3), (3, 0)]
    last_moves = [(0, 2), (3, 1)]
    first_back = [(b, a) for a, b in first_moves]
    last_back = [(b, a) for a, b in last_moves]

    head = 7 * row_count // 16
    block, *pieces = pl.pallas_call(
        unit_kernel,
        out_shape=(
            rows_of(row_count + ID_ROWS),
            rows_of(head),
            rows_of(row_count - head + ID_ROWS),
        ),
        cost_estimate=small,
        compiler_params=params,
    )(embeddings, cluster_ids.reshape(1, row_count))
    first_line = on_line(block, first_moves)
    across = [in_plane(piece, 2) for piece in pieces]
    sibling = in_plane(block, 1)
    across[0], late_block = lax.optimization_barrier((across[0], block))
    last_line = on_line(late_block, last_moves)
    first_line, across[1] = lax.optimization_barrier((first_line, across[1]))
    corner = [in_plane(piece, 1) for piece in across]
    queries = (block, sibling, *across, *corner)
    ids, first_column, first_sums, mass = pl.pallas_call(
        functools.partial(first_kernel, first_moves),
        out_shape=(lanes, vector, lanes, vector),
        cost_estimate=small,
        compiler_params=params,
    )(first_line, *queries)
    returned_first = on_line(first_column, first_back)
    last_column, *row_sums = pl.pallas_call(
        functools.partial(last_kernel, last_moves),
        out_shape=[vector] * (1 + PLANE),
        scratch_shapes=[pltpu.VMEM(lanes.shape, lanes.dtype)],
        compiler_params=params,
    )(last_line, ids, first_sums, mass, returned_first, *queries)
    returned = [on_line(last_column, last_back)]
    returned += [in_plane(row_sums[step], step) for step in (2, 3, 1)]
    return jnp.log1p(sum(returned, row_sums[0])).reshape(row_count)


def on_device(embeddings, cluster_ids):
    if lax.axis_size("gx") == 4 * PLANE and embeddings.shape[0] % (2 * LANES) == 0:
        return grid_plan(embeddings, cluster_ids)
    return plain_plan(embeddings, cluster_ids)


def solution(mesh):
    in_specs = (P(("parts", "gx"), None), P(("parts", "gx")))
    out_specs = P(("parts", "gx"))
    return jax.shard_map(
        on_device, mesh=mesh, in_specs=in_specs, out_specs=out_specs, check_vma=False
    )
```

```python
import functools

import jax
import jax.numpy as jnp
from jax import lax
from jax.experimental import pallas as pl
from jax.experimental.pallas import tpu as pltpu
from jax.sharding import PartitionSpec as P

CLU_DEV = 1
PAD_MARK = 64.0
inverse_temp = 20.0


def tile_mass(query_rows, key_rows, query_ids, key_ids, query_start):
    similar = lax.dot_general(
        query_rows, key_rows, (((1,), (1,)), ((), ())), preferred_element_type=jnp.float32
    )
    query_pos = jnp.arange(query_rows.shape[0], dtype=jnp.int32) + query_start
    key_pos = jnp.arange(key_rows.shape[0], dtype=jnp.int32)
    mate_mask = (query_ids[:, None] == key_ids[None, :]) & (query_ids[:, None] >= 0)
    mate_mask = mate_mask & (query_pos[:, None] != key_pos[None, :])
    return jnp.where(mate_mask, jnp.exp(similar * inverse_temp), 0.0)


def density_scores(key_rows, key_ids):
    total_rows = key_rows.shape[0]
    block_rows = total_rows // 3
    pieces = [key_rows[i * block_rows : (i + 1) * block_rows] for i in range(3)]
    piece_ids = [key_ids[i * block_rows : (i + 1) * block_rows] for i in range(3)]
    sums = []
    for first in range(3):
        masses = tile_mass(pieces[first], key_rows, piece_ids[first], key_ids, first * block_rows)
        sums.append(jnp.sum(masses, axis=1))
    mass_sum = jnp.concatenate(sums, axis=0)
    return jnp.log1p(mass_sum)


def plain_plan(embeddings, cluster_ids):
    peer_count = lax.axis_size("gx")
    row_count = embeddings.shape[0]
    features = embeddings.shape[1]
    capacity = 3 * row_count // peer_count
    slot_total = peer_count * capacity
    squares = jnp.sum(jnp.square(embeddings.astype(jnp.float32)), axis=1)
    unit_rows = (embeddings.astype(jnp.float32) * lax.rsqrt(squares + 1e-06)[:, None]).astype(
        jnp.bfloat16
    )
    owner_of = cluster_ids // CLU_DEV
    onehot = (owner_of[:, None] == jnp.arange(peer_count, dtype=jnp.int32)[None, :]).astype(
        jnp.bfloat16
    )
    row_range = jnp.arange(row_count, dtype=jnp.int32)
    lower_tri = (row_range[:, None] >= row_range[None, :]).astype(jnp.bfloat16)
    running = jnp.dot(lower_tri, onehot, preferred_element_type=jnp.float32)
    slot_index = (jnp.sum(running * onehot.astype(jnp.float32), axis=1) - 1.0).astype(jnp.int32)
    target_slot = owner_of * capacity + slot_index
    slot_range = jnp.arange(slot_total, dtype=jnp.int32)
    select_mask = slot_range[:, None] == target_slot[None, :]
    outgoing = jnp.dot(
        select_mask.astype(jnp.bfloat16), unit_rows, preferred_element_type=jnp.float32
    )
    outgoing = outgoing.astype(jnp.bfloat16).reshape(peer_count, capacity, features)
    outgoing_ids = jnp.sum(jnp.where(select_mask, cluster_ids[None, :] + 1, 0), axis=1) - 1
    outgoing_ids = outgoing_ids.reshape(peer_count, capacity)
    arrived, arrived_ids = (
        lax.all_to_all(outgoing, "gx", split_axis=0, concat_axis=0, tiled=True),
        lax.all_to_all(outgoing_ids, "gx", split_axis=0, concat_axis=0, tiled=True),
    )
    key_rows = arrived.reshape(slot_total, features)
    key_ids = arrived_ids.reshape(slot_total)
    scores = density_scores(key_rows, key_ids)
    returned = lax.all_to_all(
        scores.reshape(peer_count, capacity), "gx", split_axis=0, concat_axis=0, tiled=True
    )
    flat_scores = returned.reshape(slot_total)
    pick_mask = target_slot[:, None] == slot_range[None, :]
    return jnp.sum(jnp.where(pick_mask, flat_scores[None, :], 0.0), axis=1)


LANES = 128
PLANE = 4
ID_ROWS = 16
VMEM_BYTES = 16 * 1024 * 1024


def along_rows(values):
    return jnp.broadcast_to(values, (LANES, values.shape[1])).T


def ids_block(ids, width):
    wide = jnp.concatenate([ids, jnp.zeros((1, width - ids.shape[1]), jnp.float32)], axis=1)
    return jnp.broadcast_to(wide, (ID_ROWS, width)).astype(jnp.bfloat16)


def ids_of(ref):
    first = ref.shape[0] - ID_ROWS
    return ref[first:, :].astype(jnp.float32)[:1]


def mate_mass(query_rows, query_ids, key_rows, key_ids, shift=None):
    similar = lax.dot_general(
        query_rows, key_rows, (((1,), (1,)), ((), ())), preferred_element_type=jnp.float32
    )
    repeats = similar.shape[1] // LANES
    mates = jnp.concatenate([query_ids] * repeats, axis=1) == key_ids
    if shift is not None:
        query_pos = lax.broadcasted_iota(jnp.int32, similar.shape, 0) + shift
        key_pos = lax.broadcasted_iota(jnp.int32, similar.shape, 1)
        mates = mates & (query_pos != key_pos)
    return jnp.where(mates, jnp.exp(similar * inverse_temp), 0.0)


def unit_kernel(rows_ref, ids_ref, *block_refs):
    rows, width = rows_ref.shape
    features = rows_ref[...].astype(jnp.float32)
    scale = lax.rsqrt(jnp.sum(features * features, axis=1, keepdims=True) + 1e-06)
    units = (features * scale).astype(jnp.bfloat16)
    ids = ids_block(ids_ref[...].astype(jnp.float32), width)
    first = 0
    for ref in block_refs:
        size = min(ref.shape[0], rows - first)
        ref[:size, :] = units[first : first + size]
        if ref.shape[0] > size:
            ref[size:, :] = ids
        first = (first + size) % rows


def line_sums(moves, query_parts, ids_ref, line_ref, column_ref, sums_ref):
    rows = column_ref.shape[1]
    plane = lax.axis_index("gx") // PLANE
    arrived = functools.reduce(jnp.logical_or, [plane == receiver for _, receiver in moves])
    column_ref[...] = jnp.zeros_like(column_ref)

    @pl.when(arrived)
    def _():
        key_ids = ids_of(line_ref)[:, :rows]
        column = jnp.zeros((1, rows), jnp.float32)
        first = 0
        for query_ref, size in query_parts:
            part = pl.ds(first, size)
            masses = mate_mass(query_ref[:size, :], ids_ref[part, :], line_ref[:rows, :], key_ids)
            column = column + jnp.sum(masses, axis=0, keepdims=True)
            folded = masses[:, :LANES]
            for lane in range(LANES, rows, LANES):
                folded = folded + masses[:, lane : lane + LANES]
            sums_ref[part, :] += folded
            first += size
        column_ref[...] = column


def query_parts_of(refs, rows):
    head = refs[1].shape[0]
    sizes = [rows] + [head, rows - head] * (PLANE - 1)
    return list(zip(refs, sizes))


def first_kernel(moves, line_ref, *refs):
    query_refs, (ids_ref, column_ref, sums_ref, mass_ref) = refs[:-4], refs[-4:]
    rows = mass_ref.shape[1]
    query_parts = query_parts_of(query_refs, rows)
    own_ref = query_refs[0]
    own_ids = ids_of(own_ref)[:, :rows]
    for m, ref in enumerate(query_refs[::2]):
        ids_ref[pl.ds(m * rows, rows), :] = along_rows(ids_of(ref)[:, :rows])
    mass = jnp.zeros((1, rows), jnp.float32)
    first = 0
    for ref, size in query_parts:
        shift = first if first < rows else None
        masses = mate_mass(
            ref[:size, :], ids_ref[pl.ds(first, size), :], own_ref[:rows, :], own_ids, shift
        )
        mass = mass + jnp.sum(masses, axis=0, keepdims=True)
        first += size
    mass_ref[...] = mass
    sums_ref[...] = jnp.zeros_like(sums_ref)
    line_sums(moves, query_parts, ids_ref, line_ref, column_ref, sums_ref)


def last_kernel(all_moves, *refs):
    count = len(all_moves)
    line_refs, refs = refs[:count], refs[count:]
    (ids_ref, earlier_ref, mass_ref, back_ref), refs = refs[:4], refs[4:]
    out_count = count + PLANE
    query_refs, column_refs = refs[: -out_count - 1], refs[-out_count - 1 : -PLANE - 1]
    row_refs, sums_ref = refs[-PLANE - 1 : -1], refs[-1]
    rows = mass_ref.shape[1]
    sums_ref[...] = earlier_ref[...]
    query_parts = query_parts_of(query_refs, rows)
    for moves, line_ref, column_ref in zip(all_moves, line_refs, column_refs):
        line_sums(moves, query_parts, ids_ref, line_ref, column_ref, sums_ref)
    for m in range(PLANE):
        row_sum = jnp.sum(sums_ref[pl.ds(m * rows, rows), :].T, axis=0, keepdims=True)
        if m == 0:
            row_sum = row_sum + mass_ref[...] + back_ref[...]
        row_refs[m][...] = row_sum


def grid_plan(embeddings, cluster_ids):
    peers = lax.axis_size("gx")
    row_count, features = embeddings.shape
    plane_rows = PLANE * row_count
    params = pltpu.CompilerParams(vmem_limit_bytes=VMEM_BYTES)
    small = pl.CostEstimate(flops=1, bytes_accessed=1, transcendentals=0)
    vector = jax.ShapeDtypeStruct((1, row_count), jnp.float32)
    lanes = jax.ShapeDtypeStruct((plane_rows, LANES), jnp.float32)

    def rows_of(count):
        return jax.ShapeDtypeStruct((count, features), jnp.bfloat16)

    def in_plane(value, step):
        return lax.ppermute(value, "gx", [(i, i ^ step) for i in range(peers)])

    def on_line(value, moves):
        pairs = [(a * PLANE + n, b * PLANE + n) for a, b in moves for n in range(PLANE)]
        return lax.ppermute(value, "gx", pairs)

    def back(moves):
        return [(b, a) for a, b in moves]

    first_moves = [(0, 3), (3, 1), (1, 0)]
    last_moves = [[(1, 2), (2, 0)], [(2, 3)]]
    head = 3 * row_count // 8
    block, *pieces = pl.pallas_call(
        unit_kernel,
        out_shape=(
            rows_of(row_count + ID_ROWS),
            rows_of(head),
            rows_of(row_count - head + ID_ROWS),
        ),
        cost_estimate=small,
        compiler_params=params,
    )(embeddings, cluster_ids.reshape(1, row_count))
    first_line = on_line(block, first_moves)
    last_lines = [on_line(block, moves) for moves in last_moves]
    across = [in_plane(piece, 2) for piece in pieces]
    sibling = [in_plane(piece, 1) for piece in pieces]
    first_line, across[1] = lax.optimization_barrier((first_line, across[1]))
    corner = [in_plane(piece, 1) for piece in across]
    queries = (block, *sibling, *across, *corner)
    ids, first_column, first_sums, mass = pl.pallas_call(
        functools.partial(first_kernel, first_moves),
        out_shape=(lanes, vector, lanes, vector),
        cost_estimate=small,
        compiler_params=params,
    )(first_line, *queries)
    returned_first = on_line(first_column, back(first_moves))
    sums = pl.pallas_call(
        functools.partial(last_kernel, last_moves),
        out_shape=[vector] * (len(last_moves) + PLANE),
        scratch_shapes=[pltpu.VMEM(lanes.shape, lanes.dtype)],
        compiler_params=params,
    )(*last_lines, ids, first_sums, mass, returned_first, *queries)
    columns, row_sums = sums[: len(last_moves)], sums[len(last_moves) :]
    returned = [on_line(column, back(moves)) for column, moves in zip(columns, last_moves)]
    returned += [in_plane(row_sums[step], step) for step in (2, 3, 1)]
    return jnp.log1p(sum(returned, row_sums[0])).reshape(row_count)


def on_device(embeddings, cluster_ids):
    if lax.axis_size("gx") == 4 * PLANE and embeddings.shape[0] % (2 * LANES) == 0:
        return grid_plan(embeddings, cluster_ids)
    return plain_plan(embeddings, cluster_ids)


def solution(mesh):
    in_specs = (P(("parts", "gx"), None), P(("parts", "gx")))
    out_specs = P(("parts", "gx"))
    return jax.shard_map(
        on_device, mesh=mesh, in_specs=in_specs, out_specs=out_specs, check_vma=False
    )
```

```python
import functools

import jax
import jax.numpy as jnp
from jax import lax
from jax.experimental import pallas as pl
from jax.experimental.pallas import tpu as pltpu
from jax.sharding import PartitionSpec as P

CLU_DEV = 1
PAD_MARK = 64.0
inverse_temp = 20.0


def tile_mass(query_rows, key_rows, query_ids, key_ids, query_start):
    similar = lax.dot_general(
        query_rows, key_rows, (((1,), (1,)), ((), ())), preferred_element_type=jnp.float32
    )
    query_pos = jnp.arange(query_rows.shape[0], dtype=jnp.int32) + query_start
    key_pos = jnp.arange(key_rows.shape[0], dtype=jnp.int32)
    mate_mask = (query_ids[:, None] == key_ids[None, :]) & (query_ids[:, None] >= 0)
    mate_mask = mate_mask & (query_pos[:, None] != key_pos[None, :])
    return jnp.where(mate_mask, jnp.exp(similar * inverse_temp), 0.0)


def density_scores(key_rows, key_ids):
    total_rows = key_rows.shape[0]
    block_rows = total_rows // 3
    pieces = [key_rows[i * block_rows : (i + 1) * block_rows] for i in range(3)]
    piece_ids = [key_ids[i * block_rows : (i + 1) * block_rows] for i in range(3)]
    sums = []
    for first in range(3):
        masses = tile_mass(pieces[first], key_rows, piece_ids[first], key_ids, first * block_rows)
        sums.append(jnp.sum(masses, axis=1))
    mass_sum = jnp.concatenate(sums, axis=0)
    return jnp.log1p(mass_sum)


def plain_plan(embeddings, cluster_ids):
    peer_count = lax.axis_size("gx")
    row_count = embeddings.shape[0]
    features = embeddings.shape[1]
    capacity = 3 * row_count // peer_count
    slot_total = peer_count * capacity
    squares = jnp.sum(jnp.square(embeddings.astype(jnp.float32)), axis=1)
    unit_rows = (embeddings.astype(jnp.float32) * lax.rsqrt(squares + 1e-06)[:, None]).astype(
        jnp.bfloat16
    )
    owner_of = cluster_ids // CLU_DEV
    onehot = (owner_of[:, None] == jnp.arange(peer_count, dtype=jnp.int32)[None, :]).astype(
        jnp.bfloat16
    )
    row_range = jnp.arange(row_count, dtype=jnp.int32)
    lower_tri = (row_range[:, None] >= row_range[None, :]).astype(jnp.bfloat16)
    running = jnp.dot(lower_tri, onehot, preferred_element_type=jnp.float32)
    slot_index = (jnp.sum(running * onehot.astype(jnp.float32), axis=1) - 1.0).astype(jnp.int32)
    target_slot = owner_of * capacity + slot_index
    slot_range = jnp.arange(slot_total, dtype=jnp.int32)
    select_mask = slot_range[:, None] == target_slot[None, :]
    outgoing = jnp.dot(
        select_mask.astype(jnp.bfloat16), unit_rows, preferred_element_type=jnp.float32
    )
    outgoing = outgoing.astype(jnp.bfloat16).reshape(peer_count, capacity, features)
    outgoing_ids = jnp.sum(jnp.where(select_mask, cluster_ids[None, :] + 1, 0), axis=1) - 1
    outgoing_ids = outgoing_ids.reshape(peer_count, capacity)
    arrived, arrived_ids = (
        lax.all_to_all(outgoing, "gx", split_axis=0, concat_axis=0, tiled=True),
        lax.all_to_all(outgoing_ids, "gx", split_axis=0, concat_axis=0, tiled=True),
    )
    key_rows = arrived.reshape(slot_total, features)
    key_ids = arrived_ids.reshape(slot_total)
    scores = density_scores(key_rows, key_ids)
    returned = lax.all_to_all(
        scores.reshape(peer_count, capacity), "gx", split_axis=0, concat_axis=0, tiled=True
    )
    flat_scores = returned.reshape(slot_total)
    pick_mask = target_slot[:, None] == slot_range[None, :]
    return jnp.sum(jnp.where(pick_mask, flat_scores[None, :], 0.0), axis=1)


LANES = 128
PLANE = 4
ID_ROWS = 16
VMEM_BYTES = 16 * 1024 * 1024


def along_rows(values):
    return jnp.broadcast_to(values, (LANES, values.shape[1])).T


def ids_block(ids, width):
    wide = jnp.concatenate([ids, jnp.zeros((1, width - ids.shape[1]), jnp.float32)], axis=1)
    return jnp.broadcast_to(wide, (ID_ROWS, width)).astype(jnp.bfloat16)


def ids_of(ref):
    first = ref.shape[0] - ID_ROWS
    return ref[first:, :].astype(jnp.float32)[:1]


def mate_mass(query_rows, query_ids, key_rows, key_ids, shift=None):
    similar = lax.dot_general(
        query_rows, key_rows, (((1,), (1,)), ((), ())), preferred_element_type=jnp.float32
    )
    repeats = similar.shape[1] // LANES
    mates = jnp.concatenate([query_ids] * repeats, axis=1) == key_ids
    if shift is not None:
        query_pos = lax.broadcasted_iota(jnp.int32, similar.shape, 0) + shift
        key_pos = lax.broadcasted_iota(jnp.int32, similar.shape, 1)
        mates = mates & (query_pos != key_pos)
    return jnp.where(mates, jnp.exp(similar * inverse_temp), 0.0)


def unit_kernel(rows_ref, ids_ref, *block_refs):
    rows, width = rows_ref.shape
    features = rows_ref[...].astype(jnp.float32)
    scale = lax.rsqrt(jnp.sum(features * features, axis=1, keepdims=True) + 1e-06)
    units = (features * scale).astype(jnp.bfloat16)
    ids = ids_block(ids_ref[...].astype(jnp.float32), width)
    first = 0
    for ref in block_refs:
        size = min(ref.shape[0], rows - first)
        ref[:size, :] = units[first : first + size]
        if ref.shape[0] > size:
            ref[size:, :] = ids
        first = (first + size) % rows


def line_sums(moves, query_parts, ids_ref, line_ref, column_ref, sums_ref):
    rows = column_ref.shape[1]
    plane = lax.axis_index("gx") // PLANE
    arrived = functools.reduce(jnp.logical_or, [plane == receiver for _, receiver in moves])
    column_ref[...] = jnp.zeros_like(column_ref)

    @pl.when(arrived)
    def _():
        key_ids = ids_of(line_ref)[:, :rows]
        column = jnp.zeros((1, rows), jnp.float32)
        first = 0
        for query_ref, size in query_parts:
            part = pl.ds(first, size)
            masses = mate_mass(query_ref[:size, :], ids_ref[part, :], line_ref[:rows, :], key_ids)
            column = column + jnp.sum(masses, axis=0, keepdims=True)
            folded = masses[:, :LANES]
            for lane in range(LANES, rows, LANES):
                folded = folded + masses[:, lane : lane + LANES]
            sums_ref[part, :] += folded
            first += size
        column_ref[...] = column


def query_parts_of(refs, rows):
    head = refs[2].shape[0]
    sizes = [rows, rows] + [head, rows - head] * (PLANE - 2)
    return list(zip(refs, sizes))


def first_kernel(moves, line_ref, *refs):
    query_refs, (ids_ref, column_ref, sums_ref, mass_ref) = refs[:-4], refs[-4:]
    rows = mass_ref.shape[1]
    query_parts = query_parts_of(query_refs, rows)
    own_ref = query_refs[0]
    own_ids = ids_of(own_ref)[:, :rows]
    for m, ref in enumerate((*query_refs[:2], query_refs[3], query_refs[5])):
        ids_ref[pl.ds(m * rows, rows), :] = along_rows(ids_of(ref)[:, :rows])
    mass = jnp.zeros((1, rows), jnp.float32)
    first = 0
    for ref, size in query_parts:
        shift = first if first < rows else None
        masses = mate_mass(
            ref[:size, :], ids_ref[pl.ds(first, size), :], own_ref[:rows, :], own_ids, shift
        )
        mass = mass + jnp.sum(masses, axis=0, keepdims=True)
        first += size
    mass_ref[...] = mass
    sums_ref[...] = jnp.zeros_like(sums_ref)
    line_sums(moves, query_parts, ids_ref, line_ref, column_ref, sums_ref)


def last_kernel(moves, line_ref, ids_ref, earlier_ref, mass_ref, back_ref, *refs):
    query_refs, refs = refs[: -PLANE - 2], refs[-PLANE - 2 :]
    column_ref, row_refs, sums_ref = refs[0], refs[1:-1], refs[-1]
    rows = column_ref.shape[1]
    sums_ref[...] = earlier_ref[...]
    query_parts = query_parts_of(query_refs, rows)
    line_sums(moves, query_parts, ids_ref, line_ref, column_ref, sums_ref)
    for m in range(PLANE):
        row_sum = jnp.sum(sums_ref[pl.ds(m * rows, rows), :].T, axis=0, keepdims=True)
        if m == 0:
            row_sum = row_sum + mass_ref[...] + back_ref[...]
        row_refs[m][...] = row_sum


def grid_plan(embeddings, cluster_ids):
    peers = lax.axis_size("gx")
    row_count, features = embeddings.shape
    plane_rows = PLANE * row_count
    params = pltpu.CompilerParams(vmem_limit_bytes=VMEM_BYTES)
    small = pl.CostEstimate(flops=1, bytes_accessed=1, transcendentals=0)
    vector = jax.ShapeDtypeStruct((1, row_count), jnp.float32)
    lanes = jax.ShapeDtypeStruct((plane_rows, LANES), jnp.float32)

    def rows_of(count):
        return jax.ShapeDtypeStruct((count, features), jnp.bfloat16)

    def in_plane(value, step):
        return lax.ppermute(value, "gx", [(i, i ^ step) for i in range(peers)])

    def on_line(value, moves):
        pairs = [(a * PLANE + n, b * PLANE + n) for a, b in moves for n in range(PLANE)]
        return lax.ppermute(value, "gx", pairs)

    first_moves = [(0, 1), (1, 2), (3, 0)]
    last_moves = [(1, 3), (3, 2), (2, 0)]
    first_back = [(b, a) for a, b in first_moves]
    last_back = [(b, a) for a, b in last_moves]

    head = 3 * row_count // 8
    block, *pieces = pl.pallas_call(
        unit_kernel,
        out_shape=(
            rows_of(row_count + ID_ROWS),
            rows_of(head),
            rows_of(row_count - head + ID_ROWS),
        ),
        cost_estimate=small,
        compiler_params=params,
    )(embeddings, cluster_ids.reshape(1, row_count))
    first_line = on_line(block, first_moves)
    last_line = on_line(block, last_moves)
    across = [in_plane(piece, 2) for piece in pieces]
    sibling = in_plane(block, 1)
    first_line, across[1] = lax.optimization_barrier((first_line, across[1]))
    corner = [in_plane(piece, 1) for piece in across]
    queries = (block, sibling, *across, *corner)
    ids, first_column, first_sums, mass = pl.pallas_call(
        functools.partial(first_kernel, first_moves),
        out_shape=(lanes, vector, lanes, vector),
        cost_estimate=small,
        compiler_params=params,
    )(first_line, *queries)
    returned_first = on_line(first_column, first_back)
    last_column, *row_sums = pl.pallas_call(
        functools.partial(last_kernel, last_moves),
        out_shape=[vector] * (1 + PLANE),
        scratch_shapes=[pltpu.VMEM(lanes.shape, lanes.dtype)],
        compiler_params=params,
    )(last_line, ids, first_sums, mass, returned_first, *queries)
    returned = [on_line(last_column, last_back)]
    returned += [in_plane(row_sums[step], step) for step in (2, 3, 1)]
    return jnp.log1p(sum(returned, row_sums[0])).reshape(row_count)


def on_device(embeddings, cluster_ids):
    if lax.axis_size("gx") == 4 * PLANE and embeddings.shape[0] % (2 * LANES) == 0:
        return grid_plan(embeddings, cluster_ids)
    return plain_plan(embeddings, cluster_ids)


def solution(mesh):
    in_specs = (P(("parts", "gx"), None), P(("parts", "gx")))
    out_specs = P(("parts", "gx"))
    return jax.shard_map(
        on_device, mesh=mesh, in_specs=in_specs, out_specs=out_specs, check_vma=False
    )
```

```python
import functools

import jax
import jax.numpy as jnp
from jax import lax
from jax.experimental import pallas as pl
from jax.experimental.pallas import tpu as pltpu
from jax.sharding import PartitionSpec as P

CLU_DEV = 1
PAD_MARK = 64.0
inverse_temp = 20.0


def tile_mass(query_rows, key_rows, query_ids, key_ids, query_start):
    similar = lax.dot_general(
        query_rows, key_rows, (((1,), (1,)), ((), ())), preferred_element_type=jnp.float32
    )
    query_pos = jnp.arange(query_rows.shape[0], dtype=jnp.int32) + query_start
    key_pos = jnp.arange(key_rows.shape[0], dtype=jnp.int32)
    mate_mask = (query_ids[:, None] == key_ids[None, :]) & (query_ids[:, None] >= 0)
    mate_mask = mate_mask & (query_pos[:, None] != key_pos[None, :])
    return jnp.where(mate_mask, jnp.exp(similar * inverse_temp), 0.0)


def density_scores(key_rows, key_ids):
    total_rows = key_rows.shape[0]
    block_rows = total_rows // 3
    pieces = [key_rows[i * block_rows : (i + 1) * block_rows] for i in range(3)]
    piece_ids = [key_ids[i * block_rows : (i + 1) * block_rows] for i in range(3)]
    sums = []
    for first in range(3):
        masses = tile_mass(pieces[first], key_rows, piece_ids[first], key_ids, first * block_rows)
        sums.append(jnp.sum(masses, axis=1))
    mass_sum = jnp.concatenate(sums, axis=0)
    return jnp.log1p(mass_sum)


def plain_plan(embeddings, cluster_ids):
    peer_count = lax.axis_size("gx")
    row_count = embeddings.shape[0]
    features = embeddings.shape[1]
    capacity = 3 * row_count // peer_count
    slot_total = peer_count * capacity
    squares = jnp.sum(jnp.square(embeddings.astype(jnp.float32)), axis=1)
    unit_rows = (embeddings.astype(jnp.float32) * lax.rsqrt(squares + 1e-06)[:, None]).astype(
        jnp.bfloat16
    )
    owner_of = cluster_ids // CLU_DEV
    onehot = (owner_of[:, None] == jnp.arange(peer_count, dtype=jnp.int32)[None, :]).astype(
        jnp.bfloat16
    )
    row_range = jnp.arange(row_count, dtype=jnp.int32)
    lower_tri = (row_range[:, None] >= row_range[None, :]).astype(jnp.bfloat16)
    running = jnp.dot(lower_tri, onehot, preferred_element_type=jnp.float32)
    slot_index = (jnp.sum(running * onehot.astype(jnp.float32), axis=1) - 1.0).astype(jnp.int32)
    target_slot = owner_of * capacity + slot_index
    slot_range = jnp.arange(slot_total, dtype=jnp.int32)
    select_mask = slot_range[:, None] == target_slot[None, :]
    outgoing = jnp.dot(
        select_mask.astype(jnp.bfloat16), unit_rows, preferred_element_type=jnp.float32
    )
    outgoing = outgoing.astype(jnp.bfloat16).reshape(peer_count, capacity, features)
    outgoing_ids = jnp.sum(jnp.where(select_mask, cluster_ids[None, :] + 1, 0), axis=1) - 1
    outgoing_ids = outgoing_ids.reshape(peer_count, capacity)
    arrived, arrived_ids = (
        lax.all_to_all(outgoing, "gx", split_axis=0, concat_axis=0, tiled=True),
        lax.all_to_all(outgoing_ids, "gx", split_axis=0, concat_axis=0, tiled=True),
    )
    key_rows = arrived.reshape(slot_total, features)
    key_ids = arrived_ids.reshape(slot_total)
    scores = density_scores(key_rows, key_ids)
    returned = lax.all_to_all(
        scores.reshape(peer_count, capacity), "gx", split_axis=0, concat_axis=0, tiled=True
    )
    flat_scores = returned.reshape(slot_total)
    pick_mask = target_slot[:, None] == slot_range[None, :]
    return jnp.sum(jnp.where(pick_mask, flat_scores[None, :], 0.0), axis=1)


LANES = 128
PLANE = 4
ID_ROWS = 16
VMEM_BYTES = 16 * 1024 * 1024


def along_rows(values):
    return jnp.broadcast_to(values, (LANES, values.shape[1])).T


def ids_block(ids, width):
    wide = jnp.concatenate([ids, jnp.zeros((1, width - ids.shape[1]), jnp.float32)], axis=1)
    return jnp.broadcast_to(wide, (ID_ROWS, width)).astype(jnp.bfloat16)


def ids_of(ref):
    first = ref.shape[0] - ID_ROWS
    return ref[first:, :].astype(jnp.float32)[:1]


def mate_mass(query_rows, query_ids, key_rows, key_ids, shift=None):
    similar = lax.dot_general(
        query_rows, key_rows, (((1,), (1,)), ((), ())), preferred_element_type=jnp.float32
    )
    repeats = similar.shape[1] // LANES
    mates = jnp.concatenate([query_ids] * repeats, axis=1) == key_ids
    if shift is not None:
        query_pos = lax.broadcasted_iota(jnp.int32, similar.shape, 0) + shift
        key_pos = lax.broadcasted_iota(jnp.int32, similar.shape, 1)
        mates = mates & (query_pos != key_pos)
    return jnp.where(mates, jnp.exp(similar * inverse_temp), 0.0)


def unit_kernel(rows_ref, ids_ref, units_ref, info_ref, *block_refs):
    rows, width = rows_ref.shape
    features = rows_ref[...].astype(jnp.float32)
    scale = lax.rsqrt(jnp.sum(features * features, axis=1, keepdims=True) + 1e-06)
    ids = ids_ref[...].astype(jnp.float32)
    units = (features * scale).astype(jnp.bfloat16)
    units_ref[...] = units
    info_ref[:, :rows] = ids
    info_ref[:, rows:] = jnp.broadcast_to(scale, (rows, LANES)).T[:1]
    first = 0
    for ref in block_refs:
        size = min(ref.shape[0], rows - first)
        ref[:size, :] = units[first : first + size]
        if ref.shape[0] > size:
            ref[size:, :] = ids_block(ids, width)
        first = (first + size) % rows


def scaled_rows(rows_ref, info_ref):
    rows, width = rows_ref.shape
    wide = jnp.concatenate([along_rows(info_ref[:, rows:])] * (width // LANES), axis=1)
    return (rows_ref[...].astype(jnp.float32) * wide).astype(jnp.bfloat16)


def line_sums(moves, query_parts, ids_ref, info_ref, line_ref, is_raw, column_ref, sums_ref):
    rows = column_ref.shape[1]
    plane = lax.axis_index("gx") // PLANE
    arrived = functools.reduce(jnp.logical_or, [plane == receiver for _, receiver in moves])
    column_ref[...] = jnp.zeros_like(column_ref)

    @pl.when(arrived)
    def _():
        key_ids = info_ref[:, :rows]
        key_rows = scaled_rows(line_ref, info_ref) if is_raw else line_ref[...]
        column = jnp.zeros((1, rows), jnp.float32)
        first = 0
        for query_ref, size in query_parts:
            part = pl.ds(first, size)
            masses = mate_mass(query_ref[:size, :], ids_ref[part, :], key_rows, key_ids)
            column = column + jnp.sum(masses, axis=0, keepdims=True)
            folded = masses[:, :LANES]
            for lane in range(LANES, rows, LANES):
                folded = folded + masses[:, lane : lane + LANES]
            sums_ref[part, :] += folded
            first += size
        column_ref[...] = column


def query_parts_of(refs, rows):
    return [(ref, rows) for ref in refs[:3]] + [(ref, rows // 2) for ref in refs[3:]]


def first_kernel(moves, info_ref, line_ref, *refs):
    query_refs, (ids_ref, column_ref, sums_ref, mass_ref) = refs[:-4], refs[-4:]
    rows = mass_ref.shape[1]
    query_parts = query_parts_of(query_refs, rows)
    own_ref = query_refs[0]
    own_ids = ids_of(own_ref)[:, :rows]
    for m, ref in enumerate((*query_refs[:3], query_refs[4])):
        ids_ref[pl.ds(m * rows, rows), :] = along_rows(ids_of(ref)[:, :rows])
    mass = jnp.zeros((1, rows), jnp.float32)
    first = 0
    for ref, size in query_parts:
        shift = first if first < rows else None
        masses = mate_mass(
            ref[:size, :], ids_ref[pl.ds(first, size), :], own_ref[:rows, :], own_ids, shift
        )
        mass = mass + jnp.sum(masses, axis=0, keepdims=True)
        first += size
    mass_ref[...] = mass
    sums_ref[...] = jnp.zeros_like(sums_ref)
    line_sums(moves, query_parts, ids_ref, info_ref, line_ref, True, column_ref, sums_ref)


def last_kernel(moves, info_ref, line_ref, ids_ref, earlier_ref, mass_ref, *refs):
    query_refs, refs = refs[: -PLANE - 2], refs[-PLANE - 2 :]
    column_ref, row_refs, sums_ref = refs[0], refs[1:-1], refs[-1]
    rows = column_ref.shape[1]
    sums_ref[...] = earlier_ref[...]
    query_parts = query_parts_of(query_refs, rows)
    line_sums(moves, query_parts, ids_ref, info_ref, line_ref, False, column_ref, sums_ref)
    for m in range(PLANE):
        row_sum = jnp.sum(sums_ref[pl.ds(m * rows, rows), :].T, axis=0, keepdims=True)
        if m == 0:
            row_sum = row_sum + mass_ref[...]
        row_refs[m][...] = row_sum


def grid_plan(embeddings, cluster_ids):
    peers = lax.axis_size("gx")
    row_count, features = embeddings.shape
    plane_rows = PLANE * row_count
    params = pltpu.CompilerParams(vmem_limit_bytes=VMEM_BYTES)
    small = pl.CostEstimate(flops=1, bytes_accessed=1, transcendentals=0)
    vector = jax.ShapeDtypeStruct((1, row_count), jnp.float32)
    lanes = jax.ShapeDtypeStruct((plane_rows, LANES), jnp.float32)

    def rows_of(count):
        return jax.ShapeDtypeStruct((count, features), jnp.bfloat16)

    def in_plane(value, step):
        return lax.ppermute(value, "gx", [(i, i ^ step) for i in range(peers)])

    def on_line(value, moves):
        pairs = [(a * PLANE + n, b * PLANE + n) for a, b in moves for n in range(PLANE)]
        return lax.ppermute(value, "gx", pairs)

    first_moves = [(0, 1), (1, 2), (2, 3), (3, 0)]
    last_moves = [(0, 2), (3, 1)]
    first_back = [(b, a) for a, b in first_moves]
    last_back = [(b, a) for a, b in last_moves]

    half = row_count // 2
    first_line = on_line(embeddings, first_moves)
    units, info, block = pl.pallas_call(
        unit_kernel,
        out_shape=(
            rows_of(row_count),
            jax.ShapeDtypeStruct((1, 2 * row_count), jnp.float32),
            rows_of(row_count + ID_ROWS),
        ),
        cost_estimate=small,
        compiler_params=params,
    )(embeddings, cluster_ids.reshape(1, row_count))
    across = in_plane(block, 2)
    sibling = in_plane(block, 1)
    first_info, last_info = on_line(info, first_moves), on_line(info, last_moves)
    first_line, first_info, last_info, units = lax.optimization_barrier(
        (first_line, first_info, last_info, units)
    )
    last_line = on_line(units, last_moves)
    corner = [in_plane(piece, 1) for piece in (across[:half], across[half:])]
    queries = (block, sibling, across, *corner)
    ids, first_column, first_sums, mass = pl.pallas_call(
        functools.partial(first_kernel, first_moves),
        out_shape=(lanes, vector, lanes, vector),
        cost_estimate=small,
        compiler_params=params,
    )(first_info, first_line, *queries)
    returned_first = on_line(first_column, first_back)
    last_column, *row_sums = pl.pallas_call(
        functools.partial(last_kernel, last_moves),
        out_shape=[vector] * (1 + PLANE),
        scratch_shapes=[pltpu.VMEM(lanes.shape, lanes.dtype)],
        compiler_params=params,
    )(last_info, last_line, ids, first_sums, mass, *queries)
    returned_first, row_sums[1] = lax.optimization_barrier((returned_first, row_sums[1]))
    returned = [on_line(last_column, last_back)]
    returned += [in_plane(row_sums[step], step) for step in (2, 3, 1)]
    return jnp.log1p(sum(returned, row_sums[0] + returned_first)).reshape(row_count)


def on_device(embeddings, cluster_ids):
    if lax.axis_size("gx") == 4 * PLANE and embeddings.shape[0] % (2 * LANES) == 0:
        return grid_plan(embeddings, cluster_ids)
    return plain_plan(embeddings, cluster_ids)


def solution(mesh):
    in_specs = (P(("parts", "gx"), None), P(("parts", "gx")))
    out_specs = P(("parts", "gx"))
    return jax.shard_map(
        on_device, mesh=mesh, in_specs=in_specs, out_specs=out_specs, check_vma=False
    )
```

```python
import functools

import jax
import jax.numpy as jnp
from jax import lax
from jax.experimental import pallas as pl
from jax.experimental.pallas import tpu as pltpu
from jax.sharding import PartitionSpec as P

CLU_DEV = 1
PAD_MARK = 64.0
inverse_temp = 20.0


def tile_mass(query_rows, key_rows, query_ids, key_ids, query_start):
    similar = lax.dot_general(
        query_rows, key_rows, (((1,), (1,)), ((), ())), preferred_element_type=jnp.float32
    )
    query_pos = jnp.arange(query_rows.shape[0], dtype=jnp.int32) + query_start
    key_pos = jnp.arange(key_rows.shape[0], dtype=jnp.int32)
    mate_mask = (query_ids[:, None] == key_ids[None, :]) & (query_ids[:, None] >= 0)
    mate_mask = mate_mask & (query_pos[:, None] != key_pos[None, :])
    return jnp.where(mate_mask, jnp.exp(similar * inverse_temp), 0.0)


def density_scores(key_rows, key_ids):
    total_rows = key_rows.shape[0]
    block_rows = total_rows // 3
    pieces = [key_rows[i * block_rows : (i + 1) * block_rows] for i in range(3)]
    piece_ids = [key_ids[i * block_rows : (i + 1) * block_rows] for i in range(3)]
    sums = []
    for first in range(3):
        masses = tile_mass(pieces[first], key_rows, piece_ids[first], key_ids, first * block_rows)
        sums.append(jnp.sum(masses, axis=1))
    mass_sum = jnp.concatenate(sums, axis=0)
    return jnp.log1p(mass_sum)


def plain_plan(embeddings, cluster_ids):
    peer_count = lax.axis_size("gx")
    row_count = embeddings.shape[0]
    features = embeddings.shape[1]
    capacity = 3 * row_count // peer_count
    slot_total = peer_count * capacity
    squares = jnp.sum(jnp.square(embeddings.astype(jnp.float32)), axis=1)
    unit_rows = (embeddings.astype(jnp.float32) * lax.rsqrt(squares + 1e-06)[:, None]).astype(
        jnp.bfloat16
    )
    owner_of = cluster_ids // CLU_DEV
    onehot = (owner_of[:, None] == jnp.arange(peer_count, dtype=jnp.int32)[None, :]).astype(
        jnp.bfloat16
    )
    row_range = jnp.arange(row_count, dtype=jnp.int32)
    lower_tri = (row_range[:, None] >= row_range[None, :]).astype(jnp.bfloat16)
    running = jnp.dot(lower_tri, onehot, preferred_element_type=jnp.float32)
    slot_index = (jnp.sum(running * onehot.astype(jnp.float32), axis=1) - 1.0).astype(jnp.int32)
    target_slot = owner_of * capacity + slot_index
    slot_range = jnp.arange(slot_total, dtype=jnp.int32)
    select_mask = slot_range[:, None] == target_slot[None, :]
    outgoing = jnp.dot(
        select_mask.astype(jnp.bfloat16), unit_rows, preferred_element_type=jnp.float32
    )
    outgoing = outgoing.astype(jnp.bfloat16).reshape(peer_count, capacity, features)
    outgoing_ids = jnp.sum(jnp.where(select_mask, cluster_ids[None, :] + 1, 0), axis=1) - 1
    outgoing_ids = outgoing_ids.reshape(peer_count, capacity)
    arrived, arrived_ids = (
        lax.all_to_all(outgoing, "gx", split_axis=0, concat_axis=0, tiled=True),
        lax.all_to_all(outgoing_ids, "gx", split_axis=0, concat_axis=0, tiled=True),
    )
    key_rows = arrived.reshape(slot_total, features)
    key_ids = arrived_ids.reshape(slot_total)
    scores = density_scores(key_rows, key_ids)
    returned = lax.all_to_all(
        scores.reshape(peer_count, capacity), "gx", split_axis=0, concat_axis=0, tiled=True
    )
    flat_scores = returned.reshape(slot_total)
    pick_mask = target_slot[:, None] == slot_range[None, :]
    return jnp.sum(jnp.where(pick_mask, flat_scores[None, :], 0.0), axis=1)


LANES = 128
PLANE = 4
ID_ROWS = 16
VMEM_BYTES = 16 * 1024 * 1024


def along_rows(values):
    return jnp.broadcast_to(values, (LANES, values.shape[1])).T


def ids_block(ids, width):
    wide = jnp.concatenate([ids, jnp.zeros((1, width - ids.shape[1]), jnp.float32)], axis=1)
    return jnp.broadcast_to(wide, (ID_ROWS, width)).astype(jnp.bfloat16)


def ids_of(ref):
    first = ref.shape[0] - ID_ROWS
    return ref[first:, :].astype(jnp.float32)[:1]


def mate_mass(query_rows, query_ids, key_rows, key_ids, shift=None):
    similar = lax.dot_general(
        query_rows, key_rows, (((1,), (1,)), ((), ())), preferred_element_type=jnp.float32
    )
    repeats = similar.shape[1] // LANES
    mates = jnp.concatenate([query_ids] * repeats, axis=1) == key_ids
    if shift is not None:
        query_pos = lax.broadcasted_iota(jnp.int32, similar.shape, 0) + shift
        key_pos = lax.broadcasted_iota(jnp.int32, similar.shape, 1)
        mates = mates & (query_pos != key_pos)
    return jnp.where(mates, jnp.exp(similar * inverse_temp), 0.0)


def unit_kernel(rows_ref, ids_ref, info_ref, *block_refs):
    rows, width = rows_ref.shape
    features = rows_ref[...].astype(jnp.float32)
    scale = lax.rsqrt(jnp.sum(features * features, axis=1, keepdims=True) + 1e-06)
    ids = ids_ref[...].astype(jnp.float32)
    units = (features * scale).astype(jnp.bfloat16)
    info_ref[:, :rows] = ids
    info_ref[:, rows:] = jnp.broadcast_to(scale, (rows, LANES)).T[:1]
    first = 0
    for ref in block_refs:
        size = min(ref.shape[0], rows - first)
        ref[:size, :] = units[first : first + size]
        if ref.shape[0] > size:
            ref[size:, :] = ids_block(ids, width)
        first = (first + size) % rows


def scaled_rows(rows_ref, info_ref):
    rows, width = rows_ref.shape
    wide = jnp.concatenate([along_rows(info_ref[:, rows:])] * (width // LANES), axis=1)
    return (rows_ref[...].astype(jnp.float32) * wide).astype(jnp.bfloat16)


def line_sums(moves, query_parts, ids_ref, info_ref, line_ref, column_ref, sums_ref):
    rows = column_ref.shape[1]
    plane = lax.axis_index("gx") // PLANE
    arrived = functools.reduce(jnp.logical_or, [plane == receiver for _, receiver in moves])
    column_ref[...] = jnp.zeros_like(column_ref)

    @pl.when(arrived)
    def _():
        key_ids = info_ref[:, :rows]
        key_rows = scaled_rows(line_ref, info_ref)
        column = jnp.zeros((1, rows), jnp.float32)
        first = 0
        for query_ref, size in query_parts:
            part = pl.ds(first, size)
            masses = mate_mass(query_ref[:size, :], ids_ref[part, :], key_rows, key_ids)
            column = column + jnp.sum(masses, axis=0, keepdims=True)
            folded = masses[:, :LANES]
            for lane in range(LANES, rows, LANES):
                folded = folded + masses[:, lane : lane + LANES]
            sums_ref[part, :] += folded
            first += size
        column_ref[...] = column


def query_parts_of(refs, rows):
    return [(ref, rows) for ref in refs[:3]] + [(ref, rows // 2) for ref in refs[3:]]


def first_kernel(moves, info_ref, line_ref, *refs):
    query_refs, (ids_ref, column_ref, sums_ref, mass_ref) = refs[:-4], refs[-4:]
    rows = mass_ref.shape[1]
    query_parts = query_parts_of(query_refs, rows)
    own_ref = query_refs[0]
    own_ids = ids_of(own_ref)[:, :rows]
    for m, ref in enumerate((*query_refs[:3], query_refs[4])):
        ids_ref[pl.ds(m * rows, rows), :] = along_rows(ids_of(ref)[:, :rows])
    mass = jnp.zeros((1, rows), jnp.float32)
    first = 0
    for ref, size in query_parts:
        shift = first if first < rows else None
        masses = mate_mass(
            ref[:size, :], ids_ref[pl.ds(first, size), :], own_ref[:rows, :], own_ids, shift
        )
        mass = mass + jnp.sum(masses, axis=0, keepdims=True)
        first += size
    mass_ref[...] = mass
    sums_ref[...] = jnp.zeros_like(sums_ref)
    line_sums(moves, query_parts, ids_ref, info_ref, line_ref, column_ref, sums_ref)


def last_kernel(moves, info_ref, line_ref, ids_ref, earlier_ref, mass_ref, *refs):
    query_refs, refs = refs[: -PLANE - 2], refs[-PLANE - 2 :]
    column_ref, row_refs, sums_ref = refs[0], refs[1:-1], refs[-1]
    rows = column_ref.shape[1]
    sums_ref[...] = earlier_ref[...]
    query_parts = query_parts_of(query_refs, rows)
    line_sums(moves, query_parts, ids_ref, info_ref, line_ref, column_ref, sums_ref)
    for m in range(PLANE):
        row_sum = jnp.sum(sums_ref[pl.ds(m * rows, rows), :].T, axis=0, keepdims=True)
        if m == 0:
            row_sum = row_sum + mass_ref[...]
        row_refs[m][...] = row_sum


def grid_plan(embeddings, cluster_ids):
    peers = lax.axis_size("gx")
    row_count, features = embeddings.shape
    plane_rows = PLANE * row_count
    params = pltpu.CompilerParams(vmem_limit_bytes=VMEM_BYTES)
    small = pl.CostEstimate(flops=1, bytes_accessed=1, transcendentals=0)
    vector = jax.ShapeDtypeStruct((1, row_count), jnp.float32)
    lanes = jax.ShapeDtypeStruct((plane_rows, LANES), jnp.float32)

    def rows_of(count):
        return jax.ShapeDtypeStruct((count, features), jnp.bfloat16)

    def in_plane(value, step):
        return lax.ppermute(value, "gx", [(i, i ^ step) for i in range(peers)])

    def on_line(value, moves):
        pairs = [(a * PLANE + n, b * PLANE + n) for a, b in moves for n in range(PLANE)]
        return lax.ppermute(value, "gx", pairs)

    first_moves = [(0, 1), (1, 2), (2, 3), (3, 0)]
    last_moves = [(0, 2), (1, 3)]
    forward_moves = [(1, 2), (2, 3)]
    first_back = [(b, a) for a, b in first_moves]
    last_back = [(b, a) for a, b in last_moves]

    half = row_count // 2
    first_line = on_line(embeddings, first_moves)
    info, block = pl.pallas_call(
        unit_kernel,
        out_shape=(
            jax.ShapeDtypeStruct((1, 2 * row_count), jnp.float32),
            rows_of(row_count + ID_ROWS),
        ),
        cost_estimate=small,
        compiler_params=params,
    )(embeddings, cluster_ids.reshape(1, row_count))
    across = in_plane(block, 2)
    sibling = in_plane(block, 1)
    first_info, last_info = on_line(info, first_moves), on_line(info, last_moves)
    first_line, first_info, last_info = lax.optimization_barrier(
        (first_line, first_info, last_info)
    )
    last_line = on_line(first_line, forward_moves)
    corner = [in_plane(piece, 1) for piece in (across[:half], across[half:])]
    queries = (block, sibling, across, *corner)
    ids, first_column, first_sums, mass = pl.pallas_call(
        functools.partial(first_kernel, first_moves),
        out_shape=(lanes, vector, lanes, vector),
        cost_estimate=small,
        compiler_params=params,
    )(first_info, first_line, *queries)
    returned_first = on_line(first_column, first_back)
    last_column, *row_sums = pl.pallas_call(
        functools.partial(last_kernel, last_moves),
        out_shape=[vector] * (1 + PLANE),
        scratch_shapes=[pltpu.VMEM(lanes.shape, lanes.dtype)],
        compiler_params=params,
    )(last_info, last_line, ids, first_sums, mass, *queries)
    returned_first, row_sums[1] = lax.optimization_barrier((returned_first, row_sums[1]))
    returned = [on_line(last_column, last_back)]
    returned += [in_plane(row_sums[step], step) for step in (2, 3, 1)]
    return jnp.log1p(sum(returned, row_sums[0] + returned_first)).reshape(row_count)


def on_device(embeddings, cluster_ids):
    if lax.axis_size("gx") == 4 * PLANE and embeddings.shape[0] % (2 * LANES) == 0:
        return grid_plan(embeddings, cluster_ids)
    return plain_plan(embeddings, cluster_ids)


def solution(mesh):
    in_specs = (P(("parts", "gx"), None), P(("parts", "gx")))
    out_specs = P(("parts", "gx"))
    return jax.shard_map(
        on_device, mesh=mesh, in_specs=in_specs, out_specs=out_specs, check_vma=False
    )
```

```python
import functools

import jax
import jax.numpy as jnp
from jax import lax
from jax.experimental import pallas as pl
from jax.experimental.pallas import tpu as pltpu
from jax.sharding import PartitionSpec as P

CLU_DEV = 1
PAD_MARK = 64.0
inverse_temp = 20.0


def tile_mass(query_rows, key_rows, query_ids, key_ids, query_start):
    similar = lax.dot_general(
        query_rows, key_rows, (((1,), (1,)), ((), ())), preferred_element_type=jnp.float32
    )
    query_pos = jnp.arange(query_rows.shape[0], dtype=jnp.int32) + query_start
    key_pos = jnp.arange(key_rows.shape[0], dtype=jnp.int32)
    mate_mask = (query_ids[:, None] == key_ids[None, :]) & (query_ids[:, None] >= 0)
    mate_mask = mate_mask & (query_pos[:, None] != key_pos[None, :])
    return jnp.where(mate_mask, jnp.exp(similar * inverse_temp), 0.0)


def density_scores(key_rows, key_ids):
    total_rows = key_rows.shape[0]
    block_rows = total_rows // 3
    pieces = [key_rows[i * block_rows : (i + 1) * block_rows] for i in range(3)]
    piece_ids = [key_ids[i * block_rows : (i + 1) * block_rows] for i in range(3)]
    sums = []
    for first in range(3):
        masses = tile_mass(pieces[first], key_rows, piece_ids[first], key_ids, first * block_rows)
        sums.append(jnp.sum(masses, axis=1))
    mass_sum = jnp.concatenate(sums, axis=0)
    return jnp.log1p(mass_sum)


def plain_plan(embeddings, cluster_ids):
    peer_count = lax.axis_size("gx")
    row_count = embeddings.shape[0]
    features = embeddings.shape[1]
    capacity = 3 * row_count // peer_count
    slot_total = peer_count * capacity
    squares = jnp.sum(jnp.square(embeddings.astype(jnp.float32)), axis=1)
    unit_rows = (embeddings.astype(jnp.float32) * lax.rsqrt(squares + 1e-06)[:, None]).astype(
        jnp.bfloat16
    )
    owner_of = cluster_ids // CLU_DEV
    onehot = (owner_of[:, None] == jnp.arange(peer_count, dtype=jnp.int32)[None, :]).astype(
        jnp.bfloat16
    )
    row_range = jnp.arange(row_count, dtype=jnp.int32)
    lower_tri = (row_range[:, None] >= row_range[None, :]).astype(jnp.bfloat16)
    running = jnp.dot(lower_tri, onehot, preferred_element_type=jnp.float32)
    slot_index = (jnp.sum(running * onehot.astype(jnp.float32), axis=1) - 1.0).astype(jnp.int32)
    target_slot = owner_of * capacity + slot_index
    slot_range = jnp.arange(slot_total, dtype=jnp.int32)
    select_mask = slot_range[:, None] == target_slot[None, :]
    outgoing = jnp.dot(
        select_mask.astype(jnp.bfloat16), unit_rows, preferred_element_type=jnp.float32
    )
    outgoing = outgoing.astype(jnp.bfloat16).reshape(peer_count, capacity, features)
    outgoing_ids = jnp.sum(jnp.where(select_mask, cluster_ids[None, :] + 1, 0), axis=1) - 1
    outgoing_ids = outgoing_ids.reshape(peer_count, capacity)
    arrived, arrived_ids = (
        lax.all_to_all(outgoing, "gx", split_axis=0, concat_axis=0, tiled=True),
        lax.all_to_all(outgoing_ids, "gx", split_axis=0, concat_axis=0, tiled=True),
    )
    key_rows = arrived.reshape(slot_total, features)
    key_ids = arrived_ids.reshape(slot_total)
    scores = density_scores(key_rows, key_ids)
    returned = lax.all_to_all(
        scores.reshape(peer_count, capacity), "gx", split_axis=0, concat_axis=0, tiled=True
    )
    flat_scores = returned.reshape(slot_total)
    pick_mask = target_slot[:, None] == slot_range[None, :]
    return jnp.sum(jnp.where(pick_mask, flat_scores[None, :], 0.0), axis=1)


LANES = 128
PLANE = 4
ID_ROWS = 16
VMEM_BYTES = 16 * 1024 * 1024


def along_rows(values):
    return jnp.broadcast_to(values, (LANES, values.shape[1])).T


def ids_block(ids, width):
    wide = jnp.concatenate([ids, jnp.zeros((1, width - ids.shape[1]), jnp.float32)], axis=1)
    return jnp.broadcast_to(wide, (ID_ROWS, width)).astype(jnp.bfloat16)


def ids_of(ref):
    first = ref.shape[0] - ID_ROWS
    return ref[first:, :].astype(jnp.float32)[:1]


def mate_mass(query_rows, query_ids, key_rows, key_ids, shift=None):
    similar = lax.dot_general(
        query_rows, key_rows, (((1,), (1,)), ((), ())), preferred_element_type=jnp.float32
    )
    repeats = similar.shape[1] // LANES
    mates = jnp.concatenate([query_ids] * repeats, axis=1) == key_ids
    if shift is not None:
        query_pos = lax.broadcasted_iota(jnp.int32, similar.shape, 0) + shift
        key_pos = lax.broadcasted_iota(jnp.int32, similar.shape, 1)
        mates = mates & (query_pos != key_pos)
    return jnp.where(mates, jnp.exp(similar * inverse_temp), 0.0)


def unit_kernel(rows_ref, ids_ref, info_ref, *block_refs):
    rows, width = rows_ref.shape
    features = rows_ref[...].astype(jnp.float32)
    scale = lax.rsqrt(jnp.sum(features * features, axis=1, keepdims=True) + 1e-06)
    ids = ids_ref[...].astype(jnp.float32)
    units = (features * scale).astype(jnp.bfloat16)
    info_ref[:, :rows] = ids
    info_ref[:, rows:] = jnp.broadcast_to(scale, (rows, LANES)).T[:1]
    first = 0
    for ref in block_refs:
        size = min(ref.shape[0], rows - first)
        ref[:size, :] = units[first : first + size]
        if ref.shape[0] > size:
            ref[size:, :] = ids_block(ids, width)
        first = (first + size) % rows


def scaled_rows(rows_ref, info_ref):
    rows, width = rows_ref.shape
    wide = jnp.concatenate([along_rows(info_ref[:, rows:])] * (width // LANES), axis=1)
    return (rows_ref[...].astype(jnp.float32) * wide).astype(jnp.bfloat16)


def line_sums(moves, query_parts, ids_ref, info_ref, line_ref, column_ref, sums_ref):
    rows = column_ref.shape[1]
    plane = lax.axis_index("gx") // PLANE
    arrived = functools.reduce(jnp.logical_or, [plane == receiver for _, receiver in moves])
    column_ref[...] = jnp.zeros_like(column_ref)

    @pl.when(arrived)
    def _():
        key_ids = info_ref[:, :rows]
        key_rows = scaled_rows(line_ref, info_ref)
        column = jnp.zeros((1, rows), jnp.float32)
        first = 0
        for query_ref, size in query_parts:
            part = pl.ds(first, size)
            masses = mate_mass(query_ref[:size, :], ids_ref[part, :], key_rows, key_ids)
            column = column + jnp.sum(masses, axis=0, keepdims=True)
            folded = masses[:, :LANES]
            for lane in range(LANES, rows, LANES):
                folded = folded + masses[:, lane : lane + LANES]
            sums_ref[part, :] += folded
            first += size
        column_ref[...] = column


def query_parts_of(refs, rows):
    return [(ref, rows) for ref in refs[:3]] + [(ref, rows // 2) for ref in refs[3:]]


def first_kernel(moves, info_ref, line_ref, *refs):
    query_refs, (ids_ref, column_ref, sums_ref, mass_ref) = refs[:-4], refs[-4:]
    rows = mass_ref.shape[1]
    query_parts = query_parts_of(query_refs, rows)
    own_ref = query_refs[0]
    own_ids = ids_of(own_ref)[:, :rows]
    for m, ref in enumerate((*query_refs[:3], query_refs[4])):
        ids_ref[pl.ds(m * rows, rows), :] = along_rows(ids_of(ref)[:, :rows])
    mass = jnp.zeros((1, rows), jnp.float32)
    first = 0
    for ref, size in query_parts:
        shift = first if first < rows else None
        masses = mate_mass(
            ref[:size, :], ids_ref[pl.ds(first, size), :], own_ref[:rows, :], own_ids, shift
        )
        mass = mass + jnp.sum(masses, axis=0, keepdims=True)
        first += size
    mass_ref[...] = mass
    sums_ref[...] = jnp.zeros_like(sums_ref)
    line_sums(moves, query_parts, ids_ref, info_ref, line_ref, column_ref, sums_ref)


def last_kernel(moves, info_ref, line_ref, ids_ref, earlier_ref, mass_ref, *refs):
    query_refs, refs = refs[: -PLANE - 2], refs[-PLANE - 2 :]
    column_ref, row_refs, sums_ref = refs[0], refs[1:-1], refs[-1]
    rows = column_ref.shape[1]
    sums_ref[...] = earlier_ref[...]
    query_parts = query_parts_of(query_refs, rows)
    line_sums(moves, query_parts, ids_ref, info_ref, line_ref, column_ref, sums_ref)
    for m in range(PLANE):
        row_sum = jnp.sum(sums_ref[pl.ds(m * rows, rows), :].T, axis=0, keepdims=True)
        if m == 0:
            row_sum = row_sum + mass_ref[...]
        row_refs[m][...] = row_sum


def grid_plan(embeddings, cluster_ids):
    peers = lax.axis_size("gx")
    row_count, features = embeddings.shape
    plane_rows = PLANE * row_count
    params = pltpu.CompilerParams(vmem_limit_bytes=VMEM_BYTES)
    small = pl.CostEstimate(flops=1, bytes_accessed=1, transcendentals=0)
    vector = jax.ShapeDtypeStruct((1, row_count), jnp.float32)
    lanes = jax.ShapeDtypeStruct((plane_rows, LANES), jnp.float32)

    def rows_of(count):
        return jax.ShapeDtypeStruct((count, features), jnp.bfloat16)

    def in_plane(value, step):
        return lax.ppermute(value, "gx", [(i, i ^ step) for i in range(peers)])

    def on_line(value, moves):
        pairs = [(a * PLANE + n, b * PLANE + n) for a, b in moves for n in range(PLANE)]
        return lax.ppermute(value, "gx", pairs)

    first_moves = [(0, 1), (1, 2), (2, 3), (3, 0)]
    last_moves = [(0, 2), (1, 3)]
    swap_moves = last_moves + [(b, a) for a, b in last_moves]
    forward_moves = [(1, 2), (2, 3), (3, 1), (0, 0)]
    first_back = [(b, a) for a, b in first_moves]

    half = row_count // 2
    first_line = on_line(embeddings, first_moves)
    info, block = pl.pallas_call(
        unit_kernel,
        out_shape=(
            jax.ShapeDtypeStruct((1, 2 * row_count), jnp.float32),
            rows_of(row_count + ID_ROWS),
        ),
        cost_estimate=small,
        compiler_params=params,
    )(embeddings, cluster_ids.reshape(1, row_count))
    across = in_plane(block, 2)
    sibling = in_plane(block, 1)
    first_info, last_info = on_line(info, first_moves), on_line(info, swap_moves)
    first_line, first_info, last_info = lax.optimization_barrier(
        (first_line, first_info, last_info)
    )
    last_line = on_line(first_line, forward_moves)
    corner = [in_plane(piece, 1) for piece in (across[:half], across[half:])]
    queries = (block, sibling, across, *corner)
    ids, first_column, first_sums, mass = pl.pallas_call(
        functools.partial(first_kernel, first_moves),
        out_shape=(lanes, vector, lanes, vector),
        cost_estimate=small,
        compiler_params=params,
    )(first_info, first_line, *queries)
    returned_first = on_line(first_column, first_back)
    last_column, *row_sums = pl.pallas_call(
        functools.partial(last_kernel, last_moves),
        out_shape=[vector] * (1 + PLANE),
        scratch_shapes=[pltpu.VMEM(lanes.shape, lanes.dtype)],
        compiler_params=params,
    )(last_info, last_line, ids, first_sums, mass, *queries)
    returned_first, row_sums[1] = lax.optimization_barrier((returned_first, row_sums[1]))
    returned = [on_line(last_column, swap_moves)]
    returned += [in_plane(row_sums[step], step) for step in (2, 3, 1)]
    return jnp.log1p(sum(returned, row_sums[0] + returned_first)).reshape(row_count)


def on_device(embeddings, cluster_ids):
    if lax.axis_size("gx") == 4 * PLANE and embeddings.shape[0] % (2 * LANES) == 0:
        return grid_plan(embeddings, cluster_ids)
    return plain_plan(embeddings, cluster_ids)


def solution(mesh):
    in_specs = (P(("parts", "gx"), None), P(("parts", "gx")))
    out_specs = P(("parts", "gx"))
    return jax.shard_map(
        on_device, mesh=mesh, in_specs=in_specs, out_specs=out_specs, check_vma=False
    )
```

```python
import functools

import jax
import jax.numpy as jnp
from jax import lax
from jax.experimental import pallas as pl
from jax.experimental.pallas import tpu as pltpu
from jax.sharding import PartitionSpec as P

CLU_DEV = 1
PAD_MARK = 64.0
inverse_temp = 20.0


def tile_mass(query_rows, key_rows, query_ids, key_ids, query_start):
    similar = lax.dot_general(
        query_rows, key_rows, (((1,), (1,)), ((), ())), preferred_element_type=jnp.float32
    )
    query_pos = jnp.arange(query_rows.shape[0], dtype=jnp.int32) + query_start
    key_pos = jnp.arange(key_rows.shape[0], dtype=jnp.int32)
    mate_mask = (query_ids[:, None] == key_ids[None, :]) & (query_ids[:, None] >= 0)
    mate_mask = mate_mask & (query_pos[:, None] != key_pos[None, :])
    return jnp.where(mate_mask, jnp.exp(similar * inverse_temp), 0.0)


def density_scores(key_rows, key_ids):
    total_rows = key_rows.shape[0]
    block_rows = total_rows // 3
    pieces = [key_rows[i * block_rows : (i + 1) * block_rows] for i in range(3)]
    piece_ids = [key_ids[i * block_rows : (i + 1) * block_rows] for i in range(3)]
    sums = []
    for first in range(3):
        masses = tile_mass(pieces[first], key_rows, piece_ids[first], key_ids, first * block_rows)
        sums.append(jnp.sum(masses, axis=1))
    mass_sum = jnp.concatenate(sums, axis=0)
    return jnp.log1p(mass_sum)


def plain_plan(embeddings, cluster_ids):
    peer_count = lax.axis_size("gx")
    row_count = embeddings.shape[0]
    features = embeddings.shape[1]
    capacity = 3 * row_count // peer_count
    slot_total = peer_count * capacity
    squares = jnp.sum(jnp.square(embeddings.astype(jnp.float32)), axis=1)
    unit_rows = (embeddings.astype(jnp.float32) * lax.rsqrt(squares + 1e-06)[:, None]).astype(
        jnp.bfloat16
    )
    owner_of = cluster_ids // CLU_DEV
    onehot = (owner_of[:, None] == jnp.arange(peer_count, dtype=jnp.int32)[None, :]).astype(
        jnp.bfloat16
    )
    row_range = jnp.arange(row_count, dtype=jnp.int32)
    lower_tri = (row_range[:, None] >= row_range[None, :]).astype(jnp.bfloat16)
    running = jnp.dot(lower_tri, onehot, preferred_element_type=jnp.float32)
    slot_index = (jnp.sum(running * onehot.astype(jnp.float32), axis=1) - 1.0).astype(jnp.int32)
    target_slot = owner_of * capacity + slot_index
    slot_range = jnp.arange(slot_total, dtype=jnp.int32)
    select_mask = slot_range[:, None] == target_slot[None, :]
    outgoing = jnp.dot(
        select_mask.astype(jnp.bfloat16), unit_rows, preferred_element_type=jnp.float32
    )
    outgoing = outgoing.astype(jnp.bfloat16).reshape(peer_count, capacity, features)
    outgoing_ids = jnp.sum(jnp.where(select_mask, cluster_ids[None, :] + 1, 0), axis=1) - 1
    outgoing_ids = outgoing_ids.reshape(peer_count, capacity)
    arrived, arrived_ids = (
        lax.all_to_all(outgoing, "gx", split_axis=0, concat_axis=0, tiled=True),
        lax.all_to_all(outgoing_ids, "gx", split_axis=0, concat_axis=0, tiled=True),
    )
    key_rows = arrived.reshape(slot_total, features)
    key_ids = arrived_ids.reshape(slot_total)
    scores = density_scores(key_rows, key_ids)
    returned = lax.all_to_all(
        scores.reshape(peer_count, capacity), "gx", split_axis=0, concat_axis=0, tiled=True
    )
    flat_scores = returned.reshape(slot_total)
    pick_mask = target_slot[:, None] == slot_range[None, :]
    return jnp.sum(jnp.where(pick_mask, flat_scores[None, :], 0.0), axis=1)


LANES = 128
PLANE = 4
INVERSE_TEMP_BITS = 20.0 * 1.4426950408889634
ID_ROWS = 16
VMEM_BYTES = 16 * 1024 * 1024


def along_rows(values):
    return jnp.broadcast_to(values, (LANES, values.shape[1])).T


def ids_block(ids, width):
    wide = jnp.concatenate([ids, jnp.zeros((1, width - ids.shape[1]), jnp.float32)], axis=1)
    return jnp.broadcast_to(wide, (ID_ROWS, width)).astype(jnp.bfloat16)


def ids_of(ref):
    first = ref.shape[0] - ID_ROWS
    return ref[first:, :].astype(jnp.float32)[:1]


def mate_mass(query_rows, query_ids, key_rows, key_ids, shift=None):
    similar = lax.dot_general(
        query_rows, key_rows, (((1,), (1,)), ((), ())), preferred_element_type=jnp.float32
    )
    repeats = similar.shape[1] // LANES
    mates = jnp.concatenate([query_ids] * repeats, axis=1) == key_ids
    if shift is not None:
        query_pos = lax.broadcasted_iota(jnp.int32, similar.shape, 0) + shift
        key_pos = lax.broadcasted_iota(jnp.int32, similar.shape, 1)
        mates = mates & (query_pos != key_pos)
    return jnp.where(mates, jnp.exp2(similar * INVERSE_TEMP_BITS), 0.0)


def unit_rows(raw):
    features = raw.astype(jnp.float32)
    squares = jnp.sum(features * features, axis=1, keepdims=True)
    return (features * lax.rsqrt(squares + 1e-06)).astype(jnp.bfloat16)


def unit_kernel(ranges, rows_ref, ids_ref, *block_refs):
    rows, width = rows_ref.shape
    units = unit_rows(rows_ref[...])
    ids = ids_block(ids_ref[...].astype(jnp.float32), width)
    for (first, last), ref in zip(ranges, block_refs):
        size = last - first
        ref[:size, :] = units[first:last]
        if ref.shape[0] > size:
            ref[size:, :] = ids


def line_sums(moves, query_parts, ids_ref, line_refs, column_ref, sums_ref):
    raw_ref, tail_ref = line_refs
    rows = column_ref.shape[1]
    plane = lax.axis_index("gx") // PLANE
    arrived = functools.reduce(jnp.logical_or, [plane == receiver for _, receiver in moves])
    column_ref[...] = jnp.zeros_like(column_ref)

    @pl.when(arrived)
    def _():
        key_ids = ids_of(tail_ref)[:, :rows]
        tail = tail_ref[: rows - raw_ref.shape[0], :]
        key_rows = jnp.concatenate([unit_rows(raw_ref[...]), tail], axis=0)
        column = jnp.zeros((1, rows), jnp.float32)
        first = 0
        for query_ref, size in query_parts:
            part = pl.ds(first, size)
            masses = mate_mass(query_ref[:size, :], ids_ref[part, :], key_rows, key_ids)
            column = column + jnp.sum(masses, axis=0, keepdims=True)
            folded = masses[:, :LANES]
            for lane in range(LANES, rows, LANES):
                folded = folded + masses[:, lane : lane + LANES]
            sums_ref[part, :] += folded
            first += size
        column_ref[...] = column


def query_parts_of(refs, rows):
    head = refs[2].shape[0]
    sizes = [rows, rows] + [head, rows - head] * (PLANE - 2)
    return list(zip(refs, sizes))


def first_kernel(moves, raw_ref, tail_ref, *refs):
    query_refs, (ids_ref, column_ref, sums_ref, mass_ref) = refs[:-4], refs[-4:]
    rows = mass_ref.shape[1]
    query_parts = query_parts_of(query_refs, rows)
    own_ref = query_refs[0]
    own_ids = ids_of(own_ref)[:, :rows]
    for m, ref in enumerate((*query_refs[:2], query_refs[3], query_refs[5])):
        ids_ref[pl.ds(m * rows, rows), :] = along_rows(ids_of(ref)[:, :rows])
    mass = jnp.zeros((1, rows), jnp.float32)
    first = 0
    for ref, size in query_parts:
        shift = first if first < rows else None
        masses = mate_mass(
            ref[:size, :], ids_ref[pl.ds(first, size), :], own_ref[:rows, :], own_ids, shift
        )
        mass = mass + jnp.sum(masses, axis=0, keepdims=True)
        first += size
    mass_ref[...] = mass
    sums_ref[...] = jnp.zeros_like(sums_ref)
    line_sums(moves, query_parts, ids_ref, (raw_ref, tail_ref), column_ref, sums_ref)


def last_kernel(moves, raw_ref, tail_ref, ids_ref, earlier_ref, mass_ref, *refs):
    query_refs, refs = refs[: -PLANE - 2], refs[-PLANE - 2 :]
    column_ref, row_refs, sums_ref = refs[0], refs[1:-1], refs[-1]
    rows = column_ref.shape[1]
    sums_ref[...] = earlier_ref[...]
    query_parts = query_parts_of(query_refs, rows)
    line_sums(moves, query_parts, ids_ref, (raw_ref, tail_ref), column_ref, sums_ref)
    for m in range(PLANE):
        row_sum = jnp.sum(sums_ref[pl.ds(m * rows, rows), :].T, axis=0, keepdims=True)
        if m == 0:
            row_sum = row_sum + mass_ref[...]
        row_refs[m][...] = row_sum


def grid_plan(embeddings, cluster_ids):
    peers = lax.axis_size("gx")
    row_count, features = embeddings.shape
    plane_rows = PLANE * row_count
    params = pltpu.CompilerParams(vmem_limit_bytes=VMEM_BYTES)
    small = pl.CostEstimate(flops=1, bytes_accessed=1, transcendentals=0)
    vector = jax.ShapeDtypeStruct((1, row_count), jnp.float32)
    lanes = jax.ShapeDtypeStruct((plane_rows, LANES), jnp.float32)

    def rows_of(count):
        return jax.ShapeDtypeStruct((count, features), jnp.bfloat16)

    def in_plane(value, step):
        return lax.ppermute(value, "gx", [(i, i ^ step) for i in range(peers)])

    def on_line(value, moves):
        pairs = [(a * PLANE + n, b * PLANE + n) for a, b in moves for n in range(PLANE)]
        return lax.ppermute(value, "gx", pairs)

    first_moves = [(0, 1), (1, 2), (2, 3), (3, 0)]
    last_moves = [(0, 2), (1, 3)]
    forward_moves = [(1, 2), (2, 3)]
    first_back = [(b, a) for a, b in first_moves]
    last_back = [(b, a) for a, b in last_moves]

    half, part = row_count // 2, 5 * row_count // 8
    ranges = [(0, row_count), (0, half), (half, row_count), (part, row_count)]
    id_rows = [ID_ROWS, 0, ID_ROWS, ID_ROWS]
    first_raw = on_line(embeddings[:part], first_moves)
    block, *pieces, tail = pl.pallas_call(
        functools.partial(unit_kernel, ranges),
        out_shape=[rows_of(b - a + extra) for (a, b), extra in zip(ranges, id_rows)],
        cost_estimate=small,
        compiler_params=params,
    )(embeddings, cluster_ids.reshape(1, row_count))
    first_tail = on_line(tail, first_moves)
    across = [in_plane(piece, 2) for piece in pieces]
    sibling = in_plane(block, 1)
    last_line = [on_line(got, forward_moves) for got in (first_raw, first_tail)]
    corner = [in_plane(piece, 1) for piece in across]
    queries = (block, sibling, *across, *corner)
    ids, first_column, first_sums, mass = pl.pallas_call(
        functools.partial(first_kernel, first_moves),
        out_shape=(lanes, vector, lanes, vector),
        cost_estimate=small,
        compiler_params=params,
    )(first_raw, first_tail, *queries)
    returned_first = on_line(first_column, first_back)
    last_column, *row_sums = pl.pallas_call(
        functools.partial(last_kernel, last_moves),
        out_shape=[vector] * (1 + PLANE),
        scratch_shapes=[pltpu.VMEM(lanes.shape, lanes.dtype)],
        compiler_params=params,
    )(*last_line, ids, first_sums, mass, *queries)
    returned_first, row_sums[1] = lax.optimization_barrier((returned_first, row_sums[1]))
    returned = [on_line(last_column, last_back)]
    returned += [in_plane(row_sums[step], step) for step in (2, 3, 1)]
    return jnp.log1p(sum(returned, row_sums[0] + returned_first)).reshape(row_count)


def on_device(embeddings, cluster_ids):
    if lax.axis_size("gx") == 4 * PLANE and embeddings.shape[0] % (2 * LANES) == 0:
        return grid_plan(embeddings, cluster_ids)
    return plain_plan(embeddings, cluster_ids)


def solution(mesh):
    in_specs = (P(("parts", "gx"), None), P(("parts", "gx")))
    out_specs = P(("parts", "gx"))
    return jax.shard_map(
        on_device, mesh=mesh, in_specs=in_specs, out_specs=out_specs, check_vma=False
    )
```

```python
import functools

import jax
import jax.numpy as jnp
from jax import lax
from jax.experimental import pallas as pl
from jax.experimental.pallas import tpu as pltpu
from jax.sharding import PartitionSpec as P

CLU_DEV = 1
PAD_MARK = 64.0
inverse_temp = 20.0


def tile_mass(query_rows, key_rows, query_ids, key_ids, query_start):
    similar = lax.dot_general(
        query_rows, key_rows, (((1,), (1,)), ((), ())), preferred_element_type=jnp.float32
    )
    query_pos = jnp.arange(query_rows.shape[0], dtype=jnp.int32) + query_start
    key_pos = jnp.arange(key_rows.shape[0], dtype=jnp.int32)
    mate_mask = (query_ids[:, None] == key_ids[None, :]) & (query_ids[:, None] >= 0)
    mate_mask = mate_mask & (query_pos[:, None] != key_pos[None, :])
    return jnp.where(mate_mask, jnp.exp(similar * inverse_temp), 0.0)


def density_scores(key_rows, key_ids):
    total_rows = key_rows.shape[0]
    block_rows = total_rows // 3
    pieces = [key_rows[i * block_rows : (i + 1) * block_rows] for i in range(3)]
    piece_ids = [key_ids[i * block_rows : (i + 1) * block_rows] for i in range(3)]
    sums = []
    for first in range(3):
        masses = tile_mass(pieces[first], key_rows, piece_ids[first], key_ids, first * block_rows)
        sums.append(jnp.sum(masses, axis=1))
    mass_sum = jnp.concatenate(sums, axis=0)
    return jnp.log1p(mass_sum)


def plain_plan(embeddings, cluster_ids):
    peer_count = lax.axis_size("gx")
    row_count = embeddings.shape[0]
    features = embeddings.shape[1]
    capacity = 3 * row_count // peer_count
    slot_total = peer_count * capacity
    squares = jnp.sum(jnp.square(embeddings.astype(jnp.float32)), axis=1)
    unit_rows = (embeddings.astype(jnp.float32) * lax.rsqrt(squares + 1e-06)[:, None]).astype(
        jnp.bfloat16
    )
    owner_of = cluster_ids // CLU_DEV
    onehot = (owner_of[:, None] == jnp.arange(peer_count, dtype=jnp.int32)[None, :]).astype(
        jnp.bfloat16
    )
    row_range = jnp.arange(row_count, dtype=jnp.int32)
    lower_tri = (row_range[:, None] >= row_range[None, :]).astype(jnp.bfloat16)
    running = jnp.dot(lower_tri, onehot, preferred_element_type=jnp.float32)
    slot_index = (jnp.sum(running * onehot.astype(jnp.float32), axis=1) - 1.0).astype(jnp.int32)
    target_slot = owner_of * capacity + slot_index
    slot_range = jnp.arange(slot_total, dtype=jnp.int32)
    select_mask = slot_range[:, None] == target_slot[None, :]
    outgoing = jnp.dot(
        select_mask.astype(jnp.bfloat16), unit_rows, preferred_element_type=jnp.float32
    )
    outgoing = outgoing.astype(jnp.bfloat16).reshape(peer_count, capacity, features)
    outgoing_ids = jnp.sum(jnp.where(select_mask, cluster_ids[None, :] + 1, 0), axis=1) - 1
    outgoing_ids = outgoing_ids.reshape(peer_count, capacity)
    arrived, arrived_ids = (
        lax.all_to_all(outgoing, "gx", split_axis=0, concat_axis=0, tiled=True),
        lax.all_to_all(outgoing_ids, "gx", split_axis=0, concat_axis=0, tiled=True),
    )
    key_rows = arrived.reshape(slot_total, features)
    key_ids = arrived_ids.reshape(slot_total)
    scores = density_scores(key_rows, key_ids)
    returned = lax.all_to_all(
        scores.reshape(peer_count, capacity), "gx", split_axis=0, concat_axis=0, tiled=True
    )
    flat_scores = returned.reshape(slot_total)
    pick_mask = target_slot[:, None] == slot_range[None, :]
    return jnp.sum(jnp.where(pick_mask, flat_scores[None, :], 0.0), axis=1)


LANES = 128
PLANE = 4
INVERSE_TEMP_BITS = 20.0 * 1.4426950408889634
ID_ROWS = 16
VMEM_BYTES = 16 * 1024 * 1024


def along_rows(values):
    return jnp.broadcast_to(values, (LANES, values.shape[1])).T


def ids_block(ids, width):
    wide = jnp.concatenate([ids, jnp.zeros((1, width - ids.shape[1]), jnp.float32)], axis=1)
    return jnp.broadcast_to(wide, (ID_ROWS, width)).astype(jnp.bfloat16)


def ids_of(ref):
    first = ref.shape[0] - ID_ROWS
    return ref[first:, :].astype(jnp.float32)[:1]


def mate_mass(query_rows, query_ids, key_rows, key_ids, shift=None):
    similar = lax.dot_general(
        query_rows, key_rows, (((1,), (1,)), ((), ())), preferred_element_type=jnp.float32
    )
    repeats = similar.shape[1] // LANES
    mates = jnp.concatenate([query_ids] * repeats, axis=1) == key_ids
    if shift is not None:
        query_pos = lax.broadcasted_iota(jnp.int32, similar.shape, 0) + shift
        key_pos = lax.broadcasted_iota(jnp.int32, similar.shape, 1)
        mates = mates & (query_pos != key_pos)
    return jnp.where(mates, jnp.exp2(similar * INVERSE_TEMP_BITS), 0.0)


def unit_rows(raw):
    features = raw.astype(jnp.float32)
    squares = jnp.sum(features * features, axis=1, keepdims=True)
    return (features * lax.rsqrt(squares + 1e-06)).astype(jnp.bfloat16)


def unit_kernel(ranges, rows_ref, ids_ref, *block_refs):
    rows, width = rows_ref.shape
    units = unit_rows(rows_ref[...])
    ids = ids_block(ids_ref[...].astype(jnp.float32), width)
    for (first, last), ref in zip(ranges, block_refs):
        size = last - first
        ref[:size, :] = units[first:last]
        if ref.shape[0] > size:
            ref[size:, :] = ids


def line_sums(moves, query_parts, ids_ref, line_refs, column_ref, sums_ref):
    raw_ref, tail_ref = line_refs
    rows = column_ref.shape[1]
    plane = lax.axis_index("gx") // PLANE
    arrived = functools.reduce(jnp.logical_or, [plane == receiver for _, receiver in moves])
    column_ref[...] = jnp.zeros_like(column_ref)

    @pl.when(arrived)
    def _():
        key_ids = ids_of(tail_ref)[:, :rows]
        tail = tail_ref[: rows - raw_ref.shape[0], :]
        key_rows = jnp.concatenate([unit_rows(raw_ref[...]), tail], axis=0)
        column = jnp.zeros((1, rows), jnp.float32)
        first = 0
        for query_ref, size in query_parts:
            part = pl.ds(first, size)
            masses = mate_mass(query_ref[:size, :], ids_ref[part, :], key_rows, key_ids)
            column = column + jnp.sum(masses, axis=0, keepdims=True)
            folded = masses[:, :LANES]
            for lane in range(LANES, rows, LANES):
                folded = folded + masses[:, lane : lane + LANES]
            sums_ref[part, :] += folded
            first += size
        column_ref[...] = column


def query_parts_of(refs, rows):
    head = refs[2].shape[0]
    sizes = [rows, rows] + [head, rows - head] * (PLANE - 2)
    return list(zip(refs, sizes))


def first_kernel(moves, raw_ref, tail_ref, *refs):
    query_refs, (ids_ref, column_ref, sums_ref, mass_ref) = refs[:-4], refs[-4:]
    rows = mass_ref.shape[1]
    query_parts = query_parts_of(query_refs, rows)
    own_ref = query_refs[0]
    own_ids = ids_of(own_ref)[:, :rows]
    for m, ref in enumerate((*query_refs[:2], query_refs[3], query_refs[5])):
        ids_ref[pl.ds(m * rows, rows), :] = along_rows(ids_of(ref)[:, :rows])
    mass = jnp.zeros((1, rows), jnp.float32)
    first = 0
    for ref, size in query_parts:
        shift = first if first < rows else None
        masses = mate_mass(
            ref[:size, :], ids_ref[pl.ds(first, size), :], own_ref[:rows, :], own_ids, shift
        )
        mass = mass + jnp.sum(masses, axis=0, keepdims=True)
        first += size
    mass_ref[...] = mass
    sums_ref[...] = jnp.zeros_like(sums_ref)
    line_sums(moves, query_parts, ids_ref, (raw_ref, tail_ref), column_ref, sums_ref)


def last_kernel(moves, raw_ref, tail_ref, ids_ref, earlier_ref, mass_ref, *refs):
    query_refs, refs = refs[: -PLANE - 2], refs[-PLANE - 2 :]
    column_ref, row_refs, sums_ref = refs[0], refs[1:-1], refs[-1]
    rows = column_ref.shape[1]
    sums_ref[...] = earlier_ref[...]
    query_parts = query_parts_of(query_refs, rows)
    line_sums(moves, query_parts, ids_ref, (raw_ref, tail_ref), column_ref, sums_ref)
    for m in range(PLANE):
        row_sum = jnp.sum(sums_ref[pl.ds(m * rows, rows), :].T, axis=0, keepdims=True)
        if m == 0:
            row_sum = row_sum + mass_ref[...]
        row_refs[m][...] = row_sum


def grid_plan(embeddings, cluster_ids):
    peers = lax.axis_size("gx")
    row_count, features = embeddings.shape
    plane_rows = PLANE * row_count
    params = pltpu.CompilerParams(vmem_limit_bytes=VMEM_BYTES)
    small = pl.CostEstimate(flops=1, bytes_accessed=1, transcendentals=0)
    vector = jax.ShapeDtypeStruct((1, row_count), jnp.float32)
    lanes = jax.ShapeDtypeStruct((plane_rows, LANES), jnp.float32)

    def rows_of(count):
        return jax.ShapeDtypeStruct((count, features), jnp.bfloat16)

    def in_plane(value, step):
        return lax.ppermute(value, "gx", [(i, i ^ step) for i in range(peers)])

    def on_line(value, moves):
        pairs = [(a * PLANE + n, b * PLANE + n) for a, b in moves for n in range(PLANE)]
        return lax.ppermute(value, "gx", pairs)

    first_moves = [(0, 1), (1, 2), (2, 3), (3, 0)]
    last_moves = [(0, 2), (1, 3)]
    forward_moves = [(1, 2), (2, 3), (3, 1), (0, 0)]
    first_back = [(b, a) for a, b in first_moves]
    last_back = [(b, a) for a, b in last_moves]

    half, part = row_count // 2, 5 * row_count // 8
    ranges = [(0, row_count), (0, half), (half, row_count), (part, row_count)]
    id_rows = [ID_ROWS, 0, ID_ROWS, ID_ROWS]
    first_raw = on_line(embeddings[:part], first_moves)
    block, *pieces, tail = pl.pallas_call(
        functools.partial(unit_kernel, ranges),
        out_shape=[rows_of(b - a + extra) for (a, b), extra in zip(ranges, id_rows)],
        cost_estimate=small,
        compiler_params=params,
    )(embeddings, cluster_ids.reshape(1, row_count))
    first_tail = on_line(tail, first_moves)
    across = [in_plane(piece, 2) for piece in pieces]
    sibling = in_plane(block, 1)
    last_line = [on_line(got, forward_moves) for got in (first_raw, first_tail)]
    corner = [in_plane(piece, 1) for piece in across]
    queries = (block, sibling, *across, *corner)
    ids, first_column, first_sums, mass = pl.pallas_call(
        functools.partial(first_kernel, first_moves),
        out_shape=(lanes, vector, lanes, vector),
        cost_estimate=small,
        compiler_params=params,
    )(first_raw, first_tail, *queries)
    returned_first = on_line(first_column, first_back)
    last_column, *row_sums = pl.pallas_call(
        functools.partial(last_kernel, last_moves),
        out_shape=[vector] * (1 + PLANE),
        scratch_shapes=[pltpu.VMEM(lanes.shape, lanes.dtype)],
        compiler_params=params,
    )(*last_line, ids, first_sums, mass, *queries)
    returned_first, row_sums[1] = lax.optimization_barrier((returned_first, row_sums[1]))
    returned = [on_line(last_column, last_back)]
    returned += [in_plane(row_sums[step], step) for step in (2, 3, 1)]
    return jnp.log1p(sum(returned, row_sums[0] + returned_first)).reshape(row_count)


def on_device(embeddings, cluster_ids):
    if lax.axis_size("gx") == 4 * PLANE and embeddings.shape[0] % (2 * LANES) == 0:
        return grid_plan(embeddings, cluster_ids)
    return plain_plan(embeddings, cluster_ids)


def solution(mesh):
    in_specs = (P(("parts", "gx"), None), P(("parts", "gx")))
    out_specs = P(("parts", "gx"))
    return jax.shard_map(
        on_device, mesh=mesh, in_specs=in_specs, out_specs=out_specs, check_vma=False
    )
```

```python
import functools

import jax
import jax.numpy as jnp
from jax import lax
from jax.experimental import pallas as pl
from jax.experimental.pallas import tpu as pltpu
from jax.sharding import PartitionSpec as P

CLU_DEV = 1
PAD_MARK = 64.0
inverse_temp = 20.0


def tile_mass(query_rows, key_rows, query_ids, key_ids, query_start):
    similar = lax.dot_general(
        query_rows, key_rows, (((1,), (1,)), ((), ())), preferred_element_type=jnp.float32
    )
    query_pos = jnp.arange(query_rows.shape[0], dtype=jnp.int32) + query_start
    key_pos = jnp.arange(key_rows.shape[0], dtype=jnp.int32)
    mate_mask = (query_ids[:, None] == key_ids[None, :]) & (query_ids[:, None] >= 0)
    mate_mask = mate_mask & (query_pos[:, None] != key_pos[None, :])
    return jnp.where(mate_mask, jnp.exp(similar * inverse_temp), 0.0)


def density_scores(key_rows, key_ids):
    total_rows = key_rows.shape[0]
    block_rows = total_rows // 3
    pieces = [key_rows[i * block_rows : (i + 1) * block_rows] for i in range(3)]
    piece_ids = [key_ids[i * block_rows : (i + 1) * block_rows] for i in range(3)]
    sums = []
    for first in range(3):
        masses = tile_mass(pieces[first], key_rows, piece_ids[first], key_ids, first * block_rows)
        sums.append(jnp.sum(masses, axis=1))
    mass_sum = jnp.concatenate(sums, axis=0)
    return jnp.log1p(mass_sum)


def plain_plan(embeddings, cluster_ids):
    peer_count = lax.axis_size("gx")
    row_count = embeddings.shape[0]
    features = embeddings.shape[1]
    capacity = 3 * row_count // peer_count
    slot_total = peer_count * capacity
    squares = jnp.sum(jnp.square(embeddings.astype(jnp.float32)), axis=1)
    unit_rows = (embeddings.astype(jnp.float32) * lax.rsqrt(squares + 1e-06)[:, None]).astype(
        jnp.bfloat16
    )
    owner_of = cluster_ids // CLU_DEV
    onehot = (owner_of[:, None] == jnp.arange(peer_count, dtype=jnp.int32)[None, :]).astype(
        jnp.bfloat16
    )
    row_range = jnp.arange(row_count, dtype=jnp.int32)
    lower_tri = (row_range[:, None] >= row_range[None, :]).astype(jnp.bfloat16)
    running = jnp.dot(lower_tri, onehot, preferred_element_type=jnp.float32)
    slot_index = (jnp.sum(running * onehot.astype(jnp.float32), axis=1) - 1.0).astype(jnp.int32)
    target_slot = owner_of * capacity + slot_index
    slot_range = jnp.arange(slot_total, dtype=jnp.int32)
    select_mask = slot_range[:, None] == target_slot[None, :]
    outgoing = jnp.dot(
        select_mask.astype(jnp.bfloat16), unit_rows, preferred_element_type=jnp.float32
    )
    outgoing = outgoing.astype(jnp.bfloat16).reshape(peer_count, capacity, features)
    outgoing_ids = jnp.sum(jnp.where(select_mask, cluster_ids[None, :] + 1, 0), axis=1) - 1
    outgoing_ids = outgoing_ids.reshape(peer_count, capacity)
    arrived, arrived_ids = (
        lax.all_to_all(outgoing, "gx", split_axis=0, concat_axis=0, tiled=True),
        lax.all_to_all(outgoing_ids, "gx", split_axis=0, concat_axis=0, tiled=True),
    )
    key_rows = arrived.reshape(slot_total, features)
    key_ids = arrived_ids.reshape(slot_total)
    scores = density_scores(key_rows, key_ids)
    returned = lax.all_to_all(
        scores.reshape(peer_count, capacity), "gx", split_axis=0, concat_axis=0, tiled=True
    )
    flat_scores = returned.reshape(slot_total)
    pick_mask = target_slot[:, None] == slot_range[None, :]
    return jnp.sum(jnp.where(pick_mask, flat_scores[None, :], 0.0), axis=1)


LANES = 128
PLANE = 4
INVERSE_TEMP_BITS = 20.0 * 1.4426950408889634
ID_ROWS = 16
VMEM_BYTES = 16 * 1024 * 1024


def along_rows(values):
    return jnp.broadcast_to(values, (LANES, values.shape[1])).T


def ids_block(ids, width):
    wide = jnp.concatenate([ids, jnp.zeros((1, width - ids.shape[1]), jnp.float32)], axis=1)
    return jnp.broadcast_to(wide, (ID_ROWS, width)).astype(jnp.bfloat16)


def ids_of(ref):
    first = ref.shape[0] - ID_ROWS
    return ref[first:, :].astype(jnp.float32)[:1]


def mate_mass(query_rows, query_ids, key_rows, key_ids, shift=None):
    similar = lax.dot_general(
        query_rows, key_rows, (((1,), (1,)), ((), ())), preferred_element_type=jnp.float32
    )
    repeats = similar.shape[1] // LANES
    mates = jnp.concatenate([query_ids] * repeats, axis=1) == key_ids
    if shift is not None:
        query_pos = lax.broadcasted_iota(jnp.int32, similar.shape, 0) + shift
        key_pos = lax.broadcasted_iota(jnp.int32, similar.shape, 1)
        mates = mates & (query_pos != key_pos)
    return jnp.where(mates, jnp.exp2(similar * INVERSE_TEMP_BITS), 0.0)


def unit_rows(raw):
    features = raw.astype(jnp.float32)
    squares = jnp.sum(features * features, axis=1, keepdims=True)
    return (features * lax.rsqrt(squares + 1e-06)).astype(jnp.bfloat16)


def unit_kernel(ranges, rows_ref, ids_ref, *block_refs):
    rows, width = rows_ref.shape
    units = unit_rows(rows_ref[...])
    ids = ids_block(ids_ref[...].astype(jnp.float32), width)
    for (first, last), ref in zip(ranges, block_refs):
        size = last - first
        ref[:size, :] = units[first:last]
        if ref.shape[0] > size:
            ref[size:, :] = ids


def padded(values, count, fill):
    rows, columns = values.shape
    if rows == 1:
        return jnp.concatenate([values, jnp.full((1, count - columns), fill, values.dtype)], axis=1)
    return jnp.concatenate([values, jnp.full((count - rows, columns), fill, values.dtype)], axis=0)


def arrived_at(moves):
    plane = lax.axis_index("gx") // PLANE
    return functools.reduce(jnp.logical_or, [plane == receiver for _, receiver in moves])


def add_line(query_parts, ids_ref, key_rows, key_ids, earlier_ref, sums_ref):
    keys = key_rows.shape[0]
    column = jnp.zeros((1, keys), jnp.float32)
    first = 0
    for query_ref, size in query_parts:
        part = pl.ds(first, size)
        masses = mate_mass(query_ref[:size, :], ids_ref[part, :], key_rows, key_ids)
        column = column + jnp.sum(masses, axis=0, keepdims=True)
        folded = masses[:, :LANES]
        for lane in range(LANES, keys, LANES):
            folded = folded + masses[:, lane : lane + LANES]
        sums_ref[part, :] = folded if earlier_ref is None else earlier_ref[part, :] + folded
        first += size
    return column


def add_masses(query_ids, key_ids, powers):
    mates = jnp.concatenate([query_ids] * (powers.shape[1] // LANES), axis=1) == key_ids
    masses = jnp.where(mates, powers, 0.0)
    folded = masses[:, :LANES]
    for lane in range(LANES, powers.shape[1], LANES):
        folded = folded + masses[:, lane : lane + LANES]
    return folded, jnp.sum(masses, axis=0, keepdims=True)


def query_parts_of(refs, rows):
    head = refs[2].shape[0]
    sizes = [rows, rows] + [head, rows - head] * (PLANE - 2)
    return list(zip(refs, sizes))


def first_kernel(moves, head_ref, tail_ref, *refs):
    query_refs, (ids_ref, column_ref, sums_ref, mass_ref) = refs[:-4], refs[-4:]
    rows = mass_ref.shape[1]
    query_parts = query_parts_of(query_refs, rows)
    own_ref = query_refs[0]
    own_ids = ids_of(own_ref)[:, :rows]
    for m, ref in enumerate((*query_refs[:2], query_refs[3], query_refs[5])):
        ids_ref[pl.ds(m * rows, rows), :] = along_rows(ids_of(ref)[:, :rows])
    mass = jnp.zeros((1, rows), jnp.float32)
    first = 0
    for ref, size in query_parts:
        shift = first if first < rows else None
        masses = mate_mass(
            ref[:size, :], ids_ref[pl.ds(first, size), :], own_ref[:rows, :], own_ids, shift
        )
        mass = mass + jnp.sum(masses, axis=0, keepdims=True)
        first += size
    mass_ref[...] = mass
    tail = tail_ref[: rows - head_ref.shape[0], :]
    key_rows = jnp.concatenate([unit_rows(head_ref[...]), tail], axis=0)
    key_ids = ids_of(tail_ref)[:, :rows]
    column_ref[...] = add_line(query_parts, ids_ref, key_rows, key_ids, None, sums_ref)


def middle_kernel(moves, head_ref, *refs):
    query_refs, powers_ref = refs[:-1], refs[-1]

    @pl.when(arrived_at(moves))
    def _():
        keys = powers_ref.shape[1]
        key_rows = padded(unit_rows(head_ref[...]), keys, 0.0)
        first = 0
        for query_ref, size in query_parts_of(query_refs, keys):
            similar = lax.dot_general(
                query_ref[:size, :], key_rows, (((1,), (1,)), ((), ())),
                preferred_element_type=jnp.float32,
            )
            powers_ref[pl.ds(first, size), :] = jnp.exp2(similar * INVERSE_TEMP_BITS)
            first += size


def last_kernel(moves, powers_ref, tail_ref, ids_ref, earlier_ref, mass_ref, *refs):
    query_refs, refs = refs[: -PLANE - 2], refs[-PLANE - 2 :]
    column_ref, row_refs, sums_ref = refs[0], refs[1:-1], refs[-1]
    rows = column_ref.shape[1]
    arrived = arrived_at(moves)

    @pl.when(arrived)
    def _():
        tail = tail_ref.shape[0] - ID_ROWS
        keys = LANES * ((tail + LANES - 1) // LANES)
        key_ids = ids_of(tail_ref)[:, :rows]
        head_ids = padded(key_ids[:, : rows - tail], rows, -1.0)
        tail_ids = padded(key_ids[:, rows - tail :], keys, -1.0)
        key_rows = padded(tail_ref[:tail, :], keys, 0.0)
        head_column = jnp.zeros((1, rows), jnp.float32)
        tail_column = jnp.zeros((1, keys), jnp.float32)
        first = 0
        for query_ref, size in query_parts_of(query_refs, rows):
            part = pl.ds(first, size)
            query_ids = ids_ref[part, :]
            similar = lax.dot_general(
                query_ref[:size, :], key_rows, (((1,), (1,)), ((), ())),
                preferred_element_type=jnp.float32,
            )
            powers = jnp.exp2(similar * INVERSE_TEMP_BITS)
            tail_part, column = add_masses(query_ids, tail_ids, powers)
            tail_column = tail_column + column
            head_part, column = add_masses(query_ids, head_ids, powers_ref[part, :])
            head_column = head_column + column
            sums_ref[part, :] = earlier_ref[part, :] + head_part + tail_part
            first += size
        column_ref[...] = jnp.concatenate(
            [head_column[:, : rows - tail], tail_column[:, :tail]], axis=1
        )

    @pl.when(jnp.logical_not(arrived))
    def _():
        column_ref[...] = jnp.zeros_like(column_ref)
        sums_ref[...] = earlier_ref[...]

    for m in range(PLANE):
        row_sum = jnp.sum(sums_ref[pl.ds(m * rows, rows), :].T, axis=0, keepdims=True)
        row_refs[m][...] = row_sum + mass_ref[...] if m == 0 else row_sum


def grid_plan(embeddings, cluster_ids):
    peers = lax.axis_size("gx")
    row_count, features = embeddings.shape
    plane_rows = PLANE * row_count
    params = pltpu.CompilerParams(vmem_limit_bytes=VMEM_BYTES)
    small = pl.CostEstimate(flops=1, bytes_accessed=1, transcendentals=0)
    vector = jax.ShapeDtypeStruct((1, row_count), jnp.float32)
    lanes = jax.ShapeDtypeStruct((plane_rows, LANES), jnp.float32)

    def rows_of(count):
        return jax.ShapeDtypeStruct((count, features), jnp.bfloat16)

    def in_plane(value, step):
        return lax.ppermute(value, "gx", [(i, i ^ step) for i in range(peers)])

    def on_line(value, moves):
        pairs = [(a * PLANE + n, b * PLANE + n) for a, b in moves for n in range(PLANE)]
        return lax.ppermute(value, "gx", pairs)

    first_moves = [(0, 1), (1, 2), (2, 3), (3, 0)]
    last_moves = [(0, 2), (1, 3)]
    forward_moves = [(1, 2), (2, 3)]
    first_back = [(b, a) for a, b in first_moves]
    last_back = [(b, a) for a, b in last_moves]

    half, part = row_count // 2, 5 * row_count // 8
    ranges = [(0, row_count), (0, half), (half, row_count), (part, row_count)]
    id_rows = [ID_ROWS, 0, ID_ROWS, ID_ROWS]
    first_head = on_line(embeddings[:part], first_moves)
    block, *pieces, tail = pl.pallas_call(
        functools.partial(unit_kernel, ranges),
        out_shape=[rows_of(b - a + extra) for (a, b), extra in zip(ranges, id_rows)],
        cost_estimate=small,
        compiler_params=params,
    )(embeddings, cluster_ids.reshape(1, row_count))
    first_tail = on_line(tail, first_moves)
    across = [in_plane(piece, 2) for piece in pieces]
    sibling = in_plane(block, 1)
    last_head, last_tail = [on_line(got, forward_moves) for got in (first_head, first_tail)]
    corner = [in_plane(piece, 1) for piece in across]
    queries = (block, sibling, *across, *corner)
    ids, first_column, first_sums, mass = pl.pallas_call(
        functools.partial(first_kernel, first_moves),
        out_shape=(lanes, vector, lanes, vector),
        cost_estimate=small,
        compiler_params=params,
    )(first_head, first_tail, *queries)
    returned_first = on_line(first_column, first_back)
    powers = pl.pallas_call(
        functools.partial(middle_kernel, last_moves),
        out_shape=jax.ShapeDtypeStruct((plane_rows, row_count), jnp.float32),
        cost_estimate=small,
        compiler_params=params,
    )(last_head, *queries)
    last_column, *row_sums = pl.pallas_call(
        functools.partial(last_kernel, last_moves),
        out_shape=[vector] * (1 + PLANE),
        scratch_shapes=[pltpu.VMEM(lanes.shape, lanes.dtype)],
        compiler_params=params,
    )(powers, last_tail, ids, first_sums, mass, *queries)
    returned_first, row_sums[1] = lax.optimization_barrier((returned_first, row_sums[1]))
    returned = [on_line(last_column, last_back)]
    returned += [in_plane(row_sums[step], step) for step in (2, 3, 1)]
    return jnp.log1p(sum(returned, row_sums[0] + returned_first)).reshape(row_count)


def on_device(embeddings, cluster_ids):
    if lax.axis_size("gx") == 4 * PLANE and embeddings.shape[0] % (2 * LANES) == 0:
        return grid_plan(embeddings, cluster_ids)
    return plain_plan(embeddings, cluster_ids)


def solution(mesh):
    in_specs = (P(("parts", "gx"), None), P(("parts", "gx")))
    out_specs = P(("parts", "gx"))
    return jax.shard_map(
        on_device, mesh=mesh, in_specs=in_specs, out_specs=out_specs, check_vma=False
    )
```

```python
import functools

import jax
import jax.numpy as jnp
from jax import lax
from jax.experimental import pallas as pl
from jax.experimental.pallas import tpu as pltpu
from jax.sharding import PartitionSpec as P

CLU_DEV = 1
PAD_MARK = 64.0
inverse_temp = 20.0


def tile_mass(query_rows, key_rows, query_ids, key_ids, query_start):
    similar = lax.dot_general(
        query_rows, key_rows, (((1,), (1,)), ((), ())), preferred_element_type=jnp.float32
    )
    query_pos = jnp.arange(query_rows.shape[0], dtype=jnp.int32) + query_start
    key_pos = jnp.arange(key_rows.shape[0], dtype=jnp.int32)
    mate_mask = (query_ids[:, None] == key_ids[None, :]) & (query_ids[:, None] >= 0)
    mate_mask = mate_mask & (query_pos[:, None] != key_pos[None, :])
    return jnp.where(mate_mask, jnp.exp(similar * inverse_temp), 0.0)


def density_scores(key_rows, key_ids):
    total_rows = key_rows.shape[0]
    block_rows = total_rows // 3
    pieces = [key_rows[i * block_rows : (i + 1) * block_rows] for i in range(3)]
    piece_ids = [key_ids[i * block_rows : (i + 1) * block_rows] for i in range(3)]
    sums = []
    for first in range(3):
        masses = tile_mass(pieces[first], key_rows, piece_ids[first], key_ids, first * block_rows)
        sums.append(jnp.sum(masses, axis=1))
    mass_sum = jnp.concatenate(sums, axis=0)
    return jnp.log1p(mass_sum)


def plain_plan(embeddings, cluster_ids):
    peer_count = lax.axis_size("gx")
    row_count = embeddings.shape[0]
    features = embeddings.shape[1]
    capacity = 3 * row_count // peer_count
    slot_total = peer_count * capacity
    squares = jnp.sum(jnp.square(embeddings.astype(jnp.float32)), axis=1)
    unit_rows = (embeddings.astype(jnp.float32) * lax.rsqrt(squares + 1e-06)[:, None]).astype(
        jnp.bfloat16
    )
    owner_of = cluster_ids // CLU_DEV
    onehot = (owner_of[:, None] == jnp.arange(peer_count, dtype=jnp.int32)[None, :]).astype(
        jnp.bfloat16
    )
    row_range = jnp.arange(row_count, dtype=jnp.int32)
    lower_tri = (row_range[:, None] >= row_range[None, :]).astype(jnp.bfloat16)
    running = jnp.dot(lower_tri, onehot, preferred_element_type=jnp.float32)
    slot_index = (jnp.sum(running * onehot.astype(jnp.float32), axis=1) - 1.0).astype(jnp.int32)
    target_slot = owner_of * capacity + slot_index
    slot_range = jnp.arange(slot_total, dtype=jnp.int32)
    select_mask = slot_range[:, None] == target_slot[None, :]
    outgoing = jnp.dot(
        select_mask.astype(jnp.bfloat16), unit_rows, preferred_element_type=jnp.float32
    )
    outgoing = outgoing.astype(jnp.bfloat16).reshape(peer_count, capacity, features)
    outgoing_ids = jnp.sum(jnp.where(select_mask, cluster_ids[None, :] + 1, 0), axis=1) - 1
    outgoing_ids = outgoing_ids.reshape(peer_count, capacity)
    arrived, arrived_ids = (
        lax.all_to_all(outgoing, "gx", split_axis=0, concat_axis=0, tiled=True),
        lax.all_to_all(outgoing_ids, "gx", split_axis=0, concat_axis=0, tiled=True),
    )
    key_rows = arrived.reshape(slot_total, features)
    key_ids = arrived_ids.reshape(slot_total)
    scores = density_scores(key_rows, key_ids)
    returned = lax.all_to_all(
        scores.reshape(peer_count, capacity), "gx", split_axis=0, concat_axis=0, tiled=True
    )
    flat_scores = returned.reshape(slot_total)
    pick_mask = target_slot[:, None] == slot_range[None, :]
    return jnp.sum(jnp.where(pick_mask, flat_scores[None, :], 0.0), axis=1)


LANES = 128
PLANE = 4
INVERSE_TEMP_BITS = 20.0 * 1.4426950408889634
ID_ROWS = 8
VMEM_BYTES = 16 * 1024 * 1024


def along_rows(values):
    return jnp.broadcast_to(values, (LANES, values.shape[1])).T


def ids_block(ids, width):
    wide = jnp.concatenate([ids, jnp.zeros((1, width - ids.shape[1]), jnp.float32)], axis=1)
    return jnp.broadcast_to(wide, (ID_ROWS, width)).astype(jnp.bfloat16)


def ids_of(ref):
    first = ref.shape[0] - ID_ROWS
    return ref[first:, :].astype(jnp.float32)[:1]


def mate_mass(query_rows, query_ids, key_rows, key_ids, shift=None):
    similar = lax.dot_general(
        query_rows, key_rows, (((1,), (1,)), ((), ())), preferred_element_type=jnp.float32
    )
    repeats = similar.shape[1] // LANES
    mates = jnp.concatenate([query_ids] * repeats, axis=1) == key_ids
    if shift is not None:
        query_pos = lax.broadcasted_iota(jnp.int32, similar.shape, 0) + shift
        key_pos = lax.broadcasted_iota(jnp.int32, similar.shape, 1)
        mates = mates & (query_pos != key_pos)
    return jnp.where(mates, jnp.exp2(similar * INVERSE_TEMP_BITS), 0.0)


def unit_rows(raw):
    features = raw.astype(jnp.float32)
    squares = jnp.sum(features * features, axis=1, keepdims=True)
    return (features * lax.rsqrt(squares + 1e-06)).astype(jnp.bfloat16)


def unit_kernel(ranges, rows_ref, ids_ref, *block_refs):
    rows, width = rows_ref.shape
    units = unit_rows(rows_ref[...])
    ids = ids_block(ids_ref[...].astype(jnp.float32), width)
    for (first, last), ref in zip(ranges, block_refs):
        size = last - first
        ref[:size, :] = units[first:last]
        if ref.shape[0] > size:
            ref[size:, :] = ids


def padded(values, count, fill):
    rows, columns = values.shape
    if rows == 1:
        return jnp.concatenate([values, jnp.full((1, count - columns), fill, values.dtype)], axis=1)
    return jnp.concatenate([values, jnp.full((count - rows, columns), fill, values.dtype)], axis=0)


def arrived_at(moves):
    plane = lax.axis_index("gx") // PLANE
    return functools.reduce(jnp.logical_or, [plane == receiver for _, receiver in moves])


def add_line(query_parts, ids_ref, key_rows, key_ids, earlier_ref, sums_ref):
    keys = key_rows.shape[0]
    column = jnp.zeros((1, keys), jnp.float32)
    first = 0
    for query_ref, size in query_parts:
        part = pl.ds(first, size)
        masses = mate_mass(query_ref[:size, :], ids_ref[part, :], key_rows, key_ids)
        column = column + jnp.sum(masses, axis=0, keepdims=True)
        folded = masses[:, :LANES]
        for lane in range(LANES, keys, LANES):
            folded = folded + masses[:, lane : lane + LANES]
        sums_ref[part, :] = folded if earlier_ref is None else earlier_ref[part, :] + folded
        first += size
    return column


def add_masses(query_ids, key_ids, powers):
    mates = jnp.concatenate([query_ids] * (powers.shape[1] // LANES), axis=1) == key_ids
    masses = jnp.where(mates, powers, 0.0)
    folded = masses[:, :LANES]
    for lane in range(LANES, powers.shape[1], LANES):
        folded = folded + masses[:, lane : lane + LANES]
    return folded, jnp.sum(masses, axis=0, keepdims=True)


def query_parts_of(refs, rows):
    head = refs[2].shape[0]
    sizes = [rows, rows] + [head, rows - head] * (PLANE - 2)
    return list(zip(refs, sizes))


def first_kernel(moves, head_ref, tail_ref, *refs):
    query_refs, (ids_ref, column_ref, sums_ref, mass_ref) = refs[:-4], refs[-4:]
    rows = mass_ref.shape[1]
    query_parts = query_parts_of(query_refs, rows)
    own_ref = query_refs[0]
    own_ids = ids_of(own_ref)[:, :rows]
    for m, ref in enumerate((*query_refs[:2], query_refs[3], query_refs[5])):
        ids_ref[pl.ds(m * rows, rows), :] = along_rows(ids_of(ref)[:, :rows])
    mass = jnp.zeros((1, rows), jnp.float32)
    first = 0
    for ref, size in query_parts:
        shift = first if first < rows else None
        masses = mate_mass(
            ref[:size, :], ids_ref[pl.ds(first, size), :], own_ref[:rows, :], own_ids, shift
        )
        mass = mass + jnp.sum(masses, axis=0, keepdims=True)
        first += size
    mass_ref[...] = mass
    tail = tail_ref[: rows - head_ref.shape[0], :]
    key_rows = jnp.concatenate([unit_rows(head_ref[...]), tail], axis=0)
    key_ids = ids_of(tail_ref)[:, :rows]
    column_ref[...] = add_line(query_parts, ids_ref, key_rows, key_ids, None, sums_ref)


def middle_kernel(moves, head_ref, *refs):
    query_refs, powers_ref = refs[:-1], refs[-1]

    @pl.when(arrived_at(moves))
    def _():
        keys = powers_ref.shape[1]
        key_rows = padded(unit_rows(head_ref[...]), keys, 0.0)
        first = 0
        for query_ref, size in query_parts_of(query_refs, keys):
            similar = lax.dot_general(
                query_ref[:size, :], key_rows, (((1,), (1,)), ((), ())),
                preferred_element_type=jnp.float32,
            )
            powers_ref[pl.ds(first, size), :] = jnp.exp2(similar * INVERSE_TEMP_BITS)
            first += size


def last_kernel(moves, powers_ref, tail_ref, ids_ref, earlier_ref, mass_ref, *refs):
    query_refs, refs = refs[: -PLANE - 2], refs[-PLANE - 2 :]
    column_ref, row_refs, sums_ref = refs[0], refs[1:-1], refs[-1]
    rows = column_ref.shape[1]
    arrived = arrived_at(moves)

    @pl.when(arrived)
    def _():
        tail = tail_ref.shape[0] - ID_ROWS
        keys = LANES * ((tail + LANES - 1) // LANES)
        key_ids = ids_of(tail_ref)[:, :rows]
        head_ids = padded(key_ids[:, : rows - tail], rows, -1.0)
        tail_ids = padded(key_ids[:, rows - tail :], keys, -1.0)
        key_rows = padded(tail_ref[:tail, :], keys, 0.0)
        head_column = jnp.zeros((1, rows), jnp.float32)
        tail_column = jnp.zeros((1, keys), jnp.float32)
        first = 0
        for query_ref, size in query_parts_of(query_refs, rows):
            part = pl.ds(first, size)
            query_ids = ids_ref[part, :]
            similar = lax.dot_general(
                query_ref[:size, :], key_rows, (((1,), (1,)), ((), ())),
                preferred_element_type=jnp.float32,
            )
            powers = jnp.exp2(similar * INVERSE_TEMP_BITS)
            tail_part, column = add_masses(query_ids, tail_ids, powers)
            tail_column = tail_column + column
            head_part, column = add_masses(query_ids, head_ids, powers_ref[part, :])
            head_column = head_column + column
            sums_ref[part, :] = earlier_ref[part, :] + head_part + tail_part
            first += size
        column_ref[...] = jnp.concatenate(
            [head_column[:, : rows - tail], tail_column[:, :tail]], axis=1
        )

    @pl.when(jnp.logical_not(arrived))
    def _():
        column_ref[...] = jnp.zeros_like(column_ref)
        sums_ref[...] = earlier_ref[...]

    for m in range(PLANE):
        row_sum = jnp.sum(sums_ref[pl.ds(m * rows, rows), :].T, axis=0, keepdims=True)
        row_refs[m][...] = row_sum + mass_ref[...] if m == 0 else row_sum


def grid_plan(embeddings, cluster_ids):
    peers = lax.axis_size("gx")
    row_count, features = embeddings.shape
    plane_rows = PLANE * row_count
    params = pltpu.CompilerParams(vmem_limit_bytes=VMEM_BYTES)
    small = pl.CostEstimate(flops=1, bytes_accessed=1, transcendentals=0)
    vector = jax.ShapeDtypeStruct((1, row_count), jnp.float32)
    lanes = jax.ShapeDtypeStruct((plane_rows, LANES), jnp.float32)

    def rows_of(count):
        return jax.ShapeDtypeStruct((count, features), jnp.bfloat16)

    def in_plane(value, step):
        return lax.ppermute(value, "gx", [(i, i ^ step) for i in range(peers)])

    def on_line(value, moves):
        pairs = [(a * PLANE + n, b * PLANE + n) for a, b in moves for n in range(PLANE)]
        return lax.ppermute(value, "gx", pairs)

    first_moves = [(0, 1), (1, 2), (2, 3), (3, 0)]
    last_moves = [(0, 2), (1, 3)]
    forward_moves = [(1, 2), (2, 3)]
    first_back = [(b, a) for a, b in first_moves]
    last_back = [(b, a) for a, b in last_moves]

    half, part = row_count // 2, 9 * row_count // 16
    ranges = [(0, row_count), (0, half), (half, row_count), (part, row_count)]
    id_rows = [ID_ROWS, 0, ID_ROWS, ID_ROWS]
    first_head = on_line(embeddings[:part], first_moves)
    block, *pieces, tail = pl.pallas_call(
        functools.partial(unit_kernel, ranges),
        out_shape=[rows_of(b - a + extra) for (a, b), extra in zip(ranges, id_rows)],
        cost_estimate=small,
        compiler_params=params,
    )(embeddings, cluster_ids.reshape(1, row_count))
    first_tail = on_line(tail, first_moves)
    across = [in_plane(piece, 2) for piece in pieces]
    sibling = in_plane(block, 1)
    last_head, last_tail = [on_line(got, forward_moves) for got in (first_head, first_tail)]
    corner = [in_plane(piece, 1) for piece in across]
    queries = (block, sibling, *across, *corner)
    ids, first_column, first_sums, mass = pl.pallas_call(
        functools.partial(first_kernel, first_moves),
        out_shape=(lanes, vector, lanes, vector),
        cost_estimate=small,
        compiler_params=params,
    )(first_head, first_tail, *queries)
    returned_first = on_line(first_column, first_back)
    powers = pl.pallas_call(
        functools.partial(middle_kernel, last_moves),
        out_shape=jax.ShapeDtypeStruct((plane_rows, row_count), jnp.float32),
        cost_estimate=small,
        compiler_params=params,
    )(last_head, *queries)
    last_column, *row_sums = pl.pallas_call(
        functools.partial(last_kernel, last_moves),
        out_shape=[vector] * (1 + PLANE),
        scratch_shapes=[pltpu.VMEM(lanes.shape, lanes.dtype)],
        compiler_params=params,
    )(powers, last_tail, ids, first_sums, mass, *queries)
    returned_first, row_sums[1] = lax.optimization_barrier((returned_first, row_sums[1]))
    returned = [on_line(last_column, last_back)]
    returned += [in_plane(row_sums[step], step) for step in (2, 3, 1)]
    return jnp.log1p(sum(returned, row_sums[0] + returned_first)).reshape(row_count)


def on_device(embeddings, cluster_ids):
    if lax.axis_size("gx") == 4 * PLANE and embeddings.shape[0] % (2 * LANES) == 0:
        return grid_plan(embeddings, cluster_ids)
    return plain_plan(embeddings, cluster_ids)


def solution(mesh):
    in_specs = (P(("parts", "gx"), None), P(("parts", "gx")))
    out_specs = P(("parts", "gx"))
    return jax.shard_map(
        on_device, mesh=mesh, in_specs=in_specs, out_specs=out_specs, check_vma=False
    )
```

```python
import functools

import jax
import jax.numpy as jnp
from jax import lax
from jax.experimental import pallas as pl
from jax.experimental.pallas import tpu as pltpu
from jax.sharding import PartitionSpec as P

CLU_DEV = 1
PAD_MARK = 64.0
inverse_temp = 20.0


def tile_mass(query_rows, key_rows, query_ids, key_ids, query_start):
    similar = lax.dot_general(
        query_rows, key_rows, (((1,), (1,)), ((), ())), preferred_element_type=jnp.float32
    )
    query_pos = jnp.arange(query_rows.shape[0], dtype=jnp.int32) + query_start
    key_pos = jnp.arange(key_rows.shape[0], dtype=jnp.int32)
    mate_mask = (query_ids[:, None] == key_ids[None, :]) & (query_ids[:, None] >= 0)
    mate_mask = mate_mask & (query_pos[:, None] != key_pos[None, :])
    return jnp.where(mate_mask, jnp.exp(similar * inverse_temp), 0.0)


def density_scores(key_rows, key_ids):
    total_rows = key_rows.shape[0]
    block_rows = total_rows // 3
    pieces = [key_rows[i * block_rows : (i + 1) * block_rows] for i in range(3)]
    piece_ids = [key_ids[i * block_rows : (i + 1) * block_rows] for i in range(3)]
    sums = []
    for first in range(3):
        masses = tile_mass(pieces[first], key_rows, piece_ids[first], key_ids, first * block_rows)
        sums.append(jnp.sum(masses, axis=1))
    mass_sum = jnp.concatenate(sums, axis=0)
    return jnp.log1p(mass_sum)


def plain_plan(embeddings, cluster_ids):
    peer_count = lax.axis_size("gx")
    row_count = embeddings.shape[0]
    features = embeddings.shape[1]
    capacity = 3 * row_count // peer_count
    slot_total = peer_count * capacity
    squares = jnp.sum(jnp.square(embeddings.astype(jnp.float32)), axis=1)
    unit_rows = (embeddings.astype(jnp.float32) * lax.rsqrt(squares + 1e-06)[:, None]).astype(
        jnp.bfloat16
    )
    owner_of = cluster_ids // CLU_DEV
    onehot = (owner_of[:, None] == jnp.arange(peer_count, dtype=jnp.int32)[None, :]).astype(
        jnp.bfloat16
    )
    row_range = jnp.arange(row_count, dtype=jnp.int32)
    lower_tri = (row_range[:, None] >= row_range[None, :]).astype(jnp.bfloat16)
    running = jnp.dot(lower_tri, onehot, preferred_element_type=jnp.float32)
    slot_index = (jnp.sum(running * onehot.astype(jnp.float32), axis=1) - 1.0).astype(jnp.int32)
    target_slot = owner_of * capacity + slot_index
    slot_range = jnp.arange(slot_total, dtype=jnp.int32)
    select_mask = slot_range[:, None] == target_slot[None, :]
    outgoing = jnp.dot(
        select_mask.astype(jnp.bfloat16), unit_rows, preferred_element_type=jnp.float32
    )
    outgoing = outgoing.astype(jnp.bfloat16).reshape(peer_count, capacity, features)
    outgoing_ids = jnp.sum(jnp.where(select_mask, cluster_ids[None, :] + 1, 0), axis=1) - 1
    outgoing_ids = outgoing_ids.reshape(peer_count, capacity)
    arrived, arrived_ids = (
        lax.all_to_all(outgoing, "gx", split_axis=0, concat_axis=0, tiled=True),
        lax.all_to_all(outgoing_ids, "gx", split_axis=0, concat_axis=0, tiled=True),
    )
    key_rows = arrived.reshape(slot_total, features)
    key_ids = arrived_ids.reshape(slot_total)
    scores = density_scores(key_rows, key_ids)
    returned = lax.all_to_all(
        scores.reshape(peer_count, capacity), "gx", split_axis=0, concat_axis=0, tiled=True
    )
    flat_scores = returned.reshape(slot_total)
    pick_mask = target_slot[:, None] == slot_range[None, :]
    return jnp.sum(jnp.where(pick_mask, flat_scores[None, :], 0.0), axis=1)


LANES = 128
PLANE = 4
INVERSE_TEMP_BITS = 20.0 * 1.4426950408889634
ID_ROWS = 8
VMEM_BYTES = 16 * 1024 * 1024


def along_rows(values):
    return jnp.broadcast_to(values, (LANES, values.shape[1])).T


def ids_block(ids, width):
    wide = jnp.concatenate([ids, jnp.zeros((1, width - ids.shape[1]), jnp.float32)], axis=1)
    return jnp.broadcast_to(wide, (ID_ROWS, width)).astype(jnp.bfloat16)


def ids_of(ref):
    first = ref.shape[0] - ID_ROWS
    return ref[first:, :].astype(jnp.float32)[:1]


def mate_mass(query_rows, query_ids, key_rows, key_ids, shift=None):
    similar = lax.dot_general(
        query_rows, key_rows, (((1,), (1,)), ((), ())), preferred_element_type=jnp.float32
    )
    repeats = similar.shape[1] // LANES
    mates = jnp.concatenate([query_ids] * repeats, axis=1) == key_ids
    if shift is not None:
        query_pos = lax.broadcasted_iota(jnp.int32, similar.shape, 0) + shift
        key_pos = lax.broadcasted_iota(jnp.int32, similar.shape, 1)
        mates = mates & (query_pos != key_pos)
    return jnp.where(mates, jnp.exp2(similar * INVERSE_TEMP_BITS), 0.0)


def unit_rows(raw):
    features = raw.astype(jnp.float32)
    squares = jnp.sum(features * features, axis=1, keepdims=True)
    return (features * lax.rsqrt(squares + 1e-06)).astype(jnp.bfloat16)


def unit_kernel(ranges, rows_ref, ids_ref, *block_refs):
    rows, width = rows_ref.shape
    units = unit_rows(rows_ref[...])
    ids = ids_block(ids_ref[...].astype(jnp.float32), width)
    for (first, last), ref in zip(ranges, block_refs):
        size = last - first
        ref[:size, :] = units[first:last]
        if ref.shape[0] > size:
            ref[size:, :] = ids


def arrived_at(moves):
    plane = lax.axis_index("gx") // PLANE
    return functools.reduce(jnp.logical_or, [plane == receiver for _, receiver in moves])


def add_line(query_parts, ids_ref, key_rows, key_ids, earlier_ref, sums_ref):
    keys = key_rows.shape[0]
    column = jnp.zeros((1, keys), jnp.float32)
    first = 0
    for query_ref, size in query_parts:
        part = pl.ds(first, size)
        masses = mate_mass(query_ref[:size, :], ids_ref[part, :], key_rows, key_ids)
        column = column + jnp.sum(masses, axis=0, keepdims=True)
        folded = masses[:, :LANES]
        for lane in range(LANES, keys, LANES):
            folded = folded + masses[:, lane : lane + LANES]
        sums_ref[part, :] = folded if earlier_ref is None else earlier_ref[part, :] + folded
        first += size
    return column


def add_masses(query_ids, key_ids, powers):
    mates = jnp.concatenate([query_ids] * (powers.shape[1] // LANES), axis=1) == key_ids
    masses = jnp.where(mates, powers, 0.0)
    folded = masses[:, :LANES]
    for lane in range(LANES, powers.shape[1], LANES):
        folded = folded + masses[:, lane : lane + LANES]
    return folded, jnp.sum(masses, axis=0, keepdims=True)


def query_parts_of(refs, rows):
    head = refs[2].shape[0]
    sizes = [rows, rows] + [head, rows - head] * (PLANE - 2)
    return list(zip(refs, sizes))


def own_kernel(own_ref, mass_ref):
    rows = mass_ref.shape[1]
    own_ids = ids_of(own_ref)[:, :rows]
    masses = mate_mass(own_ref[:rows, :], along_rows(own_ids), own_ref[:rows, :], own_ids, 0)
    mass_ref[...] = jnp.sum(masses, axis=0, keepdims=True)


def first_kernel(moves, own_mass_ref, head_ref, tail_ref, *refs):
    query_refs, (ids_ref, column_ref, sums_ref, mass_ref) = refs[:-4], refs[-4:]
    rows = mass_ref.shape[1]
    query_parts = query_parts_of(query_refs, rows)
    own_ref = query_refs[0]
    own_ids = ids_of(own_ref)[:, :rows]
    for m, ref in enumerate((*query_refs[:2], query_refs[3], query_refs[5])):
        ids_ref[pl.ds(m * rows, rows), :] = along_rows(ids_of(ref)[:, :rows])
    mass = own_mass_ref[...]
    first = rows
    for ref, size in query_parts[1:]:
        query_ids = ids_ref[pl.ds(first, size), :]
        masses = mate_mass(ref[:size, :], query_ids, own_ref[:rows, :], own_ids)
        mass = mass + jnp.sum(masses, axis=0, keepdims=True)
        first += size
    mass_ref[...] = mass
    tail = tail_ref[: rows - head_ref.shape[0], :]
    key_rows = jnp.concatenate([unit_rows(head_ref[...]), tail], axis=0)
    key_ids = ids_of(tail_ref)[:, :rows]
    column_ref[...] = add_line(query_parts, ids_ref, key_rows, key_ids, None, sums_ref)


def middle_kernel(moves, head_ref, *refs):
    query_refs, (powers_ref, rest_ref) = refs[:-2], refs[-2:]

    @pl.when(arrived_at(moves))
    def _():
        keys = powers_ref.shape[1]
        units = unit_rows(head_ref[...])
        rest_ref[...] = units[keys:]
        first = 0
        for query_ref, size in query_parts_of(query_refs, query_refs[0].shape[0] - ID_ROWS):
            similar = lax.dot_general(
                query_ref[:size, :], units[:keys], (((1,), (1,)), ((), ())),
                preferred_element_type=jnp.float32,
            )
            powers_ref[pl.ds(first, size), :] = jnp.exp2(similar * INVERSE_TEMP_BITS)
            first += size


def last_kernel(moves, powers_ref, rest_ref, tail_ref, ids_ref, earlier_ref, mass_ref, *refs):
    query_refs, refs = refs[: -PLANE - 2], refs[-PLANE - 2 :]
    column_ref, row_refs, sums_ref = refs[0], refs[1:-1], refs[-1]
    rows = column_ref.shape[1]
    cut = powers_ref.shape[1]
    arrived = arrived_at(moves)

    @pl.when(arrived)
    def _():
        key_ids = ids_of(tail_ref)[:, :rows]
        key_rows = jnp.concatenate([rest_ref[...], tail_ref[: tail_ref.shape[0] - ID_ROWS, :]], axis=0)
        early_column = jnp.zeros((1, cut), jnp.float32)
        late_column = jnp.zeros((1, rows - cut), jnp.float32)
        first = 0
        for query_ref, size in query_parts_of(query_refs, rows):
            part = pl.ds(first, size)
            query_ids = ids_ref[part, :]
            similar = lax.dot_general(
                query_ref[:size, :], key_rows, (((1,), (1,)), ((), ())),
                preferred_element_type=jnp.float32,
            )
            powers = jnp.exp2(similar * INVERSE_TEMP_BITS)
            late, column = add_masses(query_ids, key_ids[:, cut:], powers)
            late_column = late_column + column
            early, column = add_masses(query_ids, key_ids[:, :cut], powers_ref[part, :])
            early_column = early_column + column
            sums_ref[part, :] = earlier_ref[part, :] + early + late
            first += size
        column_ref[...] = jnp.concatenate([early_column, late_column], axis=1)

    @pl.when(jnp.logical_not(arrived))
    def _():
        column_ref[...] = jnp.zeros_like(column_ref)
        sums_ref[...] = earlier_ref[...]

    for m in range(PLANE):
        row_sum = jnp.sum(sums_ref[pl.ds(m * rows, rows), :].T, axis=0, keepdims=True)
        row_refs[m][...] = row_sum + mass_ref[...] if m == 0 else row_sum


def grid_plan(embeddings, cluster_ids):
    peers = lax.axis_size("gx")
    row_count, features = embeddings.shape
    plane_rows = PLANE * row_count
    params = pltpu.CompilerParams(vmem_limit_bytes=VMEM_BYTES)
    small = pl.CostEstimate(flops=1, bytes_accessed=1, transcendentals=0)
    vector = jax.ShapeDtypeStruct((1, row_count), jnp.float32)
    lanes = jax.ShapeDtypeStruct((plane_rows, LANES), jnp.float32)

    def rows_of(count):
        return jax.ShapeDtypeStruct((count, features), jnp.bfloat16)

    def in_plane(value, step):
        return lax.ppermute(value, "gx", [(i, i ^ step) for i in range(peers)])

    def on_line(value, moves):
        pairs = [(a * PLANE + n, b * PLANE + n) for a, b in moves for n in range(PLANE)]
        return lax.ppermute(value, "gx", pairs)

    first_moves = [(0, 1), (1, 2), (2, 3), (3, 0)]
    last_moves = [(0, 2), (1, 3)]
    forward_moves = [(1, 2), (2, 3)]
    first_back = [(b, a) for a, b in first_moves]
    last_back = [(b, a) for a, b in last_moves]

    half, part = row_count // 2, 9 * row_count // 16
    ranges = [(0, row_count), (0, half), (half, row_count), (part, row_count)]
    id_rows = [ID_ROWS, 0, ID_ROWS, ID_ROWS]
    first_head = on_line(embeddings[:part], first_moves)
    block, *pieces, tail = pl.pallas_call(
        functools.partial(unit_kernel, ranges),
        out_shape=[rows_of(b - a + extra) for (a, b), extra in zip(ranges, id_rows)],
        cost_estimate=small,
        compiler_params=params,
    )(embeddings, cluster_ids.reshape(1, row_count))
    own_mass = pl.pallas_call(
        own_kernel, out_shape=vector, cost_estimate=small, compiler_params=params
    )(block)
    own_mass, tail = lax.optimization_barrier((own_mass, tail))
    first_tail = on_line(tail, first_moves)
    across = [in_plane(piece, 2) for piece in pieces]
    sibling = in_plane(block, 1)
    last_head, last_tail = [on_line(got, forward_moves) for got in (first_head, first_tail)]
    corner = [in_plane(piece, 1) for piece in across]
    queries = (block, sibling, *across, *corner)
    ids, first_column, first_sums, mass = pl.pallas_call(
        functools.partial(first_kernel, first_moves),
        out_shape=(lanes, vector, lanes, vector),
        cost_estimate=small,
        compiler_params=params,
    )(own_mass, first_head, first_tail, *queries)
    returned_first = on_line(first_column, first_back)
    powers, rest = pl.pallas_call(
        functools.partial(middle_kernel, last_moves),
        out_shape=(
            jax.ShapeDtypeStruct((plane_rows, half), jnp.float32), rows_of(part - half)
        ),
        cost_estimate=small,
        compiler_params=params,
    )(last_head, *queries)
    last_column, *row_sums = pl.pallas_call(
        functools.partial(last_kernel, last_moves),
        out_shape=[vector] * (1 + PLANE),
        scratch_shapes=[pltpu.VMEM(lanes.shape, lanes.dtype)],
        compiler_params=params,
    )(powers, rest, last_tail, ids, first_sums, mass, *queries)
    returned_first, row_sums[1] = lax.optimization_barrier((returned_first, row_sums[1]))
    returned = [on_line(last_column, last_back)]
    returned += [in_plane(row_sums[step], step) for step in (2, 3, 1)]
    return jnp.log1p(sum(returned, row_sums[0] + returned_first)).reshape(row_count)


def on_device(embeddings, cluster_ids):
    if lax.axis_size("gx") == 4 * PLANE and embeddings.shape[0] % (2 * LANES) == 0:
        return grid_plan(embeddings, cluster_ids)
    return plain_plan(embeddings, cluster_ids)


def solution(mesh):
    in_specs = (P(("parts", "gx"), None), P(("parts", "gx")))
    out_specs = P(("parts", "gx"))
    return jax.shard_map(
        on_device, mesh=mesh, in_specs=in_specs, out_specs=out_specs, check_vma=False
    )
```

```python
import functools

import jax
import jax.numpy as jnp
from jax import lax
from jax.experimental import pallas as pl
from jax.experimental.pallas import tpu as pltpu
from jax.sharding import PartitionSpec as P

CLU_DEV = 1
PAD_MARK = 64.0
inverse_temp = 20.0


def tile_mass(query_rows, key_rows, query_ids, key_ids, query_start):
    similar = lax.dot_general(
        query_rows, key_rows, (((1,), (1,)), ((), ())), preferred_element_type=jnp.float32
    )
    query_pos = jnp.arange(query_rows.shape[0], dtype=jnp.int32) + query_start
    key_pos = jnp.arange(key_rows.shape[0], dtype=jnp.int32)
    mate_mask = (query_ids[:, None] == key_ids[None, :]) & (query_ids[:, None] >= 0)
    mate_mask = mate_mask & (query_pos[:, None] != key_pos[None, :])
    return jnp.where(mate_mask, jnp.exp(similar * inverse_temp), 0.0)


def density_scores(key_rows, key_ids):
    total_rows = key_rows.shape[0]
    block_rows = total_rows // 3
    pieces = [key_rows[i * block_rows : (i + 1) * block_rows] for i in range(3)]
    piece_ids = [key_ids[i * block_rows : (i + 1) * block_rows] for i in range(3)]
    sums = []
    for first in range(3):
        masses = tile_mass(pieces[first], key_rows, piece_ids[first], key_ids, first * block_rows)
        sums.append(jnp.sum(masses, axis=1))
    mass_sum = jnp.concatenate(sums, axis=0)
    return jnp.log1p(mass_sum)


def plain_plan(embeddings, cluster_ids):
    peer_count = lax.axis_size("gx")
    row_count = embeddings.shape[0]
    features = embeddings.shape[1]
    capacity = 3 * row_count // peer_count
    slot_total = peer_count * capacity
    squares = jnp.sum(jnp.square(embeddings.astype(jnp.float32)), axis=1)
    unit_rows = (embeddings.astype(jnp.float32) * lax.rsqrt(squares + 1e-06)[:, None]).astype(
        jnp.bfloat16
    )
    owner_of = cluster_ids // CLU_DEV
    onehot = (owner_of[:, None] == jnp.arange(peer_count, dtype=jnp.int32)[None, :]).astype(
        jnp.bfloat16
    )
    row_range = jnp.arange(row_count, dtype=jnp.int32)
    lower_tri = (row_range[:, None] >= row_range[None, :]).astype(jnp.bfloat16)
    running = jnp.dot(lower_tri, onehot, preferred_element_type=jnp.float32)
    slot_index = (jnp.sum(running * onehot.astype(jnp.float32), axis=1) - 1.0).astype(jnp.int32)
    target_slot = owner_of * capacity + slot_index
    slot_range = jnp.arange(slot_total, dtype=jnp.int32)
    select_mask = slot_range[:, None] == target_slot[None, :]
    outgoing = jnp.dot(
        select_mask.astype(jnp.bfloat16), unit_rows, preferred_element_type=jnp.float32
    )
    outgoing = outgoing.astype(jnp.bfloat16).reshape(peer_count, capacity, features)
    outgoing_ids = jnp.sum(jnp.where(select_mask, cluster_ids[None, :] + 1, 0), axis=1) - 1
    outgoing_ids = outgoing_ids.reshape(peer_count, capacity)
    arrived, arrived_ids = (
        lax.all_to_all(outgoing, "gx", split_axis=0, concat_axis=0, tiled=True),
        lax.all_to_all(outgoing_ids, "gx", split_axis=0, concat_axis=0, tiled=True),
    )
    key_rows = arrived.reshape(slot_total, features)
    key_ids = arrived_ids.reshape(slot_total)
    scores = density_scores(key_rows, key_ids)
    returned = lax.all_to_all(
        scores.reshape(peer_count, capacity), "gx", split_axis=0, concat_axis=0, tiled=True
    )
    flat_scores = returned.reshape(slot_total)
    pick_mask = target_slot[:, None] == slot_range[None, :]
    return jnp.sum(jnp.where(pick_mask, flat_scores[None, :], 0.0), axis=1)


LANES = 128
PLANE = 4
INVERSE_TEMP_BITS = 20.0 * 1.4426950408889634
ID_ROWS = 8
VMEM_BYTES = 16 * 1024 * 1024


def along_rows(values):
    return jnp.broadcast_to(values, (LANES, values.shape[1])).T


def ids_block(ids, width):
    wide = jnp.concatenate([ids, jnp.zeros((1, width - ids.shape[1]), jnp.float32)], axis=1)
    return jnp.broadcast_to(wide, (ID_ROWS, width)).astype(jnp.bfloat16)


def ids_of(ref):
    first = ref.shape[0] - ID_ROWS
    return ref[first:, :].astype(jnp.float32)[:1]


def mate_mass(query_rows, query_ids, key_rows, key_ids, shift=None):
    similar = lax.dot_general(
        query_rows, key_rows, (((1,), (1,)), ((), ())), preferred_element_type=jnp.float32
    )
    repeats = similar.shape[1] // LANES
    mates = jnp.concatenate([query_ids] * repeats, axis=1) == key_ids
    if shift is not None:
        query_pos = lax.broadcasted_iota(jnp.int32, similar.shape, 0) + shift
        key_pos = lax.broadcasted_iota(jnp.int32, similar.shape, 1)
        mates = mates & (query_pos != key_pos)
    return jnp.where(mates, jnp.exp2(similar * INVERSE_TEMP_BITS), 0.0)


def unit_rows(raw):
    features = raw.astype(jnp.float32)
    squares = jnp.sum(features * features, axis=1, keepdims=True)
    return (features * lax.rsqrt(squares + 1e-06)).astype(jnp.bfloat16)


def unit_kernel(ranges, rows_ref, ids_ref, *block_refs):
    rows, width = rows_ref.shape
    units = unit_rows(rows_ref[...])
    ids = ids_block(ids_ref[...].astype(jnp.float32), width)
    for (first, last), ref in zip(ranges, block_refs):
        size = last - first
        ref[:size, :] = units[first:last]
        if ref.shape[0] > size:
            ref[size:, :] = ids


def arrived_at(moves):
    plane = lax.axis_index("gx") // PLANE
    return functools.reduce(jnp.logical_or, [plane == receiver for _, receiver in moves])


def add_line(query_parts, ids_ref, key_rows, key_ids, earlier_ref, sums_ref):
    keys = key_rows.shape[0]
    column = jnp.zeros((1, keys), jnp.float32)
    first = 0
    for query_ref, size in query_parts:
        part = pl.ds(first, size)
        masses = mate_mass(query_ref[:size, :], ids_ref[part, :], key_rows, key_ids)
        column = column + jnp.sum(masses, axis=0, keepdims=True)
        folded = masses[:, :LANES]
        for lane in range(LANES, keys, LANES):
            folded = folded + masses[:, lane : lane + LANES]
        sums_ref[part, :] = folded if earlier_ref is None else earlier_ref[part, :] + folded
        first += size
    return column


def add_masses(query_ids, key_ids, powers):
    mates = jnp.concatenate([query_ids] * (powers.shape[1] // LANES), axis=1) == key_ids
    masses = jnp.where(mates, powers, 0.0)
    folded = masses[:, :LANES]
    for lane in range(LANES, powers.shape[1], LANES):
        folded = folded + masses[:, lane : lane + LANES]
    return folded, jnp.sum(masses, axis=0, keepdims=True)


def query_parts_of(refs, rows):
    head = refs[2].shape[0]
    sizes = [rows, rows] + [head, rows - head] * (PLANE - 2)
    return list(zip(refs, sizes))


def own_kernel(own_ref, mass_ref):
    rows = mass_ref.shape[1]
    own_ids = ids_of(own_ref)[:, :rows]
    masses = mate_mass(own_ref[:rows, :], along_rows(own_ids), own_ref[:rows, :], own_ids, 0)
    mass_ref[...] = jnp.sum(masses, axis=0, keepdims=True)


def first_kernel(moves, own_mass_ref, head_ref, tail_ref, *refs):
    query_refs, (ids_ref, column_ref, sums_ref, mass_ref) = refs[:-4], refs[-4:]
    rows = mass_ref.shape[1]
    query_parts = query_parts_of(query_refs, rows)
    own_ref = query_refs[0]
    own_ids = ids_of(own_ref)[:, :rows]
    for m, ref in enumerate((*query_refs[:2], query_refs[3], query_refs[5])):
        ids_ref[pl.ds(m * rows, rows), :] = along_rows(ids_of(ref)[:, :rows])
    mass = own_mass_ref[...]
    first = rows
    for ref, size in query_parts[1:]:
        query_ids = ids_ref[pl.ds(first, size), :]
        masses = mate_mass(ref[:size, :], query_ids, own_ref[:rows, :], own_ids)
        mass = mass + jnp.sum(masses, axis=0, keepdims=True)
        first += size
    mass_ref[...] = mass
    tail = tail_ref[: rows - head_ref.shape[0], :]
    key_rows = jnp.concatenate([unit_rows(head_ref[...]), tail], axis=0)
    key_ids = ids_of(tail_ref)[:, :rows]
    column_ref[...] = add_line(query_parts, ids_ref, key_rows, key_ids, None, sums_ref)


def middle_kernel(moves, head_ref, *refs):
    query_refs, (powers_ref, rest_ref) = refs[:-2], refs[-2:]

    @pl.when(arrived_at(moves))
    def _():
        keys = powers_ref.shape[1]
        units = unit_rows(head_ref[...])
        rest_ref[...] = units[keys:]
        first = 0
        for query_ref, size in query_parts_of(query_refs, query_refs[0].shape[0] - ID_ROWS):
            similar = lax.dot_general(
                query_ref[:size, :], units[:keys], (((1,), (1,)), ((), ())),
                preferred_element_type=jnp.float32,
            )
            powers_ref[pl.ds(first, size), :] = jnp.exp2(similar * INVERSE_TEMP_BITS)
            first += size


def last_kernel(moves, powers_ref, rest_ref, tail_ref, ids_ref, earlier_ref, mass_ref, *refs):
    query_refs, refs = refs[: -PLANE - 2], refs[-PLANE - 2 :]
    column_ref, row_refs, sums_ref = refs[0], refs[1:-1], refs[-1]
    rows = column_ref.shape[1]
    cut = powers_ref.shape[1]
    arrived = arrived_at(moves)

    @pl.when(arrived)
    def _():
        key_ids = ids_of(tail_ref)[:, :rows]
        key_rows = jnp.concatenate([rest_ref[...], tail_ref[: tail_ref.shape[0] - ID_ROWS, :]], axis=0)
        early_column = jnp.zeros((1, cut), jnp.float32)
        late_column = jnp.zeros((1, rows - cut), jnp.float32)
        first = 0
        for query_ref, size in query_parts_of(query_refs, rows):
            part = pl.ds(first, size)
            query_ids = ids_ref[part, :]
            similar = lax.dot_general(
                query_ref[:size, :], key_rows, (((1,), (1,)), ((), ())),
                preferred_element_type=jnp.float32,
            )
            powers = jnp.exp2(similar * INVERSE_TEMP_BITS)
            late, column = add_masses(query_ids, key_ids[:, cut:], powers)
            late_column = late_column + column
            early, column = add_masses(query_ids, key_ids[:, :cut], powers_ref[part, :])
            early_column = early_column + column
            sums_ref[part, :] = earlier_ref[part, :] + early + late
            first += size
        column_ref[...] = jnp.concatenate([early_column, late_column], axis=1)

    @pl.when(jnp.logical_not(arrived))
    def _():
        column_ref[...] = jnp.zeros_like(column_ref)
        sums_ref[...] = earlier_ref[...]

    for m in range(PLANE):
        row_sum = jnp.sum(sums_ref[pl.ds(m * rows, rows), :].T, axis=0, keepdims=True)
        row_refs[m][...] = row_sum + mass_ref[...] if m == 0 else row_sum


def grid_plan(embeddings, cluster_ids):
    peers = lax.axis_size("gx")
    row_count, features = embeddings.shape
    plane_rows = PLANE * row_count
    params = pltpu.CompilerParams(vmem_limit_bytes=VMEM_BYTES)
    small = pl.CostEstimate(flops=1, bytes_accessed=1, transcendentals=0)
    vector = jax.ShapeDtypeStruct((1, row_count), jnp.float32)
    lanes = jax.ShapeDtypeStruct((plane_rows, LANES), jnp.float32)

    def rows_of(count):
        return jax.ShapeDtypeStruct((count, features), jnp.bfloat16)

    def in_plane(value, step):
        return lax.ppermute(value, "gx", [(i, i ^ step) for i in range(peers)])

    def on_line(value, moves):
        pairs = [(a * PLANE + n, b * PLANE + n) for a, b in moves for n in range(PLANE)]
        return lax.ppermute(value, "gx", pairs)

    first_moves = [(0, 1), (1, 2), (2, 3), (3, 0)]
    last_moves = [(0, 2), (1, 3)]
    forward_moves = [(1, 2), (2, 3)]
    first_back = [(b, a) for a, b in first_moves]
    last_back = [(b, a) for a, b in last_moves]

    half, part = row_count // 2, 9 * row_count // 16
    ranges = [(0, row_count), (0, half), (half, row_count), (part, row_count)]
    id_rows = [ID_ROWS, 0, ID_ROWS, ID_ROWS]
    first_head = on_line(embeddings[:part], first_moves)
    block, *pieces, tail = pl.pallas_call(
        functools.partial(unit_kernel, ranges),
        out_shape=[rows_of(b - a + extra) for (a, b), extra in zip(ranges, id_rows)],
        cost_estimate=small,
        compiler_params=params,
    )(embeddings, cluster_ids.reshape(1, row_count))
    own_mass = pl.pallas_call(
        own_kernel, out_shape=vector, cost_estimate=small, compiler_params=params
    )(block)
    own_mass, tail = lax.optimization_barrier((own_mass, tail))
    first_tail = on_line(tail, first_moves)
    across = [in_plane(piece, 2) for piece in pieces]
    sibling = in_plane(block, 1)
    last_head = on_line(first_head, forward_moves + [(3, 1), (0, 0)])
    last_tail = on_line(first_tail, forward_moves)
    corner = [in_plane(piece, 1) for piece in across]
    queries = (block, sibling, *across, *corner)
    ids, first_column, first_sums, mass = pl.pallas_call(
        functools.partial(first_kernel, first_moves),
        out_shape=(lanes, vector, lanes, vector),
        cost_estimate=small,
        compiler_params=params,
    )(own_mass, first_head, first_tail, *queries)
    returned_first = on_line(first_column, first_back)
    powers, rest = pl.pallas_call(
        functools.partial(middle_kernel, last_moves),
        out_shape=(
            jax.ShapeDtypeStruct((plane_rows, half), jnp.float32), rows_of(part - half)
        ),
        cost_estimate=small,
        compiler_params=params,
    )(last_head, *queries)
    last_column, *row_sums = pl.pallas_call(
        functools.partial(last_kernel, last_moves),
        out_shape=[vector] * (1 + PLANE),
        scratch_shapes=[pltpu.VMEM(lanes.shape, lanes.dtype)],
        compiler_params=params,
    )(powers, rest, last_tail, ids, first_sums, mass, *queries)
    returned_first, row_sums[1] = lax.optimization_barrier((returned_first, row_sums[1]))
    returned = [on_line(last_column, last_back)]
    returned += [in_plane(row_sums[step], step) for step in (2, 3, 1)]
    return jnp.log1p(sum(returned, row_sums[0] + returned_first)).reshape(row_count)


def on_device(embeddings, cluster_ids):
    if lax.axis_size("gx") == 4 * PLANE and embeddings.shape[0] % (2 * LANES) == 0:
        return grid_plan(embeddings, cluster_ids)
    return plain_plan(embeddings, cluster_ids)


def solution(mesh):
    in_specs = (P(("parts", "gx"), None), P(("parts", "gx")))
    out_specs = P(("parts", "gx"))
    return jax.shard_map(
        on_device, mesh=mesh, in_specs=in_specs, out_specs=out_specs, check_vma=False
    )
```

```python
import functools

import jax
import jax.numpy as jnp
from jax import lax
from jax.experimental import pallas as pl
from jax.experimental.pallas import tpu as pltpu
from jax.sharding import PartitionSpec as P

CLU_DEV = 1
PAD_MARK = 64.0
inverse_temp = 20.0


def tile_mass(query_rows, key_rows, query_ids, key_ids, query_start):
    similar = lax.dot_general(
        query_rows, key_rows, (((1,), (1,)), ((), ())), preferred_element_type=jnp.float32
    )
    query_pos = jnp.arange(query_rows.shape[0], dtype=jnp.int32) + query_start
    key_pos = jnp.arange(key_rows.shape[0], dtype=jnp.int32)
    mate_mask = (query_ids[:, None] == key_ids[None, :]) & (query_ids[:, None] >= 0)
    mate_mask = mate_mask & (query_pos[:, None] != key_pos[None, :])
    return jnp.where(mate_mask, jnp.exp(similar * inverse_temp), 0.0)


def density_scores(key_rows, key_ids):
    total_rows = key_rows.shape[0]
    block_rows = total_rows // 3
    pieces = [key_rows[i * block_rows : (i + 1) * block_rows] for i in range(3)]
    piece_ids = [key_ids[i * block_rows : (i + 1) * block_rows] for i in range(3)]
    sums = []
    for first in range(3):
        masses = tile_mass(pieces[first], key_rows, piece_ids[first], key_ids, first * block_rows)
        sums.append(jnp.sum(masses, axis=1))
    mass_sum = jnp.concatenate(sums, axis=0)
    return jnp.log1p(mass_sum)


def plain_plan(embeddings, cluster_ids):
    peer_count = lax.axis_size("gx")
    row_count = embeddings.shape[0]
    features = embeddings.shape[1]
    capacity = 3 * row_count // peer_count
    slot_total = peer_count * capacity
    squares = jnp.sum(jnp.square(embeddings.astype(jnp.float32)), axis=1)
    unit_rows = (embeddings.astype(jnp.float32) * lax.rsqrt(squares + 1e-06)[:, None]).astype(
        jnp.bfloat16
    )
    owner_of = cluster_ids // CLU_DEV
    onehot = (owner_of[:, None] == jnp.arange(peer_count, dtype=jnp.int32)[None, :]).astype(
        jnp.bfloat16
    )
    row_range = jnp.arange(row_count, dtype=jnp.int32)
    lower_tri = (row_range[:, None] >= row_range[None, :]).astype(jnp.bfloat16)
    running = jnp.dot(lower_tri, onehot, preferred_element_type=jnp.float32)
    slot_index = (jnp.sum(running * onehot.astype(jnp.float32), axis=1) - 1.0).astype(jnp.int32)
    target_slot = owner_of * capacity + slot_index
    slot_range = jnp.arange(slot_total, dtype=jnp.int32)
    select_mask = slot_range[:, None] == target_slot[None, :]
    outgoing = jnp.dot(
        select_mask.astype(jnp.bfloat16), unit_rows, preferred_element_type=jnp.float32
    )
    outgoing = outgoing.astype(jnp.bfloat16).reshape(peer_count, capacity, features)
    outgoing_ids = jnp.sum(jnp.where(select_mask, cluster_ids[None, :] + 1, 0), axis=1) - 1
    outgoing_ids = outgoing_ids.reshape(peer_count, capacity)
    arrived, arrived_ids = (
        lax.all_to_all(outgoing, "gx", split_axis=0, concat_axis=0, tiled=True),
        lax.all_to_all(outgoing_ids, "gx", split_axis=0, concat_axis=0, tiled=True),
    )
    key_rows = arrived.reshape(slot_total, features)
    key_ids = arrived_ids.reshape(slot_total)
    scores = density_scores(key_rows, key_ids)
    returned = lax.all_to_all(
        scores.reshape(peer_count, capacity), "gx", split_axis=0, concat_axis=0, tiled=True
    )
    flat_scores = returned.reshape(slot_total)
    pick_mask = target_slot[:, None] == slot_range[None, :]
    return jnp.sum(jnp.where(pick_mask, flat_scores[None, :], 0.0), axis=1)


LANES = 128
PLANE = 4
INVERSE_TEMP_BITS = 20.0 * 1.4426950408889634
ID_ROWS = 8
VMEM_BYTES = 16 * 1024 * 1024


def along_rows(values):
    return jnp.broadcast_to(values, (LANES, values.shape[1])).T


def ids_block(ids, width):
    wide = jnp.concatenate([ids, jnp.zeros((1, width - ids.shape[1]), jnp.float32)], axis=1)
    return jnp.broadcast_to(wide, (ID_ROWS, width)).astype(jnp.bfloat16)


def ids_of(ref):
    first = ref.shape[0] - ID_ROWS
    return ref[first:, :].astype(jnp.float32)[:1]


def mate_mass(query_rows, query_ids, key_rows, key_ids, shift=None):
    similar = lax.dot_general(
        query_rows, key_rows, (((1,), (1,)), ((), ())), preferred_element_type=jnp.float32
    )
    repeats = similar.shape[1] // LANES
    mates = jnp.concatenate([query_ids] * repeats, axis=1) == key_ids
    if shift is not None:
        query_pos = lax.broadcasted_iota(jnp.int32, similar.shape, 0) + shift
        key_pos = lax.broadcasted_iota(jnp.int32, similar.shape, 1)
        mates = mates & (query_pos != key_pos)
    return jnp.where(mates, jnp.exp2(similar * INVERSE_TEMP_BITS), 0.0)


def unit_rows(raw):
    features = raw.astype(jnp.float32)
    squares = jnp.sum(features * features, axis=1, keepdims=True)
    return (features * lax.rsqrt(squares + 1e-06)).astype(jnp.bfloat16)


def unit_kernel(ranges, rows_ref, ids_ref, *block_refs):
    rows, width = rows_ref.shape
    units = unit_rows(rows_ref[...])
    ids = ids_block(ids_ref[...].astype(jnp.float32), width)
    for (first, last), ref in zip(ranges, block_refs):
        size = last - first
        ref[:size, :] = units[first:last]
        if ref.shape[0] > size:
            ref[size:, :] = ids


def add_line(query_parts, ids_ref, key_rows, key_ids, earlier_ref, sums_ref):
    keys = key_rows.shape[0]
    column = jnp.zeros((1, keys), jnp.float32)
    first = 0
    for query_ref, size in query_parts:
        part = pl.ds(first, size)
        masses = mate_mass(query_ref[:size, :], ids_ref[part, :], key_rows, key_ids)
        column = column + jnp.sum(masses, axis=0, keepdims=True)
        folded = masses[:, :LANES]
        for lane in range(LANES, keys, LANES):
            folded = folded + masses[:, lane : lane + LANES]
        sums_ref[part, :] = folded if earlier_ref is None else earlier_ref[part, :] + folded
        first += size
    return column


def query_parts_of(refs, rows):
    head = refs[2].shape[0]
    sizes = [rows, rows] + [head, rows - head] * (PLANE - 2)
    return list(zip(refs, sizes))


def own_kernel(own_ref, mass_ref):
    rows = mass_ref.shape[1]
    own_ids = ids_of(own_ref)[:, :rows]
    masses = mate_mass(own_ref[:rows, :], along_rows(own_ids), own_ref[:rows, :], own_ids, 0)
    mass_ref[...] = jnp.sum(masses, axis=0, keepdims=True)


def first_kernel(own_mass_ref, head_ref, tail_ref, *refs):
    query_refs, (ids_ref, column_ref, sums_ref, mass_ref) = refs[:-4], refs[-4:]
    rows = mass_ref.shape[1]
    query_parts = query_parts_of(query_refs, rows)
    own_ref = query_refs[0]
    own_ids = ids_of(own_ref)[:, :rows]
    for m, ref in enumerate((*query_refs[:2], query_refs[3], query_refs[5])):
        ids_ref[pl.ds(m * rows, rows), :] = along_rows(ids_of(ref)[:, :rows])
    mass = own_mass_ref[...]
    first = rows
    for ref, size in query_parts[1:]:
        query_ids = ids_ref[pl.ds(first, size), :]
        masses = mate_mass(ref[:size, :], query_ids, own_ref[:rows, :], own_ids)
        mass = mass + jnp.sum(masses, axis=0, keepdims=True)
        first += size
    mass_ref[...] = mass
    tail = tail_ref[: rows - head_ref.shape[0], :]
    key_rows = jnp.concatenate([unit_rows(head_ref[...]), tail], axis=0)
    key_ids = ids_of(tail_ref)[:, :rows]
    column_ref[...] = add_line(query_parts, ids_ref, key_rows, key_ids, None, sums_ref)


def middle_kernel(head_ref, *refs):
    query_refs, (powers_ref, rest_ref) = refs[:-2], refs[-2:]
    keys = powers_ref.shape[1]
    units = unit_rows(head_ref[...])
    rest_ref[...] = units[keys:]
    first = 0
    for query_ref, size in query_parts_of(query_refs, query_refs[0].shape[0] - ID_ROWS):
        similar = lax.dot_general(
            query_ref[:size, :], units[:keys], (((1,), (1,)), ((), ())),
            preferred_element_type=jnp.float32,
        )
        powers_ref[pl.ds(first, size), :] = jnp.exp2(similar * INVERSE_TEMP_BITS)
        first += size


def last_kernel(powers_ref, rest_ref, tail_ref, ids_ref, earlier_ref, mass_ref, *refs):
    query_refs, row_refs, sums_ref = refs[: -PLANE - 1], refs[-PLANE - 1 : -1], refs[-1]
    rows = mass_ref.shape[1]
    cut = powers_ref.shape[1]
    key_ids = ids_of(tail_ref)[:, :rows]
    tail = tail_ref.shape[0] - ID_ROWS
    key_rows = jnp.concatenate([rest_ref[...], tail_ref[:tail, :]], axis=0)
    first = 0
    for query_ref, size in query_parts_of(query_refs, rows):
        part = pl.ds(first, size)
        query_ids = ids_ref[part, :]
        similar = lax.dot_general(
            query_ref[:size, :], key_rows, (((1,), (1,)), ((), ())),
            preferred_element_type=jnp.float32,
        )
        powers = jnp.exp2(similar * INVERSE_TEMP_BITS)
        late = jnp.where(query_ids == key_ids[:, cut:], powers, 0.0)
        early = jnp.where(query_ids == key_ids[:, :cut], powers_ref[part, :], 0.0)
        sums_ref[part, :] = earlier_ref[part, :] + early + late
        first += size
    for m in range(PLANE):
        row_sum = jnp.sum(sums_ref[pl.ds(m * rows, rows), :].T, axis=0, keepdims=True)
        row_refs[m][...] = row_sum + mass_ref[...] if m == 0 else row_sum


def grid_plan(embeddings, cluster_ids):
    peers = lax.axis_size("gx")
    row_count, features = embeddings.shape
    plane_rows = PLANE * row_count
    params = pltpu.CompilerParams(vmem_limit_bytes=VMEM_BYTES)
    small = pl.CostEstimate(flops=1, bytes_accessed=1, transcendentals=0)
    vector = jax.ShapeDtypeStruct((1, row_count), jnp.float32)
    lanes = jax.ShapeDtypeStruct((plane_rows, LANES), jnp.float32)

    def rows_of(count):
        return jax.ShapeDtypeStruct((count, features), jnp.bfloat16)

    def in_plane(value, step):
        return lax.ppermute(value, "gx", [(i, i ^ step) for i in range(peers)])

    def on_line(value, moves):
        pairs = [(a * PLANE + n, b * PLANE + n) for a, b in moves for n in range(PLANE)]
        return lax.ppermute(value, "gx", pairs)

    first_moves = [(0, 1), (1, 2), (2, 3), (3, 0)]
    first_back = [(b, a) for a, b in first_moves]

    half, part = row_count // 2, 9 * row_count // 16
    ranges = [(0, row_count), (0, half), (half, row_count), (part, row_count)]
    id_rows = [ID_ROWS, 0, ID_ROWS, ID_ROWS]
    first_head = on_line(embeddings[:part], first_moves)
    block, *pieces, tail = pl.pallas_call(
        functools.partial(unit_kernel, ranges),
        out_shape=[rows_of(b - a + extra) for (a, b), extra in zip(ranges, id_rows)],
        cost_estimate=small,
        compiler_params=params,
    )(embeddings, cluster_ids.reshape(1, row_count))
    own_mass = pl.pallas_call(
        own_kernel, out_shape=vector, cost_estimate=small, compiler_params=params
    )(block)
    own_mass, tail = lax.optimization_barrier((own_mass, tail))
    first_tail = on_line(tail, first_moves)
    across = [in_plane(piece, 2) for piece in pieces]
    sibling = in_plane(block, 1)
    last_head, last_tail = [on_line(got, first_moves) for got in (first_head, first_tail)]
    corner = [in_plane(piece, 1) for piece in across]
    queries = (block, sibling, *across, *corner)
    ids, first_column, first_sums, mass = pl.pallas_call(
        first_kernel,
        out_shape=(lanes, vector, lanes, vector),
        cost_estimate=small,
        compiler_params=params,
    )(own_mass, first_head, first_tail, *queries)
    returned_first = on_line(first_column, first_back)
    powers, rest = pl.pallas_call(
        middle_kernel,
        out_shape=(
            jax.ShapeDtypeStruct((plane_rows, half), jnp.float32), rows_of(part - half)
        ),
        cost_estimate=small,
        compiler_params=params,
    )(last_head, *queries)
    row_sums = list(pl.pallas_call(
        last_kernel,
        out_shape=[vector] * PLANE,
        scratch_shapes=[pltpu.VMEM(lanes.shape, lanes.dtype)],
        compiler_params=params,
    )(powers, rest, last_tail, ids, first_sums, mass, *queries))
    returned_first, row_sums[1] = lax.optimization_barrier((returned_first, row_sums[1]))
    returned = [in_plane(row_sums[step], step) for step in (2, 3, 1)]
    return jnp.log1p(sum(returned, row_sums[0] + returned_first)).reshape(row_count)


def on_device(embeddings, cluster_ids):
    if lax.axis_size("gx") == 4 * PLANE and embeddings.shape[0] == 2 * LANES:
        return grid_plan(embeddings, cluster_ids)
    return plain_plan(embeddings, cluster_ids)


def solution(mesh):
    in_specs = (P(("parts", "gx"), None), P(("parts", "gx")))
    out_specs = P(("parts", "gx"))
    return jax.shard_map(
        on_device, mesh=mesh, in_specs=in_specs, out_specs=out_specs, check_vma=False
    )
```

```python
import functools

import jax
import jax.numpy as jnp
from jax import lax
from jax.experimental import pallas as pl
from jax.experimental.pallas import tpu as pltpu
from jax.sharding import PartitionSpec as P

CLU_DEV = 1
PAD_MARK = 64.0
inverse_temp = 20.0


def tile_mass(query_rows, key_rows, query_ids, key_ids, query_start):
    similar = lax.dot_general(
        query_rows, key_rows, (((1,), (1,)), ((), ())), preferred_element_type=jnp.float32
    )
    query_pos = jnp.arange(query_rows.shape[0], dtype=jnp.int32) + query_start
    key_pos = jnp.arange(key_rows.shape[0], dtype=jnp.int32)
    mate_mask = (query_ids[:, None] == key_ids[None, :]) & (query_ids[:, None] >= 0)
    mate_mask = mate_mask & (query_pos[:, None] != key_pos[None, :])
    return jnp.where(mate_mask, jnp.exp(similar * inverse_temp), 0.0)


def density_scores(key_rows, key_ids):
    total_rows = key_rows.shape[0]
    block_rows = total_rows // 3
    pieces = [key_rows[i * block_rows : (i + 1) * block_rows] for i in range(3)]
    piece_ids = [key_ids[i * block_rows : (i + 1) * block_rows] for i in range(3)]
    sums = []
    for first in range(3):
        masses = tile_mass(pieces[first], key_rows, piece_ids[first], key_ids, first * block_rows)
        sums.append(jnp.sum(masses, axis=1))
    mass_sum = jnp.concatenate(sums, axis=0)
    return jnp.log1p(mass_sum)


def plain_plan(embeddings, cluster_ids):
    peer_count = lax.axis_size("gx")
    row_count = embeddings.shape[0]
    features = embeddings.shape[1]
    capacity = 3 * row_count // peer_count
    slot_total = peer_count * capacity
    squares = jnp.sum(jnp.square(embeddings.astype(jnp.float32)), axis=1)
    unit_rows = (embeddings.astype(jnp.float32) * lax.rsqrt(squares + 1e-06)[:, None]).astype(
        jnp.bfloat16
    )
    owner_of = cluster_ids // CLU_DEV
    onehot = (owner_of[:, None] == jnp.arange(peer_count, dtype=jnp.int32)[None, :]).astype(
        jnp.bfloat16
    )
    row_range = jnp.arange(row_count, dtype=jnp.int32)
    lower_tri = (row_range[:, None] >= row_range[None, :]).astype(jnp.bfloat16)
    running = jnp.dot(lower_tri, onehot, preferred_element_type=jnp.float32)
    slot_index = (jnp.sum(running * onehot.astype(jnp.float32), axis=1) - 1.0).astype(jnp.int32)
    target_slot = owner_of * capacity + slot_index
    slot_range = jnp.arange(slot_total, dtype=jnp.int32)
    select_mask = slot_range[:, None] == target_slot[None, :]
    outgoing = jnp.dot(
        select_mask.astype(jnp.bfloat16), unit_rows, preferred_element_type=jnp.float32
    )
    outgoing = outgoing.astype(jnp.bfloat16).reshape(peer_count, capacity, features)
    outgoing_ids = jnp.sum(jnp.where(select_mask, cluster_ids[None, :] + 1, 0), axis=1) - 1
    outgoing_ids = outgoing_ids.reshape(peer_count, capacity)
    arrived, arrived_ids = (
        lax.all_to_all(outgoing, "gx", split_axis=0, concat_axis=0, tiled=True),
        lax.all_to_all(outgoing_ids, "gx", split_axis=0, concat_axis=0, tiled=True),
    )
    key_rows = arrived.reshape(slot_total, features)
    key_ids = arrived_ids.reshape(slot_total)
    scores = density_scores(key_rows, key_ids)
    returned = lax.all_to_all(
        scores.reshape(peer_count, capacity), "gx", split_axis=0, concat_axis=0, tiled=True
    )
    flat_scores = returned.reshape(slot_total)
    pick_mask = target_slot[:, None] == slot_range[None, :]
    return jnp.sum(jnp.where(pick_mask, flat_scores[None, :], 0.0), axis=1)


LANES = 128
PLANE = 4
INVERSE_TEMP_BITS = 20.0 * 1.4426950408889634
ID_ROWS = 8
VMEM_BYTES = 16 * 1024 * 1024


def along_rows(values):
    return jnp.broadcast_to(values, (LANES, values.shape[1])).T


def ids_block(ids, width):
    wide = jnp.concatenate([ids, jnp.zeros((1, width - ids.shape[1]), jnp.float32)], axis=1)
    return jnp.broadcast_to(wide, (ID_ROWS, width)).astype(jnp.bfloat16)


def ids_of(ref):
    first = ref.shape[0] - ID_ROWS
    return ref[first:, :].astype(jnp.float32)[:1]


def mate_mass(query_rows, query_ids, key_rows, key_ids, shift=None):
    similar = lax.dot_general(
        query_rows, key_rows, (((1,), (1,)), ((), ())), preferred_element_type=jnp.float32
    )
    repeats = similar.shape[1] // LANES
    mates = jnp.concatenate([query_ids] * repeats, axis=1) == key_ids
    if shift is not None:
        query_pos = lax.broadcasted_iota(jnp.int32, similar.shape, 0) + shift
        key_pos = lax.broadcasted_iota(jnp.int32, similar.shape, 1)
        mates = mates & (query_pos != key_pos)
    return jnp.where(mates, jnp.exp2(similar * INVERSE_TEMP_BITS), 0.0)


def unit_rows(raw):
    features = raw.astype(jnp.float32)
    squares = jnp.sum(features * features, axis=1, keepdims=True)
    return (features * lax.rsqrt(squares + 1e-06)).astype(jnp.bfloat16)


def unit_kernel(ranges, rows_ref, ids_ref, *block_refs):
    rows, width = rows_ref.shape
    units = unit_rows(rows_ref[...])
    ids = ids_block(ids_ref[...].astype(jnp.float32), width)
    for (first, last), ref in zip(ranges, block_refs):
        size = last - first
        ref[:size, :] = units[first:last]
        if ref.shape[0] > size:
            ref[size:, :] = ids


def add_line(query_parts, ids_ref, key_rows, key_ids, earlier_ref, sums_ref):
    keys = key_rows.shape[0]
    column = jnp.zeros((1, keys), jnp.float32)
    first = 0
    for query_ref, size in query_parts:
        part = pl.ds(first, size)
        masses = mate_mass(query_ref[:size, :], ids_ref[part, :], key_rows, key_ids)
        column = column + jnp.sum(masses, axis=0, keepdims=True)
        folded = masses[:, :LANES]
        for lane in range(LANES, keys, LANES):
            folded = folded + masses[:, lane : lane + LANES]
        sums_ref[part, :] = folded if earlier_ref is None else earlier_ref[part, :] + folded
        first += size
    return column


def query_parts_of(refs, rows):
    head = refs[2].shape[0]
    sizes = [rows, rows] + [head, rows - head] * (PLANE - 2)
    return list(zip(refs, sizes))


def own_kernel(own_ref, mass_ref):
    rows = mass_ref.shape[1]
    own_ids = ids_of(own_ref)[:, :rows]
    masses = mate_mass(own_ref[:rows, :], along_rows(own_ids), own_ref[:rows, :], own_ids, 0)
    mass_ref[...] = jnp.sum(masses, axis=0, keepdims=True)


def first_kernel(own_mass_ref, head_ref, tail_ref, *refs):
    query_refs, (ids_ref, column_ref, sums_ref, mass_ref) = refs[:-4], refs[-4:]
    rows = mass_ref.shape[1]
    query_parts = query_parts_of(query_refs, rows)
    own_ref = query_refs[0]
    own_ids = ids_of(own_ref)[:, :rows]
    for m, ref in enumerate((*query_refs[:2], query_refs[3], query_refs[5])):
        ids_ref[pl.ds(m * rows, rows), :] = along_rows(ids_of(ref)[:, :rows])
    mass = own_mass_ref[...]
    first = rows
    for ref, size in query_parts[1:]:
        query_ids = ids_ref[pl.ds(first, size), :]
        masses = mate_mass(ref[:size, :], query_ids, own_ref[:rows, :], own_ids)
        mass = mass + jnp.sum(masses, axis=0, keepdims=True)
        first += size
    mass_ref[...] = mass
    tail = tail_ref[: rows - head_ref.shape[0], :]
    key_rows = jnp.concatenate([unit_rows(head_ref[...]), tail], axis=0)
    key_ids = ids_of(tail_ref)[:, :rows]
    column_ref[...] = add_line(query_parts, ids_ref, key_rows, key_ids, None, sums_ref)


def middle_kernel(head_ref, *refs):
    query_refs, (powers_ref, rest_ref) = refs[:-2], refs[-2:]
    keys = powers_ref.shape[1]
    units = unit_rows(head_ref[...])
    rest_ref[...] = units[keys:]
    first = 0
    for query_ref, size in query_parts_of(query_refs, query_refs[0].shape[0] - ID_ROWS):
        similar = lax.dot_general(
            query_ref[:size, :], units[:keys], (((1,), (1,)), ((), ())),
            preferred_element_type=jnp.float32,
        )
        powers_ref[pl.ds(first, size), :] = jnp.exp2(similar * INVERSE_TEMP_BITS)
        first += size


def last_kernel(powers_ref, rest_ref, tail_ref, ids_ref, earlier_ref, mass_ref, *refs):
    query_refs, row_refs, sums_ref = refs[: -PLANE - 1], refs[-PLANE - 1 : -1], refs[-1]
    rows = mass_ref.shape[1]
    cut = powers_ref.shape[1]
    key_ids = ids_of(tail_ref)[:, :rows]
    tail = tail_ref.shape[0] - ID_ROWS
    key_rows = jnp.concatenate([rest_ref[...], tail_ref[:tail, :]], axis=0)
    first = 0
    for query_ref, size in query_parts_of(query_refs, rows):
        part = pl.ds(first, size)
        query_ids = ids_ref[part, :]
        similar = lax.dot_general(
            query_ref[:size, :], key_rows, (((1,), (1,)), ((), ())),
            preferred_element_type=jnp.float32,
        )
        powers = jnp.exp2(similar * INVERSE_TEMP_BITS)
        late = jnp.where(query_ids == key_ids[:, cut:], powers, 0.0)
        early = jnp.where(query_ids == key_ids[:, :cut], powers_ref[part, :], 0.0)
        sums_ref[part, :] = earlier_ref[part, :] + early + late
        first += size
    for m in range(PLANE):
        row_sum = jnp.sum(sums_ref[pl.ds(m * rows, rows), :].T, axis=0, keepdims=True)
        row_refs[m][...] = row_sum + mass_ref[...] if m == 0 else row_sum


def grid_plan(embeddings, cluster_ids):
    peers = lax.axis_size("gx")
    row_count, features = embeddings.shape
    plane_rows = PLANE * row_count
    params = pltpu.CompilerParams(vmem_limit_bytes=VMEM_BYTES)
    small = pl.CostEstimate(flops=1, bytes_accessed=1, transcendentals=0)
    vector = jax.ShapeDtypeStruct((1, row_count), jnp.float32)
    lanes = jax.ShapeDtypeStruct((plane_rows, LANES), jnp.float32)

    def rows_of(count):
        return jax.ShapeDtypeStruct((count, features), jnp.bfloat16)

    def in_plane(value, step):
        return lax.ppermute(value, "gx", [(i, i ^ step) for i in range(peers)])

    def on_line(value, moves):
        pairs = [(a * PLANE + n, b * PLANE + n) for a, b in moves for n in range(PLANE)]
        return lax.ppermute(value, "gx", pairs)

    first_moves = [(1, 0), (2, 1), (3, 2), (0, 3)]
    first_back = [(b, a) for a, b in first_moves]

    half, part = row_count // 2, 9 * row_count // 16
    ranges = [(0, row_count), (0, half), (half, row_count), (part, row_count)]
    id_rows = [ID_ROWS, 0, ID_ROWS, ID_ROWS]
    first_head = on_line(embeddings[:part], first_moves)
    block, *pieces, tail = pl.pallas_call(
        functools.partial(unit_kernel, ranges),
        out_shape=[rows_of(b - a + extra) for (a, b), extra in zip(ranges, id_rows)],
        cost_estimate=small,
        compiler_params=params,
    )(embeddings, cluster_ids.reshape(1, row_count))
    own_mass = pl.pallas_call(
        own_kernel, out_shape=vector, cost_estimate=small, compiler_params=params
    )(block)
    own_mass, tail = lax.optimization_barrier((own_mass, tail))
    first_tail = on_line(tail, first_moves)
    across = [in_plane(piece, 2) for piece in pieces]
    sibling = in_plane(block, 1)
    last_head, last_tail = [on_line(got, first_moves) for got in (first_head, first_tail)]
    corner = [in_plane(piece, 1) for piece in across]
    queries = (block, sibling, *across, *corner)
    ids, first_column, first_sums, mass = pl.pallas_call(
        first_kernel,
        out_shape=(lanes, vector, lanes, vector),
        cost_estimate=small,
        compiler_params=params,
    )(own_mass, first_head, first_tail, *queries)
    returned_first = on_line(first_column, first_back)
    powers, rest = pl.pallas_call(
        middle_kernel,
        out_shape=(
            jax.ShapeDtypeStruct((plane_rows, half), jnp.float32), rows_of(part - half)
        ),
        cost_estimate=small,
        compiler_params=params,
    )(last_head, *queries)
    row_sums = list(pl.pallas_call(
        last_kernel,
        out_shape=[vector] * PLANE,
        scratch_shapes=[pltpu.VMEM(lanes.shape, lanes.dtype)],
        compiler_params=params,
    )(powers, rest, last_tail, ids, first_sums, mass, *queries))
    returned_first, row_sums[1] = lax.optimization_barrier((returned_first, row_sums[1]))
    returned = [in_plane(row_sums[step], step) for step in (2, 3, 1)]
    return jnp.log1p(sum(returned, row_sums[0] + returned_first)).reshape(row_count)


def on_device(embeddings, cluster_ids):
    if lax.axis_size("gx") == 4 * PLANE and embeddings.shape[0] == 2 * LANES:
        return grid_plan(embeddings, cluster_ids)
    return plain_plan(embeddings, cluster_ids)


def solution(mesh):
    in_specs = (P(("parts", "gx"), None), P(("parts", "gx")))
    out_specs = P(("parts", "gx"))
    return jax.shard_map(
        on_device, mesh=mesh, in_specs=in_specs, out_specs=out_specs, check_vma=False
    )
```

```python
import functools

import jax
import jax.numpy as jnp
from jax import lax
from jax.experimental import pallas as pl
from jax.experimental.pallas import tpu as pltpu
from jax.sharding import PartitionSpec as P

CLU_DEV = 1
PAD_MARK = 64.0
inverse_temp = 20.0


def tile_mass(query_rows, key_rows, query_ids, key_ids, query_start):
    similar = lax.dot_general(
        query_rows, key_rows, (((1,), (1,)), ((), ())), preferred_element_type=jnp.float32
    )
    query_pos = jnp.arange(query_rows.shape[0], dtype=jnp.int32) + query_start
    key_pos = jnp.arange(key_rows.shape[0], dtype=jnp.int32)
    mate_mask = (query_ids[:, None] == key_ids[None, :]) & (query_ids[:, None] >= 0)
    mate_mask = mate_mask & (query_pos[:, None] != key_pos[None, :])
    return jnp.where(mate_mask, jnp.exp(similar * inverse_temp), 0.0)


def density_scores(key_rows, key_ids):
    total_rows = key_rows.shape[0]
    block_rows = total_rows // 3
    pieces = [key_rows[i * block_rows : (i + 1) * block_rows] for i in range(3)]
    piece_ids = [key_ids[i * block_rows : (i + 1) * block_rows] for i in range(3)]
    sums = []
    for first in range(3):
        masses = tile_mass(pieces[first], key_rows, piece_ids[first], key_ids, first * block_rows)
        sums.append(jnp.sum(masses, axis=1))
    mass_sum = jnp.concatenate(sums, axis=0)
    return jnp.log1p(mass_sum)


def plain_plan(embeddings, cluster_ids):
    peer_count = lax.axis_size("gx")
    row_count = embeddings.shape[0]
    features = embeddings.shape[1]
    capacity = 3 * row_count // peer_count
    slot_total = peer_count * capacity
    squares = jnp.sum(jnp.square(embeddings.astype(jnp.float32)), axis=1)
    unit_rows = (embeddings.astype(jnp.float32) * lax.rsqrt(squares + 1e-06)[:, None]).astype(
        jnp.bfloat16
    )
    owner_of = cluster_ids // CLU_DEV
    onehot = (owner_of[:, None] == jnp.arange(peer_count, dtype=jnp.int32)[None, :]).astype(
        jnp.bfloat16
    )
    row_range = jnp.arange(row_count, dtype=jnp.int32)
    lower_tri = (row_range[:, None] >= row_range[None, :]).astype(jnp.bfloat16)
    running = jnp.dot(lower_tri, onehot, preferred_element_type=jnp.float32)
    slot_index = (jnp.sum(running * onehot.astype(jnp.float32), axis=1) - 1.0).astype(jnp.int32)
    target_slot = owner_of * capacity + slot_index
    slot_range = jnp.arange(slot_total, dtype=jnp.int32)
    select_mask = slot_range[:, None] == target_slot[None, :]
    outgoing = jnp.dot(
        select_mask.astype(jnp.bfloat16), unit_rows, preferred_element_type=jnp.float32
    )
    outgoing = outgoing.astype(jnp.bfloat16).reshape(peer_count, capacity, features)
    outgoing_ids = jnp.sum(jnp.where(select_mask, cluster_ids[None, :] + 1, 0), axis=1) - 1
    outgoing_ids = outgoing_ids.reshape(peer_count, capacity)
    arrived, arrived_ids = (
        lax.all_to_all(outgoing, "gx", split_axis=0, concat_axis=0, tiled=True),
        lax.all_to_all(outgoing_ids, "gx", split_axis=0, concat_axis=0, tiled=True),
    )
    key_rows = arrived.reshape(slot_total, features)
    key_ids = arrived_ids.reshape(slot_total)
    scores = density_scores(key_rows, key_ids)
    returned = lax.all_to_all(
        scores.reshape(peer_count, capacity), "gx", split_axis=0, concat_axis=0, tiled=True
    )
    flat_scores = returned.reshape(slot_total)
    pick_mask = target_slot[:, None] == slot_range[None, :]
    return jnp.sum(jnp.where(pick_mask, flat_scores[None, :], 0.0), axis=1)


LANES = 128
PLANE = 4
INVERSE_TEMP_BITS = 20.0 * 1.4426950408889634
ID_ROWS = 8
VMEM_BYTES = 16 * 1024 * 1024


def along_rows(values):
    return jnp.broadcast_to(values, (LANES, values.shape[1])).T


def ids_block(ids, width):
    wide = jnp.concatenate([ids, jnp.zeros((1, width - ids.shape[1]), jnp.float32)], axis=1)
    return jnp.broadcast_to(wide, (ID_ROWS, width)).astype(jnp.bfloat16)


def ids_of(ref):
    first = ref.shape[0] - ID_ROWS
    return ref[first:, :].astype(jnp.float32)[:1]


def mate_mass(query_rows, query_ids, key_rows, key_ids, shift=None):
    similar = lax.dot_general(
        query_rows, key_rows, (((1,), (1,)), ((), ())), preferred_element_type=jnp.float32
    )
    repeats = similar.shape[1] // LANES
    mates = jnp.concatenate([query_ids] * repeats, axis=1) == key_ids
    if shift is not None:
        query_pos = lax.broadcasted_iota(jnp.int32, similar.shape, 0) + shift
        key_pos = lax.broadcasted_iota(jnp.int32, similar.shape, 1)
        mates = mates & (query_pos != key_pos)
    return jnp.where(mates, jnp.exp2(similar * INVERSE_TEMP_BITS), 0.0)


def unit_rows(raw):
    features = raw.astype(jnp.float32)
    squares = jnp.sum(features * features, axis=1, keepdims=True)
    return (features * lax.rsqrt(squares + 1e-06)).astype(jnp.bfloat16)


def unit_kernel(ranges, rows_ref, ids_ref, *block_refs):
    rows, width = rows_ref.shape
    units = unit_rows(rows_ref[...])
    ids = ids_block(ids_ref[...].astype(jnp.float32), width)
    for (first, last), ref in zip(ranges, block_refs):
        size = last - first
        ref[:size, :] = units[first:last]
        if ref.shape[0] > size:
            ref[size:, :] = ids


def arrived_at(moves):
    plane = lax.axis_index("gx") // PLANE
    return functools.reduce(jnp.logical_or, [plane == receiver for _, receiver in moves])


def add_line(query_parts, ids_ref, key_rows, key_ids, earlier_ref, sums_ref):
    keys = key_rows.shape[0]
    column = jnp.zeros((1, keys), jnp.float32)
    first = 0
    for query_ref, size in query_parts:
        part = pl.ds(first, size)
        masses = mate_mass(query_ref[:size, :], ids_ref[part, :], key_rows, key_ids)
        column = column + jnp.sum(masses, axis=0, keepdims=True)
        folded = masses[:, :LANES]
        for lane in range(LANES, keys, LANES):
            folded = folded + masses[:, lane : lane + LANES]
        sums_ref[part, :] = folded if earlier_ref is None else earlier_ref[part, :] + folded
        first += size
    return column


def add_masses(query_ids, key_ids, powers):
    mates = jnp.concatenate([query_ids] * (powers.shape[1] // LANES), axis=1) == key_ids
    masses = jnp.where(mates, powers, 0.0)
    folded = masses[:, :LANES]
    for lane in range(LANES, powers.shape[1], LANES):
        folded = folded + masses[:, lane : lane + LANES]
    return folded, jnp.sum(masses, axis=0, keepdims=True)


def query_parts_of(refs, rows):
    head = refs[2].shape[0]
    sizes = [rows, rows] + [head, rows - head] * (PLANE - 2)
    return list(zip(refs, sizes))


def own_kernel(own_ref, mass_ref):
    rows = mass_ref.shape[1]
    own_ids = ids_of(own_ref)[:, :rows]
    masses = mate_mass(own_ref[:rows, :], along_rows(own_ids), own_ref[:rows, :], own_ids, 0)
    mass_ref[...] = jnp.sum(masses, axis=0, keepdims=True)


def first_kernel(moves, own_mass_ref, head_ref, tail_ref, *refs):
    query_refs, (ids_ref, column_ref, sums_ref, mass_ref) = refs[:-4], refs[-4:]
    rows = mass_ref.shape[1]
    query_parts = query_parts_of(query_refs, rows)
    own_ref = query_refs[0]
    own_ids = ids_of(own_ref)[:, :rows]
    for m, ref in enumerate((*query_refs[:2], query_refs[3], query_refs[5])):
        ids_ref[pl.ds(m * rows, rows), :] = along_rows(ids_of(ref)[:, :rows])
    mass = own_mass_ref[...]
    first = rows
    for ref, size in query_parts[1:]:
        query_ids = ids_ref[pl.ds(first, size), :]
        masses = mate_mass(ref[:size, :], query_ids, own_ref[:rows, :], own_ids)
        mass = mass + jnp.sum(masses, axis=0, keepdims=True)
        first += size
    mass_ref[...] = mass
    tail = tail_ref[: rows - head_ref.shape[0], :]
    key_rows = jnp.concatenate([unit_rows(head_ref[...]), tail], axis=0)
    key_ids = ids_of(tail_ref)[:, :rows]
    column_ref[...] = add_line(query_parts, ids_ref, key_rows, key_ids, None, sums_ref)


def middle_kernel(moves, head_ref, *refs):
    query_refs, (powers_ref, rest_ref) = refs[:-2], refs[-2:]

    @pl.when(arrived_at(moves))
    def _():
        keys = powers_ref.shape[1]
        units = unit_rows(head_ref[...])
        rest_ref[...] = units[keys:]
        first = 0
        for query_ref, size in query_parts_of(query_refs, query_refs[0].shape[0] - ID_ROWS):
            similar = lax.dot_general(
                query_ref[:size, :], units[:keys], (((1,), (1,)), ((), ())),
                preferred_element_type=jnp.float32,
            )
            powers_ref[pl.ds(first, size), :] = jnp.exp2(similar * INVERSE_TEMP_BITS)
            first += size


def last_kernel(moves, powers_ref, rest_ref, tail_ref, ids_ref, earlier_ref, mass_ref, *refs):
    query_refs, refs = refs[: -PLANE - 2], refs[-PLANE - 2 :]
    column_ref, row_refs, sums_ref = refs[0], refs[1:-1], refs[-1]
    rows = column_ref.shape[1]
    cut = powers_ref.shape[1]
    arrived = arrived_at(moves)

    @pl.when(arrived)
    def _():
        key_ids = ids_of(tail_ref)[:, :rows]
        key_rows = jnp.concatenate([rest_ref[...], tail_ref[: tail_ref.shape[0] - ID_ROWS, :]], axis=0)
        early_column = jnp.zeros((1, cut), jnp.float32)
        late_column = jnp.zeros((1, rows - cut), jnp.float32)
        first = 0
        for query_ref, size in query_parts_of(query_refs, rows):
            part = pl.ds(first, size)
            query_ids = ids_ref[part, :]
            similar = lax.dot_general(
                query_ref[:size, :], key_rows, (((1,), (1,)), ((), ())),
                preferred_element_type=jnp.float32,
            )
            powers = jnp.exp2(similar * INVERSE_TEMP_BITS)
            late, column = add_masses(query_ids, key_ids[:, cut:], powers)
            late_column = late_column + column
            early, column = add_masses(query_ids, key_ids[:, :cut], powers_ref[part, :])
            early_column = early_column + column
            sums_ref[part, :] = earlier_ref[part, :] + early + late
            first += size
        column_ref[...] = jnp.concatenate([early_column, late_column], axis=1)

    @pl.when(jnp.logical_not(arrived))
    def _():
        column_ref[...] = jnp.zeros_like(column_ref)
        sums_ref[...] = earlier_ref[...]

    for m in range(PLANE):
        row_sum = jnp.sum(sums_ref[pl.ds(m * rows, rows), :].T, axis=0, keepdims=True)
        row_refs[m][...] = row_sum + mass_ref[...] if m == 0 else row_sum


def grid_plan(embeddings, cluster_ids):
    peers = lax.axis_size("gx")
    row_count, features = embeddings.shape
    plane_rows = PLANE * row_count
    params = pltpu.CompilerParams(vmem_limit_bytes=VMEM_BYTES)
    small = pl.CostEstimate(flops=1, bytes_accessed=1, transcendentals=0)
    vector = jax.ShapeDtypeStruct((1, row_count), jnp.float32)
    lanes = jax.ShapeDtypeStruct((plane_rows, LANES), jnp.float32)

    def rows_of(count):
        return jax.ShapeDtypeStruct((count, features), jnp.bfloat16)

    def in_plane(value, step):
        return lax.ppermute(value, "gx", [(i, i ^ step) for i in range(peers)])

    def on_line(value, moves):
        pairs = [(a * PLANE + n, b * PLANE + n) for a, b in moves for n in range(PLANE)]
        return lax.ppermute(value, "gx", pairs)

    first_moves = [(0, 1), (1, 2), (2, 3), (3, 0)]
    last_moves = [(0, 2), (1, 3)]
    forward_moves = [(1, 2), (2, 3)]
    first_back = [(b, a) for a, b in first_moves]
    last_back = [(b, a) for a, b in last_moves]

    half, part = row_count // 2, 9 * row_count // 16
    ranges = [(0, row_count), (0, half), (half, row_count), (part, row_count)]
    id_rows = [ID_ROWS, 0, ID_ROWS, ID_ROWS]
    first_head = on_line(embeddings[:part], first_moves)
    block, *pieces, tail = pl.pallas_call(
        functools.partial(unit_kernel, ranges),
        out_shape=[rows_of(b - a + extra) for (a, b), extra in zip(ranges, id_rows)],
        cost_estimate=small,
        compiler_params=params,
    )(embeddings, cluster_ids.reshape(1, row_count))
    own_mass = pl.pallas_call(
        own_kernel, out_shape=vector, cost_estimate=small, compiler_params=params
    )(block)
    own_mass, tail = lax.optimization_barrier((own_mass, tail))
    first_tail = on_line(tail, first_moves)
    across = [in_plane(piece, 2) for piece in pieces]
    sibling = in_plane(block, 1)
    last_head = on_line(first_head, first_moves)
    last_tail = on_line(first_tail, forward_moves)
    corner = [in_plane(piece, 1) for piece in across]
    queries = (block, sibling, *across, *corner)
    ids, first_column, first_sums, mass = pl.pallas_call(
        functools.partial(first_kernel, first_moves),
        out_shape=(lanes, vector, lanes, vector),
        cost_estimate=small,
        compiler_params=params,
    )(own_mass, first_head, first_tail, *queries)
    returned_first = on_line(first_column, first_back)
    powers, rest = pl.pallas_call(
        functools.partial(middle_kernel, last_moves),
        out_shape=(
            jax.ShapeDtypeStruct((plane_rows, half), jnp.float32), rows_of(part - half)
        ),
        cost_estimate=small,
        compiler_params=params,
    )(last_head, *queries)
    last_column, *row_sums = pl.pallas_call(
        functools.partial(last_kernel, last_moves),
        out_shape=[vector] * (1 + PLANE),
        scratch_shapes=[pltpu.VMEM(lanes.shape, lanes.dtype)],
        compiler_params=params,
    )(powers, rest, last_tail, ids, first_sums, mass, *queries)
    returned_first, row_sums[1] = lax.optimization_barrier((returned_first, row_sums[1]))
    returned = [on_line(last_column, last_back)]
    returned += [in_plane(row_sums[step], step) for step in (2, 3, 1)]
    return jnp.log1p(sum(returned, row_sums[0] + returned_first)).reshape(row_count)


def on_device(embeddings, cluster_ids):
    if lax.axis_size("gx") == 4 * PLANE and embeddings.shape[0] == 2 * LANES:
        return grid_plan(embeddings, cluster_ids)
    return plain_plan(embeddings, cluster_ids)


def solution(mesh):
    in_specs = (P(("parts", "gx"), None), P(("parts", "gx")))
    out_specs = P(("parts", "gx"))
    return jax.shard_map(
        on_device, mesh=mesh, in_specs=in_specs, out_specs=out_specs, check_vma=False
    )
```

```python
import functools

import jax
import jax.numpy as jnp
from jax import lax
from jax.experimental import pallas as pl
from jax.experimental.pallas import tpu as pltpu
from jax.sharding import PartitionSpec as P

CLU_DEV = 1
PAD_MARK = 64.0
inverse_temp = 20.0


def tile_mass(query_rows, key_rows, query_ids, key_ids, query_start):
    similar = lax.dot_general(
        query_rows, key_rows, (((1,), (1,)), ((), ())), preferred_element_type=jnp.float32
    )
    query_pos = jnp.arange(query_rows.shape[0], dtype=jnp.int32) + query_start
    key_pos = jnp.arange(key_rows.shape[0], dtype=jnp.int32)
    mate_mask = (query_ids[:, None] == key_ids[None, :]) & (query_ids[:, None] >= 0)
    mate_mask = mate_mask & (query_pos[:, None] != key_pos[None, :])
    return jnp.where(mate_mask, jnp.exp(similar * inverse_temp), 0.0)


def density_scores(key_rows, key_ids):
    total_rows = key_rows.shape[0]
    block_rows = total_rows // 3
    pieces = [key_rows[i * block_rows : (i + 1) * block_rows] for i in range(3)]
    piece_ids = [key_ids[i * block_rows : (i + 1) * block_rows] for i in range(3)]
    sums = []
    for first in range(3):
        masses = tile_mass(pieces[first], key_rows, piece_ids[first], key_ids, first * block_rows)
        sums.append(jnp.sum(masses, axis=1))
    mass_sum = jnp.concatenate(sums, axis=0)
    return jnp.log1p(mass_sum)


def plain_plan(embeddings, cluster_ids):
    peer_count = lax.axis_size("gx")
    row_count = embeddings.shape[0]
    features = embeddings.shape[1]
    capacity = 3 * row_count // peer_count
    slot_total = peer_count * capacity
    squares = jnp.sum(jnp.square(embeddings.astype(jnp.float32)), axis=1)
    unit_rows = (embeddings.astype(jnp.float32) * lax.rsqrt(squares + 1e-06)[:, None]).astype(
        jnp.bfloat16
    )
    owner_of = cluster_ids // CLU_DEV
    onehot = (owner_of[:, None] == jnp.arange(peer_count, dtype=jnp.int32)[None, :]).astype(
        jnp.bfloat16
    )
    row_range = jnp.arange(row_count, dtype=jnp.int32)
    lower_tri = (row_range[:, None] >= row_range[None, :]).astype(jnp.bfloat16)
    running = jnp.dot(lower_tri, onehot, preferred_element_type=jnp.float32)
    slot_index = (jnp.sum(running * onehot.astype(jnp.float32), axis=1) - 1.0).astype(jnp.int32)
    target_slot = owner_of * capacity + slot_index
    slot_range = jnp.arange(slot_total, dtype=jnp.int32)
    select_mask = slot_range[:, None] == target_slot[None, :]
    outgoing = jnp.dot(
        select_mask.astype(jnp.bfloat16), unit_rows, preferred_element_type=jnp.float32
    )
    outgoing = outgoing.astype(jnp.bfloat16).reshape(peer_count, capacity, features)
    outgoing_ids = jnp.sum(jnp.where(select_mask, cluster_ids[None, :] + 1, 0), axis=1) - 1
    outgoing_ids = outgoing_ids.reshape(peer_count, capacity)
    arrived, arrived_ids = (
        lax.all_to_all(outgoing, "gx", split_axis=0, concat_axis=0, tiled=True),
        lax.all_to_all(outgoing_ids, "gx", split_axis=0, concat_axis=0, tiled=True),
    )
    key_rows = arrived.reshape(slot_total, features)
    key_ids = arrived_ids.reshape(slot_total)
    scores = density_scores(key_rows, key_ids)
    returned = lax.all_to_all(
        scores.reshape(peer_count, capacity), "gx", split_axis=0, concat_axis=0, tiled=True
    )
    flat_scores = returned.reshape(slot_total)
    pick_mask = target_slot[:, None] == slot_range[None, :]
    return jnp.sum(jnp.where(pick_mask, flat_scores[None, :], 0.0), axis=1)


LANES = 128
PLANE = 4
INVERSE_TEMP_BITS = 20.0 * 1.4426950408889634
ID_ROWS = 8
VMEM_BYTES = 16 * 1024 * 1024


def along_rows(values):
    return jnp.broadcast_to(values, (LANES, values.shape[1])).T


def ids_block(ids, width):
    wide = jnp.concatenate([ids, jnp.zeros((1, width - ids.shape[1]), jnp.float32)], axis=1)
    return jnp.broadcast_to(wide, (ID_ROWS, width)).astype(jnp.bfloat16)


def ids_of(ref):
    first = ref.shape[0] - ID_ROWS
    return ref[first:, :].astype(jnp.float32)[:1]


def mate_mass(query_rows, query_ids, key_rows, key_ids, shift=None):
    similar = lax.dot_general(
        query_rows, key_rows, (((1,), (1,)), ((), ())), preferred_element_type=jnp.float32
    )
    repeats = similar.shape[1] // LANES
    mates = jnp.concatenate([query_ids] * repeats, axis=1) == key_ids
    if shift is not None:
        query_pos = lax.broadcasted_iota(jnp.int32, similar.shape, 0) + shift
        key_pos = lax.broadcasted_iota(jnp.int32, similar.shape, 1)
        mates = mates & (query_pos != key_pos)
    return jnp.where(mates, jnp.exp2(similar * INVERSE_TEMP_BITS), 0.0)


def unit_rows(raw):
    features = raw.astype(jnp.float32)
    squares = jnp.sum(features * features, axis=1, keepdims=True)
    return (features * lax.rsqrt(squares + 1e-06)).astype(jnp.bfloat16)


def unit_kernel(ranges, rows_ref, ids_ref, *block_refs):
    rows, width = rows_ref.shape
    units = unit_rows(rows_ref[...])
    ids = ids_block(ids_ref[...].astype(jnp.float32), width)
    for (first, last), ref in zip(ranges, block_refs):
        size = last - first
        ref[:size, :] = units[first:last]
        if ref.shape[0] > size:
            ref[size:, :] = ids


def arrived_at(moves):
    plane = lax.axis_index("gx") // PLANE
    return functools.reduce(jnp.logical_or, [plane == receiver for _, receiver in moves])


def add_line(query_parts, ids_ref, key_rows, key_ids, earlier_ref, sums_ref):
    keys = key_rows.shape[0]
    column = jnp.zeros((1, keys), jnp.float32)
    first = 0
    for query_ref, size in query_parts:
        part = pl.ds(first, size)
        masses = mate_mass(query_ref[:size, :], ids_ref[part, :], key_rows, key_ids)
        column = column + jnp.sum(masses, axis=0, keepdims=True)
        folded = masses[:, :LANES]
        for lane in range(LANES, keys, LANES):
            folded = folded + masses[:, lane : lane + LANES]
        sums_ref[part, :] = folded if earlier_ref is None else earlier_ref[part, :] + folded
        first += size
    return column


def add_masses(query_ids, key_ids, powers):
    mates = jnp.concatenate([query_ids] * (powers.shape[1] // LANES), axis=1) == key_ids
    masses = jnp.where(mates, powers, 0.0)
    folded = masses[:, :LANES]
    for lane in range(LANES, powers.shape[1], LANES):
        folded = folded + masses[:, lane : lane + LANES]
    return folded, jnp.sum(masses, axis=0, keepdims=True)


def query_parts_of(refs, rows):
    head = refs[2].shape[0]
    sizes = [rows, rows] + [head, rows - head] * (PLANE - 2)
    return list(zip(refs, sizes))


def own_kernel(own_ref, mass_ref):
    rows = mass_ref.shape[1]
    own_ids = ids_of(own_ref)[:, :rows]
    masses = mate_mass(own_ref[:rows, :], along_rows(own_ids), own_ref[:rows, :], own_ids, 0)
    mass_ref[...] = jnp.sum(masses, axis=0, keepdims=True)


def first_kernel(moves, own_mass_ref, head_ref, tail_ref, *refs):
    query_refs, (ids_ref, column_ref, sums_ref, mass_ref) = refs[:-4], refs[-4:]
    rows = mass_ref.shape[1]
    query_parts = query_parts_of(query_refs, rows)
    own_ref = query_refs[0]
    own_ids = ids_of(own_ref)[:, :rows]
    for m, ref in enumerate((*query_refs[:2], query_refs[3], query_refs[5])):
        ids_ref[pl.ds(m * rows, rows), :] = along_rows(ids_of(ref)[:, :rows])
    mass = own_mass_ref[...]
    first = rows
    for ref, size in query_parts[1:]:
        query_ids = ids_ref[pl.ds(first, size), :]
        masses = mate_mass(ref[:size, :], query_ids, own_ref[:rows, :], own_ids)
        mass = mass + jnp.sum(masses, axis=0, keepdims=True)
        first += size
    mass_ref[...] = mass
    tail = tail_ref[: rows - head_ref.shape[0], :]
    key_rows = jnp.concatenate([unit_rows(head_ref[...]), tail], axis=0)
    key_ids = ids_of(tail_ref)[:, :rows]
    column_ref[...] = add_line(query_parts, ids_ref, key_rows, key_ids, None, sums_ref)


def middle_kernel(moves, head_ref, *refs):
    query_refs, (powers_ref, rest_ref) = refs[:-2], refs[-2:]

    @pl.when(arrived_at(moves))
    def _():
        keys = powers_ref.shape[1]
        units = unit_rows(head_ref[...])
        rest_ref[...] = units[keys:]
        first = 0
        for query_ref, size in query_parts_of(query_refs, query_refs[0].shape[0] - ID_ROWS):
            similar = lax.dot_general(
                query_ref[:size, :], units[:keys], (((1,), (1,)), ((), ())),
                preferred_element_type=jnp.float32,
            )
            powers_ref[pl.ds(first, size), :] = jnp.exp2(similar * INVERSE_TEMP_BITS)
            first += size


def last_kernel(moves, powers_ref, rest_ref, tail_ref, ids_ref, earlier_ref, *refs):
    query_refs, (column_ref, sums_ref) = refs[:-2], refs[-2:]
    rows = column_ref.shape[1]
    cut = powers_ref.shape[1]
    arrived = arrived_at(moves)

    @pl.when(arrived)
    def _():
        key_ids = ids_of(tail_ref)[:, :rows]
        key_rows = jnp.concatenate([rest_ref[...], tail_ref[: tail_ref.shape[0] - ID_ROWS, :]], axis=0)
        early_column = jnp.zeros((1, cut), jnp.float32)
        late_column = jnp.zeros((1, rows - cut), jnp.float32)
        first = 0
        for query_ref, size in query_parts_of(query_refs, rows):
            part = pl.ds(first, size)
            query_ids = ids_ref[part, :]
            similar = lax.dot_general(
                query_ref[:size, :], key_rows, (((1,), (1,)), ((), ())),
                preferred_element_type=jnp.float32,
            )
            powers = jnp.exp2(similar * INVERSE_TEMP_BITS)
            late, column = add_masses(query_ids, key_ids[:, cut:], powers)
            late_column = late_column + column
            early, column = add_masses(query_ids, key_ids[:, :cut], powers_ref[part, :])
            early_column = early_column + column
            sums_ref[part, :] = earlier_ref[part, :] + early + late
            first += size
        column_ref[...] = jnp.concatenate([early_column, late_column], axis=1)

    @pl.when(jnp.logical_not(arrived))
    def _():
        column_ref[...] = jnp.zeros_like(column_ref)
        sums_ref[...] = earlier_ref[...]


def fold_kernel(sums_ref, mass_ref, *row_refs):
    rows = mass_ref.shape[1]
    for m in range(PLANE):
        row_sum = jnp.sum(sums_ref[pl.ds(m * rows, rows), :].T, axis=0, keepdims=True)
        row_refs[m][...] = row_sum + mass_ref[...] if m == 0 else row_sum


def grid_plan(embeddings, cluster_ids):
    peers = lax.axis_size("gx")
    row_count, features = embeddings.shape
    plane_rows = PLANE * row_count
    params = pltpu.CompilerParams(vmem_limit_bytes=VMEM_BYTES)
    small = pl.CostEstimate(flops=1, bytes_accessed=1, transcendentals=0)
    vector = jax.ShapeDtypeStruct((1, row_count), jnp.float32)
    lanes = jax.ShapeDtypeStruct((plane_rows, LANES), jnp.float32)

    def rows_of(count):
        return jax.ShapeDtypeStruct((count, features), jnp.bfloat16)

    def in_plane(value, step):
        return lax.ppermute(value, "gx", [(i, i ^ step) for i in range(peers)])

    def on_line(value, moves):
        pairs = [(a * PLANE + n, b * PLANE + n) for a, b in moves for n in range(PLANE)]
        return lax.ppermute(value, "gx", pairs)

    first_moves = [(0, 1), (1, 2), (2, 3), (3, 0)]
    last_moves = [(0, 2), (1, 3)]
    forward_moves = [(1, 2), (2, 3)]
    first_back = [(b, a) for a, b in first_moves]
    last_back = [(b, a) for a, b in last_moves]

    half, part = row_count // 2, 9 * row_count // 16
    ranges = [(0, row_count), (0, half), (half, row_count), (part, row_count)]
    id_rows = [ID_ROWS, 0, ID_ROWS, ID_ROWS]
    first_head = on_line(embeddings[:part], first_moves)
    block, *pieces, tail = pl.pallas_call(
        functools.partial(unit_kernel, ranges),
        out_shape=[rows_of(b - a + extra) for (a, b), extra in zip(ranges, id_rows)],
        cost_estimate=small,
        compiler_params=params,
    )(embeddings, cluster_ids.reshape(1, row_count))
    own_mass = pl.pallas_call(
        own_kernel, out_shape=vector, cost_estimate=small, compiler_params=params
    )(block)
    own_mass, tail = lax.optimization_barrier((own_mass, tail))
    first_tail = on_line(tail, first_moves)
    across = [in_plane(piece, 2) for piece in pieces]
    sibling = in_plane(block, 1)
    last_head = on_line(first_head, first_moves)
    last_tail = on_line(first_tail, forward_moves)
    corner = [in_plane(piece, 1) for piece in across]
    queries = (block, sibling, *across, *corner)
    ids, first_column, first_sums, mass = pl.pallas_call(
        functools.partial(first_kernel, first_moves),
        out_shape=(lanes, vector, lanes, vector),
        cost_estimate=small,
        compiler_params=params,
    )(own_mass, first_head, first_tail, *queries)
    returned_first = on_line(first_column, first_back)
    powers, rest = pl.pallas_call(
        functools.partial(middle_kernel, last_moves),
        out_shape=(
            jax.ShapeDtypeStruct((plane_rows, half), jnp.float32), rows_of(part - half)
        ),
        cost_estimate=small,
        compiler_params=params,
    )(last_head, *queries)
    last_column, sums = pl.pallas_call(
        functools.partial(last_kernel, last_moves),
        out_shape=(vector, lanes),
        cost_estimate=small,
        compiler_params=params,
    )(powers, rest, last_tail, ids, first_sums, *queries)
    returned_first, last_column = lax.optimization_barrier((returned_first, last_column))
    row_sums = pl.pallas_call(
        fold_kernel,
        out_shape=[vector] * PLANE,
        cost_estimate=small,
        compiler_params=params,
    )(sums, mass)
    returned = [on_line(last_column, last_back)]
    returned += [in_plane(row_sums[step], step) for step in (2, 3, 1)]
    return jnp.log1p(sum(returned, row_sums[0] + returned_first)).reshape(row_count)


def on_device(embeddings, cluster_ids):
    if lax.axis_size("gx") == 4 * PLANE and embeddings.shape[0] == 2 * LANES:
        return grid_plan(embeddings, cluster_ids)
    return plain_plan(embeddings, cluster_ids)


def solution(mesh):
    in_specs = (P(("parts", "gx"), None), P(("parts", "gx")))
    out_specs = P(("parts", "gx"))
    return jax.shard_map(
        on_device, mesh=mesh, in_specs=in_specs, out_specs=out_specs, check_vma=False
    )
```

```python
import functools

import jax
import jax.numpy as jnp
from jax import lax
from jax.experimental import pallas as pl
from jax.experimental.pallas import tpu as pltpu
from jax.sharding import PartitionSpec as P

CLU_DEV = 1
PAD_MARK = 64.0
inverse_temp = 20.0


def tile_mass(query_rows, key_rows, query_ids, key_ids, query_start):
    similar = lax.dot_general(
        query_rows, key_rows, (((1,), (1,)), ((), ())), preferred_element_type=jnp.float32
    )
    query_pos = jnp.arange(query_rows.shape[0], dtype=jnp.int32) + query_start
    key_pos = jnp.arange(key_rows.shape[0], dtype=jnp.int32)
    mate_mask = (query_ids[:, None] == key_ids[None, :]) & (query_ids[:, None] >= 0)
    mate_mask = mate_mask & (query_pos[:, None] != key_pos[None, :])
    return jnp.where(mate_mask, jnp.exp(similar * inverse_temp), 0.0)


def density_scores(key_rows, key_ids):
    total_rows = key_rows.shape[0]
    block_rows = total_rows // 3
    pieces = [key_rows[i * block_rows : (i + 1) * block_rows] for i in range(3)]
    piece_ids = [key_ids[i * block_rows : (i + 1) * block_rows] for i in range(3)]
    sums = []
    for first in range(3):
        masses = tile_mass(pieces[first], key_rows, piece_ids[first], key_ids, first * block_rows)
        sums.append(jnp.sum(masses, axis=1))
    mass_sum = jnp.concatenate(sums, axis=0)
    return jnp.log1p(mass_sum)


def plain_plan(embeddings, cluster_ids):
    peer_count = lax.axis_size("gx")
    row_count = embeddings.shape[0]
    features = embeddings.shape[1]
    capacity = 3 * row_count // peer_count
    slot_total = peer_count * capacity
    squares = jnp.sum(jnp.square(embeddings.astype(jnp.float32)), axis=1)
    unit_rows = (embeddings.astype(jnp.float32) * lax.rsqrt(squares + 1e-06)[:, None]).astype(
        jnp.bfloat16
    )
    owner_of = cluster_ids // CLU_DEV
    onehot = (owner_of[:, None] == jnp.arange(peer_count, dtype=jnp.int32)[None, :]).astype(
        jnp.bfloat16
    )
    row_range = jnp.arange(row_count, dtype=jnp.int32)
    lower_tri = (row_range[:, None] >= row_range[None, :]).astype(jnp.bfloat16)
    running = jnp.dot(lower_tri, onehot, preferred_element_type=jnp.float32)
    slot_index = (jnp.sum(running * onehot.astype(jnp.float32), axis=1) - 1.0).astype(jnp.int32)
    target_slot = owner_of * capacity + slot_index
    slot_range = jnp.arange(slot_total, dtype=jnp.int32)
    select_mask = slot_range[:, None] == target_slot[None, :]
    outgoing = jnp.dot(
        select_mask.astype(jnp.bfloat16), unit_rows, preferred_element_type=jnp.float32
    )
    outgoing = outgoing.astype(jnp.bfloat16).reshape(peer_count, capacity, features)
    outgoing_ids = jnp.sum(jnp.where(select_mask, cluster_ids[None, :] + 1, 0), axis=1) - 1
    outgoing_ids = outgoing_ids.reshape(peer_count, capacity)
    arrived, arrived_ids = (
        lax.all_to_all(outgoing, "gx", split_axis=0, concat_axis=0, tiled=True),
        lax.all_to_all(outgoing_ids, "gx", split_axis=0, concat_axis=0, tiled=True),
    )
    key_rows = arrived.reshape(slot_total, features)
    key_ids = arrived_ids.reshape(slot_total)
    scores = density_scores(key_rows, key_ids)
    returned = lax.all_to_all(
        scores.reshape(peer_count, capacity), "gx", split_axis=0, concat_axis=0, tiled=True
    )
    flat_scores = returned.reshape(slot_total)
    pick_mask = target_slot[:, None] == slot_range[None, :]
    return jnp.sum(jnp.where(pick_mask, flat_scores[None, :], 0.0), axis=1)


LANES = 128
PLANE = 4
INVERSE_TEMP_BITS = 20.0 * 1.4426950408889634
ID_ROWS = 8
VMEM_BYTES = 16 * 1024 * 1024


def along_rows(values):
    return jnp.broadcast_to(values, (LANES, values.shape[1])).T


def ids_block(ids, width):
    wide = jnp.concatenate([ids, jnp.zeros((1, width - ids.shape[1]), jnp.float32)], axis=1)
    return jnp.broadcast_to(wide, (ID_ROWS, width)).astype(jnp.bfloat16)


def ids_of(ref):
    first = ref.shape[0] - ID_ROWS
    return ref[first:, :].astype(jnp.float32)[:1]


def mate_mass(query_rows, query_ids, key_rows, key_ids, shift=None):
    similar = lax.dot_general(
        query_rows, key_rows, (((1,), (1,)), ((), ())), preferred_element_type=jnp.float32
    )
    repeats = similar.shape[1] // LANES
    mates = jnp.concatenate([query_ids] * repeats, axis=1) == key_ids
    if shift is not None:
        query_pos = lax.broadcasted_iota(jnp.int32, similar.shape, 0) + shift
        key_pos = lax.broadcasted_iota(jnp.int32, similar.shape, 1)
        mates = mates & (query_pos != key_pos)
    return jnp.where(mates, jnp.exp2(similar * INVERSE_TEMP_BITS), 0.0)


def unit_rows(raw):
    features = raw.astype(jnp.float32)
    squares = jnp.sum(features * features, axis=1, keepdims=True)
    return (features * lax.rsqrt(squares + 1e-06)).astype(jnp.bfloat16)


def unit_kernel(ranges, rows_ref, ids_ref, *block_refs):
    rows, width = rows_ref.shape
    units = unit_rows(rows_ref[...])
    ids = ids_block(ids_ref[...].astype(jnp.float32), width)
    for (first, last), ref in zip(ranges, block_refs):
        size = last - first
        ref[:size, :] = units[first:last]
        if ref.shape[0] > size:
            ref[size:, :] = ids


def arrived_at(moves):
    plane = lax.axis_index("gx") // PLANE
    return functools.reduce(jnp.logical_or, [plane == receiver for _, receiver in moves])


def add_line(query_parts, ids_ref, key_rows, key_ids, earlier_ref, sums_ref):
    keys = key_rows.shape[0]
    column = jnp.zeros((1, keys), jnp.float32)
    first = 0
    for query_ref, size in query_parts:
        part = pl.ds(first, size)
        masses = mate_mass(query_ref[:size, :], ids_ref[part, :], key_rows, key_ids)
        column = column + jnp.sum(masses, axis=0, keepdims=True)
        folded = masses[:, :LANES]
        for lane in range(LANES, keys, LANES):
            folded = folded + masses[:, lane : lane + LANES]
        sums_ref[part, :] = folded if earlier_ref is None else earlier_ref[part, :] + folded
        first += size
    return column


def add_masses(query_ids, key_ids, powers):
    mates = jnp.concatenate([query_ids] * (powers.shape[1] // LANES), axis=1) == key_ids
    masses = jnp.where(mates, powers, 0.0)
    folded = masses[:, :LANES]
    for lane in range(LANES, powers.shape[1], LANES):
        folded = folded + masses[:, lane : lane + LANES]
    return folded, jnp.sum(masses, axis=0, keepdims=True)


def query_parts_of(refs, rows):
    head = refs[2].shape[0]
    sizes = [rows, rows] + [head, rows - head] * (PLANE - 2)
    return list(zip(refs, sizes))


def own_kernel(own_ref, mass_ref):
    rows = mass_ref.shape[1]
    own_ids = ids_of(own_ref)[:, :rows]
    masses = mate_mass(own_ref[:rows, :], along_rows(own_ids), own_ref[:rows, :], own_ids, 0)
    mass_ref[...] = jnp.sum(masses, axis=0, keepdims=True)


def first_kernel(moves, own_mass_ref, head_ref, tail_ref, *refs):
    query_refs, (key_ids_ref, ids_ref, column_ref, sums_ref, mass_ref) = refs[:-5], refs[-5:]
    rows = mass_ref.shape[1]
    query_parts = query_parts_of(query_refs, rows)
    own_ref = query_refs[0]
    own_ids = ids_of(own_ref)[:, :rows]
    for m, ref in enumerate((*query_refs[:2], query_refs[3], query_refs[5])):
        ids_ref[pl.ds(m * rows, rows), :] = along_rows(ids_of(ref)[:, :rows])
    mass = own_mass_ref[...]
    first = rows
    for ref, size in query_parts[1:]:
        query_ids = ids_ref[pl.ds(first, size), :]
        masses = mate_mass(ref[:size, :], query_ids, own_ref[:rows, :], own_ids)
        mass = mass + jnp.sum(masses, axis=0, keepdims=True)
        first += size
    mass_ref[...] = mass
    tail = tail_ref[: rows - head_ref.shape[0], :]
    key_rows = jnp.concatenate([unit_rows(head_ref[...]), tail], axis=0)
    key_ids = ids_of(tail_ref)[:, :rows]
    key_ids_ref[...] = key_ids
    column_ref[...] = add_line(query_parts, ids_ref, key_rows, key_ids, None, sums_ref)


def middle_kernel(moves, head_ref, *refs):
    query_refs, (powers_ref, rest_ref) = refs[:-2], refs[-2:]

    @pl.when(arrived_at(moves))
    def _():
        keys = powers_ref.shape[1]
        units = unit_rows(head_ref[...])
        rest_ref[...] = units[keys:]
        first = 0
        for query_ref, size in query_parts_of(query_refs, query_refs[0].shape[0] - ID_ROWS):
            similar = lax.dot_general(
                query_ref[:size, :], units[:keys], (((1,), (1,)), ((), ())),
                preferred_element_type=jnp.float32,
            )
            powers_ref[pl.ds(first, size), :] = jnp.exp2(similar * INVERSE_TEMP_BITS)
            first += size


def last_kernel(moves, powers_ref, rest_ref, key_ids_ref, tail_ref, ids_ref, earlier_ref, *refs):
    query_refs, (column_ref, sums_ref) = refs[:-2], refs[-2:]
    rows = column_ref.shape[1]
    cut = powers_ref.shape[1]
    arrived = arrived_at(moves)

    @pl.when(arrived)
    def _():
        key_ids = key_ids_ref[...]
        key_rows = jnp.concatenate([rest_ref[...], tail_ref[...]], axis=0)
        early_column = jnp.zeros((1, cut), jnp.float32)
        late_column = jnp.zeros((1, rows - cut), jnp.float32)
        first = 0
        for query_ref, size in query_parts_of(query_refs, rows):
            part = pl.ds(first, size)
            query_ids = ids_ref[part, :]
            similar = lax.dot_general(
                query_ref[:size, :], key_rows, (((1,), (1,)), ((), ())),
                preferred_element_type=jnp.float32,
            )
            powers = jnp.exp2(similar * INVERSE_TEMP_BITS)
            late, column = add_masses(query_ids, key_ids[:, cut:], powers)
            late_column = late_column + column
            early, column = add_masses(query_ids, key_ids[:, :cut], powers_ref[part, :])
            early_column = early_column + column
            sums_ref[part, :] = earlier_ref[part, :] + early + late
            first += size
        column_ref[...] = jnp.concatenate([early_column, late_column], axis=1)

    @pl.when(jnp.logical_not(arrived))
    def _():
        column_ref[...] = jnp.zeros_like(column_ref)
        sums_ref[...] = earlier_ref[...]


def fold_kernel(sums_ref, mass_ref, *row_refs):
    rows = mass_ref.shape[1]
    for m in range(PLANE):
        row_sum = jnp.sum(sums_ref[pl.ds(m * rows, rows), :].T, axis=0, keepdims=True)
        row_refs[m][...] = row_sum + mass_ref[...] if m == 0 else row_sum


def grid_plan(embeddings, cluster_ids):
    peers = lax.axis_size("gx")
    row_count, features = embeddings.shape
    plane_rows = PLANE * row_count
    params = pltpu.CompilerParams(vmem_limit_bytes=VMEM_BYTES)
    small = pl.CostEstimate(flops=1, bytes_accessed=1, transcendentals=0)
    vector = jax.ShapeDtypeStruct((1, row_count), jnp.float32)
    lanes = jax.ShapeDtypeStruct((plane_rows, LANES), jnp.float32)

    def rows_of(count):
        return jax.ShapeDtypeStruct((count, features), jnp.bfloat16)

    def in_plane(value, step):
        return lax.ppermute(value, "gx", [(i, i ^ step) for i in range(peers)])

    def on_line(value, moves):
        pairs = [(a * PLANE + n, b * PLANE + n) for a, b in moves for n in range(PLANE)]
        return lax.ppermute(value, "gx", pairs)

    first_moves = [(0, 1), (1, 2), (2, 3), (3, 0)]
    last_moves = [(0, 2), (1, 3)]
    forward_moves = [(1, 2), (2, 3)]
    first_back = [(b, a) for a, b in first_moves]
    last_back = [(b, a) for a, b in last_moves]

    half, part = row_count // 2, 9 * row_count // 16
    ranges = [(0, row_count), (0, half), (half, row_count), (part, row_count)]
    id_rows = [ID_ROWS, 0, ID_ROWS, ID_ROWS]
    first_head = on_line(embeddings[:part], first_moves)
    block, *pieces, tail = pl.pallas_call(
        functools.partial(unit_kernel, ranges),
        out_shape=[rows_of(b - a + extra) for (a, b), extra in zip(ranges, id_rows)],
        cost_estimate=small,
        compiler_params=params,
    )(embeddings, cluster_ids.reshape(1, row_count))
    own_mass = pl.pallas_call(
        own_kernel, out_shape=vector, cost_estimate=small, compiler_params=params
    )(block)
    own_mass, tail = lax.optimization_barrier((own_mass, tail))
    first_tail = on_line(tail, first_moves)
    across = [in_plane(piece, 2) for piece in pieces]
    sibling = in_plane(block, 1)
    last_head = on_line(first_head, first_moves)
    last_tail = on_line(first_tail[: row_count - part], forward_moves)
    corner = [in_plane(piece, 1) for piece in across]
    queries = (block, sibling, *across, *corner)
    first_ids, ids, first_column, first_sums, mass = pl.pallas_call(
        functools.partial(first_kernel, first_moves),
        out_shape=(vector, lanes, vector, lanes, vector),
        cost_estimate=small,
        compiler_params=params,
    )(own_mass, first_head, first_tail, *queries)
    last_ids = on_line(first_ids, first_moves)
    returned_first = on_line(first_column, first_back)
    powers, rest = pl.pallas_call(
        functools.partial(middle_kernel, last_moves),
        out_shape=(
            jax.ShapeDtypeStruct((plane_rows, half), jnp.float32), rows_of(part - half)
        ),
        cost_estimate=small,
        compiler_params=params,
    )(last_head, *queries)
    last_column, sums = pl.pallas_call(
        functools.partial(last_kernel, last_moves),
        out_shape=(vector, lanes),
        cost_estimate=small,
        compiler_params=params,
    )(powers, rest, last_ids, last_tail, ids, first_sums, *queries)
    returned_first, last_column = lax.optimization_barrier((returned_first, last_column))
    row_sums = pl.pallas_call(
        fold_kernel,
        out_shape=[vector] * PLANE,
        cost_estimate=small,
        compiler_params=params,
    )(sums, mass)
    returned = [on_line(last_column, last_back)]
    returned += [in_plane(row_sums[step], step) for step in (2, 3, 1)]
    return jnp.log1p(sum(returned, row_sums[0] + returned_first)).reshape(row_count)


def on_device(embeddings, cluster_ids):
    if lax.axis_size("gx") == 4 * PLANE and embeddings.shape[0] == 2 * LANES:
        return grid_plan(embeddings, cluster_ids)
    return plain_plan(embeddings, cluster_ids)


def solution(mesh):
    in_specs = (P(("parts", "gx"), None), P(("parts", "gx")))
    out_specs = P(("parts", "gx"))
    return jax.shard_map(
        on_device, mesh=mesh, in_specs=in_specs, out_specs=out_specs, check_vma=False
    )
```

```python
import functools

import jax
import jax.numpy as jnp
from jax import lax
from jax.experimental import pallas as pl
from jax.experimental.pallas import tpu as pltpu
from jax.sharding import PartitionSpec as P

CLU_DEV = 1
PAD_MARK = 64.0
inverse_temp = 20.0


def tile_mass(query_rows, key_rows, query_ids, key_ids, query_start):
    similar = lax.dot_general(
        query_rows, key_rows, (((1,), (1,)), ((), ())), preferred_element_type=jnp.float32
    )
    query_pos = jnp.arange(query_rows.shape[0], dtype=jnp.int32) + query_start
    key_pos = jnp.arange(key_rows.shape[0], dtype=jnp.int32)
    mate_mask = (query_ids[:, None] == key_ids[None, :]) & (query_ids[:, None] >= 0)
    mate_mask = mate_mask & (query_pos[:, None] != key_pos[None, :])
    return jnp.where(mate_mask, jnp.exp(similar * inverse_temp), 0.0)


def density_scores(key_rows, key_ids):
    total_rows = key_rows.shape[0]
    block_rows = total_rows // 3
    pieces = [key_rows[i * block_rows : (i + 1) * block_rows] for i in range(3)]
    piece_ids = [key_ids[i * block_rows : (i + 1) * block_rows] for i in range(3)]
    sums = []
    for first in range(3):
        masses = tile_mass(pieces[first], key_rows, piece_ids[first], key_ids, first * block_rows)
        sums.append(jnp.sum(masses, axis=1))
    mass_sum = jnp.concatenate(sums, axis=0)
    return jnp.log1p(mass_sum)


def plain_plan(embeddings, cluster_ids):
    peer_count = lax.axis_size("gx")
    row_count = embeddings.shape[0]
    features = embeddings.shape[1]
    capacity = 3 * row_count // peer_count
    slot_total = peer_count * capacity
    squares = jnp.sum(jnp.square(embeddings.astype(jnp.float32)), axis=1)
    unit_rows = (embeddings.astype(jnp.float32) * lax.rsqrt(squares + 1e-06)[:, None]).astype(
        jnp.bfloat16
    )
    owner_of = cluster_ids // CLU_DEV
    onehot = (owner_of[:, None] == jnp.arange(peer_count, dtype=jnp.int32)[None, :]).astype(
        jnp.bfloat16
    )
    row_range = jnp.arange(row_count, dtype=jnp.int32)
    lower_tri = (row_range[:, None] >= row_range[None, :]).astype(jnp.bfloat16)
    running = jnp.dot(lower_tri, onehot, preferred_element_type=jnp.float32)
    slot_index = (jnp.sum(running * onehot.astype(jnp.float32), axis=1) - 1.0).astype(jnp.int32)
    target_slot = owner_of * capacity + slot_index
    slot_range = jnp.arange(slot_total, dtype=jnp.int32)
    select_mask = slot_range[:, None] == target_slot[None, :]
    outgoing = jnp.dot(
        select_mask.astype(jnp.bfloat16), unit_rows, preferred_element_type=jnp.float32
    )
    outgoing = outgoing.astype(jnp.bfloat16).reshape(peer_count, capacity, features)
    outgoing_ids = jnp.sum(jnp.where(select_mask, cluster_ids[None, :] + 1, 0), axis=1) - 1
    outgoing_ids = outgoing_ids.reshape(peer_count, capacity)
    arrived, arrived_ids = (
        lax.all_to_all(outgoing, "gx", split_axis=0, concat_axis=0, tiled=True),
        lax.all_to_all(outgoing_ids, "gx", split_axis=0, concat_axis=0, tiled=True),
    )
    key_rows = arrived.reshape(slot_total, features)
    key_ids = arrived_ids.reshape(slot_total)
    scores = density_scores(key_rows, key_ids)
    returned = lax.all_to_all(
        scores.reshape(peer_count, capacity), "gx", split_axis=0, concat_axis=0, tiled=True
    )
    flat_scores = returned.reshape(slot_total)
    pick_mask = target_slot[:, None] == slot_range[None, :]
    return jnp.sum(jnp.where(pick_mask, flat_scores[None, :], 0.0), axis=1)


LANES = 128
PLANE = 4
INVERSE_TEMP_BITS = 20.0 * 1.4426950408889634
ID_ROWS = 8
VMEM_BYTES = 16 * 1024 * 1024


def along_rows(values):
    return jnp.broadcast_to(values, (LANES, values.shape[1])).T


def ids_block(ids, width):
    wide = jnp.concatenate([ids, jnp.zeros((1, width - ids.shape[1]), jnp.float32)], axis=1)
    return jnp.broadcast_to(wide, (ID_ROWS, width)).astype(jnp.bfloat16)


def ids_of(ref):
    first = ref.shape[0] - ID_ROWS
    return ref[first:, :].astype(jnp.float32)[:1]


def mate_mass(query_rows, query_ids, key_rows, key_ids, shift=None):
    similar = lax.dot_general(
        query_rows, key_rows, (((1,), (1,)), ((), ())), preferred_element_type=jnp.float32
    )
    repeats = similar.shape[1] // LANES
    mates = jnp.concatenate([query_ids] * repeats, axis=1) == key_ids
    if shift is not None:
        query_pos = lax.broadcasted_iota(jnp.int32, similar.shape, 0) + shift
        key_pos = lax.broadcasted_iota(jnp.int32, similar.shape, 1)
        mates = mates & (query_pos != key_pos)
    return jnp.where(mates, jnp.exp2(similar * INVERSE_TEMP_BITS), 0.0)


def unit_rows(raw):
    features = raw.astype(jnp.float32)
    squares = jnp.sum(features * features, axis=1, keepdims=True)
    return (features * lax.rsqrt(squares + 1e-06)).astype(jnp.bfloat16)


def unit_kernel(ranges, rows_ref, ids_ref, *block_refs):
    rows, width = rows_ref.shape
    units = unit_rows(rows_ref[...])
    ids = ids_block(ids_ref[...].astype(jnp.float32), width)
    for (first, last), ref in zip(ranges, block_refs):
        size = last - first
        ref[:size, :] = units[first:last]
        if ref.shape[0] > size:
            ref[size:, :] = ids


def arrived_at(moves):
    plane = lax.axis_index("gx") // PLANE
    return functools.reduce(jnp.logical_or, [plane == receiver for _, receiver in moves])


def add_line(query_parts, ids_ref, key_rows, key_ids, earlier_ref, sums_ref):
    keys = key_rows.shape[0]
    column = jnp.zeros((1, keys), jnp.float32)
    first = 0
    for query_ref, size in query_parts:
        part = pl.ds(first, size)
        masses = mate_mass(query_ref[:size, :], ids_ref[part, :], key_rows, key_ids)
        column = column + jnp.sum(masses, axis=0, keepdims=True)
        folded = masses[:, :LANES]
        for lane in range(LANES, keys, LANES):
            folded = folded + masses[:, lane : lane + LANES]
        sums_ref[part, :] = folded if earlier_ref is None else earlier_ref[part, :] + folded
        first += size
    return column


def add_masses(query_ids, key_ids, powers):
    mates = jnp.concatenate([query_ids] * (powers.shape[1] // LANES), axis=1) == key_ids
    masses = jnp.where(mates, powers, 0.0)
    folded = masses[:, :LANES]
    for lane in range(LANES, powers.shape[1], LANES):
        folded = folded + masses[:, lane : lane + LANES]
    return folded, jnp.sum(masses, axis=0, keepdims=True)


def query_parts_of(refs, rows):
    head = refs[2].shape[0]
    sizes = [rows, rows] + [head, rows - head] * (PLANE - 2)
    return list(zip(refs, sizes))


def own_kernel(own_ref, mass_ref):
    rows = mass_ref.shape[1]
    own_ids = ids_of(own_ref)[:, :rows]
    masses = mate_mass(own_ref[:rows, :], along_rows(own_ids), own_ref[:rows, :], own_ids, 0)
    mass_ref[...] = jnp.sum(masses, axis=0, keepdims=True)


def first_kernel(moves, own_mass_ref, head_ref, tail_ref, *refs):
    query_refs, (ids_ref, column_ref, sums_ref, mass_ref) = refs[:-4], refs[-4:]
    rows = mass_ref.shape[1]
    query_parts = query_parts_of(query_refs, rows)
    own_ref = query_refs[0]
    own_ids = ids_of(own_ref)[:, :rows]
    for m, ref in enumerate((*query_refs[:2], query_refs[3], query_refs[5])):
        ids_ref[pl.ds(m * rows, rows), :] = along_rows(ids_of(ref)[:, :rows])
    mass = own_mass_ref[...]
    first = rows
    for ref, size in query_parts[1:]:
        query_ids = ids_ref[pl.ds(first, size), :]
        masses = mate_mass(ref[:size, :], query_ids, own_ref[:rows, :], own_ids)
        mass = mass + jnp.sum(masses, axis=0, keepdims=True)
        first += size
    mass_ref[...] = mass
    tail = tail_ref[: rows - head_ref.shape[0], :]
    key_rows = jnp.concatenate([unit_rows(head_ref[...]), tail], axis=0)
    key_ids = ids_of(tail_ref)[:, :rows]
    column_ref[...] = add_line(query_parts, ids_ref, key_rows, key_ids, None, sums_ref)


def middle_kernel(moves, head_ref, *refs):
    query_refs, (powers_ref, rest_ref) = refs[:-2], refs[-2:]

    @pl.when(arrived_at(moves))
    def _():
        keys = powers_ref.shape[1]
        units = unit_rows(head_ref[...])
        rest_ref[...] = units[keys:]
        first = 0
        for query_ref, size in query_parts_of(query_refs, query_refs[0].shape[0] - ID_ROWS):
            similar = lax.dot_general(
                query_ref[:size, :], units[:keys], (((1,), (1,)), ((), ())),
                preferred_element_type=jnp.float32,
            )
            powers_ref[pl.ds(first, size), :] = jnp.exp2(similar * INVERSE_TEMP_BITS)
            first += size


def last_kernel(moves, powers_ref, rest_ref, key_ids_ref, tail_ref, ids_ref, earlier_ref, *refs):
    query_refs, (column_ref, sums_ref) = refs[:-2], refs[-2:]
    rows = column_ref.shape[1]
    cut = powers_ref.shape[1]
    arrived = arrived_at(moves)

    @pl.when(arrived)
    def _():
        key_ids = key_ids_ref[...].astype(jnp.float32)
        key_rows = jnp.concatenate([rest_ref[...], tail_ref[...]], axis=0)
        early_column = jnp.zeros((1, cut), jnp.float32)
        late_column = jnp.zeros((1, rows - cut), jnp.float32)
        first = 0
        for query_ref, size in query_parts_of(query_refs, rows):
            part = pl.ds(first, size)
            query_ids = ids_ref[part, :]
            similar = lax.dot_general(
                query_ref[:size, :], key_rows, (((1,), (1,)), ((), ())),
                preferred_element_type=jnp.float32,
            )
            powers = jnp.exp2(similar * INVERSE_TEMP_BITS)
            late, column = add_masses(query_ids, key_ids[:, cut:], powers)
            late_column = late_column + column
            early, column = add_masses(query_ids, key_ids[:, :cut], powers_ref[part, :])
            early_column = early_column + column
            sums_ref[part, :] = earlier_ref[part, :] + early + late
            first += size
        column_ref[...] = jnp.concatenate([early_column, late_column], axis=1)

    @pl.when(jnp.logical_not(arrived))
    def _():
        column_ref[...] = jnp.zeros_like(column_ref)
        sums_ref[...] = earlier_ref[...]


def fold_kernel(sums_ref, mass_ref, *row_refs):
    rows = mass_ref.shape[1]
    for m in range(PLANE):
        row_sum = jnp.sum(sums_ref[pl.ds(m * rows, rows), :].T, axis=0, keepdims=True)
        row_refs[m][...] = row_sum + mass_ref[...] if m == 0 else row_sum


def grid_plan(embeddings, cluster_ids):
    peers = lax.axis_size("gx")
    row_count, features = embeddings.shape
    plane_rows = PLANE * row_count
    params = pltpu.CompilerParams(vmem_limit_bytes=VMEM_BYTES)
    small = pl.CostEstimate(flops=1, bytes_accessed=1, transcendentals=0)
    vector = jax.ShapeDtypeStruct((1, row_count), jnp.float32)
    lanes = jax.ShapeDtypeStruct((plane_rows, LANES), jnp.float32)

    def rows_of(count):
        return jax.ShapeDtypeStruct((count, features), jnp.bfloat16)

    def in_plane(value, step):
        return lax.ppermute(value, "gx", [(i, i ^ step) for i in range(peers)])

    def on_line(value, moves):
        pairs = [(a * PLANE + n, b * PLANE + n) for a, b in moves for n in range(PLANE)]
        return lax.ppermute(value, "gx", pairs)

    first_moves = [(0, 1), (1, 2), (2, 3), (3, 0)]
    last_moves = [(0, 2), (1, 3)]
    forward_moves = [(1, 2), (2, 3)]
    first_back = [(b, a) for a, b in first_moves]
    last_back = [(b, a) for a, b in last_moves]

    half, part = row_count // 2, 9 * row_count // 16
    ranges = [(0, row_count), (0, half), (half, row_count), (part, row_count)]
    id_rows = [ID_ROWS, 0, ID_ROWS, ID_ROWS]
    first_head = on_line(embeddings[:part], first_moves)
    block, *pieces, tail = pl.pallas_call(
        functools.partial(unit_kernel, ranges),
        out_shape=[rows_of(b - a + extra) for (a, b), extra in zip(ranges, id_rows)],
        cost_estimate=small,
        compiler_params=params,
    )(embeddings, cluster_ids.reshape(1, row_count))
    own_mass = pl.pallas_call(
        own_kernel, out_shape=vector, cost_estimate=small, compiler_params=params
    )(block)
    own_mass, tail = lax.optimization_barrier((own_mass, tail))
    first_tail = on_line(tail, first_moves)
    across = [in_plane(piece, 2) for piece in pieces]
    sibling = in_plane(block, 1)
    last_head = on_line(first_head, first_moves)
    last_tail = on_line(first_tail[: row_count - part], forward_moves)
    last_ids = on_line(
        cluster_ids.reshape(1, row_count), last_moves + [(b, a) for a, b in last_moves]
    )
    corner = [in_plane(piece, 1) for piece in across]
    queries = (block, sibling, *across, *corner)
    ids, first_column, first_sums, mass = pl.pallas_call(
        functools.partial(first_kernel, first_moves),
        out_shape=(lanes, vector, lanes, vector),
        cost_estimate=small,
        compiler_params=params,
    )(own_mass, first_head, first_tail, *queries)
    returned_first = on_line(first_column, first_back)
    powers, rest = pl.pallas_call(
        functools.partial(middle_kernel, last_moves),
        out_shape=(
            jax.ShapeDtypeStruct((plane_rows, half), jnp.float32), rows_of(part - half)
        ),
        cost_estimate=small,
        compiler_params=params,
    )(last_head, *queries)
    last_column, sums = pl.pallas_call(
        functools.partial(last_kernel, last_moves),
        out_shape=(vector, lanes),
        cost_estimate=small,
        compiler_params=params,
    )(powers, rest, last_ids, last_tail, ids, first_sums, *queries)
    returned_first, last_column = lax.optimization_barrier((returned_first, last_column))
    row_sums = pl.pallas_call(
        fold_kernel,
        out_shape=[vector] * PLANE,
        cost_estimate=small,
        compiler_params=params,
    )(sums, mass)
    returned = [on_line(last_column, last_back)]
    returned += [in_plane(row_sums[step], step) for step in (2, 3, 1)]
    return jnp.log1p(sum(returned, row_sums[0] + returned_first)).reshape(row_count)


def on_device(embeddings, cluster_ids):
    if lax.axis_size("gx") == 4 * PLANE and embeddings.shape[0] == 2 * LANES:
        return grid_plan(embeddings, cluster_ids)
    return plain_plan(embeddings, cluster_ids)


def solution(mesh):
    in_specs = (P(("parts", "gx"), None), P(("parts", "gx")))
    out_specs = P(("parts", "gx"))
    return jax.shard_map(
        on_device, mesh=mesh, in_specs=in_specs, out_specs=out_specs, check_vma=False
    )
```

```python
import functools

import jax
import jax.numpy as jnp
from jax import lax
from jax.experimental import pallas as pl
from jax.experimental.pallas import tpu as pltpu
from jax.sharding import PartitionSpec as P

CLU_DEV = 1
PAD_MARK = 64.0
inverse_temp = 20.0


def tile_mass(query_rows, key_rows, query_ids, key_ids, query_start):
    similar = lax.dot_general(
        query_rows, key_rows, (((1,), (1,)), ((), ())), preferred_element_type=jnp.float32
    )
    query_pos = jnp.arange(query_rows.shape[0], dtype=jnp.int32) + query_start
    key_pos = jnp.arange(key_rows.shape[0], dtype=jnp.int32)
    mate_mask = (query_ids[:, None] == key_ids[None, :]) & (query_ids[:, None] >= 0)
    mate_mask = mate_mask & (query_pos[:, None] != key_pos[None, :])
    return jnp.where(mate_mask, jnp.exp(similar * inverse_temp), 0.0)


def density_scores(key_rows, key_ids):
    total_rows = key_rows.shape[0]
    block_rows = total_rows // 3
    pieces = [key_rows[i * block_rows : (i + 1) * block_rows] for i in range(3)]
    piece_ids = [key_ids[i * block_rows : (i + 1) * block_rows] for i in range(3)]
    sums = []
    for first in range(3):
        masses = tile_mass(pieces[first], key_rows, piece_ids[first], key_ids, first * block_rows)
        sums.append(jnp.sum(masses, axis=1))
    mass_sum = jnp.concatenate(sums, axis=0)
    return jnp.log1p(mass_sum)


def plain_plan(embeddings, cluster_ids):
    peer_count = lax.axis_size("gx")
    row_count = embeddings.shape[0]
    features = embeddings.shape[1]
    capacity = 3 * row_count // peer_count
    slot_total = peer_count * capacity
    squares = jnp.sum(jnp.square(embeddings.astype(jnp.float32)), axis=1)
    unit_rows = (embeddings.astype(jnp.float32) * lax.rsqrt(squares + 1e-06)[:, None]).astype(
        jnp.bfloat16
    )
    owner_of = cluster_ids // CLU_DEV
    onehot = (owner_of[:, None] == jnp.arange(peer_count, dtype=jnp.int32)[None, :]).astype(
        jnp.bfloat16
    )
    row_range = jnp.arange(row_count, dtype=jnp.int32)
    lower_tri = (row_range[:, None] >= row_range[None, :]).astype(jnp.bfloat16)
    running = jnp.dot(lower_tri, onehot, preferred_element_type=jnp.float32)
    slot_index = (jnp.sum(running * onehot.astype(jnp.float32), axis=1) - 1.0).astype(jnp.int32)
    target_slot = owner_of * capacity + slot_index
    slot_range = jnp.arange(slot_total, dtype=jnp.int32)
    select_mask = slot_range[:, None] == target_slot[None, :]
    outgoing = jnp.dot(
        select_mask.astype(jnp.bfloat16), unit_rows, preferred_element_type=jnp.float32
    )
    outgoing = outgoing.astype(jnp.bfloat16).reshape(peer_count, capacity, features)
    outgoing_ids = jnp.sum(jnp.where(select_mask, cluster_ids[None, :] + 1, 0), axis=1) - 1
    outgoing_ids = outgoing_ids.reshape(peer_count, capacity)
    arrived, arrived_ids = (
        lax.all_to_all(outgoing, "gx", split_axis=0, concat_axis=0, tiled=True),
        lax.all_to_all(outgoing_ids, "gx", split_axis=0, concat_axis=0, tiled=True),
    )
    key_rows = arrived.reshape(slot_total, features)
    key_ids = arrived_ids.reshape(slot_total)
    scores = density_scores(key_rows, key_ids)
    returned = lax.all_to_all(
        scores.reshape(peer_count, capacity), "gx", split_axis=0, concat_axis=0, tiled=True
    )
    flat_scores = returned.reshape(slot_total)
    pick_mask = target_slot[:, None] == slot_range[None, :]
    return jnp.sum(jnp.where(pick_mask, flat_scores[None, :], 0.0), axis=1)


LANES = 128
PLANE = 4
INVERSE_TEMP_BITS = 20.0 * 1.4426950408889634
ID_ROWS = 8
VMEM_BYTES = 16 * 1024 * 1024


def along_rows(values):
    return jnp.broadcast_to(values, (LANES, values.shape[1])).T


def ids_block(ids, width):
    wide = jnp.concatenate([ids, jnp.zeros((1, width - ids.shape[1]), jnp.float32)], axis=1)
    return jnp.broadcast_to(wide, (ID_ROWS, width)).astype(jnp.bfloat16)


def ids_of(ref):
    first = ref.shape[0] - ID_ROWS
    return ref[first:, :].astype(jnp.float32)[:1]


def mate_mass(query_rows, query_ids, key_rows, key_ids, shift=None):
    similar = lax.dot_general(
        query_rows, key_rows, (((1,), (1,)), ((), ())), preferred_element_type=jnp.float32
    )
    repeats = similar.shape[1] // LANES
    mates = jnp.concatenate([query_ids] * repeats, axis=1) == key_ids
    if shift is not None:
        query_pos = lax.broadcasted_iota(jnp.int32, similar.shape, 0) + shift
        key_pos = lax.broadcasted_iota(jnp.int32, similar.shape, 1)
        mates = mates & (query_pos != key_pos)
    return jnp.where(mates, jnp.exp2(similar * INVERSE_TEMP_BITS), 0.0)


def unit_rows(raw):
    features = raw.astype(jnp.float32)
    squares = jnp.sum(features * features, axis=1, keepdims=True)
    return (features * lax.rsqrt(squares + 1e-06)).astype(jnp.bfloat16)


def unit_kernel(ranges, rows_ref, ids_ref, *block_refs):
    rows, width = rows_ref.shape
    units = unit_rows(rows_ref[...])
    ids = ids_block(ids_ref[...].astype(jnp.float32), width)
    for (first, last), ref in zip(ranges, block_refs):
        size = last - first
        ref[:size, :] = units[first:last]
        if ref.shape[0] > size:
            ref[size:, :] = ids


def arrived_at(moves):
    plane = lax.axis_index("gx") // PLANE
    return functools.reduce(jnp.logical_or, [plane == receiver for _, receiver in moves])


def add_line(query_parts, ids_ref, key_rows, key_ids, earlier_ref, sums_ref):
    keys = key_rows.shape[0]
    column = jnp.zeros((1, keys), jnp.float32)
    first = 0
    for query_ref, size in query_parts:
        part = pl.ds(first, size)
        masses = mate_mass(query_ref[:size, :], ids_ref[part, :], key_rows, key_ids)
        column = column + jnp.sum(masses, axis=0, keepdims=True)
        folded = masses[:, :LANES]
        for lane in range(LANES, keys, LANES):
            folded = folded + masses[:, lane : lane + LANES]
        sums_ref[part, :] = folded if earlier_ref is None else earlier_ref[part, :] + folded
        first += size
    return column


def add_masses(query_ids, key_ids, powers):
    mates = jnp.concatenate([query_ids] * (powers.shape[1] // LANES), axis=1) == key_ids
    masses = jnp.where(mates, powers, 0.0)
    folded = masses[:, :LANES]
    for lane in range(LANES, powers.shape[1], LANES):
        folded = folded + masses[:, lane : lane + LANES]
    return folded, jnp.sum(masses, axis=0, keepdims=True)


def query_parts_of(refs, rows):
    head = refs[2].shape[0]
    sizes = [rows, rows] + [head, rows - head] * (PLANE - 2)
    return list(zip(refs, sizes))


def own_kernel(own_ref, mass_ref):
    rows = mass_ref.shape[1]
    own_ids = ids_of(own_ref)[:, :rows]
    masses = mate_mass(own_ref[:rows, :], along_rows(own_ids), own_ref[:rows, :], own_ids, 0)
    mass_ref[...] = jnp.sum(masses, axis=0, keepdims=True)


def first_kernel(moves, own_mass_ref, head_ref, tail_ref, *refs):
    query_refs, (ids_ref, column_ref, sums_ref, mass_ref) = refs[:-4], refs[-4:]
    rows = mass_ref.shape[1]
    query_parts = query_parts_of(query_refs, rows)
    own_ref = query_refs[0]
    own_ids = ids_of(own_ref)[:, :rows]
    for m, ref in enumerate((*query_refs[:2], query_refs[3], query_refs[5])):
        ids_ref[pl.ds(m * rows, rows), :] = along_rows(ids_of(ref)[:, :rows])
    mass = own_mass_ref[...]
    first = rows
    for ref, size in query_parts[1:]:
        query_ids = ids_ref[pl.ds(first, size), :]
        masses = mate_mass(ref[:size, :], query_ids, own_ref[:rows, :], own_ids)
        mass = mass + jnp.sum(masses, axis=0, keepdims=True)
        first += size
    mass_ref[...] = mass
    tail = tail_ref[: rows - head_ref.shape[0], :]
    key_rows = jnp.concatenate([unit_rows(head_ref[...]), tail], axis=0)
    key_ids = ids_of(tail_ref)[:, :rows]
    column_ref[...] = add_line(query_parts, ids_ref, key_rows, key_ids, None, sums_ref)


def middle_kernel(moves, head_ref, *refs):
    query_refs, (powers_ref, rest_ref) = refs[:-2], refs[-2:]

    @pl.when(arrived_at(moves))
    def _():
        keys = powers_ref.shape[1]
        units = unit_rows(head_ref[...])
        rest_ref[...] = units[keys:]
        first = 0
        for query_ref, size in query_parts_of(query_refs, query_refs[0].shape[0] - ID_ROWS):
            similar = lax.dot_general(
                query_ref[:size, :], units[:keys], (((1,), (1,)), ((), ())),
                preferred_element_type=jnp.float32,
            )
            powers_ref[pl.ds(first, size), :] = jnp.exp2(similar * INVERSE_TEMP_BITS)
            first += size


def last_kernel(moves, powers_ref, rest_ref, tail_ref, ids_ref, earlier_ref, *refs):
    query_refs, (column_ref, sums_ref) = refs[:-2], refs[-2:]
    rows = column_ref.shape[1]
    cut = powers_ref.shape[1]
    arrived = arrived_at(moves)

    @pl.when(arrived)
    def _():
        key_ids = ids_of(tail_ref)[:, :rows]
        key_rows = jnp.concatenate([rest_ref[...], tail_ref[: tail_ref.shape[0] - ID_ROWS, :]], axis=0)
        early_column = jnp.zeros((1, cut), jnp.float32)
        late_column = jnp.zeros((1, rows - cut), jnp.float32)
        first = 0
        for query_ref, size in query_parts_of(query_refs, rows):
            part = pl.ds(first, size)
            query_ids = ids_ref[part, :]
            similar = lax.dot_general(
                query_ref[:size, :], key_rows, (((1,), (1,)), ((), ())),
                preferred_element_type=jnp.float32,
            )
            powers = jnp.exp2(similar * INVERSE_TEMP_BITS)
            late, column = add_masses(query_ids, key_ids[:, cut:], powers)
            late_column = late_column + column
            early, column = add_masses(query_ids, key_ids[:, :cut], powers_ref[part, :])
            early_column = early_column + column
            sums_ref[part, :] = earlier_ref[part, :] + early + late
            first += size
        column_ref[...] = jnp.concatenate([early_column, late_column], axis=1)

    @pl.when(jnp.logical_not(arrived))
    def _():
        column_ref[...] = jnp.zeros_like(column_ref)
        sums_ref[...] = earlier_ref[...]


def fold_kernel(sums_ref, mass_ref, *row_refs):
    rows = mass_ref.shape[1]
    for m in range(PLANE):
        row_sum = jnp.sum(sums_ref[pl.ds(m * rows, rows), :].T, axis=0, keepdims=True)
        row_refs[m][...] = row_sum + mass_ref[...] if m == 0 else row_sum


def grid_plan(embeddings, cluster_ids):
    peers = lax.axis_size("gx")
    row_count, features = embeddings.shape
    plane_rows = PLANE * row_count
    params = pltpu.CompilerParams(vmem_limit_bytes=VMEM_BYTES)
    small = pl.CostEstimate(flops=1, bytes_accessed=1, transcendentals=0)
    vector = jax.ShapeDtypeStruct((1, row_count), jnp.float32)
    lanes = jax.ShapeDtypeStruct((plane_rows, LANES), jnp.float32)

    def rows_of(count):
        return jax.ShapeDtypeStruct((count, features), jnp.bfloat16)

    def in_plane(value, step):
        return lax.ppermute(value, "gx", [(i, i ^ step) for i in range(peers)])

    def on_line(value, moves):
        pairs = [(a * PLANE + n, b * PLANE + n) for a, b in moves for n in range(PLANE)]
        return lax.ppermute(value, "gx", pairs)

    first_moves = [(0, 1), (1, 2), (2, 3), (3, 0)]
    last_moves = [(0, 2), (1, 3)]
    forward_moves = [(1, 2), (2, 3)]
    first_back = [(b, a) for a, b in first_moves]
    last_back = [(b, a) for a, b in last_moves]

    half, part = row_count // 2, 5 * row_count // 8
    ranges = [(0, row_count), (0, half), (half, row_count), (part, row_count)]
    id_rows = [ID_ROWS, 0, ID_ROWS, ID_ROWS]
    first_head = on_line(embeddings[:part], first_moves)
    block, *pieces, tail = pl.pallas_call(
        functools.partial(unit_kernel, ranges),
        out_shape=[rows_of(b - a + extra) for (a, b), extra in zip(ranges, id_rows)],
        cost_estimate=small,
        compiler_params=params,
    )(embeddings, cluster_ids.reshape(1, row_count))
    own_mass = pl.pallas_call(
        own_kernel, out_shape=vector, cost_estimate=small, compiler_params=params
    )(block)
    own_mass, tail = lax.optimization_barrier((own_mass, tail))
    first_tail = on_line(tail, first_moves)
    across = [in_plane(piece, 2) for piece in pieces]
    sibling = in_plane(block, 1)
    last_head = on_line(first_head, first_moves)
    last_tail = on_line(first_tail, forward_moves)
    corner = [in_plane(piece, 1) for piece in across]
    queries = (block, sibling, *across, *corner)
    ids, first_column, first_sums, mass = pl.pallas_call(
        functools.partial(first_kernel, first_moves),
        out_shape=(lanes, vector, lanes, vector),
        cost_estimate=small,
        compiler_params=params,
    )(own_mass, first_head, first_tail, *queries)
    returned_first = on_line(first_column, first_back)
    powers, rest = pl.pallas_call(
        functools.partial(middle_kernel, last_moves),
        out_shape=(
            jax.ShapeDtypeStruct((plane_rows, half), jnp.float32), rows_of(part - half)
        ),
        cost_estimate=small,
        compiler_params=params,
    )(last_head, *queries)
    last_column, sums = pl.pallas_call(
        functools.partial(last_kernel, last_moves),
        out_shape=(vector, lanes),
        cost_estimate=small,
        compiler_params=params,
    )(powers, rest, last_tail, ids, first_sums, *queries)
    returned_first, last_column = lax.optimization_barrier((returned_first, last_column))
    row_sums = pl.pallas_call(
        fold_kernel,
        out_shape=[vector] * PLANE,
        cost_estimate=small,
        compiler_params=params,
    )(sums, mass)
    returned = [on_line(last_column, last_back)]
    returned += [in_plane(row_sums[step], step) for step in (2, 3, 1)]
    return jnp.log1p(sum(returned, row_sums[0] + returned_first)).reshape(row_count)


def on_device(embeddings, cluster_ids):
    if lax.axis_size("gx") == 4 * PLANE and embeddings.shape[0] == 2 * LANES:
        return grid_plan(embeddings, cluster_ids)
    return plain_plan(embeddings, cluster_ids)


def solution(mesh):
    in_specs = (P(("parts", "gx"), None), P(("parts", "gx")))
    out_specs = P(("parts", "gx"))
    return jax.shard_map(
        on_device, mesh=mesh, in_specs=in_specs, out_specs=out_specs, check_vma=False
    )
```

```python
import functools

import jax
import jax.numpy as jnp
from jax import lax
from jax.experimental import pallas as pl
from jax.experimental.pallas import tpu as pltpu
from jax.sharding import PartitionSpec as P

CLU_DEV = 1
PAD_MARK = 64.0
inverse_temp = 20.0


def tile_mass(query_rows, key_rows, query_ids, key_ids, query_start):
    similar = lax.dot_general(
        query_rows, key_rows, (((1,), (1,)), ((), ())), preferred_element_type=jnp.float32
    )
    query_pos = jnp.arange(query_rows.shape[0], dtype=jnp.int32) + query_start
    key_pos = jnp.arange(key_rows.shape[0], dtype=jnp.int32)
    mate_mask = (query_ids[:, None] == key_ids[None, :]) & (query_ids[:, None] >= 0)
    mate_mask = mate_mask & (query_pos[:, None] != key_pos[None, :])
    return jnp.where(mate_mask, jnp.exp(similar * inverse_temp), 0.0)


def density_scores(key_rows, key_ids):
    total_rows = key_rows.shape[0]
    block_rows = total_rows // 3
    pieces = [key_rows[i * block_rows : (i + 1) * block_rows] for i in range(3)]
    piece_ids = [key_ids[i * block_rows : (i + 1) * block_rows] for i in range(3)]
    sums = []
    for first in range(3):
        masses = tile_mass(pieces[first], key_rows, piece_ids[first], key_ids, first * block_rows)
        sums.append(jnp.sum(masses, axis=1))
    mass_sum = jnp.concatenate(sums, axis=0)
    return jnp.log1p(mass_sum)


def plain_plan(embeddings, cluster_ids):
    peer_count = lax.axis_size("gx")
    row_count = embeddings.shape[0]
    features = embeddings.shape[1]
    capacity = 3 * row_count // peer_count
    slot_total = peer_count * capacity
    squares = jnp.sum(jnp.square(embeddings.astype(jnp.float32)), axis=1)
    unit_rows = (embeddings.astype(jnp.float32) * lax.rsqrt(squares + 1e-06)[:, None]).astype(
        jnp.bfloat16
    )
    owner_of = cluster_ids // CLU_DEV
    onehot = (owner_of[:, None] == jnp.arange(peer_count, dtype=jnp.int32)[None, :]).astype(
        jnp.bfloat16
    )
    row_range = jnp.arange(row_count, dtype=jnp.int32)
    lower_tri = (row_range[:, None] >= row_range[None, :]).astype(jnp.bfloat16)
    running = jnp.dot(lower_tri, onehot, preferred_element_type=jnp.float32)
    slot_index = (jnp.sum(running * onehot.astype(jnp.float32), axis=1) - 1.0).astype(jnp.int32)
    target_slot = owner_of * capacity + slot_index
    slot_range = jnp.arange(slot_total, dtype=jnp.int32)
    select_mask = slot_range[:, None] == target_slot[None, :]
    outgoing = jnp.dot(
        select_mask.astype(jnp.bfloat16), unit_rows, preferred_element_type=jnp.float32
    )
    outgoing = outgoing.astype(jnp.bfloat16).reshape(peer_count, capacity, features)
    outgoing_ids = jnp.sum(jnp.where(select_mask, cluster_ids[None, :] + 1, 0), axis=1) - 1
    outgoing_ids = outgoing_ids.reshape(peer_count, capacity)
    arrived, arrived_ids = (
        lax.all_to_all(outgoing, "gx", split_axis=0, concat_axis=0, tiled=True),
        lax.all_to_all(outgoing_ids, "gx", split_axis=0, concat_axis=0, tiled=True),
    )
    key_rows = arrived.reshape(slot_total, features)
    key_ids = arrived_ids.reshape(slot_total)
    scores = density_scores(key_rows, key_ids)
    returned = lax.all_to_all(
        scores.reshape(peer_count, capacity), "gx", split_axis=0, concat_axis=0, tiled=True
    )
    flat_scores = returned.reshape(slot_total)
    pick_mask = target_slot[:, None] == slot_range[None, :]
    return jnp.sum(jnp.where(pick_mask, flat_scores[None, :], 0.0), axis=1)


LANES = 128
PLANE = 4
INVERSE_TEMP_BITS = 20.0 * 1.4426950408889634
ID_ROWS = 8
VMEM_BYTES = 16 * 1024 * 1024


def along_rows(values):
    return jnp.broadcast_to(values, (LANES, values.shape[1])).T


def ids_block(ids, width):
    wide = jnp.concatenate([ids, jnp.zeros((1, width - ids.shape[1]), jnp.float32)], axis=1)
    return jnp.broadcast_to(wide, (ID_ROWS, width)).astype(jnp.bfloat16)


def ids_of(ref):
    first = ref.shape[0] - ID_ROWS
    return ref[first:, :].astype(jnp.float32)[:1]


def mate_mass(query_rows, query_ids, key_rows, key_ids, shift=None):
    similar = lax.dot_general(
        query_rows, key_rows, (((1,), (1,)), ((), ())), preferred_element_type=jnp.float32
    )
    repeats = similar.shape[1] // LANES
    mates = jnp.concatenate([query_ids] * repeats, axis=1) == key_ids
    if shift is not None:
        query_pos = lax.broadcasted_iota(jnp.int32, similar.shape, 0) + shift
        key_pos = lax.broadcasted_iota(jnp.int32, similar.shape, 1)
        mates = mates & (query_pos != key_pos)
    return jnp.where(mates, jnp.exp2(similar * INVERSE_TEMP_BITS), 0.0)


def unit_rows(raw):
    features = raw.astype(jnp.float32)
    squares = jnp.sum(features * features, axis=1, keepdims=True)
    return (features * lax.rsqrt(squares + 1e-06)).astype(jnp.bfloat16)


def unit_kernel(ranges, rows_ref, ids_ref, *block_refs):
    rows, width = rows_ref.shape
    units = unit_rows(rows_ref[...])
    ids = ids_block(ids_ref[...].astype(jnp.float32), width)
    for (first, last), ref in zip(ranges, block_refs):
        size = last - first
        ref[:size, :] = units[first:last]
        if ref.shape[0] > size:
            ref[size:, :] = ids


def arrived_at(moves):
    plane = lax.axis_index("gx") // PLANE
    return functools.reduce(jnp.logical_or, [plane == receiver for _, receiver in moves])


def add_line(query_parts, ids_ref, key_rows, key_ids, earlier_ref, sums_ref):
    keys = key_rows.shape[0]
    column = jnp.zeros((1, keys), jnp.float32)
    first = 0
    for query_ref, size in query_parts:
        part = pl.ds(first, size)
        masses = mate_mass(query_ref[:size, :], ids_ref[part, :], key_rows, key_ids)
        column = column + jnp.sum(masses, axis=0, keepdims=True)
        folded = masses[:, :LANES]
        for lane in range(LANES, keys, LANES):
            folded = folded + masses[:, lane : lane + LANES]
        sums_ref[part, :] = folded if earlier_ref is None else earlier_ref[part, :] + folded
        first += size
    return column


def add_masses(query_ids, key_ids, powers):
    mates = jnp.concatenate([query_ids] * (powers.shape[1] // LANES), axis=1) == key_ids
    masses = jnp.where(mates, powers, 0.0)
    folded = masses[:, :LANES]
    for lane in range(LANES, powers.shape[1], LANES):
        folded = folded + masses[:, lane : lane + LANES]
    return folded, jnp.sum(masses, axis=0, keepdims=True)


def query_parts_of(refs, rows):
    head = refs[2].shape[0]
    sizes = [rows, rows] + [head, rows - head] * (PLANE - 2)
    return list(zip(refs, sizes))


def own_kernel(own_ref, mass_ref):
    rows = mass_ref.shape[1]
    own_ids = ids_of(own_ref)[:, :rows]
    masses = mate_mass(own_ref[:rows, :], along_rows(own_ids), own_ref[:rows, :], own_ids, 0)
    mass_ref[...] = jnp.sum(masses, axis=0, keepdims=True)


def first_kernel(moves, own_mass_ref, head_ref, tail_ref, *refs):
    query_refs, (ids_ref, column_ref, sums_ref, mass_ref) = refs[:-4], refs[-4:]
    rows = mass_ref.shape[1]
    query_parts = query_parts_of(query_refs, rows)
    own_ref = query_refs[0]
    own_ids = ids_of(own_ref)[:, :rows]
    for m, ref in enumerate((*query_refs[:2], query_refs[3], query_refs[5])):
        ids_ref[pl.ds(m * rows, rows), :] = along_rows(ids_of(ref)[:, :rows])
    mass = own_mass_ref[...]
    first = rows
    for ref, size in query_parts[1:]:
        query_ids = ids_ref[pl.ds(first, size), :]
        masses = mate_mass(ref[:size, :], query_ids, own_ref[:rows, :], own_ids)
        mass = mass + jnp.sum(masses, axis=0, keepdims=True)
        first += size
    mass_ref[...] = mass
    tail = tail_ref[: rows - head_ref.shape[0], :]
    key_rows = jnp.concatenate([unit_rows(head_ref[...]), tail], axis=0)
    key_ids = ids_of(tail_ref)[:, :rows]
    column_ref[...] = add_line(query_parts, ids_ref, key_rows, key_ids, None, sums_ref)


def middle_kernel(moves, head_ref, *refs):
    query_refs, (powers_ref, rest_ref) = refs[:-2], refs[-2:]

    @pl.when(arrived_at(moves))
    def _():
        keys = powers_ref.shape[1]
        units = unit_rows(head_ref[...])
        rest_ref[...] = units[keys:]
        first = 0
        for query_ref, size in query_parts_of(query_refs, query_refs[0].shape[0] - ID_ROWS):
            similar = lax.dot_general(
                query_ref[:size, :], units[:keys], (((1,), (1,)), ((), ())),
                preferred_element_type=jnp.float32,
            )
            powers_ref[pl.ds(first, size), :] = jnp.exp2(similar * INVERSE_TEMP_BITS)
            first += size


def last_kernel(moves, powers_ref, rest_ref, tail_ref, ids_ref, earlier_ref, *refs):
    query_refs, (column_ref, sums_ref) = refs[:-2], refs[-2:]
    rows = column_ref.shape[1]
    cut = powers_ref.shape[1]
    arrived = arrived_at(moves)

    @pl.when(arrived)
    def _():
        key_ids = ids_of(tail_ref)[:, :rows]
        key_rows = jnp.concatenate([rest_ref[...], tail_ref[: tail_ref.shape[0] - ID_ROWS, :]], axis=0)
        early_column = jnp.zeros((1, cut), jnp.float32)
        late_column = jnp.zeros((1, rows - cut), jnp.float32)
        first = 0
        for query_ref, size in query_parts_of(query_refs, rows):
            part = pl.ds(first, size)
            query_ids = ids_ref[part, :]
            similar = lax.dot_general(
                query_ref[:size, :], key_rows, (((1,), (1,)), ((), ())),
                preferred_element_type=jnp.float32,
            )
            powers = jnp.exp2(similar * INVERSE_TEMP_BITS)
            late, column = add_masses(query_ids, key_ids[:, cut:], powers)
            late_column = late_column + column
            early, column = add_masses(query_ids, key_ids[:, :cut], powers_ref[part, :])
            early_column = early_column + column
            sums_ref[part, :] = earlier_ref[part, :] + early + late
            first += size
        column_ref[...] = jnp.concatenate([early_column, late_column], axis=1)

    @pl.when(jnp.logical_not(arrived))
    def _():
        column_ref[...] = jnp.zeros_like(column_ref)
        sums_ref[...] = earlier_ref[...]


def fold_kernel(sums_ref, mass_ref, *row_refs):
    rows = mass_ref.shape[1]
    for m in range(PLANE):
        row_sum = jnp.sum(sums_ref[pl.ds(m * rows, rows), :].T, axis=0, keepdims=True)
        row_refs[m][...] = row_sum + mass_ref[...] if m == 0 else row_sum


def grid_plan(embeddings, cluster_ids):
    peers = lax.axis_size("gx")
    row_count, features = embeddings.shape
    plane_rows = PLANE * row_count
    params = pltpu.CompilerParams(vmem_limit_bytes=VMEM_BYTES)
    small = pl.CostEstimate(flops=1, bytes_accessed=1, transcendentals=0)
    vector = jax.ShapeDtypeStruct((1, row_count), jnp.float32)
    lanes = jax.ShapeDtypeStruct((plane_rows, LANES), jnp.float32)

    def rows_of(count):
        return jax.ShapeDtypeStruct((count, features), jnp.bfloat16)

    def in_plane(value, step):
        return lax.ppermute(value, "gx", [(i, i ^ step) for i in range(peers)])

    def on_line(value, moves, flip):
        pairs = [(a * PLANE + n, b * PLANE + (n ^ flip)) for a, b in moves for n in range(PLANE)]
        return lax.ppermute(value, "gx", pairs)

    first_moves = [(0, 1), (1, 2), (2, 3), (3, 0)]
    last_moves = [(0, 2), (1, 3)]
    forward_moves = [(1, 2), (2, 3)]
    first_back = [(b, a) for a, b in first_moves]
    last_back = [(b, a) for a, b in last_moves]

    half, part = row_count // 2, 5 * row_count // 8
    ranges = [(0, row_count), (0, half), (half, row_count), (part, row_count)]
    id_rows = [ID_ROWS, 0, ID_ROWS, ID_ROWS]
    first_head = on_line(embeddings[:part], first_moves, 1)
    block, *pieces, tail = pl.pallas_call(
        functools.partial(unit_kernel, ranges),
        out_shape=[rows_of(b - a + extra) for (a, b), extra in zip(ranges, id_rows)],
        cost_estimate=small,
        compiler_params=params,
    )(embeddings, cluster_ids.reshape(1, row_count))
    own_mass = pl.pallas_call(
        own_kernel, out_shape=vector, cost_estimate=small, compiler_params=params
    )(block)
    own_mass, tail = lax.optimization_barrier((own_mass, tail))
    first_tail = on_line(tail, first_moves, 1)
    across = [in_plane(piece, 2) for piece in pieces]
    sibling = in_plane(block, 1)
    last_head = on_line(first_head, first_moves, 1)
    last_tail = on_line(first_tail, forward_moves, 1)
    corner = [in_plane(piece, 1) for piece in across]
    queries = (block, sibling, *across, *corner)
    ids, first_column, first_sums, mass = pl.pallas_call(
        functools.partial(first_kernel, first_moves),
        out_shape=(lanes, vector, lanes, vector),
        cost_estimate=small,
        compiler_params=params,
    )(own_mass, first_head, first_tail, *queries)
    returned_first = on_line(first_column, first_back, 1)
    powers, rest = pl.pallas_call(
        functools.partial(middle_kernel, last_moves),
        out_shape=(
            jax.ShapeDtypeStruct((plane_rows, half), jnp.float32), rows_of(part - half)
        ),
        cost_estimate=small,
        compiler_params=params,
    )(last_head, *queries)
    last_column, sums = pl.pallas_call(
        functools.partial(last_kernel, last_moves),
        out_shape=(vector, lanes),
        cost_estimate=small,
        compiler_params=params,
    )(powers, rest, last_tail, ids, first_sums, *queries)
    returned_first, last_column = lax.optimization_barrier((returned_first, last_column))
    row_sums = pl.pallas_call(
        fold_kernel,
        out_shape=[vector] * PLANE,
        cost_estimate=small,
        compiler_params=params,
    )(sums, mass)
    returned = [on_line(last_column, last_back, 0)]
    returned += [in_plane(row_sums[step], step) for step in (2, 3, 1)]
    return jnp.log1p(sum(returned, row_sums[0] + returned_first)).reshape(row_count)


def on_device(embeddings, cluster_ids):
    if lax.axis_size("gx") == 4 * PLANE and embeddings.shape[0] == 2 * LANES:
        return grid_plan(embeddings, cluster_ids)
    return plain_plan(embeddings, cluster_ids)


def solution(mesh):
    in_specs = (P(("parts", "gx"), None), P(("parts", "gx")))
    out_specs = P(("parts", "gx"))
    return jax.shard_map(
        on_device, mesh=mesh, in_specs=in_specs, out_specs=out_specs, check_vma=False
    )
```

```python
import functools

import jax
import jax.numpy as jnp
from jax import lax
from jax.experimental import pallas as pl
from jax.experimental.pallas import tpu as pltpu
from jax.sharding import PartitionSpec as P

CLU_DEV = 1
PAD_MARK = 64.0
inverse_temp = 20.0


def tile_mass(query_rows, key_rows, query_ids, key_ids, query_start):
    similar = lax.dot_general(
        query_rows, key_rows, (((1,), (1,)), ((), ())), preferred_element_type=jnp.float32
    )
    query_pos = jnp.arange(query_rows.shape[0], dtype=jnp.int32) + query_start
    key_pos = jnp.arange(key_rows.shape[0], dtype=jnp.int32)
    mate_mask = (query_ids[:, None] == key_ids[None, :]) & (query_ids[:, None] >= 0)
    mate_mask = mate_mask & (query_pos[:, None] != key_pos[None, :])
    return jnp.where(mate_mask, jnp.exp(similar * inverse_temp), 0.0)


def density_scores(key_rows, key_ids):
    total_rows = key_rows.shape[0]
    block_rows = total_rows // 3
    pieces = [key_rows[i * block_rows : (i + 1) * block_rows] for i in range(3)]
    piece_ids = [key_ids[i * block_rows : (i + 1) * block_rows] for i in range(3)]
    sums = []
    for first in range(3):
        masses = tile_mass(pieces[first], key_rows, piece_ids[first], key_ids, first * block_rows)
        sums.append(jnp.sum(masses, axis=1))
    mass_sum = jnp.concatenate(sums, axis=0)
    return jnp.log1p(mass_sum)


def plain_plan(embeddings, cluster_ids):
    peer_count = lax.axis_size("gx")
    row_count = embeddings.shape[0]
    features = embeddings.shape[1]
    capacity = 3 * row_count // peer_count
    slot_total = peer_count * capacity
    squares = jnp.sum(jnp.square(embeddings.astype(jnp.float32)), axis=1)
    unit_rows = (embeddings.astype(jnp.float32) * lax.rsqrt(squares + 1e-06)[:, None]).astype(
        jnp.bfloat16
    )
    owner_of = cluster_ids // CLU_DEV
    onehot = (owner_of[:, None] == jnp.arange(peer_count, dtype=jnp.int32)[None, :]).astype(
        jnp.bfloat16
    )
    row_range = jnp.arange(row_count, dtype=jnp.int32)
    lower_tri = (row_range[:, None] >= row_range[None, :]).astype(jnp.bfloat16)
    running = jnp.dot(lower_tri, onehot, preferred_element_type=jnp.float32)
    slot_index = (jnp.sum(running * onehot.astype(jnp.float32), axis=1) - 1.0).astype(jnp.int32)
    target_slot = owner_of * capacity + slot_index
    slot_range = jnp.arange(slot_total, dtype=jnp.int32)
    select_mask = slot_range[:, None] == target_slot[None, :]
    outgoing = jnp.dot(
        select_mask.astype(jnp.bfloat16), unit_rows, preferred_element_type=jnp.float32
    )
    outgoing = outgoing.astype(jnp.bfloat16).reshape(peer_count, capacity, features)
    outgoing_ids = jnp.sum(jnp.where(select_mask, cluster_ids[None, :] + 1, 0), axis=1) - 1
    outgoing_ids = outgoing_ids.reshape(peer_count, capacity)
    arrived, arrived_ids = (
        lax.all_to_all(outgoing, "gx", split_axis=0, concat_axis=0, tiled=True),
        lax.all_to_all(outgoing_ids, "gx", split_axis=0, concat_axis=0, tiled=True),
    )
    key_rows = arrived.reshape(slot_total, features)
    key_ids = arrived_ids.reshape(slot_total)
    scores = density_scores(key_rows, key_ids)
    returned = lax.all_to_all(
        scores.reshape(peer_count, capacity), "gx", split_axis=0, concat_axis=0, tiled=True
    )
    flat_scores = returned.reshape(slot_total)
    pick_mask = target_slot[:, None] == slot_range[None, :]
    return jnp.sum(jnp.where(pick_mask, flat_scores[None, :], 0.0), axis=1)


LANES = 128
PLANE = 4
INVERSE_TEMP_BITS = 20.0 * 1.4426950408889634
ID_ROWS = 8
VMEM_BYTES = 16 * 1024 * 1024


def along_rows(values):
    return jnp.broadcast_to(values, (LANES, values.shape[1])).T


def ids_block(ids, width):
    wide = jnp.concatenate([ids, jnp.zeros((1, width - ids.shape[1]), jnp.float32)], axis=1)
    return jnp.broadcast_to(wide, (ID_ROWS, width)).astype(jnp.bfloat16)


def ids_of(ref):
    first = ref.shape[0] - ID_ROWS
    return ref[first:, :].astype(jnp.float32)[:1]


def mate_mass(query_rows, query_ids, key_rows, key_ids, shift=None):
    similar = lax.dot_general(
        query_rows, key_rows, (((1,), (1,)), ((), ())), preferred_element_type=jnp.float32
    )
    repeats = similar.shape[1] // LANES
    mates = jnp.concatenate([query_ids] * repeats, axis=1) == key_ids
    if shift is not None:
        query_pos = lax.broadcasted_iota(jnp.int32, similar.shape, 0) + shift
        key_pos = lax.broadcasted_iota(jnp.int32, similar.shape, 1)
        mates = mates & (query_pos != key_pos)
    return jnp.where(mates, jnp.exp2(similar * INVERSE_TEMP_BITS), 0.0)


def unit_rows(raw):
    features = raw.astype(jnp.float32)
    squares = jnp.sum(features * features, axis=1, keepdims=True)
    return (features * lax.rsqrt(squares + 1e-06)).astype(jnp.bfloat16)


def unit_kernel(ranges, rows_ref, ids_ref, *block_refs):
    rows, width = rows_ref.shape
    units = unit_rows(rows_ref[...])
    ids = ids_block(ids_ref[...].astype(jnp.float32), width)
    for (first, last), ref in zip(ranges, block_refs):
        size = last - first
        ref[:size, :] = units[first:last]
        if ref.shape[0] > size:
            ref[size:, :] = ids


def arrived_at(moves):
    plane = lax.axis_index("gx") // PLANE
    return functools.reduce(jnp.logical_or, [plane == receiver for _, receiver in moves])


def add_line(query_parts, ids_ref, key_rows, key_ids, earlier_ref, sums_ref):
    keys = key_rows.shape[0]
    column = jnp.zeros((1, keys), jnp.float32)
    first = 0
    for query_ref, size in query_parts:
        part = pl.ds(first, size)
        masses = mate_mass(query_ref[:size, :], ids_ref[part, :], key_rows, key_ids)
        column = column + jnp.sum(masses, axis=0, keepdims=True)
        folded = masses[:, :LANES]
        for lane in range(LANES, keys, LANES):
            folded = folded + masses[:, lane : lane + LANES]
        sums_ref[part, :] = folded if earlier_ref is None else earlier_ref[part, :] + folded
        first += size
    return column


def add_masses(query_ids, key_ids, powers):
    mates = jnp.concatenate([query_ids] * (powers.shape[1] // LANES), axis=1) == key_ids
    masses = jnp.where(mates, powers, 0.0)
    folded = masses[:, :LANES]
    for lane in range(LANES, powers.shape[1], LANES):
        folded = folded + masses[:, lane : lane + LANES]
    return folded, jnp.sum(masses, axis=0, keepdims=True)


def query_parts_of(refs, rows):
    head = refs[2].shape[0]
    sizes = [rows, rows] + [head, rows - head] * (PLANE - 2)
    return list(zip(refs, sizes))


def own_kernel(own_ref, mass_ref):
    rows = mass_ref.shape[1]
    own_ids = ids_of(own_ref)[:, :rows]
    masses = mate_mass(own_ref[:rows, :], along_rows(own_ids), own_ref[:rows, :], own_ids, 0)
    mass_ref[...] = jnp.sum(masses, axis=0, keepdims=True)


def first_kernel(moves, own_mass_ref, head_ref, tail_ref, *refs):
    query_refs, (ids_ref, column_ref, sums_ref, mass_ref) = refs[:-4], refs[-4:]
    rows = mass_ref.shape[1]
    query_parts = query_parts_of(query_refs, rows)
    own_ref = query_refs[0]
    own_ids = ids_of(own_ref)[:, :rows]
    for m, ref in enumerate((*query_refs[:2], query_refs[3], query_refs[5])):
        ids_ref[pl.ds(m * rows, rows), :] = along_rows(ids_of(ref)[:, :rows])
    mass = own_mass_ref[...]
    first = rows
    for ref, size in query_parts[1:]:
        query_ids = ids_ref[pl.ds(first, size), :]
        masses = mate_mass(ref[:size, :], query_ids, own_ref[:rows, :], own_ids)
        mass = mass + jnp.sum(masses, axis=0, keepdims=True)
        first += size
    mass_ref[...] = mass
    tail = tail_ref[: rows - head_ref.shape[0], :]
    key_rows = jnp.concatenate([unit_rows(head_ref[...]), tail], axis=0)
    key_ids = ids_of(tail_ref)[:, :rows]
    column_ref[...] = add_line(query_parts, ids_ref, key_rows, key_ids, None, sums_ref)


def middle_kernel(moves, head_ref, *refs):
    query_refs, (powers_ref, rest_ref) = refs[:-2], refs[-2:]

    @pl.when(arrived_at(moves))
    def _():
        keys = powers_ref.shape[1]
        units = unit_rows(head_ref[...])
        rest_ref[...] = units[keys:]
        first = 0
        for query_ref, size in query_parts_of(query_refs, query_refs[0].shape[0] - ID_ROWS):
            similar = lax.dot_general(
                query_ref[:size, :], units[:keys], (((1,), (1,)), ((), ())),
                preferred_element_type=jnp.float32,
            )
            powers_ref[pl.ds(first, size), :] = jnp.exp2(similar * INVERSE_TEMP_BITS)
            first += size


def last_kernel(moves, powers_ref, rest_ref, tail_ref, ids_ref, earlier_ref, *refs):
    query_refs, (column_ref, sums_ref) = refs[:-2], refs[-2:]
    rows = column_ref.shape[1]
    cut = powers_ref.shape[1]
    arrived = arrived_at(moves)

    @pl.when(arrived)
    def _():
        key_ids = ids_of(tail_ref)[:, :rows]
        key_rows = jnp.concatenate([rest_ref[...], tail_ref[: tail_ref.shape[0] - ID_ROWS, :]], axis=0)
        early_column = jnp.zeros((1, cut), jnp.float32)
        late_column = jnp.zeros((1, rows - cut), jnp.float32)
        first = 0
        for query_ref, size in query_parts_of(query_refs, rows):
            part = pl.ds(first, size)
            query_ids = ids_ref[part, :]
            similar = lax.dot_general(
                query_ref[:size, :], key_rows, (((1,), (1,)), ((), ())),
                preferred_element_type=jnp.float32,
            )
            powers = jnp.exp2(similar * INVERSE_TEMP_BITS)
            late, column = add_masses(query_ids, key_ids[:, cut:], powers)
            late_column = late_column + column
            early, column = add_masses(query_ids, key_ids[:, :cut], powers_ref[part, :])
            early_column = early_column + column
            sums_ref[part, :] = earlier_ref[part, :] + early + late
            first += size
        column_ref[...] = jnp.concatenate([early_column, late_column], axis=1)

    @pl.when(jnp.logical_not(arrived))
    def _():
        column_ref[...] = jnp.zeros_like(column_ref)
        sums_ref[...] = earlier_ref[...]


def fold_kernel(sums_ref, mass_ref, *row_refs):
    rows = mass_ref.shape[1]
    for m in range(PLANE):
        row_sum = jnp.sum(sums_ref[pl.ds(m * rows, rows), :].T, axis=0, keepdims=True)
        row_refs[m][...] = row_sum + mass_ref[...] if m == 0 else row_sum


def grid_plan(embeddings, cluster_ids):
    peers = lax.axis_size("gx")
    row_count, features = embeddings.shape
    plane_rows = PLANE * row_count
    params = pltpu.CompilerParams(vmem_limit_bytes=VMEM_BYTES)
    small = pl.CostEstimate(flops=1, bytes_accessed=1, transcendentals=0)
    vector = jax.ShapeDtypeStruct((1, row_count), jnp.float32)
    lanes = jax.ShapeDtypeStruct((plane_rows, LANES), jnp.float32)

    def rows_of(count):
        return jax.ShapeDtypeStruct((count, features), jnp.bfloat16)

    def in_plane(value, step):
        return lax.ppermute(value, "gx", [(i, i ^ step) for i in range(peers)])

    def on_line(value, moves, flip):
        pairs = [(a * PLANE + n, b * PLANE + (n ^ flip)) for a, b in moves for n in range(PLANE)]
        return lax.ppermute(value, "gx", pairs)

    first_moves = [(0, 1), (1, 2), (2, 3), (3, 0)]
    last_moves = [(0, 2), (1, 3)]
    forward_moves = [(1, 2), (2, 3)]
    first_back = [(b, a) for a, b in first_moves]
    last_back = [(b, a) for a, b in last_moves]

    half, part = row_count // 2, 5 * row_count // 8
    ranges = [(0, row_count), (0, half), (half, row_count), (part, row_count)]
    id_rows = [ID_ROWS, 0, ID_ROWS, ID_ROWS]
    first_head = on_line(embeddings[:part], first_moves, 0)
    block, *pieces, tail = pl.pallas_call(
        functools.partial(unit_kernel, ranges),
        out_shape=[rows_of(b - a + extra) for (a, b), extra in zip(ranges, id_rows)],
        cost_estimate=small,
        compiler_params=params,
    )(embeddings, cluster_ids.reshape(1, row_count))
    own_mass = pl.pallas_call(
        own_kernel, out_shape=vector, cost_estimate=small, compiler_params=params
    )(block)
    own_mass, tail = lax.optimization_barrier((own_mass, tail))
    first_tail = on_line(tail, first_moves, 0)
    across = [in_plane(piece, 2) for piece in pieces]
    sibling = in_plane(block, 1)
    last_head = on_line(first_head, first_moves, 1)
    last_tail = on_line(first_tail, forward_moves, 1)
    corner = [in_plane(piece, 1) for piece in across]
    queries = (block, sibling, *across, *corner)
    ids, first_column, first_sums, mass = pl.pallas_call(
        functools.partial(first_kernel, first_moves),
        out_shape=(lanes, vector, lanes, vector),
        cost_estimate=small,
        compiler_params=params,
    )(own_mass, first_head, first_tail, *queries)
    returned_first = on_line(first_column, first_back, 0)
    powers, rest = pl.pallas_call(
        functools.partial(middle_kernel, last_moves),
        out_shape=(
            jax.ShapeDtypeStruct((plane_rows, half), jnp.float32), rows_of(part - half)
        ),
        cost_estimate=small,
        compiler_params=params,
    )(last_head, *queries)
    last_column, sums = pl.pallas_call(
        functools.partial(last_kernel, last_moves),
        out_shape=(vector, lanes),
        cost_estimate=small,
        compiler_params=params,
    )(powers, rest, last_tail, ids, first_sums, *queries)
    returned_first, last_column = lax.optimization_barrier((returned_first, last_column))
    row_sums = pl.pallas_call(
        fold_kernel,
        out_shape=[vector] * PLANE,
        cost_estimate=small,
        compiler_params=params,
    )(sums, mass)
    returned = [on_line(last_column, last_back, 1)]
    returned += [in_plane(row_sums[step], step) for step in (2, 3, 1)]
    return jnp.log1p(sum(returned, row_sums[0] + returned_first)).reshape(row_count)


def on_device(embeddings, cluster_ids):
    if lax.axis_size("gx") == 4 * PLANE and embeddings.shape[0] == 2 * LANES:
        return grid_plan(embeddings, cluster_ids)
    return plain_plan(embeddings, cluster_ids)


def solution(mesh):
    in_specs = (P(("parts", "gx"), None), P(("parts", "gx")))
    out_specs = P(("parts", "gx"))
    return jax.shard_map(
        on_device, mesh=mesh, in_specs=in_specs, out_specs=out_specs, check_vma=False
    )
```

```python
import functools

import jax
import jax.numpy as jnp
from jax import lax
from jax.experimental import pallas as pl
from jax.experimental.pallas import tpu as pltpu
from jax.sharding import PartitionSpec as P

CLU_DEV = 1
PAD_MARK = 64.0
inverse_temp = 20.0


def tile_mass(query_rows, key_rows, query_ids, key_ids, query_start):
    similar = lax.dot_general(
        query_rows, key_rows, (((1,), (1,)), ((), ())), preferred_element_type=jnp.float32
    )
    query_pos = jnp.arange(query_rows.shape[0], dtype=jnp.int32) + query_start
    key_pos = jnp.arange(key_rows.shape[0], dtype=jnp.int32)
    mate_mask = (query_ids[:, None] == key_ids[None, :]) & (query_ids[:, None] >= 0)
    mate_mask = mate_mask & (query_pos[:, None] != key_pos[None, :])
    return jnp.where(mate_mask, jnp.exp(similar * inverse_temp), 0.0)


def density_scores(key_rows, key_ids):
    total_rows = key_rows.shape[0]
    block_rows = total_rows // 3
    pieces = [key_rows[i * block_rows : (i + 1) * block_rows] for i in range(3)]
    piece_ids = [key_ids[i * block_rows : (i + 1) * block_rows] for i in range(3)]
    sums = []
    for first in range(3):
        masses = tile_mass(pieces[first], key_rows, piece_ids[first], key_ids, first * block_rows)
        sums.append(jnp.sum(masses, axis=1))
    mass_sum = jnp.concatenate(sums, axis=0)
    return jnp.log1p(mass_sum)


def plain_plan(embeddings, cluster_ids):
    peer_count = lax.axis_size("gx")
    row_count = embeddings.shape[0]
    features = embeddings.shape[1]
    capacity = 3 * row_count // peer_count
    slot_total = peer_count * capacity
    squares = jnp.sum(jnp.square(embeddings.astype(jnp.float32)), axis=1)
    unit_rows = (embeddings.astype(jnp.float32) * lax.rsqrt(squares + 1e-06)[:, None]).astype(
        jnp.bfloat16
    )
    owner_of = cluster_ids // CLU_DEV
    onehot = (owner_of[:, None] == jnp.arange(peer_count, dtype=jnp.int32)[None, :]).astype(
        jnp.bfloat16
    )
    row_range = jnp.arange(row_count, dtype=jnp.int32)
    lower_tri = (row_range[:, None] >= row_range[None, :]).astype(jnp.bfloat16)
    running = jnp.dot(lower_tri, onehot, preferred_element_type=jnp.float32)
    slot_index = (jnp.sum(running * onehot.astype(jnp.float32), axis=1) - 1.0).astype(jnp.int32)
    target_slot = owner_of * capacity + slot_index
    slot_range = jnp.arange(slot_total, dtype=jnp.int32)
    select_mask = slot_range[:, None] == target_slot[None, :]
    outgoing = jnp.dot(
        select_mask.astype(jnp.bfloat16), unit_rows, preferred_element_type=jnp.float32
    )
    outgoing = outgoing.astype(jnp.bfloat16).reshape(peer_count, capacity, features)
    outgoing_ids = jnp.sum(jnp.where(select_mask, cluster_ids[None, :] + 1, 0), axis=1) - 1
    outgoing_ids = outgoing_ids.reshape(peer_count, capacity)
    arrived, arrived_ids = (
        lax.all_to_all(outgoing, "gx", split_axis=0, concat_axis=0, tiled=True),
        lax.all_to_all(outgoing_ids, "gx", split_axis=0, concat_axis=0, tiled=True),
    )
    key_rows = arrived.reshape(slot_total, features)
    key_ids = arrived_ids.reshape(slot_total)
    scores = density_scores(key_rows, key_ids)
    returned = lax.all_to_all(
        scores.reshape(peer_count, capacity), "gx", split_axis=0, concat_axis=0, tiled=True
    )
    flat_scores = returned.reshape(slot_total)
    pick_mask = target_slot[:, None] == slot_range[None, :]
    return jnp.sum(jnp.where(pick_mask, flat_scores[None, :], 0.0), axis=1)


LANES = 128
PLANE = 4
INVERSE_TEMP_BITS = 20.0 * 1.4426950408889634
ID_ROWS = 8
VMEM_BYTES = 16 * 1024 * 1024


def along_rows(values):
    return jnp.broadcast_to(values, (LANES, values.shape[1])).T


def ids_block(ids, width):
    wide = jnp.concatenate([ids, jnp.zeros((1, width - ids.shape[1]), jnp.float32)], axis=1)
    return jnp.broadcast_to(wide, (ID_ROWS, width)).astype(jnp.bfloat16)


def ids_of(ref):
    first = ref.shape[0] - ID_ROWS
    return ref[first:, :].astype(jnp.float32)[:1]


def mate_mass(query_rows, query_ids, key_rows, key_ids, shift=None):
    similar = lax.dot_general(
        query_rows, key_rows, (((1,), (1,)), ((), ())), preferred_element_type=jnp.float32
    )
    repeats = similar.shape[1] // LANES
    mates = jnp.concatenate([query_ids] * repeats, axis=1) == key_ids
    if shift is not None:
        query_pos = lax.broadcasted_iota(jnp.int32, similar.shape, 0) + shift
        key_pos = lax.broadcasted_iota(jnp.int32, similar.shape, 1)
        mates = mates & (query_pos != key_pos)
    return jnp.where(mates, jnp.exp2(similar * INVERSE_TEMP_BITS), 0.0)


def unit_rows(raw):
    features = raw.astype(jnp.float32)
    squares = jnp.sum(features * features, axis=1, keepdims=True)
    return (features * lax.rsqrt(squares + 1e-06)).astype(jnp.bfloat16)


def unit_kernel(ranges, rows_ref, ids_ref, *block_refs):
    rows, width = rows_ref.shape
    units = unit_rows(rows_ref[...])
    ids = ids_block(ids_ref[...].astype(jnp.float32), width)
    for (first, last), ref in zip(ranges, block_refs):
        size = last - first
        ref[:size, :] = units[first:last]
        if ref.shape[0] > size:
            ref[size:, :] = ids


def arrived_at(moves):
    plane = lax.axis_index("gx") // PLANE
    return functools.reduce(jnp.logical_or, [plane == receiver for _, receiver in moves])


def add_line(query_parts, ids_ref, key_rows, key_ids, earlier_ref, sums_ref):
    keys = key_rows.shape[0]
    column = jnp.zeros((1, keys), jnp.float32)
    first = 0
    for query_ref, size in query_parts:
        part = pl.ds(first, size)
        masses = mate_mass(query_ref[:size, :], ids_ref[part, :], key_rows, key_ids)
        column = column + jnp.sum(masses, axis=0, keepdims=True)
        folded = masses[:, :LANES]
        for lane in range(LANES, keys, LANES):
            folded = folded + masses[:, lane : lane + LANES]
        sums_ref[part, :] = folded if earlier_ref is None else earlier_ref[part, :] + folded
        first += size
    return column


def add_masses(query_ids, key_ids, powers):
    mates = jnp.concatenate([query_ids] * (powers.shape[1] // LANES), axis=1) == key_ids
    masses = jnp.where(mates, powers, 0.0)
    folded = masses[:, :LANES]
    for lane in range(LANES, powers.shape[1], LANES):
        folded = folded + masses[:, lane : lane + LANES]
    return folded, jnp.sum(masses, axis=0, keepdims=True)


def query_parts_of(refs, rows):
    head = refs[2].shape[0]
    sizes = [rows, rows] + [head, rows - head] * (PLANE - 2)
    return list(zip(refs, sizes))


def own_kernel(own_ref, mass_ref):
    rows = mass_ref.shape[1]
    own_ids = ids_of(own_ref)[:, :rows]
    masses = mate_mass(own_ref[:rows, :], along_rows(own_ids), own_ref[:rows, :], own_ids, 0)
    mass_ref[...] = jnp.sum(masses, axis=0, keepdims=True)


def first_kernel(moves, own_mass_ref, head_ref, tail_ref, *refs):
    query_refs, (ids_ref, column_ref, sums_ref, mass_ref) = refs[:-4], refs[-4:]
    rows = mass_ref.shape[1]
    query_parts = query_parts_of(query_refs, rows)
    own_ref = query_refs[0]
    own_ids = ids_of(own_ref)[:, :rows]
    for m, ref in enumerate((*query_refs[:2], query_refs[3], query_refs[5])):
        ids_ref[pl.ds(m * rows, rows), :] = along_rows(ids_of(ref)[:, :rows])
    mass = own_mass_ref[...]
    first = rows
    for ref, size in query_parts[1:]:
        query_ids = ids_ref[pl.ds(first, size), :]
        masses = mate_mass(ref[:size, :], query_ids, own_ref[:rows, :], own_ids)
        mass = mass + jnp.sum(masses, axis=0, keepdims=True)
        first += size
    mass_ref[...] = mass
    tail = tail_ref[: rows - head_ref.shape[0], :]
    key_rows = jnp.concatenate([unit_rows(head_ref[...]), tail], axis=0)
    key_ids = ids_of(tail_ref)[:, :rows]
    column_ref[...] = add_line(query_parts, ids_ref, key_rows, key_ids, None, sums_ref)


def middle_kernel(moves, head_ref, *refs):
    query_refs, (queries_ref, powers_ref, rest_ref) = refs[:-3], refs[-3:]

    @pl.when(arrived_at(moves))
    def _():
        keys = powers_ref.shape[1]
        units = unit_rows(head_ref[...])
        rest_ref[...] = units[keys:]
        first = 0
        for query_ref, size in query_parts_of(query_refs, query_refs[0].shape[0] - ID_ROWS):
            queries_ref[pl.ds(first, size), :] = query_ref[:size, :]
            first += size
        similar = lax.dot_general(
            queries_ref[...], units[:keys], (((1,), (1,)), ((), ())),
            preferred_element_type=jnp.float32,
        )
        powers_ref[...] = jnp.exp2(similar * INVERSE_TEMP_BITS)


def last_kernel(moves, queries_ref, powers_ref, rest_ref, tail_ref, ids_ref, earlier_ref, *refs):
    column_ref, sums_ref = refs
    rows = column_ref.shape[1]
    cut = powers_ref.shape[1]
    arrived = arrived_at(moves)

    @pl.when(arrived)
    def _():
        key_ids = ids_of(tail_ref)[:, :rows]
        tail = tail_ref[: tail_ref.shape[0] - ID_ROWS, :]
        key_rows = jnp.concatenate([rest_ref[...], tail], axis=0)
        similar = lax.dot_general(
            queries_ref[...], key_rows, (((1,), (1,)), ((), ())),
            preferred_element_type=jnp.float32,
        )
        query_ids = ids_ref[...]
        powers = jnp.exp2(similar * INVERSE_TEMP_BITS)
        late, late_column = add_masses(query_ids, key_ids[:, cut:], powers)
        early, early_column = add_masses(query_ids, key_ids[:, :cut], powers_ref[...])
        sums_ref[...] = earlier_ref[...] + early + late
        column_ref[...] = jnp.concatenate([early_column, late_column], axis=1)

    @pl.when(jnp.logical_not(arrived))
    def _():
        column_ref[...] = jnp.zeros_like(column_ref)
        sums_ref[...] = earlier_ref[...]


def fold_kernel(sums_ref, mass_ref, *row_refs):
    rows = mass_ref.shape[1]
    for m in range(PLANE):
        row_sum = jnp.sum(sums_ref[pl.ds(m * rows, rows), :].T, axis=0, keepdims=True)
        row_refs[m][...] = row_sum + mass_ref[...] if m == 0 else row_sum


def grid_plan(embeddings, cluster_ids):
    peers = lax.axis_size("gx")
    row_count, features = embeddings.shape
    plane_rows = PLANE * row_count
    params = pltpu.CompilerParams(vmem_limit_bytes=VMEM_BYTES)
    small = pl.CostEstimate(flops=1, bytes_accessed=1, transcendentals=0)
    vector = jax.ShapeDtypeStruct((1, row_count), jnp.float32)
    lanes = jax.ShapeDtypeStruct((plane_rows, LANES), jnp.float32)

    def rows_of(count):
        return jax.ShapeDtypeStruct((count, features), jnp.bfloat16)

    def in_plane(value, step):
        return lax.ppermute(value, "gx", [(i, i ^ step) for i in range(peers)])

    def on_line(value, moves, flip):
        pairs = [(a * PLANE + n, b * PLANE + (n ^ flip)) for a, b in moves for n in range(PLANE)]
        return lax.ppermute(value, "gx", pairs)

    first_moves = [(0, 1), (1, 2), (2, 3), (3, 0)]
    last_moves = [(0, 2), (1, 3)]
    forward_moves = [(1, 2), (2, 3)]
    first_back = [(b, a) for a, b in first_moves]
    last_back = [(b, a) for a, b in last_moves]

    half, part = row_count // 2, 5 * row_count // 8
    ranges = [(0, row_count), (0, half), (half, row_count), (part, row_count)]
    id_rows = [ID_ROWS, 0, ID_ROWS, ID_ROWS]
    first_head = on_line(embeddings[:part], first_moves, 0)
    block, *pieces, tail = pl.pallas_call(
        functools.partial(unit_kernel, ranges),
        out_shape=[rows_of(b - a + extra) for (a, b), extra in zip(ranges, id_rows)],
        cost_estimate=small,
        compiler_params=params,
    )(embeddings, cluster_ids.reshape(1, row_count))
    own_mass = pl.pallas_call(
        own_kernel, out_shape=vector, cost_estimate=small, compiler_params=params
    )(block)
    own_mass, tail = lax.optimization_barrier((own_mass, tail))
    first_tail = on_line(tail, first_moves, 0)
    across = [in_plane(piece, 2) for piece in pieces]
    sibling = in_plane(block, 1)
    last_head = on_line(first_head, first_moves, 1)
    last_tail = on_line(first_tail, forward_moves, 1)
    corner = [in_plane(piece, 1) for piece in across]
    queries = (block, sibling, *across, *corner)
    ids, first_column, first_sums, mass = pl.pallas_call(
        functools.partial(first_kernel, first_moves),
        out_shape=(lanes, vector, lanes, vector),
        cost_estimate=small,
        compiler_params=params,
    )(own_mass, first_head, first_tail, *queries)
    returned_first = on_line(first_column, first_back, 0)
    plane_queries, powers, rest = pl.pallas_call(
        functools.partial(middle_kernel, last_moves),
        out_shape=(
            rows_of(plane_rows),
            jax.ShapeDtypeStruct((plane_rows, half), jnp.float32),
            rows_of(part - half),
        ),
        cost_estimate=small,
        compiler_params=params,
    )(last_head, *queries)
    last_column, sums = pl.pallas_call(
        functools.partial(last_kernel, last_moves),
        out_shape=(vector, lanes),
        cost_estimate=small,
        compiler_params=params,
    )(plane_queries, powers, rest, last_tail, ids, first_sums)
    returned_first, last_column = lax.optimization_barrier((returned_first, last_column))
    row_sums = pl.pallas_call(
        fold_kernel,
        out_shape=[vector] * PLANE,
        cost_estimate=small,
        compiler_params=params,
    )(sums, mass)
    returned = [on_line(last_column, last_back, 1)]
    returned += [in_plane(row_sums[step], step) for step in (2, 3, 1)]
    return jnp.log1p(sum(returned, row_sums[0] + returned_first)).reshape(row_count)


def on_device(embeddings, cluster_ids):
    if lax.axis_size("gx") == 4 * PLANE and embeddings.shape[0] == 2 * LANES:
        return grid_plan(embeddings, cluster_ids)
    return plain_plan(embeddings, cluster_ids)


def solution(mesh):
    in_specs = (P(("parts", "gx"), None), P(("parts", "gx")))
    out_specs = P(("parts", "gx"))
    return jax.shard_map(
        on_device, mesh=mesh, in_specs=in_specs, out_specs=out_specs, check_vma=False
    )
```

```python
import functools

import jax
import jax.numpy as jnp
from jax import lax
from jax.experimental import pallas as pl
from jax.experimental.pallas import tpu as pltpu
from jax.sharding import PartitionSpec as P

CLU_DEV = 1
PAD_MARK = 64.0
inverse_temp = 20.0


def tile_mass(query_rows, key_rows, query_ids, key_ids, query_start):
    similar = lax.dot_general(
        query_rows, key_rows, (((1,), (1,)), ((), ())), preferred_element_type=jnp.float32
    )
    query_pos = jnp.arange(query_rows.shape[0], dtype=jnp.int32) + query_start
    key_pos = jnp.arange(key_rows.shape[0], dtype=jnp.int32)
    mate_mask = (query_ids[:, None] == key_ids[None, :]) & (query_ids[:, None] >= 0)
    mate_mask = mate_mask & (query_pos[:, None] != key_pos[None, :])
    return jnp.where(mate_mask, jnp.exp(similar * inverse_temp), 0.0)


def density_scores(key_rows, key_ids):
    total_rows = key_rows.shape[0]
    block_rows = total_rows // 3
    pieces = [key_rows[i * block_rows : (i + 1) * block_rows] for i in range(3)]
    piece_ids = [key_ids[i * block_rows : (i + 1) * block_rows] for i in range(3)]
    sums = []
    for first in range(3):
        masses = tile_mass(pieces[first], key_rows, piece_ids[first], key_ids, first * block_rows)
        sums.append(jnp.sum(masses, axis=1))
    mass_sum = jnp.concatenate(sums, axis=0)
    return jnp.log1p(mass_sum)


def plain_plan(embeddings, cluster_ids):
    peer_count = lax.axis_size("gx")
    row_count = embeddings.shape[0]
    features = embeddings.shape[1]
    capacity = 3 * row_count // peer_count
    slot_total = peer_count * capacity
    squares = jnp.sum(jnp.square(embeddings.astype(jnp.float32)), axis=1)
    unit_rows = (embeddings.astype(jnp.float32) * lax.rsqrt(squares + 1e-06)[:, None]).astype(
        jnp.bfloat16
    )
    owner_of = cluster_ids // CLU_DEV
    onehot = (owner_of[:, None] == jnp.arange(peer_count, dtype=jnp.int32)[None, :]).astype(
        jnp.bfloat16
    )
    row_range = jnp.arange(row_count, dtype=jnp.int32)
    lower_tri = (row_range[:, None] >= row_range[None, :]).astype(jnp.bfloat16)
    running = jnp.dot(lower_tri, onehot, preferred_element_type=jnp.float32)
    slot_index = (jnp.sum(running * onehot.astype(jnp.float32), axis=1) - 1.0).astype(jnp.int32)
    target_slot = owner_of * capacity + slot_index
    slot_range = jnp.arange(slot_total, dtype=jnp.int32)
    select_mask = slot_range[:, None] == target_slot[None, :]
    outgoing = jnp.dot(
        select_mask.astype(jnp.bfloat16), unit_rows, preferred_element_type=jnp.float32
    )
    outgoing = outgoing.astype(jnp.bfloat16).reshape(peer_count, capacity, features)
    outgoing_ids = jnp.sum(jnp.where(select_mask, cluster_ids[None, :] + 1, 0), axis=1) - 1
    outgoing_ids = outgoing_ids.reshape(peer_count, capacity)
    arrived, arrived_ids = (
        lax.all_to_all(outgoing, "gx", split_axis=0, concat_axis=0, tiled=True),
        lax.all_to_all(outgoing_ids, "gx", split_axis=0, concat_axis=0, tiled=True),
    )
    key_rows = arrived.reshape(slot_total, features)
    key_ids = arrived_ids.reshape(slot_total)
    scores = density_scores(key_rows, key_ids)
    returned = lax.all_to_all(
        scores.reshape(peer_count, capacity), "gx", split_axis=0, concat_axis=0, tiled=True
    )
    flat_scores = returned.reshape(slot_total)
    pick_mask = target_slot[:, None] == slot_range[None, :]
    return jnp.sum(jnp.where(pick_mask, flat_scores[None, :], 0.0), axis=1)


LANES = 128
PLANE = 4
INVERSE_TEMP_BITS = 20.0 * 1.4426950408889634
ID_ROWS = 8
VMEM_BYTES = 16 * 1024 * 1024


def along_rows(values):
    return jnp.broadcast_to(values, (LANES, values.shape[1])).T


def ids_block(ids, width):
    wide = jnp.concatenate([ids, jnp.zeros((1, width - ids.shape[1]), jnp.float32)], axis=1)
    return jnp.broadcast_to(wide, (ID_ROWS, width)).astype(jnp.bfloat16)


def ids_of(ref):
    first = ref.shape[0] - ID_ROWS
    return ref[first:, :].astype(jnp.float32)[:1]


def mate_mass(query_rows, query_ids, key_rows, key_ids, shift=None):
    similar = lax.dot_general(
        query_rows, key_rows, (((1,), (1,)), ((), ())), preferred_element_type=jnp.float32
    )
    repeats = similar.shape[1] // LANES
    mates = jnp.concatenate([query_ids] * repeats, axis=1) == key_ids
    if shift is not None:
        query_pos = lax.broadcasted_iota(jnp.int32, similar.shape, 0) + shift
        key_pos = lax.broadcasted_iota(jnp.int32, similar.shape, 1)
        mates = mates & (query_pos != key_pos)
    return jnp.where(mates, jnp.exp2(similar * INVERSE_TEMP_BITS), 0.0)


def unit_rows(raw):
    features = raw.astype(jnp.float32)
    squares = jnp.sum(features * features, axis=1, keepdims=True)
    return (features * lax.rsqrt(squares + 1e-06)).astype(jnp.bfloat16)


def unit_kernel(ranges, rows_ref, ids_ref, *block_refs):
    rows, width = rows_ref.shape
    units = unit_rows(rows_ref[...])
    ids = ids_block(ids_ref[...].astype(jnp.float32), width)
    for (first, last), ref in zip(ranges, block_refs):
        size = last - first
        ref[:size, :] = units[first:last]
        if ref.shape[0] > size:
            ref[size:, :] = ids


def arrived_at(moves):
    plane = lax.axis_index("gx") // PLANE
    return functools.reduce(jnp.logical_or, [plane == receiver for _, receiver in moves])


def add_line(query_parts, ids_ref, key_rows, key_ids, earlier_ref, sums_ref):
    keys = key_rows.shape[0]
    column = jnp.zeros((1, keys), jnp.float32)
    first = 0
    for query_ref, size in query_parts:
        part = pl.ds(first, size)
        masses = mate_mass(query_ref[:size, :], ids_ref[part, :], key_rows, key_ids)
        column = column + jnp.sum(masses, axis=0, keepdims=True)
        folded = masses[:, :LANES]
        for lane in range(LANES, keys, LANES):
            folded = folded + masses[:, lane : lane + LANES]
        sums_ref[part, :] = folded if earlier_ref is None else earlier_ref[part, :] + folded
        first += size
    return column


def add_masses(query_ids, key_ids, powers):
    mates = jnp.concatenate([query_ids] * (powers.shape[1] // LANES), axis=1) == key_ids
    masses = jnp.where(mates, powers, 0.0)
    folded = masses[:, :LANES]
    for lane in range(LANES, powers.shape[1], LANES):
        folded = folded + masses[:, lane : lane + LANES]
    return folded, jnp.sum(masses, axis=0, keepdims=True)


def query_parts_of(refs, rows):
    head = refs[2].shape[0]
    sizes = [rows, rows] + [head, rows - head] * (PLANE - 2)
    return list(zip(refs, sizes))


def own_kernel(own_ref, mass_ref):
    rows = mass_ref.shape[1]
    own_ids = ids_of(own_ref)[:, :rows]
    masses = mate_mass(own_ref[:rows, :], along_rows(own_ids), own_ref[:rows, :], own_ids, 0)
    mass_ref[...] = jnp.sum(masses, axis=0, keepdims=True)


def first_kernel(moves, own_mass_ref, head_ref, tail_ref, *refs):
    query_refs, (ids_ref, column_ref, sums_ref, mass_ref) = refs[:-4], refs[-4:]
    rows = mass_ref.shape[1]
    query_parts = query_parts_of(query_refs, rows)
    own_ref = query_refs[0]
    own_ids = ids_of(own_ref)[:, :rows]
    for m, ref in enumerate((*query_refs[:2], query_refs[3], query_refs[5])):
        ids_ref[pl.ds(m * rows, rows), :] = along_rows(ids_of(ref)[:, :rows])
    mass = own_mass_ref[...]
    first = rows
    for ref, size in query_parts[1:]:
        query_ids = ids_ref[pl.ds(first, size), :]
        masses = mate_mass(ref[:size, :], query_ids, own_ref[:rows, :], own_ids)
        mass = mass + jnp.sum(masses, axis=0, keepdims=True)
        first += size
    mass_ref[...] = mass
    tail = tail_ref[: rows - head_ref.shape[0], :]
    key_rows = jnp.concatenate([unit_rows(head_ref[...]), tail], axis=0)
    key_ids = ids_of(tail_ref)[:, :rows]
    column_ref[...] = add_line(query_parts, ids_ref, key_rows, key_ids, None, sums_ref)


def middle_kernel(moves, head_ref, *refs):
    query_refs, (powers_ref, rest_ref) = refs[:-2], refs[-2:]

    @pl.when(arrived_at(moves))
    def _():
        keys = powers_ref.shape[1]
        units = unit_rows(head_ref[...])
        rest_ref[...] = units[keys:]
        first = 0
        for query_ref, size in query_parts_of(query_refs, query_refs[0].shape[0] - ID_ROWS):
            similar = lax.dot_general(
                query_ref[:size, :], units[:keys], (((1,), (1,)), ((), ())),
                preferred_element_type=jnp.float32,
            )
            powers_ref[pl.ds(first, size), :] = jnp.exp2(similar * INVERSE_TEMP_BITS)
            first += size


def last_kernel(moves, powers_ref, rest_ref, tail_ref, ids_ref, earlier_ref, *refs):
    query_refs, (column_ref, sums_ref) = refs[:-2], refs[-2:]
    rows = column_ref.shape[1]
    cut = powers_ref.shape[1]
    arrived = arrived_at(moves)

    @pl.when(arrived)
    def _():
        key_ids = ids_of(tail_ref)[:, :rows]
        key_rows = jnp.concatenate([rest_ref[...], tail_ref[: tail_ref.shape[0] - ID_ROWS, :]], axis=0)
        early_column = jnp.zeros((1, cut), jnp.float32)
        late_column = jnp.zeros((1, rows - cut), jnp.float32)
        first = 0
        for query_ref, size in query_parts_of(query_refs, rows):
            part = pl.ds(first, size)
            query_ids = ids_ref[part, :]
            similar = lax.dot_general(
                query_ref[:size, :], key_rows, (((1,), (1,)), ((), ())),
                preferred_element_type=jnp.float32,
            )
            powers = jnp.exp2(similar * INVERSE_TEMP_BITS)
            late, column = add_masses(query_ids, key_ids[:, cut:], powers)
            late_column = late_column + column
            early, column = add_masses(query_ids, key_ids[:, :cut], powers_ref[part, :])
            early_column = early_column + column
            sums_ref[part, :] = earlier_ref[part, :] + early + late
            first += size
        column_ref[...] = jnp.concatenate([early_column, late_column], axis=1)

    @pl.when(jnp.logical_not(arrived))
    def _():
        column_ref[...] = jnp.zeros_like(column_ref)
        sums_ref[...] = earlier_ref[...]


def fold_kernel(sums_ref, mass_ref, *row_refs):
    rows = mass_ref.shape[1]
    for m in range(PLANE):
        row_sum = jnp.sum(sums_ref[pl.ds(m * rows, rows), :].T, axis=0, keepdims=True)
        row_refs[m][...] = row_sum + mass_ref[...] if m == 0 else row_sum


def grid_plan(embeddings, cluster_ids):
    peers = lax.axis_size("gx")
    row_count, features = embeddings.shape
    plane_rows = PLANE * row_count
    params = pltpu.CompilerParams(vmem_limit_bytes=VMEM_BYTES)
    small = pl.CostEstimate(flops=1, bytes_accessed=1, transcendentals=0)
    vector = jax.ShapeDtypeStruct((1, row_count), jnp.float32)
    lanes = jax.ShapeDtypeStruct((plane_rows, LANES), jnp.float32)

    def rows_of(count):
        return jax.ShapeDtypeStruct((count, features), jnp.bfloat16)

    def in_plane(value, step):
        return lax.ppermute(value, "gx", [(i, i ^ step) for i in range(peers)])

    def on_line(value, moves, flip):
        pairs = [(a * PLANE + n, b * PLANE + (n ^ flip)) for a, b in moves for n in range(PLANE)]
        return lax.ppermute(value, "gx", pairs)

    first_moves = [(0, 1), (1, 2), (2, 3), (3, 0)]
    last_moves = [(0, 2), (1, 3)]
    forward_moves = [(1, 2), (2, 3)]
    first_back = [(b, a) for a, b in first_moves]
    last_back = [(b, a) for a, b in last_moves]

    half, part = row_count // 2, 5 * row_count // 8
    ranges = [(0, row_count), (0, half), (half, row_count), (part, row_count)]
    id_rows = [ID_ROWS, 0, ID_ROWS, ID_ROWS]
    first_head = on_line(embeddings[:part], first_moves, 0)
    block, *pieces, tail = pl.pallas_call(
        functools.partial(unit_kernel, ranges),
        out_shape=[rows_of(b - a + extra) for (a, b), extra in zip(ranges, id_rows)],
        cost_estimate=small,
        compiler_params=params,
    )(embeddings, cluster_ids.reshape(1, row_count))
    own_mass = pl.pallas_call(
        own_kernel, out_shape=vector, cost_estimate=small, compiler_params=params
    )(block)
    own_mass, tail = lax.optimization_barrier((own_mass, tail))
    first_tail = on_line(tail, first_moves, 0)
    across = [in_plane(piece, 2) for piece in pieces]
    sibling = in_plane(block, 1)
    last_head = on_line(first_head, first_moves, 1)
    last_tail = on_line(first_tail, forward_moves, 1)
    corner = [in_plane(piece, 1) for piece in across]
    queries = (block, sibling, *across, *corner)
    ids, first_column, first_sums, mass = pl.pallas_call(
        functools.partial(first_kernel, first_moves),
        out_shape=(lanes, vector, lanes, vector),
        cost_estimate=small,
        compiler_params=params,
    )(own_mass, first_head, first_tail, *queries)
    returned_first = on_line(first_column, first_back, 0)
    powers, rest = pl.pallas_call(
        functools.partial(middle_kernel, last_moves),
        out_shape=(
            jax.ShapeDtypeStruct((plane_rows, half), jnp.float32), rows_of(part - half)
        ),
        cost_estimate=small,
        compiler_params=params,
    )(last_head, *queries)
    last_column, sums = pl.pallas_call(
        functools.partial(last_kernel, last_moves),
        out_shape=(vector, lanes),
        cost_estimate=small,
        compiler_params=params,
    )(powers, rest, last_tail, ids, first_sums, *queries)
    returned_first, last_column = lax.optimization_barrier((returned_first, last_column))
    row_sums = pl.pallas_call(
        fold_kernel,
        out_shape=[vector] * PLANE,
        cost_estimate=small,
        compiler_params=params,
    )(sums, mass)
    returned = [on_line(last_column, last_back, 1)]
    returned += [in_plane(row_sums[step], step) for step in (3, 2, 1)]
    return jnp.log1p(sum(returned, row_sums[0] + returned_first)).reshape(row_count)


def on_device(embeddings, cluster_ids):
    if lax.axis_size("gx") == 4 * PLANE and embeddings.shape[0] == 2 * LANES:
        return grid_plan(embeddings, cluster_ids)
    return plain_plan(embeddings, cluster_ids)


def solution(mesh):
    in_specs = (P(("parts", "gx"), None), P(("parts", "gx")))
    out_specs = P(("parts", "gx"))
    return jax.shard_map(
        on_device, mesh=mesh, in_specs=in_specs, out_specs=out_specs, check_vma=False
    )
```

```python
import functools

import jax
import jax.numpy as jnp
from jax import lax
from jax.experimental import pallas as pl
from jax.experimental.pallas import tpu as pltpu
from jax.sharding import PartitionSpec as P

CLU_DEV = 1
PAD_MARK = 64.0
inverse_temp = 20.0


def tile_mass(query_rows, key_rows, query_ids, key_ids, query_start):
    similar = lax.dot_general(
        query_rows, key_rows, (((1,), (1,)), ((), ())), preferred_element_type=jnp.float32
    )
    query_pos = jnp.arange(query_rows.shape[0], dtype=jnp.int32) + query_start
    key_pos = jnp.arange(key_rows.shape[0], dtype=jnp.int32)
    mate_mask = (query_ids[:, None] == key_ids[None, :]) & (query_ids[:, None] >= 0)
    mate_mask = mate_mask & (query_pos[:, None] != key_pos[None, :])
    return jnp.where(mate_mask, jnp.exp(similar * inverse_temp), 0.0)


def density_scores(key_rows, key_ids):
    total_rows = key_rows.shape[0]
    block_rows = total_rows // 3
    pieces = [key_rows[i * block_rows : (i + 1) * block_rows] for i in range(3)]
    piece_ids = [key_ids[i * block_rows : (i + 1) * block_rows] for i in range(3)]
    sums = []
    for first in range(3):
        masses = tile_mass(pieces[first], key_rows, piece_ids[first], key_ids, first * block_rows)
        sums.append(jnp.sum(masses, axis=1))
    mass_sum = jnp.concatenate(sums, axis=0)
    return jnp.log1p(mass_sum)


def plain_plan(embeddings, cluster_ids):
    peer_count = lax.axis_size("gx")
    row_count = embeddings.shape[0]
    features = embeddings.shape[1]
    capacity = 3 * row_count // peer_count
    slot_total = peer_count * capacity
    squares = jnp.sum(jnp.square(embeddings.astype(jnp.float32)), axis=1)
    unit_rows = (embeddings.astype(jnp.float32) * lax.rsqrt(squares + 1e-06)[:, None]).astype(
        jnp.bfloat16
    )
    owner_of = cluster_ids // CLU_DEV
    onehot = (owner_of[:, None] == jnp.arange(peer_count, dtype=jnp.int32)[None, :]).astype(
        jnp.bfloat16
    )
    row_range = jnp.arange(row_count, dtype=jnp.int32)
    lower_tri = (row_range[:, None] >= row_range[None, :]).astype(jnp.bfloat16)
    running = jnp.dot(lower_tri, onehot, preferred_element_type=jnp.float32)
    slot_index = (jnp.sum(running * onehot.astype(jnp.float32), axis=1) - 1.0).astype(jnp.int32)
    target_slot = owner_of * capacity + slot_index
    slot_range = jnp.arange(slot_total, dtype=jnp.int32)
    select_mask = slot_range[:, None] == target_slot[None, :]
    outgoing = jnp.dot(
        select_mask.astype(jnp.bfloat16), unit_rows, preferred_element_type=jnp.float32
    )
    outgoing = outgoing.astype(jnp.bfloat16).reshape(peer_count, capacity, features)
    outgoing_ids = jnp.sum(jnp.where(select_mask, cluster_ids[None, :] + 1, 0), axis=1) - 1
    outgoing_ids = outgoing_ids.reshape(peer_count, capacity)
    arrived, arrived_ids = (
        lax.all_to_all(outgoing, "gx", split_axis=0, concat_axis=0, tiled=True),
        lax.all_to_all(outgoing_ids, "gx", split_axis=0, concat_axis=0, tiled=True),
    )
    key_rows = arrived.reshape(slot_total, features)
    key_ids = arrived_ids.reshape(slot_total)
    scores = density_scores(key_rows, key_ids)
    returned = lax.all_to_all(
        scores.reshape(peer_count, capacity), "gx", split_axis=0, concat_axis=0, tiled=True
    )
    flat_scores = returned.reshape(slot_total)
    pick_mask = target_slot[:, None] == slot_range[None, :]
    return jnp.sum(jnp.where(pick_mask, flat_scores[None, :], 0.0), axis=1)


LANES = 128
PLANE = 4
INVERSE_TEMP_BITS = 20.0 * 1.4426950408889634
ID_ROWS = 8
VMEM_BYTES = 16 * 1024 * 1024


def along_rows(values):
    return jnp.broadcast_to(values, (LANES, values.shape[1])).T


def ids_block(ids, width):
    wide = jnp.concatenate([ids, jnp.zeros((1, width - ids.shape[1]), jnp.float32)], axis=1)
    return jnp.broadcast_to(wide, (ID_ROWS, width)).astype(jnp.bfloat16)


def ids_of(ref):
    first = ref.shape[0] - ID_ROWS
    return ref[first:, :].astype(jnp.float32)[:1]


def mate_mass(query_rows, query_ids, key_rows, key_ids, shift=None):
    similar = lax.dot_general(
        query_rows, key_rows, (((1,), (1,)), ((), ())), preferred_element_type=jnp.float32
    )
    repeats = similar.shape[1] // LANES
    mates = jnp.concatenate([query_ids] * repeats, axis=1) == key_ids
    if shift is not None:
        query_pos = lax.broadcasted_iota(jnp.int32, similar.shape, 0) + shift
        key_pos = lax.broadcasted_iota(jnp.int32, similar.shape, 1)
        mates = mates & (query_pos != key_pos)
    return jnp.where(mates, jnp.exp2(similar * INVERSE_TEMP_BITS), 0.0)


def unit_rows(raw):
    features = raw.astype(jnp.float32)
    squares = jnp.sum(features * features, axis=1, keepdims=True)
    return (features * lax.rsqrt(squares + 1e-06)).astype(jnp.bfloat16)


def unit_kernel(ranges, rows_ref, ids_ref, *block_refs):
    rows, width = rows_ref.shape
    units = unit_rows(rows_ref[...])
    ids = ids_block(ids_ref[...].astype(jnp.float32), width)
    for (first, last), ref in zip(ranges, block_refs):
        size = last - first
        ref[:size, :] = units[first:last]
        if ref.shape[0] > size:
            ref[size:, :] = ids


def arrived_at(moves):
    plane = lax.axis_index("gx") // PLANE
    return functools.reduce(jnp.logical_or, [plane == receiver for _, receiver in moves])


def add_line(query_parts, ids_ref, key_rows, key_ids, earlier_ref, sums_ref):
    keys = key_rows.shape[0]
    column = jnp.zeros((1, keys), jnp.float32)
    first = 0
    for query_ref, size in query_parts:
        part = pl.ds(first, size)
        masses = mate_mass(query_ref[:size, :], ids_ref[part, :], key_rows, key_ids)
        column = column + jnp.sum(masses, axis=0, keepdims=True)
        folded = masses[:, :LANES]
        for lane in range(LANES, keys, LANES):
            folded = folded + masses[:, lane : lane + LANES]
        sums_ref[part, :] = folded if earlier_ref is None else earlier_ref[part, :] + folded
        first += size
    return column


def add_masses(query_ids, key_ids, powers):
    mates = jnp.concatenate([query_ids] * (powers.shape[1] // LANES), axis=1) == key_ids
    masses = jnp.where(mates, powers, 0.0)
    folded = masses[:, :LANES]
    for lane in range(LANES, powers.shape[1], LANES):
        folded = folded + masses[:, lane : lane + LANES]
    return folded, jnp.sum(masses, axis=0, keepdims=True)


def query_parts_of(refs, rows):
    head = refs[2].shape[0]
    sizes = [rows, rows] + [head, rows - head] * (PLANE - 2)
    return list(zip(refs, sizes))


def own_kernel(own_ref, mass_ref):
    rows = mass_ref.shape[1]
    own_ids = ids_of(own_ref)[:, :rows]
    masses = mate_mass(own_ref[:rows, :], along_rows(own_ids), own_ref[:rows, :], own_ids, 0)
    mass_ref[...] = jnp.sum(masses, axis=0, keepdims=True)


def first_kernel(moves, own_mass_ref, head_ref, tail_ref, *refs):
    query_refs, (ids_ref, column_ref, sums_ref, mass_ref) = refs[:-4], refs[-4:]
    rows = mass_ref.shape[1]
    query_parts = query_parts_of(query_refs, rows)
    own_ref = query_refs[0]
    own_ids = ids_of(own_ref)[:, :rows]
    for m, ref in enumerate((*query_refs[:2], query_refs[3], query_refs[5])):
        ids_ref[pl.ds(m * rows, rows), :] = along_rows(ids_of(ref)[:, :rows])
    mass = own_mass_ref[...]
    first = rows
    for ref, size in query_parts[1:]:
        query_ids = ids_ref[pl.ds(first, size), :]
        masses = mate_mass(ref[:size, :], query_ids, own_ref[:rows, :], own_ids)
        mass = mass + jnp.sum(masses, axis=0, keepdims=True)
        first += size
    mass_ref[...] = mass
    tail = tail_ref[: rows - head_ref.shape[0], :]
    key_rows = jnp.concatenate([unit_rows(head_ref[...]), tail], axis=0)
    key_ids = ids_of(tail_ref)[:, :rows]
    column_ref[...] = add_line(query_parts, ids_ref, key_rows, key_ids, None, sums_ref)


def middle_kernel(moves, head_ref, *refs):
    query_refs, (powers_ref, rest_ref) = refs[:-2], refs[-2:]

    @pl.when(arrived_at(moves))
    def _():
        keys = powers_ref.shape[1]
        units = unit_rows(head_ref[...])
        rest_ref[...] = units[keys:]
        first = 0
        for query_ref, size in query_parts_of(query_refs, query_refs[0].shape[0] - ID_ROWS):
            similar = lax.dot_general(
                query_ref[:size, :], units[:keys], (((1,), (1,)), ((), ())),
                preferred_element_type=jnp.float32,
            )
            powers_ref[pl.ds(first, size), :] = jnp.exp2(similar * INVERSE_TEMP_BITS)
            first += size


def last_kernel(moves, powers_ref, rest_ref, tail_ref, ids_ref, earlier_ref, *refs):
    query_refs, (column_ref, sums_ref) = refs[:-2], refs[-2:]
    rows = column_ref.shape[1]
    cut = powers_ref.shape[1]
    arrived = arrived_at(moves)

    @pl.when(arrived)
    def _():
        key_ids = ids_of(tail_ref)[:, :rows]
        key_rows = jnp.concatenate([rest_ref[...], tail_ref[: tail_ref.shape[0] - ID_ROWS, :]], axis=0)
        early_column = jnp.zeros((1, cut), jnp.float32)
        late_column = jnp.zeros((1, rows - cut), jnp.float32)
        first = 0
        for query_ref, size in query_parts_of(query_refs, rows):
            part = pl.ds(first, size)
            query_ids = ids_ref[part, :]
            similar = lax.dot_general(
                query_ref[:size, :], key_rows, (((1,), (1,)), ((), ())),
                preferred_element_type=jnp.float32,
            )
            powers = jnp.exp2(similar * INVERSE_TEMP_BITS)
            late, column = add_masses(query_ids, key_ids[:, cut:], powers)
            late_column = late_column + column
            early, column = add_masses(query_ids, key_ids[:, :cut], powers_ref[part, :])
            early_column = early_column + column
            sums_ref[part, :] = earlier_ref[part, :] + early + late
            first += size
        column_ref[...] = jnp.concatenate([early_column, late_column], axis=1)

    @pl.when(jnp.logical_not(arrived))
    def _():
        column_ref[...] = jnp.zeros_like(column_ref)
        sums_ref[...] = earlier_ref[...]


def fold_kernel(sums_ref, mass_ref, *row_refs):
    rows = mass_ref.shape[1]
    for m in range(PLANE):
        row_sum = jnp.sum(sums_ref[pl.ds(m * rows, rows), :].T, axis=0, keepdims=True)
        row_refs[m][...] = row_sum + mass_ref[...] if m == 0 else row_sum


def grid_plan(embeddings, cluster_ids):
    peers = lax.axis_size("gx")
    row_count, features = embeddings.shape
    plane_rows = PLANE * row_count
    params = pltpu.CompilerParams(vmem_limit_bytes=VMEM_BYTES)
    small = pl.CostEstimate(flops=1, bytes_accessed=1, transcendentals=0)
    vector = jax.ShapeDtypeStruct((1, row_count), jnp.float32)
    lanes = jax.ShapeDtypeStruct((plane_rows, LANES), jnp.float32)

    def rows_of(count):
        return jax.ShapeDtypeStruct((count, features), jnp.bfloat16)

    def in_plane(value, step):
        return lax.ppermute(value, "gx", [(i, i ^ step) for i in range(peers)])

    def on_line(value, moves, flip):
        pairs = [(a * PLANE + n, b * PLANE + (n ^ flip)) for a, b in moves for n in range(PLANE)]
        return lax.ppermute(value, "gx", pairs)

    first_moves = [(0, 1), (1, 2), (2, 3), (3, 0)]
    last_moves = [(0, 2), (1, 3)]
    forward_moves = [(1, 2), (2, 3)]
    first_back = [(b, a) for a, b in first_moves]
    last_back = [(b, a) for a, b in last_moves]

    half, part = row_count // 2, 11 * row_count // 16
    ranges = [(0, row_count), (0, half), (half, row_count), (part, row_count)]
    id_rows = [ID_ROWS, 0, ID_ROWS, ID_ROWS]
    first_head = on_line(embeddings[:part], first_moves, 0)
    block, *pieces, tail = pl.pallas_call(
        functools.partial(unit_kernel, ranges),
        out_shape=[rows_of(b - a + extra) for (a, b), extra in zip(ranges, id_rows)],
        cost_estimate=small,
        compiler_params=params,
    )(embeddings, cluster_ids.reshape(1, row_count))
    own_mass = pl.pallas_call(
        own_kernel, out_shape=vector, cost_estimate=small, compiler_params=params
    )(block)
    own_mass, tail = lax.optimization_barrier((own_mass, tail))
    first_tail = on_line(tail, first_moves, 0)
    across = [in_plane(piece, 2) for piece in pieces]
    sibling = in_plane(block, 1)
    last_head = on_line(first_head, first_moves, 1)
    last_tail = on_line(first_tail, forward_moves, 1)
    corner = [in_plane(piece, 1) for piece in across]
    queries = (block, sibling, *across, *corner)
    ids, first_column, first_sums, mass = pl.pallas_call(
        functools.partial(first_kernel, first_moves),
        out_shape=(lanes, vector, lanes, vector),
        cost_estimate=small,
        compiler_params=params,
    )(own_mass, first_head, first_tail, *queries)
    returned_first = on_line(first_column, first_back, 0)
    powers, rest = pl.pallas_call(
        functools.partial(middle_kernel, last_moves),
        out_shape=(
            jax.ShapeDtypeStruct((plane_rows, half), jnp.float32), rows_of(part - half)
        ),
        cost_estimate=small,
        compiler_params=params,
    )(last_head, *queries)
    last_column, sums = pl.pallas_call(
        functools.partial(last_kernel, last_moves),
        out_shape=(vector, lanes),
        cost_estimate=small,
        compiler_params=params,
    )(powers, rest, last_tail, ids, first_sums, *queries)
    returned_first, last_column = lax.optimization_barrier((returned_first, last_column))
    row_sums = pl.pallas_call(
        fold_kernel,
        out_shape=[vector] * PLANE,
        cost_estimate=small,
        compiler_params=params,
    )(sums, mass)
    returned = [on_line(last_column, last_back, 1)]
    returned += [in_plane(row_sums[step], step) for step in (3, 2, 1)]
    return jnp.log1p(sum(returned, row_sums[0] + returned_first)).reshape(row_count)


def on_device(embeddings, cluster_ids):
    if lax.axis_size("gx") == 4 * PLANE and embeddings.shape[0] == 2 * LANES:
        return grid_plan(embeddings, cluster_ids)
    return plain_plan(embeddings, cluster_ids)


def solution(mesh):
    in_specs = (P(("parts", "gx"), None), P(("parts", "gx")))
    out_specs = P(("parts", "gx"))
    return jax.shard_map(
        on_device, mesh=mesh, in_specs=in_specs, out_specs=out_specs, check_vma=False
    )
```

```python
import functools

import jax
import jax.numpy as jnp
from jax import lax
from jax.experimental import pallas as pl
from jax.experimental.pallas import tpu as pltpu
from jax.sharding import PartitionSpec as P

CLU_DEV = 1
PAD_MARK = 64.0
inverse_temp = 20.0


def tile_mass(query_rows, key_rows, query_ids, key_ids, query_start):
    similar = lax.dot_general(
        query_rows, key_rows, (((1,), (1,)), ((), ())), preferred_element_type=jnp.float32
    )
    query_pos = jnp.arange(query_rows.shape[0], dtype=jnp.int32) + query_start
    key_pos = jnp.arange(key_rows.shape[0], dtype=jnp.int32)
    mate_mask = (query_ids[:, None] == key_ids[None, :]) & (query_ids[:, None] >= 0)
    mate_mask = mate_mask & (query_pos[:, None] != key_pos[None, :])
    return jnp.where(mate_mask, jnp.exp(similar * inverse_temp), 0.0)


def density_scores(key_rows, key_ids):
    total_rows = key_rows.shape[0]
    block_rows = total_rows // 3
    pieces = [key_rows[i * block_rows : (i + 1) * block_rows] for i in range(3)]
    piece_ids = [key_ids[i * block_rows : (i + 1) * block_rows] for i in range(3)]
    sums = []
    for first in range(3):
        masses = tile_mass(pieces[first], key_rows, piece_ids[first], key_ids, first * block_rows)
        sums.append(jnp.sum(masses, axis=1))
    mass_sum = jnp.concatenate(sums, axis=0)
    return jnp.log1p(mass_sum)


def plain_plan(embeddings, cluster_ids):
    peer_count = lax.axis_size("gx")
    row_count = embeddings.shape[0]
    features = embeddings.shape[1]
    capacity = 3 * row_count // peer_count
    slot_total = peer_count * capacity
    squares = jnp.sum(jnp.square(embeddings.astype(jnp.float32)), axis=1)
    unit_rows = (embeddings.astype(jnp.float32) * lax.rsqrt(squares + 1e-06)[:, None]).astype(
        jnp.bfloat16
    )
    owner_of = cluster_ids // CLU_DEV
    onehot = (owner_of[:, None] == jnp.arange(peer_count, dtype=jnp.int32)[None, :]).astype(
        jnp.bfloat16
    )
    row_range = jnp.arange(row_count, dtype=jnp.int32)
    lower_tri = (row_range[:, None] >= row_range[None, :]).astype(jnp.bfloat16)
    running = jnp.dot(lower_tri, onehot, preferred_element_type=jnp.float32)
    slot_index = (jnp.sum(running * onehot.astype(jnp.float32), axis=1) - 1.0).astype(jnp.int32)
    target_slot = owner_of * capacity + slot_index
    slot_range = jnp.arange(slot_total, dtype=jnp.int32)
    select_mask = slot_range[:, None] == target_slot[None, :]
    outgoing = jnp.dot(
        select_mask.astype(jnp.bfloat16), unit_rows, preferred_element_type=jnp.float32
    )
    outgoing = outgoing.astype(jnp.bfloat16).reshape(peer_count, capacity, features)
    outgoing_ids = jnp.sum(jnp.where(select_mask, cluster_ids[None, :] + 1, 0), axis=1) - 1
    outgoing_ids = outgoing_ids.reshape(peer_count, capacity)
    arrived, arrived_ids = (
        lax.all_to_all(outgoing, "gx", split_axis=0, concat_axis=0, tiled=True),
        lax.all_to_all(outgoing_ids, "gx", split_axis=0, concat_axis=0, tiled=True),
    )
    key_rows = arrived.reshape(slot_total, features)
    key_ids = arrived_ids.reshape(slot_total)
    scores = density_scores(key_rows, key_ids)
    returned = lax.all_to_all(
        scores.reshape(peer_count, capacity), "gx", split_axis=0, concat_axis=0, tiled=True
    )
    flat_scores = returned.reshape(slot_total)
    pick_mask = target_slot[:, None] == slot_range[None, :]
    return jnp.sum(jnp.where(pick_mask, flat_scores[None, :], 0.0), axis=1)


LANES = 128
PLANE = 4
ID_ROWS = 8
VMEM_BYTES = 16 * 1024 * 1024


def along_rows(values):
    return jnp.broadcast_to(values, (LANES, values.shape[1])).T


def ids_block(ids, width):
    wide = jnp.concatenate([ids, jnp.zeros((1, width - ids.shape[1]), jnp.float32)], axis=1)
    return jnp.broadcast_to(wide, (ID_ROWS, width)).astype(jnp.bfloat16)


def ids_of(ref):
    first = ref.shape[0] - ID_ROWS
    return ref[first:, :].astype(jnp.float32)[:1]


def mate_mass(query_rows, query_ids, key_rows, key_ids, shift=None):
    similar = lax.dot_general(
        query_rows, key_rows, (((1,), (1,)), ((), ())), preferred_element_type=jnp.float32
    )
    repeats = similar.shape[1] // LANES
    mates = jnp.concatenate([query_ids] * repeats, axis=1) == key_ids
    if shift is not None:
        query_pos = lax.broadcasted_iota(jnp.int32, similar.shape, 0) + shift
        key_pos = lax.broadcasted_iota(jnp.int32, similar.shape, 1)
        mates = mates & (query_pos != key_pos)
    return jnp.where(mates, jnp.exp(similar * inverse_temp), 0.0)


def unit_rows(raw):
    features = raw.astype(jnp.float32)
    squares = jnp.sum(features * features, axis=1, keepdims=True)
    return (features * lax.rsqrt(squares + 1e-06)).astype(jnp.bfloat16)


def unit_kernel(ranges, rows_ref, ids_ref, *block_refs):
    rows, width = rows_ref.shape
    units = unit_rows(rows_ref[...])
    ids = ids_block(ids_ref[...].astype(jnp.float32), width)
    for (first, last), ref in zip(ranges, block_refs):
        size = last - first
        ref[:size, :] = units[first:last]
        if ref.shape[0] > size:
            ref[size:, :] = ids


def arrived_at(moves):
    plane = lax.axis_index("gx") // PLANE
    return functools.reduce(jnp.logical_or, [plane == receiver for _, receiver in moves])


def add_line(query_parts, ids_ref, key_rows, key_ids, earlier_ref, sums_ref):
    keys = key_rows.shape[0]
    column = jnp.zeros((1, keys), jnp.float32)
    first = 0
    for query_ref, size in query_parts:
        part = pl.ds(first, size)
        masses = mate_mass(query_ref[:size, :], ids_ref[part, :], key_rows, key_ids)
        column = column + jnp.sum(masses, axis=0, keepdims=True)
        folded = masses[:, :LANES]
        for lane in range(LANES, keys, LANES):
            folded = folded + masses[:, lane : lane + LANES]
        sums_ref[part, :] = folded if earlier_ref is None else earlier_ref[part, :] + folded
        first += size
    return column


def query_parts_of(refs, rows):
    head = refs[2].shape[0]
    sizes = [rows, rows] + [head, rows - head] * (PLANE - 2)
    return list(zip(refs, sizes))


def own_kernel(own_ref, mass_ref):
    rows = mass_ref.shape[1]
    own_ids = ids_of(own_ref)[:, :rows]
    masses = mate_mass(own_ref[:rows, :], along_rows(own_ids), own_ref[:rows, :], own_ids, 0)
    mass_ref[...] = jnp.sum(masses, axis=0, keepdims=True)


def first_kernel(moves, own_mass_ref, head_ref, tail_ref, *refs):
    query_refs, (column_ref, sums_ref, mass_ref, ids_ref) = refs[:-4], refs[-4:]
    rows = mass_ref.shape[1]
    query_parts = query_parts_of(query_refs, rows)
    own_ref = query_refs[0]
    own_ids = ids_of(own_ref)[:, :rows]
    for m, ref in enumerate((*query_refs[:2], query_refs[3], query_refs[5])):
        ids_ref[pl.ds(m * rows, rows), :] = along_rows(ids_of(ref)[:, :rows])
    mass = own_mass_ref[...]
    first = rows
    for ref, size in query_parts[1:]:
        query_ids = ids_ref[pl.ds(first, size), :]
        masses = mate_mass(ref[:size, :], query_ids, own_ref[:rows, :], own_ids)
        mass = mass + jnp.sum(masses, axis=0, keepdims=True)
        first += size
    mass_ref[...] = mass
    tail = tail_ref[: rows - head_ref.shape[0], :]
    key_rows = jnp.concatenate([unit_rows(head_ref[...]), tail], axis=0)
    key_ids = ids_of(tail_ref)[:, :rows]
    column_ref[...] = add_line(query_parts, ids_ref, key_rows, key_ids, None, sums_ref)


def transposed_powers(key_rows, query_rows):
    similar = lax.dot_general(
        key_rows, query_rows, (((1,), (1,)), ((), ())), preferred_element_type=jnp.float32
    )
    return jnp.exp(similar * inverse_temp)


def middle_kernel(moves, head_ref, sums_ref, mass_ref, *refs):
    query_refs, (row_ref, query_ids_ref, powers_ref, rest_ref) = refs[:-4], refs[-4:]
    rows = mass_ref.shape[1]
    for m, ref in enumerate((*query_refs[:2], query_refs[3], query_refs[5])):
        part = pl.ds(m * rows, rows)
        row_sum = jnp.sum(sums_ref[part, :].T, axis=0, keepdims=True)
        row_ref[:, part] = row_sum + mass_ref[...] if m == 0 else row_sum
        query_ids_ref[:, part] = ids_of(ref)[:, :rows]

    @pl.when(arrived_at(moves))
    def _():
        keys = powers_ref.shape[0]
        units = unit_rows(head_ref[...])
        rest_ref[...] = units[keys:]
        first = 0
        for query_ref, size in query_parts_of(query_refs, rows):
            powers_ref[:, pl.ds(first, size)] = transposed_powers(
                units[:keys], query_ref[:size, :]
            )
            first += size


def fold_lanes(values):
    folded = values[:, :LANES]
    for lane in range(LANES, values.shape[1], LANES):
        folded = folded + values[:, lane : lane + LANES]
    return folded


def last_kernel(moves, row_ref, query_ids_ref, powers_ref, rest_ref, tail_ref, *refs):
    query_refs, (column_ref, *row_refs) = refs[: -PLANE - 1], refs[-PLANE - 1 :]
    rows = column_ref.shape[1]
    cut = powers_ref.shape[0]
    arrived = arrived_at(moves)

    @pl.when(arrived)
    def _():
        key_ids = ids_of(tail_ref)[:, :rows]
        early_ids, late_ids = along_rows(key_ids[:, :cut]), along_rows(key_ids[:, cut:])
        tail = tail_ref[: tail_ref.shape[0] - ID_ROWS, :]
        key_rows = jnp.concatenate([rest_ref[...], tail], axis=0)
        early_column = jnp.zeros((cut, LANES), jnp.float32)
        late_column = jnp.zeros((rows - cut, LANES), jnp.float32)
        first = 0
        for query_ref, size in query_parts_of(query_refs, rows):
            part = pl.ds(first, size)
            query_ids = query_ids_ref[:, part]
            repeats = size // LANES
            late = jnp.where(
                jnp.concatenate([late_ids] * repeats, axis=1) == query_ids,
                transposed_powers(key_rows, query_ref[:size, :]), 0.0,
            )
            early = jnp.where(
                jnp.concatenate([early_ids] * repeats, axis=1) == query_ids,
                powers_ref[:, part], 0.0,
            )
            early_column = early_column + fold_lanes(early)
            late_column = late_column + fold_lanes(late)
            inside = first % rows
            row_refs[first // rows][:, inside : inside + size] = row_ref[:, part] + jnp.sum(
                early + late, axis=0, keepdims=True
            )
            first += size
        column_ref[:, :cut] = jnp.sum(early_column.T, axis=0, keepdims=True)
        column_ref[:, cut:] = jnp.sum(late_column.T, axis=0, keepdims=True)

    @pl.when(jnp.logical_not(arrived))
    def _():
        column_ref[...] = jnp.zeros_like(column_ref)
        for m in range(PLANE):
            row_refs[m][...] = row_ref[:, m * rows : (m + 1) * rows]


def grid_plan(embeddings, cluster_ids):
    peers = lax.axis_size("gx")
    row_count, features = embeddings.shape
    plane_rows = PLANE * row_count
    params = pltpu.CompilerParams(vmem_limit_bytes=VMEM_BYTES)
    small = pl.CostEstimate(flops=1, bytes_accessed=1, transcendentals=0)
    vector = jax.ShapeDtypeStruct((1, row_count), jnp.float32)
    lanes = jax.ShapeDtypeStruct((plane_rows, LANES), jnp.float32)

    def rows_of(count):
        return jax.ShapeDtypeStruct((count, features), jnp.bfloat16)

    def in_plane(value, step):
        return lax.ppermute(value, "gx", [(i, i ^ step) for i in range(peers)])

    def on_line(value, moves, flip):
        pairs = [(a * PLANE + n, b * PLANE + (n ^ flip)) for a, b in moves for n in range(PLANE)]
        return lax.ppermute(value, "gx", pairs)

    first_moves = [(0, 1), (1, 2), (2, 3), (3, 0)]
    last_moves = [(0, 2), (1, 3)]
    forward_moves = [(1, 2), (2, 3)]
    first_back = [(b, a) for a, b in first_moves]
    last_back = [(b, a) for a, b in last_moves]

    half, part = row_count // 2, 5 * row_count // 8
    ranges = [(0, row_count), (0, half), (half, row_count), (part, row_count)]
    id_rows = [ID_ROWS, 0, ID_ROWS, ID_ROWS]
    first_head = on_line(embeddings[:part], first_moves, 0)
    block, *pieces, tail = pl.pallas_call(
        functools.partial(unit_kernel, ranges),
        out_shape=[rows_of(b - a + extra) for (a, b), extra in zip(ranges, id_rows)],
        cost_estimate=small,
        compiler_params=params,
    )(embeddings, cluster_ids.reshape(1, row_count))
    own_mass = pl.pallas_call(
        own_kernel, out_shape=vector, cost_estimate=small, compiler_params=params
    )(block)
    own_mass, tail = lax.optimization_barrier((own_mass, tail))
    first_tail = on_line(tail, first_moves, 0)
    across = [in_plane(piece, 2) for piece in pieces]
    sibling = in_plane(block, 1)
    last_head = on_line(first_head, first_moves, 1)
    last_tail = on_line(first_tail, forward_moves, 1)
    corner = [in_plane(piece, 1) for piece in across]
    queries = (block, sibling, *across, *corner)
    first_column, first_sums, mass = pl.pallas_call(
        functools.partial(first_kernel, first_moves),
        out_shape=(vector, lanes, vector),
        scratch_shapes=[pltpu.VMEM(lanes.shape, lanes.dtype)],
        cost_estimate=small,
        compiler_params=params,
    )(own_mass, first_head, first_tail, *queries)
    returned_first = on_line(first_column, first_back, 0)
    plane_vector = jax.ShapeDtypeStruct((1, plane_rows), jnp.float32)
    rows_before, query_ids, powers, rest = pl.pallas_call(
        functools.partial(middle_kernel, last_moves),
        out_shape=(
            plane_vector,
            plane_vector,
            jax.ShapeDtypeStruct((half, plane_rows), jnp.float32),
            rows_of(part - half),
        ),
        cost_estimate=small,
        compiler_params=params,
    )(last_head, first_sums, mass, *queries)
    last_column, *row_sums = pl.pallas_call(
        functools.partial(last_kernel, last_moves),
        out_shape=[vector] * (1 + PLANE),
        cost_estimate=small,
        compiler_params=params,
    )(rows_before, query_ids, powers, rest, last_tail, *queries)
    returned_first, last_column = lax.optimization_barrier((returned_first, last_column))
    returned = [on_line(last_column, last_back, 1)]
    returned += [in_plane(row_sums[step], step) for step in (2, 3, 1)]
    return jnp.log1p(sum(returned, row_sums[0] + returned_first)).reshape(row_count)


def on_device(embeddings, cluster_ids):
    if lax.axis_size("gx") == 4 * PLANE and embeddings.shape[0] == 2 * LANES:
        return grid_plan(embeddings, cluster_ids)
    return plain_plan(embeddings, cluster_ids)


def solution(mesh):
    in_specs = (P(("parts", "gx"), None), P(("parts", "gx")))
    out_specs = P(("parts", "gx"))
    return jax.shard_map(
        on_device, mesh=mesh, in_specs=in_specs, out_specs=out_specs, check_vma=False
    )
```

```python
import functools

import jax
import jax.numpy as jnp
from jax import lax
from jax.experimental import pallas as pl
from jax.experimental.pallas import tpu as pltpu
from jax.sharding import PartitionSpec as P

CLU_DEV = 1
PAD_MARK = 64.0
inverse_temp = 20.0


def tile_mass(query_rows, key_rows, query_ids, key_ids, query_start):
    similar = lax.dot_general(
        query_rows, key_rows, (((1,), (1,)), ((), ())), preferred_element_type=jnp.float32
    )
    query_pos = jnp.arange(query_rows.shape[0], dtype=jnp.int32) + query_start
    key_pos = jnp.arange(key_rows.shape[0], dtype=jnp.int32)
    mate_mask = (query_ids[:, None] == key_ids[None, :]) & (query_ids[:, None] >= 0)
    mate_mask = mate_mask & (query_pos[:, None] != key_pos[None, :])
    return jnp.where(mate_mask, jnp.exp(similar * inverse_temp), 0.0)


def density_scores(key_rows, key_ids):
    total_rows = key_rows.shape[0]
    block_rows = total_rows // 3
    pieces = [key_rows[i * block_rows : (i + 1) * block_rows] for i in range(3)]
    piece_ids = [key_ids[i * block_rows : (i + 1) * block_rows] for i in range(3)]
    sums = []
    for first in range(3):
        masses = tile_mass(pieces[first], key_rows, piece_ids[first], key_ids, first * block_rows)
        sums.append(jnp.sum(masses, axis=1))
    mass_sum = jnp.concatenate(sums, axis=0)
    return jnp.log1p(mass_sum)


def plain_plan(embeddings, cluster_ids):
    peer_count = lax.axis_size("gx")
    row_count = embeddings.shape[0]
    features = embeddings.shape[1]
    capacity = 3 * row_count // peer_count
    slot_total = peer_count * capacity
    squares = jnp.sum(jnp.square(embeddings.astype(jnp.float32)), axis=1)
    unit_rows = (embeddings.astype(jnp.float32) * lax.rsqrt(squares + 1e-06)[:, None]).astype(
        jnp.bfloat16
    )
    owner_of = cluster_ids // CLU_DEV
    onehot = (owner_of[:, None] == jnp.arange(peer_count, dtype=jnp.int32)[None, :]).astype(
        jnp.bfloat16
    )
    row_range = jnp.arange(row_count, dtype=jnp.int32)
    lower_tri = (row_range[:, None] >= row_range[None, :]).astype(jnp.bfloat16)
    running = jnp.dot(lower_tri, onehot, preferred_element_type=jnp.float32)
    slot_index = (jnp.sum(running * onehot.astype(jnp.float32), axis=1) - 1.0).astype(jnp.int32)
    target_slot = owner_of * capacity + slot_index
    slot_range = jnp.arange(slot_total, dtype=jnp.int32)
    select_mask = slot_range[:, None] == target_slot[None, :]
    outgoing = jnp.dot(
        select_mask.astype(jnp.bfloat16), unit_rows, preferred_element_type=jnp.float32
    )
    outgoing = outgoing.astype(jnp.bfloat16).reshape(peer_count, capacity, features)
    outgoing_ids = jnp.sum(jnp.where(select_mask, cluster_ids[None, :] + 1, 0), axis=1) - 1
    outgoing_ids = outgoing_ids.reshape(peer_count, capacity)
    arrived, arrived_ids = (
        lax.all_to_all(outgoing, "gx", split_axis=0, concat_axis=0, tiled=True),
        lax.all_to_all(outgoing_ids, "gx", split_axis=0, concat_axis=0, tiled=True),
    )
    key_rows = arrived.reshape(slot_total, features)
    key_ids = arrived_ids.reshape(slot_total)
    scores = density_scores(key_rows, key_ids)
    returned = lax.all_to_all(
        scores.reshape(peer_count, capacity), "gx", split_axis=0, concat_axis=0, tiled=True
    )
    flat_scores = returned.reshape(slot_total)
    pick_mask = target_slot[:, None] == slot_range[None, :]
    return jnp.sum(jnp.where(pick_mask, flat_scores[None, :], 0.0), axis=1)


LANES = 128
PLANE = 4
ID_ROWS = 8
VMEM_BYTES = 16 * 1024 * 1024


def along_rows(values):
    return jnp.broadcast_to(values, (LANES, values.shape[1])).T


def ids_block(ids, width):
    wide = jnp.concatenate([ids, jnp.zeros((1, width - ids.shape[1]), jnp.float32)], axis=1)
    return jnp.broadcast_to(wide, (ID_ROWS, width)).astype(jnp.bfloat16)


def ids_of(ref):
    first = ref.shape[0] - ID_ROWS
    return ref[first:, :].astype(jnp.float32)[:1]


def mate_mass(query_rows, query_ids, key_rows, key_ids, shift=None):
    similar = lax.dot_general(
        query_rows, key_rows, (((1,), (1,)), ((), ())), preferred_element_type=jnp.float32
    )
    repeats = similar.shape[1] // LANES
    mates = jnp.concatenate([query_ids] * repeats, axis=1) == key_ids
    if shift is not None:
        query_pos = lax.broadcasted_iota(jnp.int32, similar.shape, 0) + shift
        key_pos = lax.broadcasted_iota(jnp.int32, similar.shape, 1)
        mates = mates & (query_pos != key_pos)
    return jnp.where(mates, jnp.exp(similar * inverse_temp), 0.0)


def unit_rows(raw):
    features = raw.astype(jnp.float32)
    squares = jnp.sum(features * features, axis=1, keepdims=True)
    return (features * lax.rsqrt(squares + 1e-06)).astype(jnp.bfloat16)


def unit_kernel(ranges, rows_ref, ids_ref, *block_refs):
    rows, width = rows_ref.shape
    units = unit_rows(rows_ref[...])
    ids = ids_block(ids_ref[...].astype(jnp.float32), width)
    for (first, last), ref in zip(ranges, block_refs):
        size = last - first
        ref[:size, :] = units[first:last]
        if ref.shape[0] > size:
            ref[size:, :] = ids


def arrived_at(moves):
    plane = lax.axis_index("gx") // PLANE
    return functools.reduce(jnp.logical_or, [plane == receiver for _, receiver in moves])


def add_line(query_parts, ids_ref, key_rows, key_ids, earlier_ref, sums_ref):
    keys = key_rows.shape[0]
    column = jnp.zeros((1, keys), jnp.float32)
    first = 0
    for query_ref, size in query_parts:
        part = pl.ds(first, size)
        masses = mate_mass(query_ref[:size, :], ids_ref[part, :], key_rows, key_ids)
        column = column + jnp.sum(masses, axis=0, keepdims=True)
        folded = masses[:, :LANES]
        for lane in range(LANES, keys, LANES):
            folded = folded + masses[:, lane : lane + LANES]
        sums_ref[part, :] = folded if earlier_ref is None else earlier_ref[part, :] + folded
        first += size
    return column


def query_parts_of(refs, rows):
    head = refs[2].shape[0]
    sizes = [rows, rows] + [head, rows - head] * (PLANE - 2)
    return list(zip(refs, sizes))


def own_kernel(own_ref, mass_ref):
    rows = mass_ref.shape[1]
    own_ids = ids_of(own_ref)[:, :rows]
    masses = mate_mass(own_ref[:rows, :], along_rows(own_ids), own_ref[:rows, :], own_ids, 0)
    mass_ref[...] = jnp.sum(masses, axis=0, keepdims=True)


def first_kernel(moves, own_mass_ref, head_ref, tail_ref, *refs):
    query_refs, (ids_ref, column_ref, sums_ref, mass_ref) = refs[:-4], refs[-4:]
    rows = mass_ref.shape[1]
    query_parts = query_parts_of(query_refs, rows)
    own_ref = query_refs[0]
    own_ids = ids_of(own_ref)[:, :rows]
    for m, ref in enumerate((*query_refs[:2], query_refs[3], query_refs[5])):
        ids_ref[pl.ds(m * rows, rows), :] = along_rows(ids_of(ref)[:, :rows])
    mass = own_mass_ref[...]
    first = rows
    for ref, size in query_parts[1:]:
        query_ids = ids_ref[pl.ds(first, size), :]
        masses = mate_mass(ref[:size, :], query_ids, own_ref[:rows, :], own_ids)
        mass = mass + jnp.sum(masses, axis=0, keepdims=True)
        first += size
    mass_ref[...] = mass
    tail = tail_ref[: rows - head_ref.shape[0], :]
    key_rows = jnp.concatenate([unit_rows(head_ref[...]), tail], axis=0)
    key_ids = ids_of(tail_ref)[:, :rows]
    column_ref[...] = add_line(query_parts, ids_ref, key_rows, key_ids, None, sums_ref)


def transposed_powers(key_rows, query_rows):
    similar = lax.dot_general(
        key_rows, query_rows, (((1,), (1,)), ((), ())), preferred_element_type=jnp.float32
    )
    return jnp.exp(similar * inverse_temp)


def middle_kernel(moves, head_ref, sums_ref, mass_ref, *refs):
    query_refs, (row_ref, query_ids_ref, powers_ref, rest_ref) = refs[:-4], refs[-4:]
    rows = mass_ref.shape[1]
    for m, ref in enumerate((*query_refs[:2], query_refs[3], query_refs[5])):
        part = pl.ds(m * rows, rows)
        row_sum = jnp.sum(sums_ref[part, :].T, axis=0, keepdims=True)
        row_ref[:, part] = row_sum + mass_ref[...] if m == 0 else row_sum
        query_ids_ref[:, part] = ids_of(ref)[:, :rows]

    @pl.when(arrived_at(moves))
    def _():
        keys = powers_ref.shape[0]
        units = unit_rows(head_ref[...])
        rest_ref[...] = units[keys:]
        first = 0
        for query_ref, size in query_parts_of(query_refs, rows):
            powers_ref[:, pl.ds(first, size)] = transposed_powers(
                units[:keys], query_ref[:size, :]
            )
            first += size


def fold_lanes(values):
    folded = values[:, :LANES]
    for lane in range(LANES, values.shape[1], LANES):
        folded = folded + values[:, lane : lane + LANES]
    return folded


def last_kernel(moves, row_ref, query_ids_ref, powers_ref, rest_ref, tail_ref, *refs):
    query_refs, (column_ref, *row_refs) = refs[: -PLANE - 1], refs[-PLANE - 1 :]
    rows = column_ref.shape[1]
    cut = powers_ref.shape[0]
    arrived = arrived_at(moves)

    @pl.when(arrived)
    def _():
        key_ids = ids_of(tail_ref)[:, :rows]
        early_ids, late_ids = along_rows(key_ids[:, :cut]), along_rows(key_ids[:, cut:])
        tail = tail_ref[: tail_ref.shape[0] - ID_ROWS, :]
        key_rows = jnp.concatenate([rest_ref[...], tail], axis=0)
        early_column = jnp.zeros((cut, LANES), jnp.float32)
        late_column = jnp.zeros((rows - cut, LANES), jnp.float32)
        first = 0
        for query_ref, size in query_parts_of(query_refs, rows):
            part = pl.ds(first, size)
            query_ids = query_ids_ref[:, part]
            repeats = size // LANES
            late = jnp.where(
                jnp.concatenate([late_ids] * repeats, axis=1) == query_ids,
                transposed_powers(key_rows, query_ref[:size, :]), 0.0,
            )
            early = jnp.where(
                jnp.concatenate([early_ids] * repeats, axis=1) == query_ids,
                powers_ref[:, part], 0.0,
            )
            early_column = early_column + fold_lanes(early)
            late_column = late_column + fold_lanes(late)
            inside = first % rows
            row_refs[first // rows][:, inside : inside + size] = row_ref[:, part] + jnp.sum(
                early + late, axis=0, keepdims=True
            )
            first += size
        column_ref[:, :cut] = jnp.sum(early_column.T, axis=0, keepdims=True)
        column_ref[:, cut:] = jnp.sum(late_column.T, axis=0, keepdims=True)

    @pl.when(jnp.logical_not(arrived))
    def _():
        column_ref[...] = jnp.zeros_like(column_ref)
        for m in range(PLANE):
            row_refs[m][...] = row_ref[:, m * rows : (m + 1) * rows]


def grid_plan(embeddings, cluster_ids):
    peers = lax.axis_size("gx")
    row_count, features = embeddings.shape
    plane_rows = PLANE * row_count
    params = pltpu.CompilerParams(vmem_limit_bytes=VMEM_BYTES)
    small = pl.CostEstimate(flops=1, bytes_accessed=1, transcendentals=0)
    vector = jax.ShapeDtypeStruct((1, row_count), jnp.float32)
    lanes = jax.ShapeDtypeStruct((plane_rows, LANES), jnp.float32)

    def rows_of(count):
        return jax.ShapeDtypeStruct((count, features), jnp.bfloat16)

    def in_plane(value, step):
        return lax.ppermute(value, "gx", [(i, i ^ step) for i in range(peers)])

    def on_line(value, moves, flip):
        pairs = [(a * PLANE + n, b * PLANE + (n ^ flip)) for a, b in moves for n in range(PLANE)]
        return lax.ppermute(value, "gx", pairs)

    first_moves = [(0, 1), (1, 2), (2, 3), (3, 0)]
    last_moves = [(0, 2), (1, 3)]
    forward_moves = [(1, 2), (2, 3)]
    first_back = [(b, a) for a, b in first_moves]
    last_back = [(b, a) for a, b in last_moves]

    half, part = row_count // 2, 5 * row_count // 8
    ranges = [(0, row_count), (0, half), (half, row_count), (part, row_count)]
    id_rows = [ID_ROWS, 0, ID_ROWS, ID_ROWS]
    first_head = on_line(embeddings[:part], first_moves, 0)
    block, *pieces, tail = pl.pallas_call(
        functools.partial(unit_kernel, ranges),
        out_shape=[rows_of(b - a + extra) for (a, b), extra in zip(ranges, id_rows)],
        cost_estimate=small,
        compiler_params=params,
    )(embeddings, cluster_ids.reshape(1, row_count))
    own_mass = pl.pallas_call(
        own_kernel, out_shape=vector, cost_estimate=small, compiler_params=params
    )(block)
    own_mass, tail = lax.optimization_barrier((own_mass, tail))
    first_tail = on_line(tail, first_moves, 0)
    across = [in_plane(piece, 2) for piece in pieces]
    sibling = in_plane(block, 1)
    last_head = on_line(first_head, first_moves, 1)
    last_tail = on_line(first_tail, forward_moves, 1)
    corner = [in_plane(piece, 1) for piece in across]
    queries = (block, sibling, *across, *corner)
    _, first_column, first_sums, mass = pl.pallas_call(
        functools.partial(first_kernel, first_moves),
        out_shape=(lanes, vector, lanes, vector),
        cost_estimate=small,
        compiler_params=params,
    )(own_mass, first_head, first_tail, *queries)
    returned_first = on_line(first_column, first_back, 0)
    plane_vector = jax.ShapeDtypeStruct((1, plane_rows), jnp.float32)
    rows_before, query_ids, powers, rest = pl.pallas_call(
        functools.partial(middle_kernel, last_moves),
        out_shape=(
            plane_vector,
            plane_vector,
            jax.ShapeDtypeStruct((half, plane_rows), jnp.float32),
            rows_of(part - half),
        ),
        cost_estimate=small,
        compiler_params=params,
    )(last_head, first_sums, mass, *queries)
    last_column, *row_sums = pl.pallas_call(
        functools.partial(last_kernel, last_moves),
        out_shape=[vector] * (1 + PLANE),
        cost_estimate=small,
        compiler_params=params,
    )(rows_before, query_ids, powers, rest, last_tail, *queries)
    returned_first, last_column = lax.optimization_barrier((returned_first, last_column))
    returned = [on_line(last_column, last_back, 1)]
    returned += [in_plane(row_sums[step], step) for step in (2, 3, 1)]
    return jnp.log1p(sum(returned, row_sums[0] + returned_first)).reshape(row_count)


def on_device(embeddings, cluster_ids):
    if lax.axis_size("gx") == 4 * PLANE and embeddings.shape[0] == 2 * LANES:
        return grid_plan(embeddings, cluster_ids)
    return plain_plan(embeddings, cluster_ids)


def solution(mesh):
    in_specs = (P(("parts", "gx"), None), P(("parts", "gx")))
    out_specs = P(("parts", "gx"))
    return jax.shard_map(
        on_device, mesh=mesh, in_specs=in_specs, out_specs=out_specs, check_vma=False
    )
```

```python
import functools

import jax
import jax.numpy as jnp
from jax import lax
from jax.experimental import pallas as pl
from jax.experimental.pallas import tpu as pltpu
from jax.sharding import PartitionSpec as P

CLU_DEV = 1
PAD_MARK = 64.0
inverse_temp = 20.0


def tile_mass(query_rows, key_rows, query_ids, key_ids, query_start):
    similar = lax.dot_general(
        query_rows, key_rows, (((1,), (1,)), ((), ())), preferred_element_type=jnp.float32
    )
    query_pos = jnp.arange(query_rows.shape[0], dtype=jnp.int32) + query_start
    key_pos = jnp.arange(key_rows.shape[0], dtype=jnp.int32)
    mate_mask = (query_ids[:, None] == key_ids[None, :]) & (query_ids[:, None] >= 0)
    mate_mask = mate_mask & (query_pos[:, None] != key_pos[None, :])
    return jnp.where(mate_mask, jnp.exp(similar * inverse_temp), 0.0)


def density_scores(key_rows, key_ids):
    total_rows = key_rows.shape[0]
    block_rows = total_rows // 3
    pieces = [key_rows[i * block_rows : (i + 1) * block_rows] for i in range(3)]
    piece_ids = [key_ids[i * block_rows : (i + 1) * block_rows] for i in range(3)]
    sums = []
    for first in range(3):
        masses = tile_mass(pieces[first], key_rows, piece_ids[first], key_ids, first * block_rows)
        sums.append(jnp.sum(masses, axis=1))
    mass_sum = jnp.concatenate(sums, axis=0)
    return jnp.log1p(mass_sum)


def plain_plan(embeddings, cluster_ids):
    peer_count = lax.axis_size("gx")
    row_count = embeddings.shape[0]
    features = embeddings.shape[1]
    capacity = 3 * row_count // peer_count
    slot_total = peer_count * capacity
    squares = jnp.sum(jnp.square(embeddings.astype(jnp.float32)), axis=1)
    unit_rows = (embeddings.astype(jnp.float32) * lax.rsqrt(squares + 1e-06)[:, None]).astype(
        jnp.bfloat16
    )
    owner_of = cluster_ids // CLU_DEV
    onehot = (owner_of[:, None] == jnp.arange(peer_count, dtype=jnp.int32)[None, :]).astype(
        jnp.bfloat16
    )
    row_range = jnp.arange(row_count, dtype=jnp.int32)
    lower_tri = (row_range[:, None] >= row_range[None, :]).astype(jnp.bfloat16)
    running = jnp.dot(lower_tri, onehot, preferred_element_type=jnp.float32)
    slot_index = (jnp.sum(running * onehot.astype(jnp.float32), axis=1) - 1.0).astype(jnp.int32)
    target_slot = owner_of * capacity + slot_index
    slot_range = jnp.arange(slot_total, dtype=jnp.int32)
    select_mask = slot_range[:, None] == target_slot[None, :]
    outgoing = jnp.dot(
        select_mask.astype(jnp.bfloat16), unit_rows, preferred_element_type=jnp.float32
    )
    outgoing = outgoing.astype(jnp.bfloat16).reshape(peer_count, capacity, features)
    outgoing_ids = jnp.sum(jnp.where(select_mask, cluster_ids[None, :] + 1, 0), axis=1) - 1
    outgoing_ids = outgoing_ids.reshape(peer_count, capacity)
    arrived, arrived_ids = (
        lax.all_to_all(outgoing, "gx", split_axis=0, concat_axis=0, tiled=True),
        lax.all_to_all(outgoing_ids, "gx", split_axis=0, concat_axis=0, tiled=True),
    )
    key_rows = arrived.reshape(slot_total, features)
    key_ids = arrived_ids.reshape(slot_total)
    scores = density_scores(key_rows, key_ids)
    returned = lax.all_to_all(
        scores.reshape(peer_count, capacity), "gx", split_axis=0, concat_axis=0, tiled=True
    )
    flat_scores = returned.reshape(slot_total)
    pick_mask = target_slot[:, None] == slot_range[None, :]
    return jnp.sum(jnp.where(pick_mask, flat_scores[None, :], 0.0), axis=1)


LANES = 128
PLANE = 4
ID_ROWS = 8
VMEM_BYTES = 16 * 1024 * 1024


def along_rows(values):
    return jnp.broadcast_to(values, (LANES, values.shape[1])).T


def ids_block(ids, width):
    wide = jnp.concatenate([ids, jnp.zeros((1, width - ids.shape[1]), jnp.float32)], axis=1)
    return jnp.broadcast_to(wide, (ID_ROWS, width)).astype(jnp.bfloat16)


def ids_of(ref):
    first = ref.shape[0] - ID_ROWS
    return ref[first:, :].astype(jnp.float32)[:1]


def mate_mass(query_rows, query_ids, key_rows, key_ids, shift=None):
    similar = lax.dot_general(
        query_rows, key_rows, (((1,), (1,)), ((), ())), preferred_element_type=jnp.float32
    )
    repeats = similar.shape[1] // LANES
    mates = jnp.concatenate([query_ids] * repeats, axis=1) == key_ids
    if shift is not None:
        query_pos = lax.broadcasted_iota(jnp.int32, similar.shape, 0) + shift
        key_pos = lax.broadcasted_iota(jnp.int32, similar.shape, 1)
        mates = mates & (query_pos != key_pos)
    return jnp.where(mates, jnp.exp(similar * inverse_temp), 0.0)


def unit_rows(raw):
    features = raw.astype(jnp.float32)
    squares = jnp.sum(features * features, axis=1, keepdims=True)
    return (features * lax.rsqrt(squares + 1e-06)).astype(jnp.bfloat16)


def unit_kernel(ranges, rows_ref, ids_ref, *block_refs):
    rows, width = rows_ref.shape
    units = unit_rows(rows_ref[...])
    ids = ids_block(ids_ref[...].astype(jnp.float32), width)
    for (first, last), ref in zip(ranges, block_refs):
        size = last - first
        ref[:size, :] = units[first:last]
        if ref.shape[0] > size:
            ref[size:, :] = ids


def arrived_at(moves):
    plane = lax.axis_index("gx") // PLANE
    return functools.reduce(jnp.logical_or, [plane == receiver for _, receiver in moves])


def add_line(query_parts, ids_ref, key_rows, key_ids, earlier_ref, sums_ref):
    keys = key_rows.shape[0]
    column = jnp.zeros((1, keys), jnp.float32)
    first = 0
    for query_ref, size in query_parts:
        part = pl.ds(first, size)
        masses = mate_mass(query_ref[:size, :], ids_ref[part, :], key_rows, key_ids)
        column = column + jnp.sum(masses, axis=0, keepdims=True)
        folded = masses[:, :LANES]
        for lane in range(LANES, keys, LANES):
            folded = folded + masses[:, lane : lane + LANES]
        sums_ref[part, :] = folded if earlier_ref is None else earlier_ref[part, :] + folded
        first += size
    return column


def add_masses(query_ids, key_ids, powers):
    mates = jnp.concatenate([query_ids] * (powers.shape[1] // LANES), axis=1) == key_ids
    masses = jnp.where(mates, powers, 0.0)
    folded = masses[:, :LANES]
    for lane in range(LANES, powers.shape[1], LANES):
        folded = folded + masses[:, lane : lane + LANES]
    return folded, jnp.sum(masses, axis=0, keepdims=True)


def query_parts_of(refs, rows):
    head = refs[2].shape[0]
    sizes = [rows, rows] + [head, rows - head] * (PLANE - 2)
    return list(zip(refs, sizes))


def own_kernel(own_ref, mass_ref):
    rows = mass_ref.shape[1]
    own_ids = ids_of(own_ref)[:, :rows]
    masses = mate_mass(own_ref[:rows, :], along_rows(own_ids), own_ref[:rows, :], own_ids, 0)
    mass_ref[...] = jnp.sum(masses, axis=0, keepdims=True)


def first_kernel(moves, own_mass_ref, head_ref, tail_ref, *refs):
    query_refs, (ids_ref, column_ref, sums_ref, mass_ref) = refs[:-4], refs[-4:]
    rows = mass_ref.shape[1]
    query_parts = query_parts_of(query_refs, rows)
    own_ref = query_refs[0]
    own_ids = ids_of(own_ref)[:, :rows]
    for m, ref in enumerate((*query_refs[:2], query_refs[3], query_refs[5])):
        ids_ref[pl.ds(m * rows, rows), :] = along_rows(ids_of(ref)[:, :rows])
    mass = own_mass_ref[...]
    first = rows
    for ref, size in query_parts[1:]:
        query_ids = ids_ref[pl.ds(first, size), :]
        masses = mate_mass(ref[:size, :], query_ids, own_ref[:rows, :], own_ids)
        mass = mass + jnp.sum(masses, axis=0, keepdims=True)
        first += size
    mass_ref[...] = mass
    tail = tail_ref[: rows - head_ref.shape[0], :]
    key_rows = jnp.concatenate([unit_rows(head_ref[...]), tail], axis=0)
    key_ids = ids_of(tail_ref)[:, :rows]
    column_ref[...] = add_line(query_parts, ids_ref, key_rows, key_ids, None, sums_ref)


def middle_kernel(moves, head_ref, *refs):
    query_refs, (powers_ref, rest_ref) = refs[:-2], refs[-2:]

    @pl.when(arrived_at(moves))
    def _():
        keys = powers_ref.shape[1]
        units = unit_rows(head_ref[...])
        rest_ref[...] = units[keys:]
        first = 0
        for query_ref, size in query_parts_of(query_refs, query_refs[0].shape[0] - ID_ROWS):
            similar = lax.dot_general(
                query_ref[:size, :], units[:keys], (((1,), (1,)), ((), ())),
                preferred_element_type=jnp.float32,
            )
            powers_ref[pl.ds(first, size), :] = jnp.exp(similar * inverse_temp)
            first += size


def last_kernel(moves, powers_ref, rest_ref, tail_ref, ids_ref, earlier_ref, *refs):
    query_refs, (column_ref, sums_ref) = refs[:-2], refs[-2:]
    rows = column_ref.shape[1]
    cut = powers_ref.shape[1]
    arrived = arrived_at(moves)

    @pl.when(arrived)
    def _():
        key_ids = ids_of(tail_ref)[:, :rows]
        key_rows = jnp.concatenate([rest_ref[...], tail_ref[: tail_ref.shape[0] - ID_ROWS, :]], axis=0)
        early_column = jnp.zeros((1, cut), jnp.float32)
        late_column = jnp.zeros((1, rows - cut), jnp.float32)
        first = 0
        for query_ref, size in query_parts_of(query_refs, rows):
            part = pl.ds(first, size)
            query_ids = ids_ref[part, :]
            similar = lax.dot_general(
                query_ref[:size, :], key_rows, (((1,), (1,)), ((), ())),
                preferred_element_type=jnp.float32,
            )
            powers = jnp.exp(similar * inverse_temp)
            late, column = add_masses(query_ids, key_ids[:, cut:], powers)
            late_column = late_column + column
            early, column = add_masses(query_ids, key_ids[:, :cut], powers_ref[part, :])
            early_column = early_column + column
            sums_ref[part, :] = earlier_ref[part, :] + early + late
            first += size
        column_ref[...] = jnp.concatenate([early_column, late_column], axis=1)

    @pl.when(jnp.logical_not(arrived))
    def _():
        column_ref[...] = jnp.zeros_like(column_ref)
        sums_ref[...] = earlier_ref[...]


def fold_kernel(sums_ref, mass_ref, *row_refs):
    rows = mass_ref.shape[1]
    for m in range(PLANE):
        row_sum = jnp.sum(sums_ref[pl.ds(m * rows, rows), :].T, axis=0, keepdims=True)
        row_refs[m][...] = row_sum + mass_ref[...] if m == 0 else row_sum


def grid_plan(embeddings, cluster_ids):
    peers = lax.axis_size("gx")
    row_count, features = embeddings.shape
    plane_rows = PLANE * row_count
    params = pltpu.CompilerParams(vmem_limit_bytes=VMEM_BYTES)
    small = pl.CostEstimate(flops=1, bytes_accessed=1, transcendentals=0)
    vector = jax.ShapeDtypeStruct((1, row_count), jnp.float32)
    lanes = jax.ShapeDtypeStruct((plane_rows, LANES), jnp.float32)

    def rows_of(count):
        return jax.ShapeDtypeStruct((count, features), jnp.bfloat16)

    def in_plane(value, step):
        return lax.ppermute(value, "gx", [(i, i ^ step) for i in range(peers)])

    def on_line(value, moves, flip):
        pairs = [(a * PLANE + n, b * PLANE + (n ^ flip)) for a, b in moves for n in range(PLANE)]
        return lax.ppermute(value, "gx", pairs)

    first_moves = [(0, 1), (1, 2), (2, 3), (3, 0)]
    last_moves = [(0, 2), (1, 3)]
    forward_moves = [(1, 2), (2, 3)]
    first_back = [(b, a) for a, b in first_moves]
    last_back = [(b, a) for a, b in last_moves]

    half, part = row_count // 2, 5 * row_count // 8
    ranges = [(0, row_count), (0, half), (half, row_count), (part, row_count)]
    id_rows = [ID_ROWS, 0, ID_ROWS, ID_ROWS]
    first_head = on_line(embeddings[:part], first_moves, 0)
    block, *pieces, tail = pl.pallas_call(
        functools.partial(unit_kernel, ranges),
        out_shape=[rows_of(b - a + extra) for (a, b), extra in zip(ranges, id_rows)],
        cost_estimate=small,
        compiler_params=params,
    )(embeddings, cluster_ids.reshape(1, row_count))
    own_mass = pl.pallas_call(
        own_kernel, out_shape=vector, cost_estimate=small, compiler_params=params
    )(block)
    first_tail = on_line(tail, first_moves, 0)
    across = [in_plane(piece, 2) for piece in pieces]
    sibling = in_plane(block, 1)
    last_head = on_line(first_head, first_moves, 1)
    last_tail = on_line(first_tail, forward_moves, 1)
    corner = [in_plane(piece, 1) for piece in across]
    queries = (block, sibling, *across, *corner)
    ids, first_column, first_sums, mass = pl.pallas_call(
        functools.partial(first_kernel, first_moves),
        out_shape=(lanes, vector, lanes, vector),
        cost_estimate=small,
        compiler_params=params,
    )(own_mass, first_head, first_tail, *queries)
    returned_first = on_line(first_column, first_back, 0)
    powers, rest = pl.pallas_call(
        functools.partial(middle_kernel, last_moves),
        out_shape=(
            jax.ShapeDtypeStruct((plane_rows, half), jnp.float32), rows_of(part - half)
        ),
        cost_estimate=small,
        compiler_params=params,
    )(last_head, *queries)
    last_column, sums = pl.pallas_call(
        functools.partial(last_kernel, last_moves),
        out_shape=(vector, lanes),
        cost_estimate=small,
        compiler_params=params,
    )(powers, rest, last_tail, ids, first_sums, *queries)
    returned_first, last_column = lax.optimization_barrier((returned_first, last_column))
    row_sums = pl.pallas_call(
        fold_kernel,
        out_shape=[vector] * PLANE,
        cost_estimate=small,
        compiler_params=params,
    )(sums, mass)
    returned = [on_line(last_column, last_back, 1)]
    returned += [in_plane(row_sums[step], step) for step in (2, 3, 1)]
    return jnp.log1p(sum(returned, row_sums[0] + returned_first)).reshape(row_count)


def on_device(embeddings, cluster_ids):
    if lax.axis_size("gx") == 4 * PLANE and embeddings.shape[0] == 2 * LANES:
        return grid_plan(embeddings, cluster_ids)
    return plain_plan(embeddings, cluster_ids)


def solution(mesh):
    in_specs = (P(("parts", "gx"), None), P(("parts", "gx")))
    out_specs = P(("parts", "gx"))
    return jax.shard_map(
        on_device, mesh=mesh, in_specs=in_specs, out_specs=out_specs, check_vma=False
    )
```

```python
import functools

import jax
import jax.numpy as jnp
from jax import lax
from jax.experimental import pallas as pl
from jax.experimental.pallas import tpu as pltpu
from jax.sharding import PartitionSpec as P

CLU_DEV = 1
PAD_MARK = 64.0
inverse_temp = 20.0


def tile_mass(query_rows, key_rows, query_ids, key_ids, query_start):
    similar = lax.dot_general(
        query_rows, key_rows, (((1,), (1,)), ((), ())), preferred_element_type=jnp.float32
    )
    query_pos = jnp.arange(query_rows.shape[0], dtype=jnp.int32) + query_start
    key_pos = jnp.arange(key_rows.shape[0], dtype=jnp.int32)
    mate_mask = (query_ids[:, None] == key_ids[None, :]) & (query_ids[:, None] >= 0)
    mate_mask = mate_mask & (query_pos[:, None] != key_pos[None, :])
    return jnp.where(mate_mask, jnp.exp(similar * inverse_temp), 0.0)


def density_scores(key_rows, key_ids):
    total_rows = key_rows.shape[0]
    block_rows = total_rows // 3
    pieces = [key_rows[i * block_rows : (i + 1) * block_rows] for i in range(3)]
    piece_ids = [key_ids[i * block_rows : (i + 1) * block_rows] for i in range(3)]
    sums = []
    for first in range(3):
        masses = tile_mass(pieces[first], key_rows, piece_ids[first], key_ids, first * block_rows)
        sums.append(jnp.sum(masses, axis=1))
    mass_sum = jnp.concatenate(sums, axis=0)
    return jnp.log1p(mass_sum)


def plain_plan(embeddings, cluster_ids):
    peer_count = lax.axis_size("gx")
    row_count = embeddings.shape[0]
    features = embeddings.shape[1]
    capacity = 3 * row_count // peer_count
    slot_total = peer_count * capacity
    squares = jnp.sum(jnp.square(embeddings.astype(jnp.float32)), axis=1)
    unit_rows = (embeddings.astype(jnp.float32) * lax.rsqrt(squares + 1e-06)[:, None]).astype(
        jnp.bfloat16
    )
    owner_of = cluster_ids // CLU_DEV
    onehot = (owner_of[:, None] == jnp.arange(peer_count, dtype=jnp.int32)[None, :]).astype(
        jnp.bfloat16
    )
    row_range = jnp.arange(row_count, dtype=jnp.int32)
    lower_tri = (row_range[:, None] >= row_range[None, :]).astype(jnp.bfloat16)
    running = jnp.dot(lower_tri, onehot, preferred_element_type=jnp.float32)
    slot_index = (jnp.sum(running * onehot.astype(jnp.float32), axis=1) - 1.0).astype(jnp.int32)
    target_slot = owner_of * capacity + slot_index
    slot_range = jnp.arange(slot_total, dtype=jnp.int32)
    select_mask = slot_range[:, None] == target_slot[None, :]
    outgoing = jnp.dot(
        select_mask.astype(jnp.bfloat16), unit_rows, preferred_element_type=jnp.float32
    )
    outgoing = outgoing.astype(jnp.bfloat16).reshape(peer_count, capacity, features)
    outgoing_ids = jnp.sum(jnp.where(select_mask, cluster_ids[None, :] + 1, 0), axis=1) - 1
    outgoing_ids = outgoing_ids.reshape(peer_count, capacity)
    arrived, arrived_ids = (
        lax.all_to_all(outgoing, "gx", split_axis=0, concat_axis=0, tiled=True),
        lax.all_to_all(outgoing_ids, "gx", split_axis=0, concat_axis=0, tiled=True),
    )
    key_rows = arrived.reshape(slot_total, features)
    key_ids = arrived_ids.reshape(slot_total)
    scores = density_scores(key_rows, key_ids)
    returned = lax.all_to_all(
        scores.reshape(peer_count, capacity), "gx", split_axis=0, concat_axis=0, tiled=True
    )
    flat_scores = returned.reshape(slot_total)
    pick_mask = target_slot[:, None] == slot_range[None, :]
    return jnp.sum(jnp.where(pick_mask, flat_scores[None, :], 0.0), axis=1)


LANES = 128
PLANE = 4
ID_ROWS = 8
VMEM_BYTES = 16 * 1024 * 1024


def along_rows(values):
    return jnp.broadcast_to(values, (LANES, values.shape[1])).T


def ids_block(ids, width):
    wide = jnp.concatenate([ids, jnp.zeros((1, width - ids.shape[1]), jnp.float32)], axis=1)
    return jnp.broadcast_to(wide, (ID_ROWS, width)).astype(jnp.bfloat16)


def ids_of(ref):
    first = ref.shape[0] - ID_ROWS
    return ref[first:, :].astype(jnp.float32)[:1]


def mate_mass(query_rows, query_ids, key_rows, key_ids, shift=None):
    similar = lax.dot_general(
        query_rows, key_rows, (((1,), (1,)), ((), ())), preferred_element_type=jnp.float32
    )
    repeats = similar.shape[1] // LANES
    mates = jnp.concatenate([query_ids] * repeats, axis=1) == key_ids
    if shift is not None:
        query_pos = lax.broadcasted_iota(jnp.int32, similar.shape, 0) + shift
        key_pos = lax.broadcasted_iota(jnp.int32, similar.shape, 1)
        mates = mates & (query_pos != key_pos)
    return jnp.where(mates, jnp.exp(similar * inverse_temp), 0.0)


def unit_rows(raw):
    features = raw.astype(jnp.float32)
    squares = jnp.sum(features * features, axis=1, keepdims=True)
    return (features * lax.rsqrt(squares + 1e-06)).astype(jnp.bfloat16)


def unit_kernel(ranges, rows_ref, ids_ref, *block_refs):
    rows, width = rows_ref.shape
    units = unit_rows(rows_ref[...])
    ids = ids_block(ids_ref[...].astype(jnp.float32), width)
    for (first, last), ref in zip(ranges, block_refs):
        size = last - first
        ref[:size, :] = units[first:last]
        if ref.shape[0] > size:
            ref[size:, :] = ids


def arrived_at(moves):
    plane = lax.axis_index("gx") // PLANE
    return functools.reduce(jnp.logical_or, [plane == receiver for _, receiver in moves])


def add_line(query_parts, ids_ref, key_rows, key_ids, earlier_ref, sums_ref):
    keys = key_rows.shape[0]
    column = jnp.zeros((1, keys), jnp.float32)
    first = 0
    for query_ref, size in query_parts:
        part = pl.ds(first, size)
        masses = mate_mass(query_ref[:size, :], ids_ref[part, :], key_rows, key_ids)
        column = column + jnp.sum(masses, axis=0, keepdims=True)
        folded = masses[:, :LANES]
        for lane in range(LANES, keys, LANES):
            folded = folded + masses[:, lane : lane + LANES]
        sums_ref[part, :] = folded if earlier_ref is None else earlier_ref[part, :] + folded
        first += size
    return column


def add_masses(query_ids, key_ids, powers):
    mates = jnp.concatenate([query_ids] * (powers.shape[1] // LANES), axis=1) == key_ids
    masses = jnp.where(mates, powers, 0.0)
    folded = masses[:, :LANES]
    for lane in range(LANES, powers.shape[1], LANES):
        folded = folded + masses[:, lane : lane + LANES]
    return folded, jnp.sum(masses, axis=0, keepdims=True)


def query_parts_of(refs, rows):
    head = refs[2].shape[0]
    sizes = [rows, rows] + [head, rows - head] * (PLANE - 2)
    return list(zip(refs, sizes))


def own_kernel(own_ref, mass_ref):
    rows = mass_ref.shape[1]
    own_ids = ids_of(own_ref)[:, :rows]
    masses = mate_mass(own_ref[:rows, :], along_rows(own_ids), own_ref[:rows, :], own_ids, 0)
    mass_ref[...] = jnp.sum(masses, axis=0, keepdims=True)


def folded_rows(sums_ref, m, rows):
    return jnp.sum(sums_ref[pl.ds(m * rows, rows), :].T, axis=0, keepdims=True)


def first_kernel(moves, own_mass_ref, head_ref, tail_ref, *refs):
    query_refs, (ids_ref, column_ref, sums_ref, mass_ref) = refs[:-4], refs[-4:]
    rows = mass_ref.shape[1] // PLANE
    query_parts = query_parts_of(query_refs, rows)
    own_ref = query_refs[0]
    own_ids = ids_of(own_ref)[:, :rows]
    for m, ref in enumerate((*query_refs[:2], query_refs[3], query_refs[5])):
        ids_ref[pl.ds(m * rows, rows), :] = along_rows(ids_of(ref)[:, :rows])
    mass = own_mass_ref[...]
    first = rows
    for ref, size in query_parts[1:]:
        query_ids = ids_ref[pl.ds(first, size), :]
        masses = mate_mass(ref[:size, :], query_ids, own_ref[:rows, :], own_ids)
        mass = mass + jnp.sum(masses, axis=0, keepdims=True)
        first += size
    tail = tail_ref[: rows - head_ref.shape[0], :]
    key_rows = jnp.concatenate([unit_rows(head_ref[...]), tail], axis=0)
    key_ids = ids_of(tail_ref)[:, :rows]
    column_ref[...] = add_line(query_parts, ids_ref, key_rows, key_ids, None, sums_ref)
    for m in range(PLANE):
        row_sum = folded_rows(sums_ref, m, rows)
        mass_ref[:, m * rows : (m + 1) * rows] = row_sum + mass if m == 0 else row_sum


def middle_kernel(moves, head_ref, *refs):
    query_refs, (powers_ref, rest_ref) = refs[:-2], refs[-2:]

    @pl.when(arrived_at(moves))
    def _():
        keys = powers_ref.shape[1]
        units = unit_rows(head_ref[...])
        rest_ref[...] = units[keys:]
        first = 0
        for query_ref, size in query_parts_of(query_refs, query_refs[0].shape[0] - ID_ROWS):
            similar = lax.dot_general(
                query_ref[:size, :], units[:keys], (((1,), (1,)), ((), ())),
                preferred_element_type=jnp.float32,
            )
            powers_ref[pl.ds(first, size), :] = jnp.exp(similar * inverse_temp)
            first += size


def last_kernel(moves, powers_ref, rest_ref, tail_ref, ids_ref, *refs):
    query_refs, (column_ref, sums_ref) = refs[:-2], refs[-2:]
    rows = column_ref.shape[1]
    cut = powers_ref.shape[1]
    arrived = arrived_at(moves)

    @pl.when(arrived)
    def _():
        key_ids = ids_of(tail_ref)[:, :rows]
        key_rows = jnp.concatenate([rest_ref[...], tail_ref[: tail_ref.shape[0] - ID_ROWS, :]], axis=0)
        early_column = jnp.zeros((1, cut), jnp.float32)
        late_column = jnp.zeros((1, rows - cut), jnp.float32)
        first = 0
        for query_ref, size in query_parts_of(query_refs, rows):
            part = pl.ds(first, size)
            query_ids = ids_ref[part, :]
            similar = lax.dot_general(
                query_ref[:size, :], key_rows, (((1,), (1,)), ((), ())),
                preferred_element_type=jnp.float32,
            )
            powers = jnp.exp(similar * inverse_temp)
            late, column = add_masses(query_ids, key_ids[:, cut:], powers)
            late_column = late_column + column
            early, column = add_masses(query_ids, key_ids[:, :cut], powers_ref[part, :])
            early_column = early_column + column
            sums_ref[part, :] = early + late
            first += size
        column_ref[...] = jnp.concatenate([early_column, late_column], axis=1)

    @pl.when(jnp.logical_not(arrived))
    def _():
        column_ref[...] = jnp.zeros_like(column_ref)
        sums_ref[...] = jnp.zeros_like(sums_ref)


def fold_kernel(sums_ref, row_ref, *row_refs):
    rows = row_refs[0].shape[1]
    for m in range(PLANE):
        row_refs[m][...] = row_ref[:, m * rows : (m + 1) * rows] + folded_rows(sums_ref, m, rows)


def grid_plan(embeddings, cluster_ids):
    peers = lax.axis_size("gx")
    row_count, features = embeddings.shape
    plane_rows = PLANE * row_count
    params = pltpu.CompilerParams(vmem_limit_bytes=VMEM_BYTES)
    small = pl.CostEstimate(flops=1, bytes_accessed=1, transcendentals=0)
    vector = jax.ShapeDtypeStruct((1, row_count), jnp.float32)
    lanes = jax.ShapeDtypeStruct((plane_rows, LANES), jnp.float32)

    def rows_of(count):
        return jax.ShapeDtypeStruct((count, features), jnp.bfloat16)

    def in_plane(value, step):
        return lax.ppermute(value, "gx", [(i, i ^ step) for i in range(peers)])

    def on_line(value, moves, flip):
        pairs = [(a * PLANE + n, b * PLANE + (n ^ flip)) for a, b in moves for n in range(PLANE)]
        return lax.ppermute(value, "gx", pairs)

    first_moves = [(0, 1), (1, 2), (2, 3), (3, 0)]
    last_moves = [(0, 2), (1, 3)]
    forward_moves = [(1, 2), (2, 3)]
    first_back = [(b, a) for a, b in first_moves]
    last_back = [(b, a) for a, b in last_moves]

    half, part = row_count // 2, 5 * row_count // 8
    ranges = [(0, row_count), (0, half), (half, row_count), (part, row_count)]
    id_rows = [ID_ROWS, 0, ID_ROWS, ID_ROWS]
    first_head = on_line(embeddings[:part], first_moves, 0)
    block, *pieces, tail = pl.pallas_call(
        functools.partial(unit_kernel, ranges),
        out_shape=[rows_of(b - a + extra) for (a, b), extra in zip(ranges, id_rows)],
        cost_estimate=small,
        compiler_params=params,
    )(embeddings, cluster_ids.reshape(1, row_count))
    own_mass = pl.pallas_call(
        own_kernel, out_shape=vector, cost_estimate=small, compiler_params=params
    )(block)
    first_tail = on_line(tail, first_moves, 0)
    across = [in_plane(piece, 2) for piece in pieces]
    sibling = in_plane(block, 1)
    last_head = on_line(first_head, first_moves, 1)
    last_tail = on_line(first_tail, forward_moves, 1)
    corner = [in_plane(piece, 1) for piece in across]
    queries = (block, sibling, *across, *corner)
    ids, first_column, _, rows_before = pl.pallas_call(
        functools.partial(first_kernel, first_moves),
        out_shape=(
            lanes, vector, lanes, jax.ShapeDtypeStruct((1, plane_rows), jnp.float32)
        ),
        cost_estimate=small,
        compiler_params=params,
    )(own_mass, first_head, first_tail, *queries)
    returned_first = on_line(first_column, first_back, 0)
    powers, rest = pl.pallas_call(
        functools.partial(middle_kernel, last_moves),
        out_shape=(
            jax.ShapeDtypeStruct((plane_rows, half), jnp.float32),
            rows_of(part - half),
        ),
        cost_estimate=small,
        compiler_params=params,
    )(last_head, *queries)
    last_column, sums = pl.pallas_call(
        functools.partial(last_kernel, last_moves),
        out_shape=(vector, lanes),
        cost_estimate=small,
        compiler_params=params,
    )(powers, rest, last_tail, ids, *queries)
    returned_first, last_column = lax.optimization_barrier((returned_first, last_column))
    row_sums = pl.pallas_call(
        fold_kernel,
        out_shape=[vector] * PLANE,
        cost_estimate=small,
        compiler_params=params,
    )(sums, rows_before)
    returned = [on_line(last_column, last_back, 1)]
    returned += [in_plane(row_sums[step], step) for step in (2, 3, 1)]
    return jnp.log1p(sum(returned, row_sums[0] + returned_first)).reshape(row_count)


def on_device(embeddings, cluster_ids):
    if lax.axis_size("gx") == 4 * PLANE and embeddings.shape[0] == 2 * LANES:
        return grid_plan(embeddings, cluster_ids)
    return plain_plan(embeddings, cluster_ids)


def solution(mesh):
    in_specs = (P(("parts", "gx"), None), P(("parts", "gx")))
    out_specs = P(("parts", "gx"))
    return jax.shard_map(
        on_device, mesh=mesh, in_specs=in_specs, out_specs=out_specs, check_vma=False
    )
```

```python
import functools

import jax
import jax.numpy as jnp
from jax import lax
from jax.experimental import pallas as pl
from jax.experimental.pallas import tpu as pltpu
from jax.sharding import PartitionSpec as P

CLU_DEV = 1
PAD_MARK = 64.0
inverse_temp = 20.0


def tile_mass(query_rows, key_rows, query_ids, key_ids, query_start):
    similar = lax.dot_general(
        query_rows, key_rows, (((1,), (1,)), ((), ())), preferred_element_type=jnp.float32
    )
    query_pos = jnp.arange(query_rows.shape[0], dtype=jnp.int32) + query_start
    key_pos = jnp.arange(key_rows.shape[0], dtype=jnp.int32)
    mate_mask = (query_ids[:, None] == key_ids[None, :]) & (query_ids[:, None] >= 0)
    mate_mask = mate_mask & (query_pos[:, None] != key_pos[None, :])
    return jnp.where(mate_mask, jnp.exp(similar * inverse_temp), 0.0)


def density_scores(key_rows, key_ids):
    total_rows = key_rows.shape[0]
    block_rows = total_rows // 3
    pieces = [key_rows[i * block_rows : (i + 1) * block_rows] for i in range(3)]
    piece_ids = [key_ids[i * block_rows : (i + 1) * block_rows] for i in range(3)]
    sums = []
    for first in range(3):
        masses = tile_mass(pieces[first], key_rows, piece_ids[first], key_ids, first * block_rows)
        sums.append(jnp.sum(masses, axis=1))
    mass_sum = jnp.concatenate(sums, axis=0)
    return jnp.log1p(mass_sum)


def plain_plan(embeddings, cluster_ids):
    peer_count = lax.axis_size("gx")
    row_count = embeddings.shape[0]
    features = embeddings.shape[1]
    capacity = 3 * row_count // peer_count
    slot_total = peer_count * capacity
    squares = jnp.sum(jnp.square(embeddings.astype(jnp.float32)), axis=1)
    unit_rows = (embeddings.astype(jnp.float32) * lax.rsqrt(squares + 1e-06)[:, None]).astype(
        jnp.bfloat16
    )
    owner_of = cluster_ids // CLU_DEV
    onehot = (owner_of[:, None] == jnp.arange(peer_count, dtype=jnp.int32)[None, :]).astype(
        jnp.bfloat16
    )
    row_range = jnp.arange(row_count, dtype=jnp.int32)
    lower_tri = (row_range[:, None] >= row_range[None, :]).astype(jnp.bfloat16)
    running = jnp.dot(lower_tri, onehot, preferred_element_type=jnp.float32)
    slot_index = (jnp.sum(running * onehot.astype(jnp.float32), axis=1) - 1.0).astype(jnp.int32)
    target_slot = owner_of * capacity + slot_index
    slot_range = jnp.arange(slot_total, dtype=jnp.int32)
    select_mask = slot_range[:, None] == target_slot[None, :]
    outgoing = jnp.dot(
        select_mask.astype(jnp.bfloat16), unit_rows, preferred_element_type=jnp.float32
    )
    outgoing = outgoing.astype(jnp.bfloat16).reshape(peer_count, capacity, features)
    outgoing_ids = jnp.sum(jnp.where(select_mask, cluster_ids[None, :] + 1, 0), axis=1) - 1
    outgoing_ids = outgoing_ids.reshape(peer_count, capacity)
    arrived, arrived_ids = (
        lax.all_to_all(outgoing, "gx", split_axis=0, concat_axis=0, tiled=True),
        lax.all_to_all(outgoing_ids, "gx", split_axis=0, concat_axis=0, tiled=True),
    )
    key_rows = arrived.reshape(slot_total, features)
    key_ids = arrived_ids.reshape(slot_total)
    scores = density_scores(key_rows, key_ids)
    returned = lax.all_to_all(
        scores.reshape(peer_count, capacity), "gx", split_axis=0, concat_axis=0, tiled=True
    )
    flat_scores = returned.reshape(slot_total)
    pick_mask = target_slot[:, None] == slot_range[None, :]
    return jnp.sum(jnp.where(pick_mask, flat_scores[None, :], 0.0), axis=1)


LANES = 128
PLANE = 4
ID_ROWS = 8
VMEM_BYTES = 16 * 1024 * 1024


def along_rows(values):
    return jnp.broadcast_to(values, (LANES, values.shape[1])).T


def ids_block(ids, width):
    wide = jnp.concatenate([ids, jnp.zeros((1, width - ids.shape[1]), jnp.float32)], axis=1)
    return jnp.broadcast_to(wide, (ID_ROWS, width)).astype(jnp.bfloat16)


def ids_of(ref):
    first = ref.shape[0] - ID_ROWS
    return ref[first:, :].astype(jnp.float32)[:1]


def mate_mass(query_rows, query_ids, key_rows, key_ids, shift=None):
    similar = lax.dot_general(
        query_rows, key_rows, (((1,), (1,)), ((), ())), preferred_element_type=jnp.float32
    )
    repeats = similar.shape[1] // LANES
    mates = jnp.concatenate([query_ids] * repeats, axis=1) == key_ids
    if shift is not None:
        query_pos = lax.broadcasted_iota(jnp.int32, similar.shape, 0) + shift
        key_pos = lax.broadcasted_iota(jnp.int32, similar.shape, 1)
        mates = mates & (query_pos != key_pos)
    return jnp.where(mates, jnp.exp(similar * inverse_temp), 0.0)


def unit_rows(raw):
    features = raw.astype(jnp.float32)
    squares = jnp.sum(features * features, axis=1, keepdims=True)
    return (features * lax.rsqrt(squares + 1e-06)).astype(jnp.bfloat16)


def unit_kernel(ranges, rows_ref, ids_ref, *block_refs):
    rows, width = rows_ref.shape
    units = unit_rows(rows_ref[...])
    ids = ids_block(ids_ref[...].astype(jnp.float32), width)
    for (first, last), ref in zip(ranges, block_refs):
        size = last - first
        ref[:size, :] = units[first:last]
        if ref.shape[0] > size:
            ref[size:, :] = ids


def arrived_at(moves):
    plane = lax.axis_index("gx") // PLANE
    return functools.reduce(jnp.logical_or, [plane == receiver for _, receiver in moves])


def add_line(query_parts, ids_ref, key_rows, key_ids, earlier_ref, sums_ref):
    keys = key_rows.shape[0]
    column = jnp.zeros((1, keys), jnp.float32)
    first = 0
    for query_ref, size in query_parts:
        part = pl.ds(first, size)
        masses = mate_mass(query_ref[:size, :], ids_ref[part, :], key_rows, key_ids)
        column = column + jnp.sum(masses, axis=0, keepdims=True)
        folded = masses[:, :LANES]
        for lane in range(LANES, keys, LANES):
            folded = folded + masses[:, lane : lane + LANES]
        sums_ref[part, :] = folded if earlier_ref is None else earlier_ref[part, :] + folded
        first += size
    return column


def add_masses(query_ids, key_ids, powers):
    mates = jnp.concatenate([query_ids] * (powers.shape[1] // LANES), axis=1) == key_ids
    masses = jnp.where(mates, powers, 0.0)
    folded = masses[:, :LANES]
    for lane in range(LANES, powers.shape[1], LANES):
        folded = folded + masses[:, lane : lane + LANES]
    return folded, jnp.sum(masses, axis=0, keepdims=True)


def query_parts_of(refs, rows):
    head = refs[2].shape[0]
    sizes = [rows, rows] + [head, rows - head] * (PLANE - 2)
    return list(zip(refs, sizes))


def own_kernel(own_ref, mass_ref):
    rows = mass_ref.shape[1]
    own_ids = ids_of(own_ref)[:, :rows]
    masses = mate_mass(own_ref[:rows, :], along_rows(own_ids), own_ref[:rows, :], own_ids, 0)
    mass_ref[...] = jnp.sum(masses, axis=0, keepdims=True)


def first_kernel(moves, own_mass_ref, head_ref, tail_ref, *refs):
    query_refs, (ids_ref, column_ref, sums_ref, mass_ref) = refs[:-4], refs[-4:]
    rows = mass_ref.shape[1]
    query_parts = query_parts_of(query_refs, rows)
    own_ref = query_refs[0]
    own_ids = ids_of(own_ref)[:, :rows]
    for m, ref in enumerate((*query_refs[:2], query_refs[3], query_refs[5])):
        ids_ref[pl.ds(m * rows, rows), :] = along_rows(ids_of(ref)[:, :rows])
    mass = own_mass_ref[...]
    first = rows
    for ref, size in query_parts[1:]:
        query_ids = ids_ref[pl.ds(first, size), :]
        masses = mate_mass(ref[:size, :], query_ids, own_ref[:rows, :], own_ids)
        mass = mass + jnp.sum(masses, axis=0, keepdims=True)
        first += size
    mass_ref[...] = mass
    tail = tail_ref[: rows - head_ref.shape[0], :]
    key_rows = jnp.concatenate([unit_rows(head_ref[...]), tail], axis=0)
    key_ids = ids_of(tail_ref)[:, :rows]
    column_ref[...] = add_line(query_parts, ids_ref, key_rows, key_ids, None, sums_ref)


def middle_kernel(moves, head_ref, *refs):
    query_refs, (powers_ref, rest_ref) = refs[:-2], refs[-2:]

    @pl.when(arrived_at(moves))
    def _():
        keys = powers_ref.shape[1]
        units = unit_rows(head_ref[...])
        rest_ref[...] = units[keys:]
        first = 0
        for query_ref, size in query_parts_of(query_refs, query_refs[0].shape[0] - ID_ROWS):
            similar = lax.dot_general(
                query_ref[:size, :], units[:keys], (((1,), (1,)), ((), ())),
                preferred_element_type=jnp.float32,
            )
            powers_ref[pl.ds(first, size), :] = jnp.exp(similar * inverse_temp)
            first += size


def last_kernel(moves, powers_ref, rest_ref, tail_ref, ids_ref, *refs):
    query_refs, (column_ref, sums_ref) = refs[:-2], refs[-2:]
    rows = column_ref.shape[1]
    cut = powers_ref.shape[1]
    arrived = arrived_at(moves)

    @pl.when(arrived)
    def _():
        key_ids = ids_of(tail_ref)[:, :rows]
        key_rows = jnp.concatenate([rest_ref[...], tail_ref[: tail_ref.shape[0] - ID_ROWS, :]], axis=0)
        early_column = jnp.zeros((1, cut), jnp.float32)
        late_column = jnp.zeros((1, rows - cut), jnp.float32)
        first = 0
        for query_ref, size in query_parts_of(query_refs, rows):
            part = pl.ds(first, size)
            query_ids = ids_ref[part, :]
            similar = lax.dot_general(
                query_ref[:size, :], key_rows, (((1,), (1,)), ((), ())),
                preferred_element_type=jnp.float32,
            )
            powers = jnp.exp(similar * inverse_temp)
            late, column = add_masses(query_ids, key_ids[:, cut:], powers)
            late_column = late_column + column
            early, column = add_masses(query_ids, key_ids[:, :cut], powers_ref[part, :])
            early_column = early_column + column
            sums_ref[part, :] = early + late
            first += size
        column_ref[...] = jnp.concatenate([early_column, late_column], axis=1)

    @pl.when(jnp.logical_not(arrived))
    def _():
        column_ref[...] = jnp.zeros_like(column_ref)
        sums_ref[...] = jnp.zeros_like(sums_ref)


def fold_kernel(sums_ref, *refs):
    before_refs, row_refs = refs[:-PLANE], refs[-PLANE:]
    rows = row_refs[0].shape[1]
    for m in range(PLANE):
        row_sum = jnp.sum(sums_ref[pl.ds(m * rows, rows), :].T, axis=0, keepdims=True)
        row_refs[m][...] = row_sum + before_refs[m][...] if m < len(before_refs) else row_sum


def grid_plan(embeddings, cluster_ids):
    peers = lax.axis_size("gx")
    row_count, features = embeddings.shape
    plane_rows = PLANE * row_count
    params = pltpu.CompilerParams(vmem_limit_bytes=VMEM_BYTES)
    small = pl.CostEstimate(flops=1, bytes_accessed=1, transcendentals=0)
    vector = jax.ShapeDtypeStruct((1, row_count), jnp.float32)
    lanes = jax.ShapeDtypeStruct((plane_rows, LANES), jnp.float32)

    def rows_of(count):
        return jax.ShapeDtypeStruct((count, features), jnp.bfloat16)

    def in_plane(value, step):
        return lax.ppermute(value, "gx", [(i, i ^ step) for i in range(peers)])

    def on_line(value, moves, flip):
        pairs = [(a * PLANE + n, b * PLANE + (n ^ flip)) for a, b in moves for n in range(PLANE)]
        return lax.ppermute(value, "gx", pairs)

    first_moves = [(0, 1), (1, 2), (2, 3), (3, 0)]
    last_moves = [(0, 2), (1, 3)]
    forward_moves = [(1, 2), (2, 3)]
    first_back = [(b, a) for a, b in first_moves]
    last_back = [(b, a) for a, b in last_moves]

    half, part = row_count // 2, 5 * row_count // 8
    ranges = [(0, row_count), (0, half), (half, row_count), (part, row_count)]
    id_rows = [ID_ROWS, 0, ID_ROWS, ID_ROWS]
    first_head = on_line(embeddings[:part], first_moves, 0)
    block, *pieces, tail = pl.pallas_call(
        functools.partial(unit_kernel, ranges),
        out_shape=[rows_of(b - a + extra) for (a, b), extra in zip(ranges, id_rows)],
        cost_estimate=small,
        compiler_params=params,
    )(embeddings, cluster_ids.reshape(1, row_count))
    own_mass = pl.pallas_call(
        own_kernel, out_shape=vector, cost_estimate=small, compiler_params=params
    )(block)
    first_tail = on_line(tail, first_moves, 0)
    across = [in_plane(piece, 2) for piece in pieces]
    sibling = in_plane(block, 1)
    last_head = on_line(first_head, first_moves, 1)
    last_tail = on_line(first_tail, forward_moves, 1)
    corner = [in_plane(piece, 1) for piece in across]
    queries = (block, sibling, *across, *corner)
    ids, first_column, first_sums, mass = pl.pallas_call(
        functools.partial(first_kernel, first_moves),
        out_shape=(lanes, vector, lanes, vector),
        cost_estimate=small,
        compiler_params=params,
    )(own_mass, first_head, first_tail, *queries)
    returned_first = on_line(first_column, first_back, 0)
    powers, rest = pl.pallas_call(
        functools.partial(middle_kernel, last_moves),
        out_shape=(
            jax.ShapeDtypeStruct((plane_rows, half), jnp.float32), rows_of(part - half)
        ),
        cost_estimate=small,
        compiler_params=params,
    )(last_head, *queries)
    last_column, sums = pl.pallas_call(
        functools.partial(last_kernel, last_moves),
        out_shape=(vector, lanes),
        cost_estimate=small,
        compiler_params=params,
    )(powers, rest, last_tail, ids, *queries)
    returned_first, last_column = lax.optimization_barrier((returned_first, last_column))
    fold = pl.pallas_call(
        fold_kernel,
        out_shape=[vector] * PLANE,
        cost_estimate=small,
        compiler_params=params,
    )
    row_sums = fold(sums, *fold(first_sums, mass))
    returned = [on_line(last_column, last_back, 1)]
    returned += [in_plane(row_sums[step], step) for step in (2, 3, 1)]
    return jnp.log1p(sum(returned, row_sums[0] + returned_first)).reshape(row_count)


def on_device(embeddings, cluster_ids):
    if lax.axis_size("gx") == 4 * PLANE and embeddings.shape[0] == 2 * LANES:
        return grid_plan(embeddings, cluster_ids)
    return plain_plan(embeddings, cluster_ids)


def solution(mesh):
    in_specs = (P(("parts", "gx"), None), P(("parts", "gx")))
    out_specs = P(("parts", "gx"))
    return jax.shard_map(
        on_device, mesh=mesh, in_specs=in_specs, out_specs=out_specs, check_vma=False
    )
```

```python
import functools

import jax
import jax.numpy as jnp
from jax import lax
from jax.experimental import pallas as pl
from jax.experimental.pallas import tpu as pltpu
from jax.sharding import PartitionSpec as P

CLU_DEV = 1
PAD_MARK = 64.0
inverse_temp = 20.0


def tile_mass(query_rows, key_rows, query_ids, key_ids, query_start):
    similar = lax.dot_general(
        query_rows, key_rows, (((1,), (1,)), ((), ())), preferred_element_type=jnp.float32
    )
    query_pos = jnp.arange(query_rows.shape[0], dtype=jnp.int32) + query_start
    key_pos = jnp.arange(key_rows.shape[0], dtype=jnp.int32)
    mate_mask = (query_ids[:, None] == key_ids[None, :]) & (query_ids[:, None] >= 0)
    mate_mask = mate_mask & (query_pos[:, None] != key_pos[None, :])
    return jnp.where(mate_mask, jnp.exp(similar * inverse_temp), 0.0)


def density_scores(key_rows, key_ids):
    total_rows = key_rows.shape[0]
    block_rows = total_rows // 3
    pieces = [key_rows[i * block_rows : (i + 1) * block_rows] for i in range(3)]
    piece_ids = [key_ids[i * block_rows : (i + 1) * block_rows] for i in range(3)]
    sums = []
    for first in range(3):
        masses = tile_mass(pieces[first], key_rows, piece_ids[first], key_ids, first * block_rows)
        sums.append(jnp.sum(masses, axis=1))
    mass_sum = jnp.concatenate(sums, axis=0)
    return jnp.log1p(mass_sum)


def plain_plan(embeddings, cluster_ids):
    peer_count = lax.axis_size("gx")
    row_count = embeddings.shape[0]
    features = embeddings.shape[1]
    capacity = 3 * row_count // peer_count
    slot_total = peer_count * capacity
    squares = jnp.sum(jnp.square(embeddings.astype(jnp.float32)), axis=1)
    unit_rows = (embeddings.astype(jnp.float32) * lax.rsqrt(squares + 1e-06)[:, None]).astype(
        jnp.bfloat16
    )
    owner_of = cluster_ids // CLU_DEV
    onehot = (owner_of[:, None] == jnp.arange(peer_count, dtype=jnp.int32)[None, :]).astype(
        jnp.bfloat16
    )
    row_range = jnp.arange(row_count, dtype=jnp.int32)
    lower_tri = (row_range[:, None] >= row_range[None, :]).astype(jnp.bfloat16)
    running = jnp.dot(lower_tri, onehot, preferred_element_type=jnp.float32)
    slot_index = (jnp.sum(running * onehot.astype(jnp.float32), axis=1) - 1.0).astype(jnp.int32)
    target_slot = owner_of * capacity + slot_index
    slot_range = jnp.arange(slot_total, dtype=jnp.int32)
    select_mask = slot_range[:, None] == target_slot[None, :]
    outgoing = jnp.dot(
        select_mask.astype(jnp.bfloat16), unit_rows, preferred_element_type=jnp.float32
    )
    outgoing = outgoing.astype(jnp.bfloat16).reshape(peer_count, capacity, features)
    outgoing_ids = jnp.sum(jnp.where(select_mask, cluster_ids[None, :] + 1, 0), axis=1) - 1
    outgoing_ids = outgoing_ids.reshape(peer_count, capacity)
    arrived, arrived_ids = (
        lax.all_to_all(outgoing, "gx", split_axis=0, concat_axis=0, tiled=True),
        lax.all_to_all(outgoing_ids, "gx", split_axis=0, concat_axis=0, tiled=True),
    )
    key_rows = arrived.reshape(slot_total, features)
    key_ids = arrived_ids.reshape(slot_total)
    scores = density_scores(key_rows, key_ids)
    returned = lax.all_to_all(
        scores.reshape(peer_count, capacity), "gx", split_axis=0, concat_axis=0, tiled=True
    )
    flat_scores = returned.reshape(slot_total)
    pick_mask = target_slot[:, None] == slot_range[None, :]
    return jnp.sum(jnp.where(pick_mask, flat_scores[None, :], 0.0), axis=1)


LANES = 128
PLANE = 4
ID_ROWS = 8
VMEM_BYTES = 16 * 1024 * 1024


def along_rows(values):
    return jnp.broadcast_to(values, (LANES, values.shape[1])).T


def ids_block(ids, width):
    wide = jnp.concatenate([ids, jnp.zeros((1, width - ids.shape[1]), jnp.float32)], axis=1)
    return jnp.broadcast_to(wide, (ID_ROWS, width)).astype(jnp.bfloat16)


def ids_of(ref):
    first = ref.shape[0] - ID_ROWS
    return ref[first:, :].astype(jnp.float32)[:1]


def mate_mass(query_rows, query_ids, key_rows, key_ids, shift=None):
    similar = lax.dot_general(
        query_rows, key_rows, (((1,), (1,)), ((), ())), preferred_element_type=jnp.float32
    )
    repeats = similar.shape[1] // LANES
    mates = jnp.concatenate([query_ids] * repeats, axis=1) == key_ids
    if shift is not None:
        query_pos = lax.broadcasted_iota(jnp.int32, similar.shape, 0) + shift
        key_pos = lax.broadcasted_iota(jnp.int32, similar.shape, 1)
        mates = mates & (query_pos != key_pos)
    return jnp.where(mates, jnp.exp(similar * inverse_temp), 0.0)


def unit_rows(raw):
    features = raw.astype(jnp.float32)
    squares = jnp.sum(features * features, axis=1, keepdims=True)
    return (features * lax.rsqrt(squares + 1e-06)).astype(jnp.bfloat16)


def unit_kernel(ranges, rows_ref, ids_ref, *block_refs):
    rows, width = rows_ref.shape
    units = unit_rows(rows_ref[...])
    ids = ids_block(ids_ref[...].astype(jnp.float32), width)
    for (first, last), ref in zip(ranges, block_refs):
        size = last - first
        ref[:size, :] = units[first:last]
        if ref.shape[0] > size:
            ref[size:, :] = ids


def arrived_at(moves):
    plane = lax.axis_index("gx") // PLANE
    return functools.reduce(jnp.logical_or, [plane == receiver for _, receiver in moves])


def add_line(query_parts, ids_ref, key_rows, key_ids, earlier_ref, sums_ref):
    keys = key_rows.shape[0]
    column = jnp.zeros((1, keys), jnp.float32)
    first = 0
    for query_ref, size in query_parts:
        part = pl.ds(first, size)
        masses = mate_mass(query_ref[:size, :], ids_ref[part, :], key_rows, key_ids)
        column = column + jnp.sum(masses, axis=0, keepdims=True)
        folded = masses[:, :LANES]
        for lane in range(LANES, keys, LANES):
            folded = folded + masses[:, lane : lane + LANES]
        sums_ref[part, :] = folded if earlier_ref is None else earlier_ref[part, :] + folded
        first += size
    return column


def add_masses(query_ids, key_ids, powers):
    mates = jnp.concatenate([query_ids] * (powers.shape[1] // LANES), axis=1) == key_ids
    masses = jnp.where(mates, powers, 0.0)
    folded = masses[:, :LANES]
    for lane in range(LANES, powers.shape[1], LANES):
        folded = folded + masses[:, lane : lane + LANES]
    return folded, jnp.sum(masses, axis=0, keepdims=True)


def query_parts_of(refs, rows):
    head = refs[2].shape[0]
    sizes = [rows, rows] + [head, rows - head] * (PLANE - 2)
    return list(zip(refs, sizes))


def own_kernel(own_ref, mass_ref):
    rows = mass_ref.shape[1]
    own_ids = ids_of(own_ref)[:, :rows]
    masses = mate_mass(own_ref[:rows, :], along_rows(own_ids), own_ref[:rows, :], own_ids, 0)
    mass_ref[...] = jnp.sum(masses, axis=0, keepdims=True)


def first_kernel(moves, own_mass_ref, head_ref, tail_ref, *refs):
    query_refs, (ids_ref, column_ref, sums_ref, mass_ref) = refs[:-4], refs[-4:]
    rows = mass_ref.shape[1]
    query_parts = query_parts_of(query_refs, rows)
    own_ref = query_refs[0]
    own_ids = ids_of(own_ref)[:, :rows]
    for m, ref in enumerate((*query_refs[:2], query_refs[3], query_refs[5])):
        ids_ref[pl.ds(m * rows, rows), :] = along_rows(ids_of(ref)[:, :rows])
    mass = own_mass_ref[...]
    first = rows
    for ref, size in query_parts[1:]:
        query_ids = ids_ref[pl.ds(first, size), :]
        masses = mate_mass(ref[:size, :], query_ids, own_ref[:rows, :], own_ids)
        mass = mass + jnp.sum(masses, axis=0, keepdims=True)
        first += size
    mass_ref[...] = mass
    tail = tail_ref[: rows - head_ref.shape[0], :]
    key_rows = jnp.concatenate([unit_rows(head_ref[...]), tail], axis=0)
    key_ids = ids_of(tail_ref)[:, :rows]
    column_ref[...] = add_line(query_parts, ids_ref, key_rows, key_ids, None, sums_ref)


def middle_kernel(moves, head_ref, *refs):
    query_refs, (powers_ref, rest_ref) = refs[:-2], refs[-2:]

    @pl.when(arrived_at(moves))
    def _():
        keys = powers_ref.shape[1]
        units = unit_rows(head_ref[...])
        rest_ref[...] = units[keys:]
        first = 0
        for query_ref, size in query_parts_of(query_refs, query_refs[0].shape[0] - ID_ROWS):
            similar = lax.dot_general(
                query_ref[:size, :], units[:keys], (((1,), (1,)), ((), ())),
                preferred_element_type=jnp.float32,
            )
            powers_ref[pl.ds(first, size), :] = jnp.exp(similar * inverse_temp)
            first += size


def last_kernel(moves, powers_ref, rest_ref, tail_ref, ids_ref, *refs):
    query_refs, (column_ref, sums_ref) = refs[:-2], refs[-2:]
    rows = column_ref.shape[1]
    cut = powers_ref.shape[1]
    arrived = arrived_at(moves)

    @pl.when(arrived)
    def _():
        key_ids = ids_of(tail_ref)[:, :rows]
        key_rows = jnp.concatenate([rest_ref[...], tail_ref[: tail_ref.shape[0] - ID_ROWS, :]], axis=0)
        early_column = jnp.zeros((1, cut), jnp.float32)
        late_column = jnp.zeros((1, rows - cut), jnp.float32)
        first = 0
        for query_ref, size in query_parts_of(query_refs, rows):
            part = pl.ds(first, size)
            query_ids = ids_ref[part, :]
            similar = lax.dot_general(
                query_ref[:size, :], key_rows, (((1,), (1,)), ((), ())),
                preferred_element_type=jnp.float32,
            )
            powers = jnp.exp(similar * inverse_temp)
            late, column = add_masses(query_ids, key_ids[:, cut:], powers)
            late_column = late_column + column
            early, column = add_masses(query_ids, key_ids[:, :cut], powers_ref[part, :])
            early_column = early_column + column
            sums_ref[part, :] = early + late
            first += size
        column_ref[...] = jnp.concatenate([early_column, late_column], axis=1)

    @pl.when(jnp.logical_not(arrived))
    def _():
        column_ref[...] = jnp.zeros_like(column_ref)
        sums_ref[...] = jnp.zeros_like(sums_ref)


def fold_kernel(sums_ref, *refs):
    before_refs, row_refs = refs[:-PLANE], refs[-PLANE:]
    rows = row_refs[0].shape[1]
    for m in range(PLANE):
        row_sum = jnp.sum(sums_ref[pl.ds(m * rows, rows), :].T, axis=0, keepdims=True)
        row_refs[m][...] = row_sum + before_refs[m][...] if m < len(before_refs) else row_sum


def grid_plan(embeddings, cluster_ids):
    peers = lax.axis_size("gx")
    row_count, features = embeddings.shape
    plane_rows = PLANE * row_count
    params = pltpu.CompilerParams(vmem_limit_bytes=VMEM_BYTES)
    small = pl.CostEstimate(flops=1, bytes_accessed=1, transcendentals=0)
    vector = jax.ShapeDtypeStruct((1, row_count), jnp.float32)
    lanes = jax.ShapeDtypeStruct((plane_rows, LANES), jnp.float32)

    def rows_of(count):
        return jax.ShapeDtypeStruct((count, features), jnp.bfloat16)

    def in_plane(value, step):
        return lax.ppermute(value, "gx", [(i, i ^ step) for i in range(peers)])

    def on_line(value, moves, flip):
        pairs = [(a * PLANE + n, b * PLANE + (n ^ flip)) for a, b in moves for n in range(PLANE)]
        return lax.ppermute(value, "gx", pairs)

    first_moves = [(0, 1), (1, 2), (2, 3), (3, 0)]
    last_moves = [(0, 2), (1, 3)]
    forward_moves = [(1, 2), (2, 3)]
    first_back = [(b, a) for a, b in first_moves]
    last_back = [(b, a) for a, b in last_moves]

    half, part = row_count // 2, 5 * row_count // 8
    ranges = [(0, row_count), (0, half), (half, row_count), (part, row_count)]
    id_rows = [ID_ROWS, 0, ID_ROWS, ID_ROWS]
    first_head = on_line(embeddings[:part], first_moves, 0)
    block, *pieces, tail = pl.pallas_call(
        functools.partial(unit_kernel, ranges),
        out_shape=[rows_of(b - a + extra) for (a, b), extra in zip(ranges, id_rows)],
        cost_estimate=small,
        compiler_params=params,
    )(embeddings, cluster_ids.reshape(1, row_count))
    own_mass = pl.pallas_call(
        own_kernel, out_shape=vector, cost_estimate=small, compiler_params=params
    )(block)
    first_tail = on_line(tail, first_moves, 0)
    across = [in_plane(piece, 2) for piece in pieces]
    sibling = in_plane(block, 1)
    last_head = on_line(first_head, first_moves, 1)
    last_tail = on_line(first_tail, forward_moves, 1)
    corner = [in_plane(piece, 1) for piece in across]
    queries = (block, sibling, *across, *corner)
    ids, first_column, first_sums, mass = pl.pallas_call(
        functools.partial(first_kernel, first_moves),
        out_shape=(lanes, vector, lanes, vector),
        cost_estimate=small,
        compiler_params=params,
    )(own_mass, first_head, first_tail, *queries)
    returned_first = on_line(first_column, first_back, 0)
    powers, rest = pl.pallas_call(
        functools.partial(middle_kernel, last_moves),
        out_shape=(
            jax.ShapeDtypeStruct((plane_rows, half), jnp.float32), rows_of(part - half)
        ),
        cost_estimate=small,
        compiler_params=params,
    )(last_head, *queries)
    last_column, sums = pl.pallas_call(
        functools.partial(last_kernel, last_moves),
        out_shape=(vector, lanes),
        cost_estimate=small,
        compiler_params=params,
    )(powers, rest, last_tail, ids, *queries)
    returned_first, last_column = lax.optimization_barrier((returned_first, last_column))
    fold = pl.pallas_call(
        fold_kernel,
        out_shape=[vector] * PLANE,
        cost_estimate=small,
        compiler_params=params,
    )
    row_sums = fold(sums, *fold(first_sums, mass))
    returned = [on_line(last_column, last_back, 1)]
    returned += [in_plane(row_sums[step], step) for step in (3, 2, 1)]
    return jnp.log1p(sum(returned, row_sums[0] + returned_first)).reshape(row_count)


def on_device(embeddings, cluster_ids):
    if lax.axis_size("gx") == 4 * PLANE and embeddings.shape[0] == 2 * LANES:
        return grid_plan(embeddings, cluster_ids)
    return plain_plan(embeddings, cluster_ids)


def solution(mesh):
    in_specs = (P(("parts", "gx"), None), P(("parts", "gx")))
    out_specs = P(("parts", "gx"))
    return jax.shard_map(
        on_device, mesh=mesh, in_specs=in_specs, out_specs=out_specs, check_vma=False
    )
```

```python
import functools

import jax
import jax.numpy as jnp
from jax import lax
from jax.experimental import pallas as pl
from jax.experimental.pallas import tpu as pltpu
from jax.sharding import PartitionSpec as P

CLU_DEV = 1
PAD_MARK = 64.0
inverse_temp = 20.0


def tile_mass(query_rows, key_rows, query_ids, key_ids, query_start):
    similar = lax.dot_general(
        query_rows, key_rows, (((1,), (1,)), ((), ())), preferred_element_type=jnp.float32
    )
    query_pos = jnp.arange(query_rows.shape[0], dtype=jnp.int32) + query_start
    key_pos = jnp.arange(key_rows.shape[0], dtype=jnp.int32)
    mate_mask = (query_ids[:, None] == key_ids[None, :]) & (query_ids[:, None] >= 0)
    mate_mask = mate_mask & (query_pos[:, None] != key_pos[None, :])
    return jnp.where(mate_mask, jnp.exp(similar * inverse_temp), 0.0)


def density_scores(key_rows, key_ids):
    total_rows = key_rows.shape[0]
    block_rows = total_rows // 3
    pieces = [key_rows[i * block_rows : (i + 1) * block_rows] for i in range(3)]
    piece_ids = [key_ids[i * block_rows : (i + 1) * block_rows] for i in range(3)]
    sums = []
    for first in range(3):
        masses = tile_mass(pieces[first], key_rows, piece_ids[first], key_ids, first * block_rows)
        sums.append(jnp.sum(masses, axis=1))
    mass_sum = jnp.concatenate(sums, axis=0)
    return jnp.log1p(mass_sum)


def plain_plan(embeddings, cluster_ids):
    peer_count = lax.axis_size("gx")
    row_count = embeddings.shape[0]
    features = embeddings.shape[1]
    capacity = 3 * row_count // peer_count
    slot_total = peer_count * capacity
    squares = jnp.sum(jnp.square(embeddings.astype(jnp.float32)), axis=1)
    unit_rows = (embeddings.astype(jnp.float32) * lax.rsqrt(squares + 1e-06)[:, None]).astype(
        jnp.bfloat16
    )
    owner_of = cluster_ids // CLU_DEV
    onehot = (owner_of[:, None] == jnp.arange(peer_count, dtype=jnp.int32)[None, :]).astype(
        jnp.bfloat16
    )
    row_range = jnp.arange(row_count, dtype=jnp.int32)
    lower_tri = (row_range[:, None] >= row_range[None, :]).astype(jnp.bfloat16)
    running = jnp.dot(lower_tri, onehot, preferred_element_type=jnp.float32)
    slot_index = (jnp.sum(running * onehot.astype(jnp.float32), axis=1) - 1.0).astype(jnp.int32)
    target_slot = owner_of * capacity + slot_index
    slot_range = jnp.arange(slot_total, dtype=jnp.int32)
    select_mask = slot_range[:, None] == target_slot[None, :]
    outgoing = jnp.dot(
        select_mask.astype(jnp.bfloat16), unit_rows, preferred_element_type=jnp.float32
    )
    outgoing = outgoing.astype(jnp.bfloat16).reshape(peer_count, capacity, features)
    outgoing_ids = jnp.sum(jnp.where(select_mask, cluster_ids[None, :] + 1, 0), axis=1) - 1
    outgoing_ids = outgoing_ids.reshape(peer_count, capacity)
    arrived, arrived_ids = (
        lax.all_to_all(outgoing, "gx", split_axis=0, concat_axis=0, tiled=True),
        lax.all_to_all(outgoing_ids, "gx", split_axis=0, concat_axis=0, tiled=True),
    )
    key_rows = arrived.reshape(slot_total, features)
    key_ids = arrived_ids.reshape(slot_total)
    scores = density_scores(key_rows, key_ids)
    returned = lax.all_to_all(
        scores.reshape(peer_count, capacity), "gx", split_axis=0, concat_axis=0, tiled=True
    )
    flat_scores = returned.reshape(slot_total)
    pick_mask = target_slot[:, None] == slot_range[None, :]
    return jnp.sum(jnp.where(pick_mask, flat_scores[None, :], 0.0), axis=1)


LANES = 128
PLANE = 4
INVERSE_TEMP_BITS = 20.0 * 1.4426950408889634
ID_ROWS = 8
VMEM_BYTES = 8 * 1024 * 1024


def along_rows(values):
    return jnp.broadcast_to(values, (LANES, values.shape[1])).T


def ids_block(ids, width):
    wide = jnp.concatenate([ids, jnp.zeros((1, width - ids.shape[1]), jnp.float32)], axis=1)
    return jnp.broadcast_to(wide, (ID_ROWS, width)).astype(jnp.bfloat16)


def ids_of(ref):
    first = ref.shape[0] - ID_ROWS
    return ref[first:, :].astype(jnp.float32)[:1]


def mate_mass(query_rows, query_ids, key_rows, key_ids, shift=None):
    similar = lax.dot_general(
        query_rows, key_rows, (((1,), (1,)), ((), ())), preferred_element_type=jnp.float32
    )
    repeats = similar.shape[1] // LANES
    mates = jnp.concatenate([query_ids] * repeats, axis=1) == key_ids
    if shift is not None:
        query_pos = lax.broadcasted_iota(jnp.int32, similar.shape, 0) + shift
        key_pos = lax.broadcasted_iota(jnp.int32, similar.shape, 1)
        mates = mates & (query_pos != key_pos)
    return jnp.where(mates, jnp.exp2(similar * INVERSE_TEMP_BITS), 0.0)


def unit_rows(raw):
    features = raw.astype(jnp.float32)
    squares = jnp.sum(features * features, axis=1, keepdims=True)
    return (features * lax.rsqrt(squares + 1e-06)).astype(jnp.bfloat16)


def unit_kernel(ranges, rows_ref, ids_ref, *block_refs):
    rows, width = rows_ref.shape
    units = unit_rows(rows_ref[...])
    ids = ids_block(ids_ref[...].astype(jnp.float32), width)
    for (first, last), ref in zip(ranges, block_refs):
        size = last - first
        ref[:size, :] = units[first:last]
        if ref.shape[0] > size:
            ref[size:, :] = ids


def arrived_at(moves):
    plane = lax.axis_index("gx") // PLANE
    return functools.reduce(jnp.logical_or, [plane == receiver for _, receiver in moves])


def add_line(query_parts, ids_ref, key_rows, key_ids, earlier_ref, sums_ref):
    keys = key_rows.shape[0]
    column = jnp.zeros((1, keys), jnp.float32)
    first = 0
    for query_ref, size in query_parts:
        part = pl.ds(first, size)
        masses = mate_mass(query_ref[:size, :], ids_ref[part, :], key_rows, key_ids)
        column = column + jnp.sum(masses, axis=0, keepdims=True)
        folded = masses[:, :LANES]
        for lane in range(LANES, keys, LANES):
            folded = folded + masses[:, lane : lane + LANES]
        sums_ref[part, :] = folded if earlier_ref is None else earlier_ref[part, :] + folded
        first += size
    return column


def add_masses(query_ids, key_ids, powers):
    mates = jnp.concatenate([query_ids] * (powers.shape[1] // LANES), axis=1) == key_ids
    masses = jnp.where(mates, powers, 0.0)
    folded = masses[:, :LANES]
    for lane in range(LANES, powers.shape[1], LANES):
        folded = folded + masses[:, lane : lane + LANES]
    return folded, jnp.sum(masses, axis=0, keepdims=True)


def query_parts_of(refs, rows):
    head = refs[2].shape[0]
    sizes = [rows, rows] + [head, rows - head] * (PLANE - 2)
    return list(zip(refs, sizes))


def own_kernel(own_ref, mass_ref):
    rows = mass_ref.shape[1]
    own_ids = ids_of(own_ref)[:, :rows]
    masses = mate_mass(own_ref[:rows, :], along_rows(own_ids), own_ref[:rows, :], own_ids, 0)
    mass_ref[...] = jnp.sum(masses, axis=0, keepdims=True)


def first_kernel(moves, own_mass_ref, head_ref, tail_ref, *refs):
    query_refs, (ids_ref, column_ref, sums_ref, mass_ref) = refs[:-4], refs[-4:]
    rows = mass_ref.shape[1]
    query_parts = query_parts_of(query_refs, rows)
    own_ref = query_refs[0]
    own_ids = ids_of(own_ref)[:, :rows]
    for m, ref in enumerate((*query_refs[:2], query_refs[3], query_refs[5])):
        ids_ref[pl.ds(m * rows, rows), :] = along_rows(ids_of(ref)[:, :rows])
    mass = own_mass_ref[...]
    first = rows
    for ref, size in query_parts[1:]:
        query_ids = ids_ref[pl.ds(first, size), :]
        masses = mate_mass(ref[:size, :], query_ids, own_ref[:rows, :], own_ids)
        mass = mass + jnp.sum(masses, axis=0, keepdims=True)
        first += size
    mass_ref[...] = mass
    tail = tail_ref[: rows - head_ref.shape[0], :]
    key_rows = jnp.concatenate([unit_rows(head_ref[...]), tail], axis=0)
    key_ids = ids_of(tail_ref)[:, :rows]
    column_ref[...] = add_line(query_parts, ids_ref, key_rows, key_ids, None, sums_ref)


def middle_kernel(moves, head_ref, *refs):
    query_refs, (powers_ref, rest_ref) = refs[:-2], refs[-2:]

    @pl.when(arrived_at(moves))
    def _():
        keys = powers_ref.shape[1]
        units = unit_rows(head_ref[...])
        rest_ref[...] = units[keys:]
        first = 0
        for query_ref, size in query_parts_of(query_refs, query_refs[0].shape[0] - ID_ROWS):
            similar = lax.dot_general(
                query_ref[:size, :], units[:keys], (((1,), (1,)), ((), ())),
                preferred_element_type=jnp.float32,
            )
            powers_ref[pl.ds(first, size), :] = jnp.exp2(similar * INVERSE_TEMP_BITS)
            first += size


def last_kernel(moves, powers_ref, rest_ref, tail_ref, ids_ref, earlier_ref, *refs):
    query_refs, (column_ref, sums_ref) = refs[:-2], refs[-2:]
    rows = column_ref.shape[1]
    cut = powers_ref.shape[1]
    arrived = arrived_at(moves)

    @pl.when(arrived)
    def _():
        key_ids = ids_of(tail_ref)[:, :rows]
        key_rows = jnp.concatenate([rest_ref[...], tail_ref[: tail_ref.shape[0] - ID_ROWS, :]], axis=0)
        early_column = jnp.zeros((1, cut), jnp.float32)
        late_column = jnp.zeros((1, rows - cut), jnp.float32)
        first = 0
        for query_ref, size in query_parts_of(query_refs, rows):
            part = pl.ds(first, size)
            query_ids = ids_ref[part, :]
            similar = lax.dot_general(
                query_ref[:size, :], key_rows, (((1,), (1,)), ((), ())),
                preferred_element_type=jnp.float32,
            )
            powers = jnp.exp2(similar * INVERSE_TEMP_BITS)
            late, column = add_masses(query_ids, key_ids[:, cut:], powers)
            late_column = late_column + column
            early, column = add_masses(query_ids, key_ids[:, :cut], powers_ref[part, :])
            early_column = early_column + column
            sums_ref[part, :] = earlier_ref[part, :] + early + late
            first += size
        column_ref[...] = jnp.concatenate([early_column, late_column], axis=1)

    @pl.when(jnp.logical_not(arrived))
    def _():
        column_ref[...] = jnp.zeros_like(column_ref)
        sums_ref[...] = earlier_ref[...]


def fold_kernel(sums_ref, mass_ref, *row_refs):
    rows = mass_ref.shape[1]
    for m in range(PLANE):
        row_sum = jnp.sum(sums_ref[pl.ds(m * rows, rows), :].T, axis=0, keepdims=True)
        row_refs[m][...] = row_sum + mass_ref[...] if m == 0 else row_sum


def grid_plan(embeddings, cluster_ids):
    peers = lax.axis_size("gx")
    row_count, features = embeddings.shape
    plane_rows = PLANE * row_count
    params = pltpu.CompilerParams(vmem_limit_bytes=VMEM_BYTES)
    small = pl.CostEstimate(flops=1, bytes_accessed=1, transcendentals=0)
    vector = jax.ShapeDtypeStruct((1, row_count), jnp.float32)
    lanes = jax.ShapeDtypeStruct((plane_rows, LANES), jnp.float32)

    def rows_of(count):
        return jax.ShapeDtypeStruct((count, features), jnp.bfloat16)

    def in_plane(value, step):
        return lax.ppermute(value, "gx", [(i, i ^ step) for i in range(peers)])

    def on_line(value, moves, flip):
        pairs = [(a * PLANE + n, b * PLANE + (n ^ flip)) for a, b in moves for n in range(PLANE)]
        return lax.ppermute(value, "gx", pairs)

    first_moves = [(0, 1), (1, 2), (2, 3), (3, 0)]
    last_moves = [(0, 2), (1, 3)]
    forward_moves = [(1, 2), (2, 3)]
    first_back = [(b, a) for a, b in first_moves]
    last_back = [(b, a) for a, b in last_moves]

    half, part = row_count // 2, 5 * row_count // 8
    ranges = [(0, row_count), (0, half), (half, row_count), (part, row_count)]
    id_rows = [ID_ROWS, 0, ID_ROWS, ID_ROWS]
    first_head = on_line(embeddings[:part], first_moves, 0)
    block, *pieces, tail = pl.pallas_call(
        functools.partial(unit_kernel, ranges),
        out_shape=[rows_of(b - a + extra) for (a, b), extra in zip(ranges, id_rows)],
        cost_estimate=small,
        compiler_params=params,
    )(embeddings, cluster_ids.reshape(1, row_count))
    own_mass = pl.pallas_call(
        own_kernel, out_shape=vector, cost_estimate=small, compiler_params=params
    )(block)
    own_mass, tail = lax.optimization_barrier((own_mass, tail))
    first_tail = on_line(tail, first_moves, 0)
    across = [in_plane(piece, 2) for piece in pieces]
    sibling = in_plane(block, 1)
    last_head = on_line(first_head, first_moves, 1)
    last_tail = on_line(first_tail, forward_moves, 1)
    corner = [in_plane(piece, 1) for piece in across]
    queries = (block, sibling, *across, *corner)
    ids, first_column, first_sums, mass = pl.pallas_call(
        functools.partial(first_kernel, first_moves),
        out_shape=(lanes, vector, lanes, vector),
        cost_estimate=small,
        compiler_params=params,
    )(own_mass, first_head, first_tail, *queries)
    returned_first = on_line(first_column, first_back, 0)
    powers, rest = pl.pallas_call(
        functools.partial(middle_kernel, last_moves),
        out_shape=(
            jax.ShapeDtypeStruct((plane_rows, half), jnp.float32), rows_of(part - half)
        ),
        cost_estimate=small,
        compiler_params=params,
    )(last_head, *queries)
    last_column, sums = pl.pallas_call(
        functools.partial(last_kernel, last_moves),
        out_shape=(vector, lanes),
        cost_estimate=small,
        compiler_params=params,
    )(powers, rest, last_tail, ids, first_sums, *queries)
    returned_first, last_column = lax.optimization_barrier((returned_first, last_column))
    row_sums = pl.pallas_call(
        fold_kernel,
        out_shape=[vector] * PLANE,
        cost_estimate=small,
        compiler_params=params,
    )(sums, mass)
    returned = [on_line(last_column, last_back, 1)]
    returned += [in_plane(row_sums[step], step) for step in (2, 3, 1)]
    return jnp.log1p(sum(returned, row_sums[0] + returned_first)).reshape(row_count)


def on_device(embeddings, cluster_ids):
    if lax.axis_size("gx") == 4 * PLANE and embeddings.shape[0] == 2 * LANES:
        return grid_plan(embeddings, cluster_ids)
    return plain_plan(embeddings, cluster_ids)


def solution(mesh):
    in_specs = (P(("parts", "gx"), None), P(("parts", "gx")))
    out_specs = P(("parts", "gx"))
    return jax.shard_map(
        on_device, mesh=mesh, in_specs=in_specs, out_specs=out_specs, check_vma=False
    )
```

```python
import functools

import jax
import jax.numpy as jnp
from jax import lax
from jax.experimental import pallas as pl
from jax.experimental.pallas import tpu as pltpu
from jax.sharding import PartitionSpec as P

CLU_DEV = 1
PAD_MARK = 64.0
inverse_temp = 20.0


def tile_mass(query_rows, key_rows, query_ids, key_ids, query_start):
    similar = lax.dot_general(
        query_rows, key_rows, (((1,), (1,)), ((), ())), preferred_element_type=jnp.float32
    )
    query_pos = jnp.arange(query_rows.shape[0], dtype=jnp.int32) + query_start
    key_pos = jnp.arange(key_rows.shape[0], dtype=jnp.int32)
    mate_mask = (query_ids[:, None] == key_ids[None, :]) & (query_ids[:, None] >= 0)
    mate_mask = mate_mask & (query_pos[:, None] != key_pos[None, :])
    return jnp.where(mate_mask, jnp.exp(similar * inverse_temp), 0.0)


def density_scores(key_rows, key_ids):
    total_rows = key_rows.shape[0]
    block_rows = total_rows // 3
    pieces = [key_rows[i * block_rows : (i + 1) * block_rows] for i in range(3)]
    piece_ids = [key_ids[i * block_rows : (i + 1) * block_rows] for i in range(3)]
    sums = []
    for first in range(3):
        masses = tile_mass(pieces[first], key_rows, piece_ids[first], key_ids, first * block_rows)
        sums.append(jnp.sum(masses, axis=1))
    mass_sum = jnp.concatenate(sums, axis=0)
    return jnp.log1p(mass_sum)


def plain_plan(embeddings, cluster_ids):
    peer_count = lax.axis_size("gx")
    row_count = embeddings.shape[0]
    features = embeddings.shape[1]
    capacity = 3 * row_count // peer_count
    slot_total = peer_count * capacity
    squares = jnp.sum(jnp.square(embeddings.astype(jnp.float32)), axis=1)
    unit_rows = (embeddings.astype(jnp.float32) * lax.rsqrt(squares + 1e-06)[:, None]).astype(
        jnp.bfloat16
    )
    owner_of = cluster_ids // CLU_DEV
    onehot = (owner_of[:, None] == jnp.arange(peer_count, dtype=jnp.int32)[None, :]).astype(
        jnp.bfloat16
    )
    row_range = jnp.arange(row_count, dtype=jnp.int32)
    lower_tri = (row_range[:, None] >= row_range[None, :]).astype(jnp.bfloat16)
    running = jnp.dot(lower_tri, onehot, preferred_element_type=jnp.float32)
    slot_index = (jnp.sum(running * onehot.astype(jnp.float32), axis=1) - 1.0).astype(jnp.int32)
    target_slot = owner_of * capacity + slot_index
    slot_range = jnp.arange(slot_total, dtype=jnp.int32)
    select_mask = slot_range[:, None] == target_slot[None, :]
    outgoing = jnp.dot(
        select_mask.astype(jnp.bfloat16), unit_rows, preferred_element_type=jnp.float32
    )
    outgoing = outgoing.astype(jnp.bfloat16).reshape(peer_count, capacity, features)
    outgoing_ids = jnp.sum(jnp.where(select_mask, cluster_ids[None, :] + 1, 0), axis=1) - 1
    outgoing_ids = outgoing_ids.reshape(peer_count, capacity)
    arrived, arrived_ids = (
        lax.all_to_all(outgoing, "gx", split_axis=0, concat_axis=0, tiled=True),
        lax.all_to_all(outgoing_ids, "gx", split_axis=0, concat_axis=0, tiled=True),
    )
    key_rows = arrived.reshape(slot_total, features)
    key_ids = arrived_ids.reshape(slot_total)
    scores = density_scores(key_rows, key_ids)
    returned = lax.all_to_all(
        scores.reshape(peer_count, capacity), "gx", split_axis=0, concat_axis=0, tiled=True
    )
    flat_scores = returned.reshape(slot_total)
    pick_mask = target_slot[:, None] == slot_range[None, :]
    return jnp.sum(jnp.where(pick_mask, flat_scores[None, :], 0.0), axis=1)


LANES = 128
PLANE = 4
INVERSE_TEMP_BITS = 20.0 * 1.4426950408889634
ID_ROWS = 8
VMEM_BYTES = 16 * 1024 * 1024


def along_rows(values):
    return jnp.broadcast_to(values, (LANES, values.shape[1])).T


def ids_block(ids, width):
    wide = jnp.concatenate([ids, jnp.zeros((1, width - ids.shape[1]), jnp.float32)], axis=1)
    return jnp.broadcast_to(wide, (ID_ROWS, width)).astype(jnp.bfloat16)


def ids_of(ref):
    first = ref.shape[0] - ID_ROWS
    return ref[first:, :].astype(jnp.float32)[:1]


def mate_mass(query_rows, query_ids, key_rows, key_ids, shift=None):
    similar = lax.dot_general(
        query_rows, key_rows, (((1,), (1,)), ((), ())), preferred_element_type=jnp.float32
    )
    repeats = similar.shape[1] // LANES
    mates = jnp.concatenate([query_ids] * repeats, axis=1) == key_ids
    if shift is not None:
        query_pos = lax.broadcasted_iota(jnp.int32, similar.shape, 0) + shift
        key_pos = lax.broadcasted_iota(jnp.int32, similar.shape, 1)
        mates = mates & (query_pos != key_pos)
    return jnp.where(mates, jnp.exp2(similar * INVERSE_TEMP_BITS), 0.0)


def unit_rows(raw):
    features = raw.astype(jnp.float32)
    squares = jnp.sum(features * features, axis=1, keepdims=True)
    return (features * lax.rsqrt(squares + 1e-06)).astype(jnp.bfloat16)


def unit_kernel(ranges, rows_ref, ids_ref, *block_refs):
    rows, width = rows_ref.shape
    units = unit_rows(rows_ref[...])
    ids = ids_block(ids_ref[...].astype(jnp.float32), width)
    for (first, last), ref in zip(ranges, block_refs):
        size = last - first
        ref[:size, :] = units[first:last]
        if ref.shape[0] > size:
            ref[size:, :] = ids


def arrived_at(moves):
    plane = lax.axis_index("gx") // PLANE
    return functools.reduce(jnp.logical_or, [plane == receiver for _, receiver in moves])


def add_line(query_parts, ids_ref, key_rows, key_ids, earlier_ref, sums_ref):
    keys = key_rows.shape[0]
    column = jnp.zeros((1, keys), jnp.float32)
    first = 0
    for query_ref, size in query_parts:
        part = pl.ds(first, size)
        masses = mate_mass(query_ref[:size, :], ids_ref[part, :], key_rows, key_ids)
        column = column + jnp.sum(masses, axis=0, keepdims=True)
        folded = masses[:, :LANES]
        for lane in range(LANES, keys, LANES):
            folded = folded + masses[:, lane : lane + LANES]
        sums_ref[part, :] = folded if earlier_ref is None else earlier_ref[part, :] + folded
        first += size
    return column


def add_masses(query_ids, key_ids, powers):
    mates = jnp.concatenate([query_ids] * (powers.shape[1] // LANES), axis=1) == key_ids
    masses = jnp.where(mates, powers, 0.0)
    folded = masses[:, :LANES]
    for lane in range(LANES, powers.shape[1], LANES):
        folded = folded + masses[:, lane : lane + LANES]
    return folded, jnp.sum(masses, axis=0, keepdims=True)


def query_parts_of(refs, rows):
    head = refs[2].shape[0]
    sizes = [rows, rows] + [head, rows - head] * (PLANE - 2)
    return list(zip(refs, sizes))


def own_kernel(own_ref, mass_ref):
    rows = mass_ref.shape[1]
    own_ids = ids_of(own_ref)[:, :rows]
    masses = mate_mass(own_ref[:rows, :], along_rows(own_ids), own_ref[:rows, :], own_ids, 0)
    mass_ref[...] = jnp.sum(masses, axis=0, keepdims=True)


def first_kernel(moves, own_mass_ref, head_ref, tail_ref, *refs):
    query_refs, (ids_ref, column_ref, sums_ref, mass_ref) = refs[:-4], refs[-4:]
    rows = mass_ref.shape[1]
    query_parts = query_parts_of(query_refs, rows)
    own_ref = query_refs[0]
    own_ids = ids_of(own_ref)[:, :rows]
    for m, ref in enumerate((*query_refs[:2], query_refs[3], query_refs[5])):
        ids_ref[pl.ds(m * rows, rows), :] = along_rows(ids_of(ref)[:, :rows])
    mass = own_mass_ref[...]
    first = rows
    for ref, size in query_parts[1:]:
        query_ids = ids_ref[pl.ds(first, size), :]
        masses = mate_mass(ref[:size, :], query_ids, own_ref[:rows, :], own_ids)
        mass = mass + jnp.sum(masses, axis=0, keepdims=True)
        first += size
    mass_ref[...] = mass
    tail = tail_ref[: rows - head_ref.shape[0], :]
    key_rows = jnp.concatenate([unit_rows(head_ref[...]), tail], axis=0)
    key_ids = ids_of(tail_ref)[:, :rows]
    column_ref[...] = add_line(query_parts, ids_ref, key_rows, key_ids, None, sums_ref)


def middle_kernel(moves, head_ref, *refs):
    query_refs, (powers_ref, rest_ref) = refs[:-2], refs[-2:]

    @pl.when(arrived_at(moves))
    def _():
        keys = powers_ref.shape[1]
        units = unit_rows(head_ref[...])
        rest_ref[...] = units[keys:]
        first = 0
        for query_ref, size in query_parts_of(query_refs, query_refs[0].shape[0] - ID_ROWS):
            similar = lax.dot_general(
                query_ref[:size, :], units[:keys], (((1,), (1,)), ((), ())),
                preferred_element_type=jnp.float32,
            )
            powers_ref[pl.ds(first, size), :] = jnp.exp2(similar * INVERSE_TEMP_BITS)
            first += size


def last_kernel(moves, powers_ref, rest_ref, tail_ref, ids_ref, earlier_ref, *refs):
    query_refs, (column_ref, sums_ref) = refs[:-2], refs[-2:]
    rows = column_ref.shape[1]
    cut = powers_ref.shape[1]
    arrived = arrived_at(moves)

    @pl.when(arrived)
    def _():
        key_ids = ids_of(tail_ref)[:, :rows]
        key_rows = jnp.concatenate([rest_ref[...], tail_ref[: tail_ref.shape[0] - ID_ROWS, :]], axis=0)
        early_column = jnp.zeros((1, cut), jnp.float32)
        late_column = jnp.zeros((1, rows - cut), jnp.float32)
        first = 0
        for query_ref, size in query_parts_of(query_refs, rows):
            part = pl.ds(first, size)
            query_ids = ids_ref[part, :]
            similar = lax.dot_general(
                query_ref[:size, :], key_rows, (((1,), (1,)), ((), ())),
                preferred_element_type=jnp.float32,
            )
            powers = jnp.exp2(similar * INVERSE_TEMP_BITS)
            late, column = add_masses(query_ids, key_ids[:, cut:], powers)
            late_column = late_column + column
            early, column = add_masses(query_ids, key_ids[:, :cut], powers_ref[part, :])
            early_column = early_column + column
            sums_ref[part, :] = earlier_ref[part, :] + early + late
            first += size
        column_ref[...] = jnp.concatenate([early_column, late_column], axis=1)

    @pl.when(jnp.logical_not(arrived))
    def _():
        column_ref[...] = jnp.zeros_like(column_ref)
        sums_ref[...] = earlier_ref[...]


def fold_kernel(sums_ref, mass_ref, *row_refs):
    rows = mass_ref.shape[1]
    for m in range(PLANE):
        row_sum = jnp.sum(sums_ref[pl.ds(m * rows, rows), :].T, axis=0, keepdims=True)
        row_refs[m][...] = row_sum + mass_ref[...] if m == 0 else row_sum


def grid_plan(embeddings, cluster_ids):
    peers = lax.axis_size("gx")
    row_count, features = embeddings.shape
    plane_rows = PLANE * row_count
    params = pltpu.CompilerParams(vmem_limit_bytes=VMEM_BYTES)
    small = pl.CostEstimate(flops=1, bytes_accessed=1, transcendentals=0)
    vector = jax.ShapeDtypeStruct((1, row_count), jnp.float32)
    lanes = jax.ShapeDtypeStruct((plane_rows, LANES), jnp.float32)

    def rows_of(count):
        return jax.ShapeDtypeStruct((count, features), jnp.bfloat16)

    def in_plane(value, step):
        return lax.ppermute(value, "gx", [(i, i ^ step) for i in range(peers)])

    def on_line(value, moves, flip):
        pairs = [(a * PLANE + n, b * PLANE + (n ^ flip)) for a, b in moves for n in range(PLANE)]
        return lax.ppermute(value, "gx", pairs)

    first_moves = [(0, 1), (1, 2), (2, 3), (3, 0)]
    last_moves = [(0, 2), (1, 3)]
    forward_moves = [(1, 2), (2, 3)]
    first_back = [(b, a) for a, b in first_moves]
    last_back = [(b, a) for a, b in last_moves]

    half, part = row_count // 2, 5 * row_count // 8
    ranges = [(0, row_count), (0, half), (half, row_count), (part, row_count)]
    id_rows = [ID_ROWS, 0, ID_ROWS, ID_ROWS]
    first_head = on_line(embeddings[:part], first_moves, 0)
    block, *pieces, tail = pl.pallas_call(
        functools.partial(unit_kernel, ranges),
        out_shape=[rows_of(b - a + extra) for (a, b), extra in zip(ranges, id_rows)],
        cost_estimate=small,
        compiler_params=params,
    )(embeddings, cluster_ids.reshape(1, row_count))
    own_mass = pl.pallas_call(
        own_kernel, out_shape=vector, cost_estimate=small, compiler_params=params
    )(block)
    own_mass, tail = lax.optimization_barrier((own_mass, tail))
    first_tail = on_line(tail, first_moves, 0)
    across = [in_plane(piece, 2) for piece in pieces]
    sibling = in_plane(block, 1)
    last_head = on_line(first_head, first_moves, 1)
    last_tail = on_line(first_tail, forward_moves, 1)
    corner = [in_plane(piece, 1) for piece in across]
    queries = (block, sibling, *across, *corner)
    ids, first_column, first_sums, mass = pl.pallas_call(
        functools.partial(first_kernel, first_moves),
        out_shape=(lanes, vector, lanes, vector),
        cost_estimate=small,
        compiler_params=params,
    )(own_mass, first_head, first_tail, *queries)
    returned_first = on_line(first_column, first_back, 0)
    powers, rest = pl.pallas_call(
        functools.partial(middle_kernel, last_moves),
        out_shape=(
            jax.ShapeDtypeStruct((plane_rows, half), jnp.float32), rows_of(part - half)
        ),
        cost_estimate=small,
        compiler_params=params,
    )(last_head, *queries)
    last_column, sums = pl.pallas_call(
        functools.partial(last_kernel, last_moves),
        out_shape=(vector, lanes),
        cost_estimate=small,
        compiler_params=params,
    )(powers, rest, last_tail, ids, first_sums, *queries)
    returned_first, last_column = lax.optimization_barrier((returned_first, last_column))
    row_sums = pl.pallas_call(
        fold_kernel,
        out_shape=[vector] * PLANE,
        cost_estimate=small,
        compiler_params=params,
    )(sums, mass)
    returned = [on_line(last_column, last_back, 1)]
    returned += [in_plane(row_sums[step], step) for step in (1, 3, 2)]
    return jnp.log1p(sum(returned, row_sums[0] + returned_first)).reshape(row_count)


def on_device(embeddings, cluster_ids):
    if lax.axis_size("gx") == 4 * PLANE and embeddings.shape[0] == 2 * LANES:
        return grid_plan(embeddings, cluster_ids)
    return plain_plan(embeddings, cluster_ids)


def solution(mesh):
    in_specs = (P(("parts", "gx"), None), P(("parts", "gx")))
    out_specs = P(("parts", "gx"))
    return jax.shard_map(
        on_device, mesh=mesh, in_specs=in_specs, out_specs=out_specs, check_vma=False
    )
```

```python
import functools

import jax
import jax.numpy as jnp
from jax import lax
from jax.experimental import pallas as pl
from jax.experimental.pallas import tpu as pltpu
from jax.sharding import PartitionSpec as P

CLU_DEV = 1
PAD_MARK = 64.0
inverse_temp = 20.0


def tile_mass(query_rows, key_rows, query_ids, key_ids, query_start):
    similar = lax.dot_general(
        query_rows, key_rows, (((1,), (1,)), ((), ())), preferred_element_type=jnp.float32
    )
    query_pos = jnp.arange(query_rows.shape[0], dtype=jnp.int32) + query_start
    key_pos = jnp.arange(key_rows.shape[0], dtype=jnp.int32)
    mate_mask = (query_ids[:, None] == key_ids[None, :]) & (query_ids[:, None] >= 0)
    mate_mask = mate_mask & (query_pos[:, None] != key_pos[None, :])
    return jnp.where(mate_mask, jnp.exp(similar * inverse_temp), 0.0)


def density_scores(key_rows, key_ids):
    total_rows = key_rows.shape[0]
    block_rows = total_rows // 3
    pieces = [key_rows[i * block_rows : (i + 1) * block_rows] for i in range(3)]
    piece_ids = [key_ids[i * block_rows : (i + 1) * block_rows] for i in range(3)]
    sums = []
    for first in range(3):
        masses = tile_mass(pieces[first], key_rows, piece_ids[first], key_ids, first * block_rows)
        sums.append(jnp.sum(masses, axis=1))
    mass_sum = jnp.concatenate(sums, axis=0)
    return jnp.log1p(mass_sum)


def plain_plan(embeddings, cluster_ids):
    peer_count = lax.axis_size("gx")
    row_count = embeddings.shape[0]
    features = embeddings.shape[1]
    capacity = 3 * row_count // peer_count
    slot_total = peer_count * capacity
    squares = jnp.sum(jnp.square(embeddings.astype(jnp.float32)), axis=1)
    unit_rows = (embeddings.astype(jnp.float32) * lax.rsqrt(squares + 1e-06)[:, None]).astype(
        jnp.bfloat16
    )
    owner_of = cluster_ids // CLU_DEV
    onehot = (owner_of[:, None] == jnp.arange(peer_count, dtype=jnp.int32)[None, :]).astype(
        jnp.bfloat16
    )
    row_range = jnp.arange(row_count, dtype=jnp.int32)
    lower_tri = (row_range[:, None] >= row_range[None, :]).astype(jnp.bfloat16)
    running = jnp.dot(lower_tri, onehot, preferred_element_type=jnp.float32)
    slot_index = (jnp.sum(running * onehot.astype(jnp.float32), axis=1) - 1.0).astype(jnp.int32)
    target_slot = owner_of * capacity + slot_index
    slot_range = jnp.arange(slot_total, dtype=jnp.int32)
    select_mask = slot_range[:, None] == target_slot[None, :]
    outgoing = jnp.dot(
        select_mask.astype(jnp.bfloat16), unit_rows, preferred_element_type=jnp.float32
    )
    outgoing = outgoing.astype(jnp.bfloat16).reshape(peer_count, capacity, features)
    outgoing_ids = jnp.sum(jnp.where(select_mask, cluster_ids[None, :] + 1, 0), axis=1) - 1
    outgoing_ids = outgoing_ids.reshape(peer_count, capacity)
    arrived, arrived_ids = (
        lax.all_to_all(outgoing, "gx", split_axis=0, concat_axis=0, tiled=True),
        lax.all_to_all(outgoing_ids, "gx", split_axis=0, concat_axis=0, tiled=True),
    )
    key_rows = arrived.reshape(slot_total, features)
    key_ids = arrived_ids.reshape(slot_total)
    scores = density_scores(key_rows, key_ids)
    returned = lax.all_to_all(
        scores.reshape(peer_count, capacity), "gx", split_axis=0, concat_axis=0, tiled=True
    )
    flat_scores = returned.reshape(slot_total)
    pick_mask = target_slot[:, None] == slot_range[None, :]
    return jnp.sum(jnp.where(pick_mask, flat_scores[None, :], 0.0), axis=1)


LANES = 128
PLANE = 4
INVERSE_TEMP_BITS = 20.0 * 1.4426950408889634
ID_ROWS = 8
VMEM_BYTES = 16 * 1024 * 1024


def along_rows(values):
    return jnp.broadcast_to(values, (LANES, values.shape[1])).T


def ids_block(ids, width):
    wide = jnp.concatenate([ids, jnp.zeros((1, width - ids.shape[1]), jnp.float32)], axis=1)
    return jnp.broadcast_to(wide, (ID_ROWS, width)).astype(jnp.bfloat16)


def ids_of(ref):
    first = ref.shape[0] - ID_ROWS
    return ref[first:, :].astype(jnp.float32)[:1]


def mate_mass(query_rows, query_ids, key_rows, key_ids, shift=None):
    similar = lax.dot_general(
        query_rows, key_rows, (((1,), (1,)), ((), ())), preferred_element_type=jnp.float32
    )
    repeats = similar.shape[1] // LANES
    mates = jnp.concatenate([query_ids] * repeats, axis=1) == key_ids
    if shift is not None:
        query_pos = lax.broadcasted_iota(jnp.int32, similar.shape, 0) + shift
        key_pos = lax.broadcasted_iota(jnp.int32, similar.shape, 1)
        mates = mates & (query_pos != key_pos)
    return jnp.where(mates, jnp.exp2(similar * INVERSE_TEMP_BITS), 0.0)


def unit_rows(raw):
    features = raw.astype(jnp.float32)
    squares = jnp.sum(features * features, axis=1, keepdims=True)
    return (features * lax.rsqrt(squares + 1e-06)).astype(jnp.bfloat16)


def unit_kernel(ranges, rows_ref, ids_ref, *block_refs):
    rows, width = rows_ref.shape
    units = unit_rows(rows_ref[...])
    ids = ids_block(ids_ref[...].astype(jnp.float32), width)
    for (first, last), ref in zip(ranges, block_refs):
        size = last - first
        ref[:size, :] = units[first:last]
        if ref.shape[0] > size:
            ref[size:, :] = ids


def arrived_at(moves):
    plane = lax.axis_index("gx") // PLANE
    return functools.reduce(jnp.logical_or, [plane == receiver for _, receiver in moves])


def add_line(query_parts, ids_ref, key_rows, key_ids, earlier_ref, sums_ref):
    keys = key_rows.shape[0]
    column = jnp.zeros((1, keys), jnp.float32)
    first = 0
    for query_ref, size in query_parts:
        part = pl.ds(first, size)
        masses = mate_mass(query_ref[:size, :], ids_ref[part, :], key_rows, key_ids)
        column = column + jnp.sum(masses, axis=0, keepdims=True)
        folded = masses[:, :LANES]
        for lane in range(LANES, keys, LANES):
            folded = folded + masses[:, lane : lane + LANES]
        sums_ref[part, :] = folded if earlier_ref is None else earlier_ref[part, :] + folded
        first += size
    return column


def add_masses(query_ids, key_ids, powers):
    mates = jnp.concatenate([query_ids] * (powers.shape[1] // LANES), axis=1) == key_ids
    masses = jnp.where(mates, powers, 0.0)
    folded = masses[:, :LANES]
    for lane in range(LANES, powers.shape[1], LANES):
        folded = folded + masses[:, lane : lane + LANES]
    return folded, jnp.sum(masses, axis=0, keepdims=True)


def query_parts_of(refs, rows):
    head = refs[2].shape[0]
    sizes = [rows, rows] + [head, rows - head] * (PLANE - 2)
    return list(zip(refs, sizes))


def own_kernel(own_ref, mass_ref):
    rows = mass_ref.shape[1]
    own_ids = ids_of(own_ref)[:, :rows]
    masses = mate_mass(own_ref[:rows, :], along_rows(own_ids), own_ref[:rows, :], own_ids, 0)
    mass_ref[...] = jnp.sum(masses, axis=0, keepdims=True)


def first_kernel(moves, own_mass_ref, head_ref, tail_ref, *refs):
    query_refs, (ids_ref, column_ref, sums_ref, mass_ref) = refs[:-4], refs[-4:]
    rows = mass_ref.shape[1]
    query_parts = query_parts_of(query_refs, rows)
    own_ref = query_refs[0]
    own_ids = ids_of(own_ref)[:, :rows]
    for m, ref in enumerate((*query_refs[:2], query_refs[3], query_refs[5])):
        ids_ref[pl.ds(m * rows, rows), :] = along_rows(ids_of(ref)[:, :rows])
    mass = own_mass_ref[...]
    first = rows
    for ref, size in query_parts[1:]:
        query_ids = ids_ref[pl.ds(first, size), :]
        masses = mate_mass(ref[:size, :], query_ids, own_ref[:rows, :], own_ids)
        mass = mass + jnp.sum(masses, axis=0, keepdims=True)
        first += size
    mass_ref[...] = mass
    tail = tail_ref[: rows - head_ref.shape[0], :]
    key_rows = jnp.concatenate([unit_rows(head_ref[...]), tail], axis=0)
    key_ids = ids_of(tail_ref)[:, :rows]
    column_ref[...] = add_line(query_parts, ids_ref, key_rows, key_ids, None, sums_ref)


def middle_kernel(moves, head_ref, *refs):
    query_refs, (powers_ref, rest_ref) = refs[:-2], refs[-2:]

    @pl.when(arrived_at(moves))
    def _():
        keys = powers_ref.shape[1]
        units = unit_rows(head_ref[...])
        rest_ref[...] = units[keys:]
        first = 0
        for query_ref, size in query_parts_of(query_refs, query_refs[0].shape[0] - ID_ROWS):
            similar = lax.dot_general(
                query_ref[:size, :], units[:keys], (((1,), (1,)), ((), ())),
                preferred_element_type=jnp.float32,
            )
            powers_ref[pl.ds(first, size), :] = jnp.exp2(similar * INVERSE_TEMP_BITS)
            first += size


def last_kernel(moves, powers_ref, rest_ref, tail_ref, ids_ref, earlier_ref, *refs):
    query_refs, (column_ref, sums_ref) = refs[:-2], refs[-2:]
    rows = column_ref.shape[1]
    cut = powers_ref.shape[1]
    arrived = arrived_at(moves)

    @pl.when(arrived)
    def _():
        key_ids = ids_of(tail_ref)[:, :rows]
        key_rows = jnp.concatenate([rest_ref[...], tail_ref[: tail_ref.shape[0] - ID_ROWS, :]], axis=0)
        early_column = jnp.zeros((1, cut), jnp.float32)
        late_column = jnp.zeros((1, rows - cut), jnp.float32)
        first = 0
        for query_ref, size in query_parts_of(query_refs, rows):
            part = pl.ds(first, size)
            query_ids = ids_ref[part, :]
            similar = lax.dot_general(
                query_ref[:size, :], key_rows, (((1,), (1,)), ((), ())),
                preferred_element_type=jnp.float32,
            )
            powers = jnp.exp2(similar * INVERSE_TEMP_BITS)
            late, column = add_masses(query_ids, key_ids[:, cut:], powers)
            late_column = late_column + column
            early, column = add_masses(query_ids, key_ids[:, :cut], powers_ref[part, :])
            early_column = early_column + column
            sums_ref[part, :] = earlier_ref[part, :] + early + late
            first += size
        column_ref[...] = jnp.concatenate([early_column, late_column], axis=1)

    @pl.when(jnp.logical_not(arrived))
    def _():
        column_ref[...] = jnp.zeros_like(column_ref)
        sums_ref[...] = earlier_ref[...]


def fold_kernel(sums_ref, mass_ref, *row_refs):
    rows = mass_ref.shape[1]
    for m in range(PLANE):
        row_sum = jnp.sum(sums_ref[pl.ds(m * rows, rows), :].T, axis=0, keepdims=True)
        row_refs[m][...] = row_sum + mass_ref[...] if m == 0 else row_sum


def grid_plan(embeddings, cluster_ids):
    peers = lax.axis_size("gx")
    row_count, features = embeddings.shape
    plane_rows = PLANE * row_count
    params = pltpu.CompilerParams(vmem_limit_bytes=VMEM_BYTES)
    small = pl.CostEstimate(flops=1, bytes_accessed=1, transcendentals=0)
    vector = jax.ShapeDtypeStruct((1, row_count), jnp.float32)
    lanes = jax.ShapeDtypeStruct((plane_rows, LANES), jnp.float32)

    def rows_of(count):
        return jax.ShapeDtypeStruct((count, features), jnp.bfloat16)

    def in_plane(value, step):
        return lax.ppermute(value, "gx", [(i, i ^ step) for i in range(peers)])

    def on_line(value, moves, flip):
        pairs = [(a * PLANE + n, b * PLANE + (n ^ flip)) for a, b in moves for n in range(PLANE)]
        return lax.ppermute(value, "gx", pairs)

    first_moves = [(0, 1), (1, 2), (2, 3), (3, 0)]
    last_moves = [(0, 2), (1, 3)]
    forward_moves = [(1, 2), (2, 3)]
    first_back = [(b, a) for a, b in first_moves]
    last_back = [(b, a) for a, b in last_moves]

    half, part = row_count // 2, 5 * row_count // 8
    ranges = [(0, row_count), (0, half), (half, row_count), (part, row_count)]
    id_rows = [ID_ROWS, 0, ID_ROWS, ID_ROWS]
    first_head = on_line(embeddings[:part], first_moves, 0)
    block, *pieces, tail = pl.pallas_call(
        functools.partial(unit_kernel, ranges),
        out_shape=[rows_of(b - a + extra) for (a, b), extra in zip(ranges, id_rows)],
        cost_estimate=small,
        compiler_params=params,
    )(embeddings, cluster_ids.reshape(1, row_count))
    own_mass = pl.pallas_call(
        own_kernel, out_shape=vector, cost_estimate=small, compiler_params=params
    )(block)
    own_mass, tail = lax.optimization_barrier((own_mass, tail))
    first_tail = on_line(tail, first_moves, 0)
    across = [in_plane(piece, 2) for piece in pieces]
    sibling = in_plane(block, 1)
    last_head = on_line(first_head, first_moves, 1)
    last_tail = on_line(first_tail, forward_moves, 1)
    corner = [in_plane(piece, 1) for piece in across]
    queries = (block, sibling, *across, *corner)
    ids, first_column, first_sums, mass = pl.pallas_call(
        functools.partial(first_kernel, first_moves),
        out_shape=(lanes, vector, lanes, vector),
        cost_estimate=small,
        compiler_params=params,
    )(own_mass, first_head, first_tail, *queries)
    returned_first = on_line(first_column, first_back, 0)
    powers, rest = pl.pallas_call(
        functools.partial(middle_kernel, last_moves),
        out_shape=(
            jax.ShapeDtypeStruct((plane_rows, half), jnp.float32), rows_of(part - half)
        ),
        cost_estimate=small,
        compiler_params=params,
    )(last_head, *queries)
    last_column, sums = pl.pallas_call(
        functools.partial(last_kernel, last_moves),
        out_shape=(vector, lanes),
        cost_estimate=small,
        compiler_params=params,
    )(powers, rest, last_tail, ids, first_sums, *queries)
    returned_first, last_column = lax.optimization_barrier((returned_first, last_column))
    row_sums = pl.pallas_call(
        fold_kernel,
        out_shape=[vector] * PLANE,
        cost_estimate=small,
        compiler_params=params,
    )(sums, mass)
    returned = [in_plane(row_sums[step], step) for step in (2, 3, 1)]
    returned += [on_line(last_column, last_back, 1)]
    return jnp.log1p(sum(returned, row_sums[0] + returned_first)).reshape(row_count)


def on_device(embeddings, cluster_ids):
    if lax.axis_size("gx") == 4 * PLANE and embeddings.shape[0] == 2 * LANES:
        return grid_plan(embeddings, cluster_ids)
    return plain_plan(embeddings, cluster_ids)


def solution(mesh):
    in_specs = (P(("parts", "gx"), None), P(("parts", "gx")))
    out_specs = P(("parts", "gx"))
    return jax.shard_map(
        on_device, mesh=mesh, in_specs=in_specs, out_specs=out_specs, check_vma=False
    )
```
